32 devices in a mesh: dp: 16 (over z, y, x), tensor: 2 (over core).
Axes of the slice: x: 2, y: 2, z: 4, core: 2. Of those that a mesh axis runs over, the one named last changes fastest.
Arguments:
- tokens: bfloat16 [16, 1024, 576], P('dp', 'tensor'), may hold values from -6 to 6
- segments: int32 [16, 1024], P('dp'), may hold values from 0 to 4, as said below
- cotangent: bfloat16 [16, 1024, 576], P('dp', 'tensor'), may hold values from -6 to 6
- attn_gain: float32 [576], replicated, may hold values from 0.5 to 1.5
- w_query: bfloat16 [576, 576], replicated, may hold values from -0.25 to 0.25
- w_key: bfloat16 [576, 192], replicated, may hold values from -0.25 to 0.25
- w_value: bfloat16 [576, 192], replicated, may hold values from -0.25 to 0.25
- w_out: bfloat16 [576, 576], replicated, may hold values from -1 to 1
- ffn_gain: float32 [576], replicated, may hold values from 0.5 to 1.5
- w_gate: bfloat16 [576, 1536], P(None, 'tensor'), may hold values from -0.25 to 0.25
- w_up: bfloat16 [576, 1536], P(None, 'tensor'), may hold values from -0.25 to 0.25
- w_down: bfloat16 [1536, 576], P('tensor'), may hold values from -0.15625 to 0.15625
Outputs:
- output: bfloat16 [16, 1024, 576], P('dp', 'tensor')
- grad_input: float32 [16, 1024, 576], P('dp', 'tensor')
- grad_attn_gain: float32 [576], replicated
- grad_w_query: float32 [576, 576], replicated
- grad_w_key: float32 [576, 192], replicated
- grad_w_value: float32 [576, 192], replicated
- grad_w_out: float32 [576, 576], replicated
- grad_ffn_gain: float32 [576], replicated
- grad_w_gate: float32 [576, 1536], P(None, 'tensor')
- grad_w_up: float32 [576, 1536], P(None, 'tensor')
- grad_w_down: float32 [1536, 576], P('tensor')
The draws below stay inside these ranges and needn't reach their ends.
Inputs may be any that keep to these rules, and one draw needn't show every extreme that they name: `segments`: each row holds exactly five documents numbered 0 to 4 in order, starting at document 0 and rising by one at each document start; no document starts at positions 385 to 640, so one document of each row spans them.
All inputs are finite; a program needn't handle non-finite values.
Results may differ from the reference program's by a relative error of at most 0.023.
Values may be sent and summed in bfloat16 or wider, within the bound.
No kernel may reach another device: no remote copies, remote signals or barrier semaphores. Data moves between devices by JAX's collectives and lax.ppermute only.
A program may use at most 128 MiB of HBM per device.

```python
import jax
import jax.numpy as jnp
from jax import lax

D = 576
HEADS = 9
KV_HEADS = 3
HEAD_DIM = 64
FF = 1536
LENGTH = 1024
SEQS = 16


def draw_segments(key, part):
    key = jax.random.fold_in(key, 7)
    places = jnp.arange(LENGTH).astype(jnp.int32)
    middle_zone = (places > LENGTH // 2 - LENGTH // 8) & (places <= LENGTH // 2 + LENGTH // 8)
    eligible = (places > 0) & jnp.logical_not(middle_zone)
    random_part = jax.random.randint(key, (SEQS, LENGTH), 0, 1048576).astype(jnp.int32)
    ranking = jnp.where(eligible[None, :], random_part * LENGTH + places[None, :], -1)
    best_values, _ = lax.top_k(ranking, 4)
    threshold = best_values[:, 3:4]
    starts_new = jnp.where(ranking >= threshold, 1, 0).astype(jnp.int32)
    return jnp.cumsum(starts_new, axis=1).astype(jnp.int32)


def levels(key, extent, pieces, low, largest):
    factor_of, own = 1.0, jax.random.fold_in(key, 6)
    for dim, shards_of in pieces:
        steps = jnp.exp(jax.random.uniform(jax.random.fold_in(own, dim), (shards_of,), jnp.float32, low / len(pieces), largest / len(pieces)))
        factor_of = factor_of * jnp.repeat(steps, extent[dim] // shards_of).reshape([-1 if axis == dim else 1 for axis in range(len(extent))])
    return factor_of


def gaussian(stream_key, shape, spread, reach, split=(), kind=jnp.bfloat16):
    values = jax.random.normal(stream_key, shape, jnp.float32) * spread
    if len(split) > 0:
        values = levels(stream_key, shape, split, -0.22, 0.18) * values
    return jnp.clip(values, min=-reach, max=reach).astype(kind)


def setup_inputs(seed: int = 0) -> dict:
    key_list = jax.random.split(jax.random.key(seed), 13)
    tokens = gaussian(key_list[0], (SEQS, LENGTH, D), 1.0, 6.0, ((0, 16), (1, 2)))
    segments = draw_segments(jax.random.fold_in(key_list[12], 71), 0)
    cotangent = gaussian(key_list[2], (SEQS, LENGTH, D), 1.0, 6.0, ((0, 16), (1, 2)))
    attn_gain = jnp.clip(1.0 + 0.1 * jax.random.normal(key_list[3], (D,), jnp.float32), 0.5, 1.5)
    w_query = gaussian(key_list[4], (D, D), D ** -0.5, 0.25)
    w_key = gaussian(key_list[5], (D, KV_HEADS * HEAD_DIM), D ** -0.5, 0.25)
    w_value = gaussian(key_list[6], (D, KV_HEADS * HEAD_DIM), D ** -0.5, 0.25)
    w_out = gaussian(key_list[7], (D, D), (D // 16) ** -0.5, 1.0)
    ffn_gain = jnp.clip(1.0 + 0.1 * jax.random.normal(key_list[8], (D,), jnp.float32), 0.5, 1.5)
    w_gate = gaussian(key_list[9], (D, FF), D ** -0.5, 0.25, ((1, 2),))
    w_up = gaussian(key_list[10], (D, FF), D ** -0.5, 0.25, ((1, 2),))
    w_down = gaussian(key_list[11], (FF, D), FF ** -0.5, 0.15625, ((0, 2),))
    return dict(tokens=tokens, segments=segments, cotangent=cotangent, attn_gain=attn_gain, w_query=w_query, w_key=w_key, w_value=w_value, w_out=w_out, ffn_gain=ffn_gain, w_gate=w_gate, w_up=w_up, w_down=w_down)


@jax.custom_vjp
def low(v):
    return lax.optimization_barrier(v.astype(jnp.bfloat16)).astype(jnp.float32)

@jax.custom_vjp
def low_back(v):
    return v

def low_keep(v):
    return (low(v), None)

def low_pass(kept, grad):
    return (grad,)

def back_keep(v):
    return (v, None)

def back_low(kept, grad):
    return (low(grad),)
low.defvjp(low_keep, low_pass)
low_back.defvjp(back_keep, back_low)
EPSILON = 1e-05

def rms_norm(values, gain_vec):
    return values * lax.rsqrt(lax.optimization_barrier(jnp.mean(values * values, axis=-1, keepdims=True)) + EPSILON) * gain_vec

def rotate(values, cos_table, sin_table):
    half_dim = values.shape[-1] // 2
    front_part = values[..., :half_dim]
    back_part = values[..., half_dim:]
    return jnp.concatenate([front_part * cos_table - back_part * sin_table, back_part * cos_table + front_part * sin_table], axis=-1)

def tables(positions):
    half_dim = HEAD_DIM // 2
    inverse = 10000.0 ** (-2.0 * jnp.arange(half_dim).astype(jnp.float32) / HEAD_DIM)
    angles = positions[:, None] * inverse[None, :]
    return (jnp.cos(angles)[:, None, :], jnp.sin(angles)[:, None, :])

def matmul(left_mat, right_mat):
    return jnp.dot(left_mat, right_mat, precision=lax.Precision.HIGHEST)

def block(stream, allowed, cos_table, sin_table, params):
    attn_gain, w_query, w_key, w_value, w_out, ffn_gain, w_gate, w_up, w_down = params
    group_size = HEADS // KV_HEADS
    normed = low(rms_norm(stream, attn_gain))
    query_pre = low_back(matmul(normed, w_query)).reshape(LENGTH, HEADS, HEAD_DIM)
    key_pre = low_back(matmul(normed, w_key)).reshape(LENGTH, KV_HEADS, HEAD_DIM)
    value_low = low(low_back(matmul(normed, w_value))).reshape(LENGTH, KV_HEADS, HEAD_DIM)
    query_rot = low(rotate(query_pre, cos_table, sin_table)).reshape(LENGTH, KV_HEADS, group_size, HEAD_DIM)
    key_rot = low(rotate(key_pre, cos_table, sin_table))
    scores = jnp.einsum('qgrd,kgd->grqk', query_rot, key_rot, precision=lax.Precision.HIGHEST)
    scores = low_back(scores * HEAD_DIM ** (-0.5))
    scores = jnp.where(allowed[None, None], scores, -1e+30)
    top_score = lax.optimization_barrier(jnp.max(scores, axis=-1, keepdims=True))
    exp_scores = jnp.exp(scores - top_score)
    attn_probs = low(exp_scores / lax.optimization_barrier(jnp.sum(exp_scores, axis=-1, keepdims=True)))
    context = jnp.einsum('grqk,kgd->qgrd', attn_probs, value_low, precision=lax.Precision.HIGHEST).reshape(LENGTH, D)
    context = low_back(low(context))
    middle = stream + low_back(matmul(context, w_out))
    ffn_in = low(rms_norm(middle, ffn_gain))
    gate_pre = low_back(matmul(ffn_in, w_gate))
    up_pre = low_back(matmul(ffn_in, w_up))
    product = low(jax.nn.silu(gate_pre) * up_pre)
    return middle + low_back(matmul(product, w_down))

def reference(tokens, segments, cotangent, attn_gain, w_query, w_key, w_value, w_out, ffn_gain, w_gate, w_up, w_down):
    params = tuple((array_in.astype(jnp.float32) for array_in in (attn_gain, w_query, w_key, w_value, w_out, ffn_gain, w_gate, w_up, w_down)))
    positions = jnp.arange(LENGTH).astype(jnp.float32)
    cos_table, sin_table = tables(positions)
    causal = positions[:, None] >= positions[None, :]

    def per_sequence(totals, operands):
        stream, labels, upstream = operands
        allowed = causal & (labels[:, None] == labels[None, :])

        def forward(start_stream, weights):
            first_pass = block(start_stream, allowed, cos_table, sin_table, weights)
            return block(first_pass, allowed, cos_table, sin_table, weights)
        result, pull = jax.vjp(forward, stream.astype(jnp.float32), params)
        grad_stream, grad_params = pull(upstream.astype(jnp.float32))
        new_totals = tuple((left_sum + right_sum for left_sum, right_sum in zip(totals, grad_params)))
        return (new_totals, (result.astype(jnp.bfloat16), grad_stream))
    zeros_init = tuple((jnp.zeros(array_in.shape, jnp.float32) for array_in in params))
    grad_sums, (outputs, grad_inputs) = lax.scan(per_sequence, zeros_init, (tokens, segments, cotangent))
    return (outputs, grad_inputs) + grad_sums
```

```python
import math

import jax
import jax.numpy as jnp
from jax import lax
from jax.experimental import pallas as pl
from jax.experimental.pallas import tpu as pltpu
from jax.sharding import PartitionSpec as P

HEADS = 9
KV_HEADS = 3
GROUP = HEADS // KV_HEADS
HEAD_DIM = 64
HALF = HEAD_DIM // 2
EPSILON = 1e-05
MASKED = -1e30
BLOCK = 256
SCALE = HEAD_DIM ** (-0.5)
F32 = jnp.float32
BF16 = jnp.bfloat16
VMEM_LIMIT = 50 * 2**20


def dot(left, right, left_dim, right_dim):
    return lax.dot_general(
        left, right, (((left_dim,), (right_dim,)), ((), ())), preferred_element_type=F32
    )


def pieces(size, step):
    return [slice(start, start + step) for start in range(0, size, step)]


def inverse_rms(x_ref):
    total = None
    for rows in pieces(x_ref.shape[0], 64):
        x = x_ref[rows, :]
        part = jnp.sum(x * x, axis=0, keepdims=True)
        total = part if total is None else total + part
    return lax.rsqrt(total / x_ref.shape[0] + EPSILON)


def norm_forward(x_ref, gain_ref, out_ref):
    scale = inverse_rms(x_ref)
    for rows in pieces(x_ref.shape[0], 64):
        out_ref[rows, :] = (x_ref[rows, :] * scale * gain_ref[rows, :]).astype(BF16)


def norm_backward(x_ref, gain_ref, grad_ref, add_ref, out_ref, gain_grad_ref):
    scale = inverse_rms(x_ref)
    inner = None
    for rows in pieces(x_ref.shape[0], 64):
        x, e = x_ref[rows, :], grad_ref[rows, :]
        xe = x * e
        gain_grad_ref[rows, :] = jnp.sum(xe * scale, axis=1, keepdims=True)
        part = jnp.sum(xe * gain_ref[rows, :], axis=0, keepdims=True)
        inner = part if inner is None else inner + part
    cubed = scale * scale * scale * (inner / x_ref.shape[0])
    for rows in pieces(x_ref.shape[0], 64):
        out_ref[rows, :] = (
            add_ref[rows, :].astype(F32)
            + scale * gain_ref[rows, :] * grad_ref[rows, :]
            - x_ref[rows, :] * cubed
        )


def rotated(x, cos_table, sin_table):
    front, back = x[:HALF], x[HALF:]
    return jnp.concatenate(
        [front * cos_table - back * sin_table, back * cos_table + front * sin_table], axis=0
    )


def project_qkv(normed_ref, wq_ref, wk_ref, wv_ref, cos_ref, sin_ref, q_ref, kv_ref):
    normed = normed_ref[...]
    cos_table, sin_table = cos_ref[...], sin_ref[...]
    key = dot(wk_ref[...], normed, 0, 0)
    for head in pieces(KV_HEADS * HEAD_DIM, HEAD_DIM):
        kv_ref[head, :] = rotated(key[head], cos_table, sin_table).astype(BF16)
    kv_ref[KV_HEADS * HEAD_DIM :, :] = dot(wv_ref[...], normed, 0, 0).astype(BF16)
    query = dot(wq_ref[...], normed, 0, 0)
    for head in pieces(HEADS * HEAD_DIM, HEAD_DIM):
        q_ref[head, :] = (rotated(query[head], cos_table, sin_table) * SCALE).astype(BF16)


def first_kernel(
    tokens_ref, gain_ref, wq_ref, wk_ref, wv_ref, cos_ref, sin_ref, x_ref, normed_ref, q_ref, kv_ref
):
    x_ref[...] = tokens_ref[...].astype(F32).T
    norm_forward(x_ref, gain_ref, normed_ref)
    project_qkv(normed_ref, wq_ref, wk_ref, wv_ref, cos_ref, sin_ref, q_ref, kv_ref)


def load_keys(core, own_ref, other_ref, all_ref, tok_ref):
    half = own_ref.shape[1]
    all_ref[core] = own_ref[...]
    all_ref[1 - core] = other_ref[...]
    for part in range(2):
        for head in range(2 * KV_HEADS):
            rows = slice(head * HEAD_DIM, (head + 1) * HEAD_DIM)
            tok_ref[head, part * half : (part + 1) * half, :] = all_ref[part, rows, :].T


def set_mask(bias_ref, place, kb, doc_start):
    key_place = kb * BLOCK + lax.broadcasted_iota(jnp.int32, (BLOCK, BLOCK), 0)
    bias_ref[...] = jnp.where((key_place >= doc_start) & (key_place <= place), 0.0, MASKED)


def attend_kernel(
    info_ref, start_ref, q_ref, own_ref, other_ref, ctx_ref, lse_ref,
    all_ref, tok_ref, bias_ref, m_ref, l_ref, acc_ref,
):
    core = info_ref[0]
    half = own_ref.shape[1]
    tiles = half // BLOCK
    load_keys(core, own_ref, other_ref, all_ref, tok_ref)
    for tile in range(tiles):
        cols = slice(tile * BLOCK, (tile + 1) * BLOCK)
        doc_start = start_ref[0:1, cols]
        place = core * half + tile * BLOCK + lax.broadcasted_iota(jnp.int32, (1, BLOCK), 1)
        m_ref[...] = jnp.full(m_ref.shape, MASKED, F32)
        l_ref[...] = jnp.zeros(l_ref.shape, F32)
        acc_ref[...] = jnp.zeros(acc_ref.shape, F32)

        def step(kb, carry):
            set_mask(bias_ref, place, kb, doc_start)
            part, inside = kb // tiles, kb % tiles
            keys = pl.ds(pl.multiple_of(kb * BLOCK, BLOCK), BLOCK)
            inner = pl.ds(pl.multiple_of(inside * BLOCK, BLOCK), BLOCK)
            for group in range(KV_HEADS):
                key = tok_ref[group, keys, :]
                value = all_ref[
                    part, (KV_HEADS + group) * HEAD_DIM : (KV_HEADS + group + 1) * HEAD_DIM, inner
                ]
                for head in range(group * GROUP, (group + 1) * GROUP):
                    rows = slice(head * HEAD_DIM, (head + 1) * HEAD_DIM)
                    scores = dot(key, q_ref[rows, cols], 1, 0) + bias_ref[...]
                    m_old = m_ref[head : head + 1, :]
                    m_new = jnp.maximum(m_old, jnp.max(scores, axis=0, keepdims=True))
                    probs = jnp.exp(scores - m_new)
                    fade = jnp.exp(m_old - m_new)
                    m_ref[head : head + 1, :] = m_new
                    l_ref[head : head + 1, :] = l_ref[head : head + 1, :] * fade + jnp.sum(
                        probs, axis=0, keepdims=True
                    )
                    acc_ref[rows, :] = acc_ref[rows, :] * fade + dot(
                        value, probs.astype(BF16), 1, 0
                    )
            return carry

        lax.fori_loop(info_ref[1 + tile], core * tiles + tile + 1, step, 0)
        for head in range(HEADS):
            rows = slice(head * HEAD_DIM, (head + 1) * HEAD_DIM)
            total = l_ref[head : head + 1, :]
            ctx_ref[rows, cols] = acc_ref[rows, :] * (1.0 / total)
            lse_ref[head : head + 1, cols] = m_ref[head : head + 1, :] + jnp.log(total)


def attend_back_kernel(
    info_ref, start_ref, q_ref, own_ref, other_ref, ctx_ref, lse_ref, grad_ref,
    dq_ref, dkv_own_ref, dkv_other_ref,
    all_ref, tok_ref, bias_ref, delta_ref, dkv_ref,
):
    core = info_ref[0]
    half = own_ref.shape[1]
    tiles = half // BLOCK
    load_keys(core, own_ref, other_ref, all_ref, tok_ref)
    dkv_ref[...] = jnp.zeros(dkv_ref.shape, F32)
    for head in range(HEADS):
        rows = slice(head * HEAD_DIM, (head + 1) * HEAD_DIM)
        delta_ref[head : head + 1, :] = jnp.sum(
            grad_ref[rows, :].astype(F32) * ctx_ref[rows, :], axis=0, keepdims=True
        )
    for tile in range(tiles):
        cols = slice(tile * BLOCK, (tile + 1) * BLOCK)
        doc_start = start_ref[0:1, cols]
        place = core * half + tile * BLOCK + lax.broadcasted_iota(jnp.int32, (1, BLOCK), 1)
        dq_ref[:, cols] = jnp.zeros((HEADS * HEAD_DIM, BLOCK), F32)

        def step(kb, carry):
            set_mask(bias_ref, place, kb, doc_start)
            part, inside = kb // tiles, kb % tiles
            keys = pl.ds(pl.multiple_of(kb * BLOCK, BLOCK), BLOCK)
            inner = pl.ds(pl.multiple_of(inside * BLOCK, BLOCK), BLOCK)
            for group in range(KV_HEADS):
                key = tok_ref[group, keys, :]
                value = tok_ref[KV_HEADS + group, keys, :]
                key_rows = slice(group * HEAD_DIM, (group + 1) * HEAD_DIM)
                value_rows = slice((KV_HEADS + group) * HEAD_DIM, (KV_HEADS + group + 1) * HEAD_DIM)
                key_cols = all_ref[part, key_rows, inner]
                dk = dkv_ref[part, key_rows, inner]
                dv = dkv_ref[part, value_rows, inner]
                for head in range(group * GROUP, (group + 1) * GROUP):
                    rows = slice(head * HEAD_DIM, (head + 1) * HEAD_DIM)
                    query = q_ref[rows, cols]
                    grad = grad_ref[rows, cols]
                    scores = dot(key, query, 1, 0) + bias_ref[...]
                    probs = jnp.exp(scores - lse_ref[head : head + 1, cols])
                    grad_probs = dot(value, grad, 1, 0)
                    grad_scores = (probs * (grad_probs - delta_ref[head : head + 1, cols])).astype(
                        BF16
                    )
                    dv = dv + dot(grad, probs.astype(BF16), 1, 1)
                    dk = dk + dot(query, grad_scores, 1, 1)
                    dq_ref[rows, cols] += dot(key_cols, grad_scores, 1, 0)
                dkv_ref[part, key_rows, inner] = dk
                dkv_ref[part, value_rows, inner] = dv
            return carry

        lax.fori_loop(info_ref[1 + tile], core * tiles + tile + 1, step, 0)
    dkv_own_ref[...] = dkv_ref[core]
    dkv_other_ref[...] = dkv_ref[1 - core].astype(BF16)


def attend_out(x_ref, ctx_ref, wo_ref, ctx_low_ref, mid_ref):
    ctx_low_ref[...] = ctx_ref[...].astype(BF16)
    mid_ref[...] = x_ref[...] + dot(wo_ref[...], ctx_low_ref[...], 0, 0)


def middle_kernel(
    x_ref, ctx_ref, wo_ref, ffn_gain_ref, wg_refs, wu_refs, wd_refs,
    gain_ref, wq_ref, wk_ref, wv_ref, cos_ref, sin_ref,
    ctx_low_ref, mid_ref, ffn_ref, x2_ref, normed_ref, q_ref, kv_ref,
):
    attend_out(x_ref, ctx_ref, wo_ref, ctx_low_ref, mid_ref)
    norm_forward(mid_ref, ffn_gain_ref, ffn_ref)
    ffn_in = ffn_ref[...]
    x2_ref[...] = mid_ref[...]
    for part in range(2):
        for hidden in pieces(wg_refs[part].shape[1], BLOCK):
            gate = dot(wg_refs[part][:, hidden], ffn_in, 0, 0)
            up = dot(wu_refs[part][:, hidden], ffn_in, 0, 0)
            product = (gate * jax.nn.sigmoid(gate) * up).astype(BF16)
            x2_ref[...] += dot(wd_refs[part][hidden, :], product, 0, 0)
    norm_forward(x2_ref, gain_ref, normed_ref)
    project_qkv(normed_ref, wq_ref, wk_ref, wv_ref, cos_ref, sin_ref, q_ref, kv_ref)


def ffn_terms(gate, up, grad_product):
    sig = jax.nn.sigmoid(gate)
    silu = gate * sig
    grad_gate = (grad_product * up * (sig + silu * (1.0 - sig))).astype(BF16)
    grad_up = (grad_product * silu).astype(BF16)
    return (silu * up).astype(BF16), grad_gate, grad_up


def out_back(grad_mid_ref, ctx_low_ref, wo_ref, low_ref, dwo_ref, grad_ctx_ref, earlier_ref):
    low_ref[...] = grad_mid_ref[...].astype(BF16)
    low = low_ref[...]
    term = dot(low, ctx_low_ref[...], 1, 1)
    dwo_ref[...] = term if earlier_ref is None else term + earlier_ref[...]
    grad_ctx_ref[...] = dot(wo_ref[...], low, 1, 0).astype(BF16)


def turn_kernel(
    x_ref, ctx_ref, wo_ref, ffn_gain_ref, wg_refs, wu_refs, wd_refs, cotangent_ref,
    output_ref, grad_low_ref, ffn_ref, prod_ref, gg_ref, gu_ref,
    grad_mid_ref, dwo_ref, grad_ctx_ref, dgain_ref,
    mid_ref, ctx_low_ref, acc_ref, low_ref,
):
    attend_out(x_ref, ctx_ref, wo_ref, ctx_low_ref, mid_ref)
    norm_forward(mid_ref, ffn_gain_ref, ffn_ref)
    ffn_in = ffn_ref[...]
    grad_low_ref[...] = cotangent_ref[...].T
    grad_low = grad_low_ref[...]
    half_hidden = wg_refs[0].shape[1]
    acc_ref[...] = mid_ref[...]
    grad_mid_ref[...] = jnp.zeros(grad_mid_ref.shape, F32)
    for part in range(2):
        for hidden in pieces(half_hidden, BLOCK):
            rows = slice(part * half_hidden + hidden.start, part * half_hidden + hidden.stop)
            gate = dot(wg_refs[part][:, hidden], ffn_in, 0, 0)
            up = dot(wu_refs[part][:, hidden], ffn_in, 0, 0)
            grad_product = dot(wd_refs[part][hidden, :], grad_low, 1, 0)
            product, grad_gate, grad_up = ffn_terms(gate, up, grad_product)
            prod_ref[rows, :] = product
            gg_ref[rows, :] = grad_gate
            gu_ref[rows, :] = grad_up
            acc_ref[...] += dot(wd_refs[part][hidden, :], product, 0, 0)
            grad_mid_ref[...] += dot(wg_refs[part][:, hidden], grad_gate, 1, 0) + dot(
                wu_refs[part][:, hidden], grad_up, 1, 0
            )
    output_ref[...] = acc_ref[...].T.astype(BF16)
    acc_ref[...] = grad_mid_ref[...]
    norm_backward(mid_ref, ffn_gain_ref, acc_ref, grad_low_ref, grad_mid_ref, dgain_ref)
    out_back(grad_mid_ref, ctx_low_ref, wo_ref, low_ref, dwo_ref, grad_ctx_ref, None)


def qkv_back(
    dq_ref, dkv_own_ref, dkv_got_ref, normed_ref, wq_ref, wk_ref, wv_ref, cos_ref, sin_ref,
    dpre_ref, dw_ref, dnormed_ref, earlier_ref,
):
    cos_table, sin_table = cos_ref[...], sin_ref[...]
    width, kv_width = HEADS * HEAD_DIM, KV_HEADS * HEAD_DIM
    for head in pieces(width, HEAD_DIM):
        dpre_ref[head, :] = rotated(dq_ref[head, :] * SCALE, cos_table, -sin_table).astype(BF16)
    for head in pieces(kv_width, HEAD_DIM):
        total = dkv_own_ref[head, :] + dkv_got_ref[head, :].astype(F32)
        rows = slice(width + head.start, width + head.stop)
        dpre_ref[rows, :] = rotated(total, cos_table, -sin_table).astype(BF16)
    dpre_ref[width + kv_width :, :] = (
        dkv_own_ref[kv_width:, :] + dkv_got_ref[kv_width:, :].astype(F32)
    ).astype(BF16)
    term = dot(dpre_ref[...], normed_ref[...], 1, 1)
    dw_ref[...] = term if earlier_ref is None else term + earlier_ref[...]
    dnormed_ref[...] = (
        dot(wq_ref[...], dpre_ref[:width, :], 1, 0)
        + dot(wk_ref[...], dpre_ref[width : width + kv_width, :], 1, 0)
        + dot(wv_ref[...], dpre_ref[width + kv_width :, :], 1, 0)
    )


def between_kernel(
    dq_ref, dkv_own_ref, dkv_got_ref, normed_ref, x_ref, grad_mid_ref,
    gain_ref, wq_ref, wk_ref, wv_ref, cos_ref, sin_ref,
    mid1_ref, ffn1_ref, ctx_low1_ref, wo_ref, ffn_gain_ref, wg_refs, wu_refs, wd_refs,
    ffn2_ref, low2_ref, prod2_ref, gg2_ref, gu2_ref, dwo2_ref,
    dwqkv_ref, dgain_ref, grad_mid1_ref, dwo_ref, grad_ctx_ref, dffn_gain_ref,
    dwg_refs, dwu_refs, dwd_refs,
    dpre_ref, dnormed_ref, gstream_ref, low_ref, acc_ref,
):
    qkv_back(
        dq_ref, dkv_own_ref, dkv_got_ref, normed_ref, wq_ref, wk_ref, wv_ref, cos_ref, sin_ref,
        dpre_ref, dwqkv_ref, dnormed_ref, None,
    )
    norm_backward(x_ref, gain_ref, dnormed_ref, grad_mid_ref, gstream_ref, dgain_ref)
    low_ref[...] = gstream_ref[...].astype(BF16)
    low = low_ref[...]
    ffn_in = ffn1_ref[...]
    half_hidden = wg_refs[0].shape[1]
    acc_ref[...] = jnp.zeros(acc_ref.shape, F32)
    for part in range(2):
        for hidden in pieces(half_hidden, BLOCK):
            rows = slice(part * half_hidden + hidden.start, part * half_hidden + hidden.stop)
            gate = dot(wg_refs[part][:, hidden], ffn_in, 0, 0)
            up = dot(wu_refs[part][:, hidden], ffn_in, 0, 0)
            grad_product = dot(wd_refs[part][hidden, :], low, 1, 0)
            product, grad_gate, grad_up = ffn_terms(gate, up, grad_product)
            acc_ref[...] += dot(wg_refs[part][:, hidden], grad_gate, 1, 0) + dot(
                wu_refs[part][:, hidden], grad_up, 1, 0
            )
            dwg_refs[part][:, hidden] = (
                dot(ffn_in, grad_gate, 1, 1) + dot(ffn2_ref[...], gg2_ref[rows, :], 1, 1)
            ).astype(BF16)
            dwu_refs[part][:, hidden] = (
                dot(ffn_in, grad_up, 1, 1) + dot(ffn2_ref[...], gu2_ref[rows, :], 1, 1)
            ).astype(BF16)
            dwd_refs[part][hidden, :] = (
                dot(product, low, 1, 1) + dot(prod2_ref[rows, :], low2_ref[...], 1, 1)
            ).astype(BF16)
    norm_backward(mid1_ref, ffn_gain_ref, acc_ref, gstream_ref, grad_mid1_ref, dffn_gain_ref)
    out_back(grad_mid1_ref, ctx_low1_ref, wo_ref, low_ref, dwo_ref, grad_ctx_ref, dwo2_ref)


def last_kernel(
    dq_ref, dkv_own_ref, dkv_got_ref, normed_ref, x_ref, grad_mid_ref,
    gain_ref, wq_ref, wk_ref, wv_ref, cos_ref, sin_ref, dwqkv2_ref,
    dwqkv_ref, dgain_ref, out_ref,
    dpre_ref, dnormed_ref, gstream_ref,
):
    qkv_back(
        dq_ref, dkv_own_ref, dkv_got_ref, normed_ref, wq_ref, wk_ref, wv_ref, cos_ref, sin_ref,
        dpre_ref, dwqkv_ref, dnormed_ref, dwqkv2_ref,
    )
    norm_backward(x_ref, gain_ref, dnormed_ref, grad_mid_ref, gstream_ref, dgain_ref)
    out_ref[...] = gstream_ref[...].T


def shape(dims, dtype):
    return jax.ShapeDtypeStruct(dims, dtype)


def run(kernel, args, outs, scratch=(), smem=0, name=None):
    leaves, tree = jax.tree.flatten(args)
    out_leaves, out_tree = jax.tree.flatten(outs)
    n_in, n_out = len(leaves), len(out_leaves)

    def body(*refs):
        ins = jax.tree.unflatten(tree, refs[:n_in])
        results = jax.tree.unflatten(out_tree, refs[n_in : n_in + n_out])
        kernel(*ins, *results, *refs[n_in + n_out :])

    in_specs = [
        pl.BlockSpec(memory_space=pltpu.SMEM if index < smem else pltpu.VMEM)
        for index in range(n_in)
    ]
    results = pl.pallas_call(
        body,
        out_shape=out_leaves,
        in_specs=in_specs,
        out_specs=[pl.BlockSpec(memory_space=pltpu.VMEM)] * n_out,
        scratch_shapes=list(scratch),
        compiler_params=pltpu.CompilerParams(vmem_limit_bytes=VMEM_LIMIT),
        name=name,
    )(*leaves)
    return jax.tree.unflatten(out_tree, results)


def swap(array):
    return lax.ppermute(array, "tensor", [(0, 1), (1, 0)])


def partners(sizes, bits):
    n, cores = sizes
    return [
        (place * cores + core, (place ^ (1 << bits[core])) * cores + core)
        for place in range(n)
        for core in range(cores)
    ]


def reduce_chunks(array, sizes, orders):
    n, cores = sizes
    steps = len(orders[0])
    if n != 1 << steps:
        return lax.psum(array.astype(F32), "dp").astype(BF16)
    place = lax.axis_index("dp")
    core = lax.axis_index("tensor")
    bits = [
        jnp.where(core == 0, (place >> orders[0][step]) & 1, (place >> orders[1][step]) & 1)
        for step in range(steps)
    ]
    perms = [partners(sizes, (orders[0][step], orders[1][step])) for step in range(steps)]
    rest = array.shape[1:]
    for step in range(steps):
        halves = array.reshape((2, -1) + rest)
        kept = lax.dynamic_index_in_dim(halves, bits[step], 0, keepdims=False)
        sent = lax.dynamic_index_in_dim(halves, 1 - bits[step], 0, keepdims=False)
        got = lax.ppermute(sent, ("dp", "tensor"), perms[step])
        array = (kept.astype(F32) + got.astype(F32)).astype(BF16)
    for step in reversed(range(steps)):
        got = lax.ppermute(array, ("dp", "tensor"), perms[step])
        array = jnp.where(
            bits[step] == 0, jnp.concatenate([array, got]), jnp.concatenate([got, array])
        )
    return array


def sum_small(array, sizes):
    n, _ = sizes
    array = array + swap(array)
    steps = int(math.log2(n))
    if n != 1 << steps:
        return lax.psum(array, "dp")
    for step in range(steps):
        array = array + lax.ppermute(array, "dp", [(i, i ^ (1 << step)) for i in range(n)])
    return array


def per_device(
    sizes, tokens, segments, cotangent, attn_gain, w_query, w_key, w_value, w_out, ffn_gain,
    w_gate, w_up, w_down,
):
    _, half, width = tokens.shape
    kv_width = KV_HEADS * HEAD_DIM
    hidden = w_gate.shape[1]
    core = lax.axis_index("tensor")
    offset = core * half
    tokens, cotangent = tokens[0], cotangent[0]
    segments = segments[0]

    place = (offset + jnp.arange(half)).astype(F32)
    inverse = 10000.0 ** (-2.0 * jnp.arange(HALF).astype(F32) / HEAD_DIM)
    angles = inverse[:, None] * place[None, :]
    tables = (jnp.cos(angles), jnp.sin(angles))
    own_labels = lax.dynamic_slice_in_dim(segments, offset, half, 0)
    doc_start = jnp.sum((segments[:, None] < own_labels[None, :]).astype(jnp.int32), axis=0)
    info = jnp.concatenate([core[None], doc_start[::BLOCK] // BLOCK]).astype(jnp.int32)
    doc_start = doc_start[None, :]

    gate_pair = (w_gate, swap(w_gate))
    up_pair = (w_up, swap(w_up))
    down_pair = (w_down, swap(w_down))
    gain_col, ffn_gain_col = attn_gain[:, None], ffn_gain[:, None]
    projections = (w_query, w_key, w_value)

    act = shape((width, half), F32)
    low = shape((width, half), BF16)
    kv = shape((2 * kv_width, half), BF16)
    wide = shape((2 * hidden, half), BF16)
    column = shape((width, 1), F32)
    key_scratch = [
        pltpu.VMEM((2, 2 * kv_width, half), BF16),
        pltpu.VMEM((2 * KV_HEADS, 2 * half, HEAD_DIM), BF16),
        pltpu.VMEM((BLOCK, BLOCK), F32),
    ]
    act_scratch = pltpu.VMEM((width, half), F32)
    low_scratch = pltpu.VMEM((width, half), BF16)

    def attend(query, kv_own, kv_other):
        return run(
            attend_kernel,
            (info, doc_start, query, kv_own, kv_other),
            (act, shape((16, half), F32)),
            key_scratch
            + [pltpu.VMEM((16, BLOCK), F32), pltpu.VMEM((16, BLOCK), F32),
               pltpu.VMEM((width, BLOCK), F32)],
            smem=1,
            name="attend",
        )

    def attend_back(query, kv_own, kv_other, ctx, lse, grad):
        return run(
            attend_back_kernel,
            (info, doc_start, query, kv_own, kv_other, ctx, lse, grad),
            (act, shape((2 * kv_width, half), F32), kv),
            key_scratch
            + [pltpu.VMEM((16, half), F32), pltpu.VMEM((2, 2 * kv_width, half), F32)],
            smem=1,
            name="attend_back",
        )

    x1, normed1, query1, kv1 = run(
        first_kernel, (tokens, gain_col) + projections + tables, (act, low, low, kv), name="first"
    )
    kv1_other = swap(kv1)
    ctx1, lse1 = attend(query1, kv1, kv1_other)
    ctx_low1, mid1, ffn1, x2, normed2, query2, kv2 = run(
        middle_kernel,
        (x1, ctx1, w_out, ffn_gain_col, gate_pair, up_pair, down_pair, gain_col)
        + projections + tables,
        (low, act, low, act, low, low, kv),
        name="middle",
    )
    kv2_other = swap(kv2)
    ctx2, lse2 = attend(query2, kv2, kv2_other)
    (
        output, grad_low2, ffn2, prod2, gg2, gu2, grad_mid2, dwo2, grad_ctx2, dffn_gain2,
    ) = run(
        turn_kernel,
        (x2, ctx2, w_out, ffn_gain_col, gate_pair, up_pair, down_pair, cotangent),
        (shape((half, width), BF16), low, low, wide, wide, wide, act,
         shape((width, width), F32), low, column),
        [act_scratch, low_scratch, act_scratch, low_scratch],
        name="turn",
    )
    dq2, dkv_own2, dkv_sent2 = attend_back(query2, kv2, kv2_other, ctx2, lse2, grad_ctx2)
    dkv_got2 = swap(dkv_sent2)
    half_in = shape((width, hidden), BF16)
    half_out = shape((hidden, width), BF16)
    qkv_scratch = [
        pltpu.VMEM((width + 2 * kv_width, half), BF16), act_scratch, act_scratch,
    ]
    dw_qkv_shape = shape((width + 2 * kv_width, width), F32)
    (
        dw_qkv2, dgain2, grad_mid1, dwo, grad_ctx1, dffn_gain1, dw_gate, dw_up, dw_down,
    ) = run(
        between_kernel,
        (dq2, dkv_own2, dkv_got2, normed2, x2, grad_mid2, gain_col) + projections + tables
        + (mid1, ffn1, ctx_low1, w_out, ffn_gain_col, gate_pair, up_pair, down_pair,
           ffn2, grad_low2, prod2, gg2, gu2, dwo2),
        (dw_qkv_shape, column, act, shape((width, width), F32), low, column,
         (half_in, half_in), (half_in, half_in), (half_out, half_out)),
        qkv_scratch + [low_scratch, act_scratch],
        name="between",
    )
    n = sizes[0]
    steps = int(math.log2(n))
    order_a = list(range(steps))
    order_b = [1, 0] + order_a[2:] if steps > 1 else order_a
    orders = (order_a, order_b)

    def to_chunks(array):
        return array.reshape((n, -1) + array.shape[1:])

    def pair_sum(pair):
        return (pair[0].astype(F32) + swap(pair[1]).astype(F32)).astype(BF16)

    gate_up = jnp.concatenate([pair_sum(dw_gate), pair_sum(dw_up)], axis=0)
    gate_up = reduce_chunks(to_chunks(gate_up), sizes, orders)
    gate_up = gate_up.reshape(2, width, hidden).astype(F32)
    down = reduce_chunks(to_chunks(pair_sum(dw_down)), sizes, orders)
    down = down.reshape(hidden, width).astype(F32)

    dq1, dkv_own1, dkv_sent1 = attend_back(query1, kv1, kv1_other, ctx1, lse1, grad_ctx1)
    dkv_got1 = swap(dkv_sent1)
    dw_qkv, dgain1, grad_input = run(
        last_kernel,
        (dq1, dkv_own1, dkv_got1, normed1, x1, grad_mid1, gain_col) + projections + tables
        + (dw_qkv2,),
        (dw_qkv_shape, column, shape((half, width), F32)),
        qkv_scratch,
        name="last",
    )
    packed = jnp.concatenate([dw_qkv, dwo], axis=0).astype(BF16)
    rows = packed.shape[0] // 2
    mine = lax.dynamic_slice_in_dim(packed, core * rows, rows, 0)
    theirs = lax.dynamic_slice_in_dim(packed, (1 - core) * rows, rows, 0)
    part = (mine.astype(F32) + swap(theirs).astype(F32)).astype(BF16)
    part = reduce_chunks(to_chunks(part), sizes, orders).reshape(rows, width)
    got = swap(part)
    packed = jnp.where(
        core == 0, jnp.concatenate([part, got]), jnp.concatenate([got, part])
    ).astype(F32).T
    gains = jnp.concatenate([dgain1 + dgain2, dffn_gain1 + dffn_gain2], axis=1).T
    gains = sum_small(gains, sizes)
    ends = (width, width + kv_width, width + 2 * kv_width)
    return (
        output[None],
        grad_input[None],
        gains[0],
        packed[:, : ends[0]],
        packed[:, ends[0] : ends[1]],
        packed[:, ends[1] : ends[2]],
        packed[:, ends[2] :],
        gains[1],
        gate_up[0],
        gate_up[1],
        down,
    )


def solution(mesh):
    sizes = (mesh.shape["dp"], mesh.shape["tensor"])

    def local(*args):
        return per_device(sizes, *args)

    split = P("dp", "tensor", None)
    in_specs = (
        split, P("dp", None), split, P(), P(), P(), P(), P(), P(),
        P(None, "tensor"), P(None, "tensor"), P("tensor", None),
    )
    out_specs = (
        split, split, P(), P(), P(), P(), P(), P(),
        P(None, "tensor"), P(None, "tensor"), P("tensor", None),
    )
    return jax.shard_map(
        local, mesh=mesh, in_specs=in_specs, out_specs=out_specs, check_vma=False
    )
```

```python
import jax
import jax.numpy as jnp
from jax import lax
from jax.experimental import pallas as pl
from jax.experimental.pallas import tpu as pltpu
from jax.sharding import PartitionSpec as P

HEADS = 9
KV_HEADS = 3
GROUP = HEADS // KV_HEADS
HEAD_DIM = 64
HALF = HEAD_DIM // 2
EPSILON = 1e-05
MASKED = -1e30
BLOCK = 256
SCALE = HEAD_DIM ** (-0.5)
F32 = jnp.float32
BF16 = jnp.bfloat16
VMEM_LIMIT = 16 * 2**20


def dot(left, right, left_dim, right_dim):
    return lax.dot_general(
        left, right, (((left_dim,), (right_dim,)), ((), ())), preferred_element_type=F32
    )


def pieces(size, step):
    return [slice(start, start + step) for start in range(0, size, step)]


def inverse_rms(x_ref):
    total = None
    for rows in pieces(x_ref.shape[0], 64):
        x = x_ref[rows, :]
        part = jnp.sum(x * x, axis=0, keepdims=True)
        total = part if total is None else total + part
    return lax.rsqrt(total / x_ref.shape[0] + EPSILON)


def norm_forward(x_ref, gain_ref, out_ref):
    scale = inverse_rms(x_ref)
    for rows in pieces(x_ref.shape[0], 64):
        out_ref[rows, :] = (x_ref[rows, :] * scale * gain_ref[rows, :]).astype(BF16)


def norm_backward(x_ref, gain_ref, grad_ref, add_ref, out_ref, gain_grad_ref):
    scale = inverse_rms(x_ref)
    inner = None
    for rows in pieces(x_ref.shape[0], 64):
        x, e = x_ref[rows, :], grad_ref[rows, :]
        xe = x * e
        gain_grad_ref[rows, :] = jnp.sum(xe * scale, axis=1, keepdims=True)
        part = jnp.sum(xe * gain_ref[rows, :], axis=0, keepdims=True)
        inner = part if inner is None else inner + part
    cubed = scale * scale * scale * (inner / x_ref.shape[0])
    for rows in pieces(x_ref.shape[0], 64):
        out_ref[rows, :] = (
            add_ref[rows, :].astype(F32)
            + scale * gain_ref[rows, :] * grad_ref[rows, :]
            - x_ref[rows, :] * cubed
        )


def rotated(x, cos_table, sin_table):
    front, back = x[:HALF], x[HALF:]
    return jnp.concatenate(
        [front * cos_table - back * sin_table, back * cos_table + front * sin_table], axis=0
    )


def project_qkv(normed_ref, wq_ref, wk_ref, wv_ref, cos_ref, sin_ref, q_ref, kv_ref):
    normed = normed_ref[...]
    cos_table, sin_table = cos_ref[...], sin_ref[...]
    key = dot(wk_ref[...], normed, 1, 0)
    for head in pieces(KV_HEADS * HEAD_DIM, HEAD_DIM):
        kv_ref[head, :] = rotated(key[head], cos_table, sin_table).astype(BF16)
    kv_ref[KV_HEADS * HEAD_DIM :, :] = dot(wv_ref[...], normed, 1, 0).astype(BF16)
    query = dot(wq_ref[...], normed, 0, 0)
    for head in pieces(HEADS * HEAD_DIM, HEAD_DIM):
        q_ref[head, :] = (rotated(query[head], cos_table, sin_table) * SCALE).astype(BF16)


def first_kernel(
    tokens_ref, got_ref, gain_ref, wq_ref, wk_ref, wv_ref, cos_ref, sin_ref,
    low_ref, q_ref, kv_ref, x_ref, normed_ref,
):
    cut = got_ref.shape[1] // 2
    low_ref[:, :cut] = tokens_ref[:, :cut]
    low_ref[:, cut:] = got_ref[:, cut:]
    x_ref[...] = low_ref[...].astype(F32)
    norm_forward(x_ref, gain_ref, normed_ref)
    project_qkv(normed_ref, wq_ref, wk_ref, wv_ref, cos_ref, sin_ref, q_ref, kv_ref)


def tile_places(core):
    return 2 * core, 3 - 2 * core


def load_keys(core, own_ref, other_ref, all_ref, tok_ref):
    for which, ref in ((core, own_ref), (1 - core, other_ref)):
        for local, tile in enumerate(tile_places(which)):
            all_ref[tile] = ref[:, local * BLOCK : (local + 1) * BLOCK]
    for tile in range(4):
        for head in range(2 * KV_HEADS):
            rows = slice(head * HEAD_DIM, (head + 1) * HEAD_DIM)
            tok_ref[head, tile * BLOCK : (tile + 1) * BLOCK, :] = all_ref[tile, rows, :].T


def set_mask(bias_ref, tile, kb, doc_start):
    place = tile * BLOCK + lax.broadcasted_iota(jnp.int32, (1, BLOCK), 1)
    key_place = kb * BLOCK + lax.broadcasted_iota(jnp.int32, (BLOCK, BLOCK), 0)
    bias_ref[...] = jnp.where((key_place >= doc_start) & (key_place <= place), 0.0, MASKED)


def head_rows(head):
    return slice(head * HEAD_DIM, (head + 1) * HEAD_DIM)


def attend_kernel(
    info_ref, start_ref, q_ref, own_ref, other_ref, ctx_ref, lse_ref,
    all_ref, tok_ref, bias_ref, scores_ref, m_ref, l_ref, acc_ref,
):
    core = info_ref[0]
    load_keys(core, own_ref, other_ref, all_ref, tok_ref)
    for local, tile in enumerate(tile_places(core)):
        cols = slice(local * BLOCK, (local + 1) * BLOCK)
        doc_start = start_ref[0:1, cols]
        m_ref[...] = jnp.full(m_ref.shape, MASKED, F32)
        l_ref[...] = jnp.zeros(l_ref.shape, F32)
        acc_ref[...] = jnp.zeros(acc_ref.shape, F32)

        def step(kb, carry):
            set_mask(bias_ref, tile, kb, doc_start)
            keys = pl.ds(pl.multiple_of(kb * BLOCK, BLOCK), BLOCK)
            for head in range(HEADS):
                key = tok_ref[head // GROUP, keys, :]
                scores_ref[head] = dot(key, q_ref[head_rows(head), cols], 1, 0) + bias_ref[...]
            for head in range(HEADS):
                rows = head_rows(head)
                m_old = m_ref[head : head + 1, :]
                m_new = jnp.maximum(m_old, jnp.max(scores_ref[head], axis=0, keepdims=True))
                m_ref[head : head + 1, :] = m_new
                fade = jnp.exp(m_old - m_new)
                probs = jnp.exp(scores_ref[head] - m_new)
                l_ref[head : head + 1, :] = l_ref[head : head + 1, :] * fade + jnp.sum(
                    probs, axis=0, keepdims=True
                )
                value = all_ref[kb, head_rows(KV_HEADS + head // GROUP), :]
                acc_ref[rows, :] = acc_ref[rows, :] * fade + dot(value, probs.astype(BF16), 1, 0)
            return carry

        lax.fori_loop(info_ref[1 + local], tile + 1, step, 0)
        for head in range(HEADS):
            total = l_ref[head : head + 1, :]
            ctx_ref[head_rows(head), cols] = (acc_ref[head_rows(head), :] * (1.0 / total)).astype(
                BF16
            )
            lse_ref[head : head + 1, cols] = m_ref[head : head + 1, :] + jnp.log(total)


def attend_back_kernel(
    info_ref, start_ref, q_ref, own_ref, other_ref, ctx_ref, lse_ref, grad_ref,
    dq_ref, dkv_own_ref, dkv_other_ref,
    all_ref, tok_ref, bias_ref, probs_ref, probs_low_ref, gs_ref, delta_ref, dkv_ref,
):
    core = info_ref[0]
    load_keys(core, own_ref, other_ref, all_ref, tok_ref)
    dkv_ref[...] = jnp.zeros(dkv_ref.shape, F32)
    for head in range(HEADS):
        rows = head_rows(head)
        delta_ref[head : head + 1, :] = jnp.sum(
            grad_ref[rows, :].astype(F32) * ctx_ref[rows, :].astype(F32), axis=0, keepdims=True
        )
    for local, tile in enumerate(tile_places(core)):
        cols = slice(local * BLOCK, (local + 1) * BLOCK)
        doc_start = start_ref[0:1, cols]
        dq_ref[:, cols] = jnp.zeros((HEADS * HEAD_DIM, BLOCK), F32)

        def step(kb, carry):
            set_mask(bias_ref, tile, kb, doc_start)
            keys = pl.ds(pl.multiple_of(kb * BLOCK, BLOCK), BLOCK)
            for head in range(HEADS):
                key = tok_ref[head // GROUP, keys, :]
                scores = dot(key, q_ref[head_rows(head), cols], 1, 0) + bias_ref[...]
                probs = jnp.exp(scores - lse_ref[head : head + 1, cols])
                probs_ref[head] = probs
                probs_low_ref[head] = probs.astype(BF16)
            for head in range(HEADS):
                value = tok_ref[KV_HEADS + head // GROUP, keys, :]
                grad_probs = dot(value, grad_ref[head_rows(head), cols], 1, 0)
                gs_ref[head] = (
                    probs_ref[head] * (grad_probs - delta_ref[head : head + 1, cols])
                ).astype(BF16)
            for group in range(KV_HEADS):
                rows = head_rows(KV_HEADS + group)
                dv = dkv_ref[kb, rows, :]
                for head in range(group * GROUP, (group + 1) * GROUP):
                    dv = dv + dot(grad_ref[head_rows(head), cols], probs_low_ref[head], 1, 1)
                dkv_ref[kb, rows, :] = dv
            for group in range(KV_HEADS):
                rows = head_rows(group)
                dk = dkv_ref[kb, rows, :]
                for head in range(group * GROUP, (group + 1) * GROUP):
                    dk = dk + dot(q_ref[head_rows(head), cols], gs_ref[head], 1, 1)
                dkv_ref[kb, rows, :] = dk
            for head in range(HEADS):
                key_cols = all_ref[kb, head_rows(head // GROUP), :]
                dq_ref[head_rows(head), cols] += dot(key_cols, gs_ref[head], 1, 0)
            return carry

        lax.fori_loop(info_ref[1 + local], tile + 1, step, 0)
    for local, (own, other) in enumerate(zip(tile_places(core), tile_places(1 - core))):
        cols = slice(local * BLOCK, (local + 1) * BLOCK)
        dkv_own_ref[:, cols] = dkv_ref[own]
        dkv_other_ref[:, cols] = dkv_ref[other].astype(BF16)


def middle_kernel(
    low_ref, ctx_ref, wo_ref, ffn_gain_ref, wg_refs, wu_refs, wd_refs,
    gain_ref, wq_ref, wk_ref, wv_ref, cos_ref, sin_ref,
    mid_ref, ffn_ref, x2_ref, q_ref, kv_ref, normed_ref,
):
    mid_ref[...] = low_ref[...].astype(F32) + dot(wo_ref[...], ctx_ref[...], 0, 0)
    norm_forward(mid_ref, ffn_gain_ref, ffn_ref)
    ffn_in = ffn_ref[...]
    x2_ref[...] = mid_ref[...]
    for part in range(2):
        for hidden in pieces(wg_refs[part].shape[1], BLOCK):
            gate = dot(wg_refs[part][:, hidden], ffn_in, 0, 0)
            up = dot(wu_refs[part][:, hidden], ffn_in, 0, 0)
            product = (gate * jax.nn.sigmoid(gate) * up).astype(BF16)
            x2_ref[...] += dot(wd_refs[part][:, hidden], product, 1, 0)
    norm_forward(x2_ref, gain_ref, normed_ref)
    project_qkv(normed_ref, wq_ref, wk_ref, wv_ref, cos_ref, sin_ref, q_ref, kv_ref)


def ffn_terms(gate, up, grad_product):
    sig = jax.nn.sigmoid(gate)
    silu = gate * sig
    grad_gate = (grad_product * up * (sig + silu * (1.0 - sig))).astype(BF16)
    grad_up = (grad_product * silu).astype(BF16)
    return (silu * up).astype(BF16), grad_gate, grad_up


def out_back(grad_mid_ref, ctx_low_ref, wo_ref, low_ref, dwo_ref, grad_ctx_ref, earlier_ref):
    low_ref[...] = grad_mid_ref[...].astype(BF16)
    low = low_ref[...]
    term = dot(ctx_low_ref[...], low, 1, 1)
    dwo_ref[...] = term if earlier_ref is None else term + earlier_ref[...]
    grad_ctx_ref[...] = dot(wo_ref[...], low, 1, 0).astype(BF16)


def turn_kernel(
    x_ref, ctx_ref, wo_ref, ffn_gain_ref, wg_refs, wu_refs, wd_refs, cotangent_ref, cot_got_ref,
    output_refs, cot_ref, ffn_ref, prod_ref, gg_ref, gu_ref,
    grad_mid_ref, dwo_ref, grad_ctx_ref, dgain_ref,
    mid_ref, acc_ref, low_ref,
):
    mid_ref[...] = x_ref[...] + dot(wo_ref[...], ctx_ref[...], 0, 0)
    norm_forward(mid_ref, ffn_gain_ref, ffn_ref)
    ffn_in = ffn_ref[...]
    cut = cot_got_ref.shape[1] // 2
    cot_ref[:, :cut] = cotangent_ref[:, :cut]
    cot_ref[:, cut:] = cot_got_ref[:, cut:]
    grad_low = cot_ref[...]
    half_hidden = wg_refs[0].shape[1]
    acc_ref[...] = mid_ref[...]
    grad_mid_ref[...] = jnp.zeros(grad_mid_ref.shape, F32)
    for part in range(2):
        for hidden in pieces(half_hidden, BLOCK):
            rows = slice(part * half_hidden + hidden.start, part * half_hidden + hidden.stop)
            gate = dot(wg_refs[part][:, hidden], ffn_in, 0, 0)
            up = dot(wu_refs[part][:, hidden], ffn_in, 0, 0)
            grad_product = dot(wd_refs[part][:, hidden], grad_low, 0, 0)
            product, grad_gate, grad_up = ffn_terms(gate, up, grad_product)
            prod_ref[rows, :] = product
            gg_ref[rows, :] = grad_gate
            gu_ref[rows, :] = grad_up
            acc_ref[...] += dot(wd_refs[part][:, hidden], product, 1, 0)
            grad_mid_ref[...] += dot(wg_refs[part][:, hidden], grad_gate, 1, 0) + dot(
                wu_refs[part][:, hidden], grad_up, 1, 0
            )
    output_refs[0][...] = acc_ref[:, :cut].astype(BF16)
    output_refs[1][...] = acc_ref[:, cut:].astype(BF16)
    acc_ref[...] = grad_mid_ref[...]
    norm_backward(mid_ref, ffn_gain_ref, acc_ref, cot_ref, grad_mid_ref, dgain_ref)
    out_back(grad_mid_ref, ctx_ref, wo_ref, low_ref, dwo_ref, grad_ctx_ref, None)


def qkv_back(
    dq_ref, dkv_own_ref, dkv_got_ref, x_ref, gain_ref, wq_ref, wk_ref, wv_ref, cos_ref, sin_ref,
    dpre_ref, dnormed_ref, normed_ref,
):
    cos_table, sin_table = cos_ref[...], sin_ref[...]
    width, kv_width = HEADS * HEAD_DIM, KV_HEADS * HEAD_DIM
    for head in pieces(width, HEAD_DIM):
        dpre_ref[head, :] = rotated(dq_ref[head, :] * SCALE, cos_table, -sin_table).astype(BF16)
    for head in pieces(kv_width, HEAD_DIM):
        total = dkv_own_ref[head, :] + dkv_got_ref[head, :].astype(F32)
        rows = slice(width + head.start, width + head.stop)
        dpre_ref[rows, :] = rotated(total, cos_table, -sin_table).astype(BF16)
    dpre_ref[width + kv_width :, :] = (
        dkv_own_ref[kv_width:, :] + dkv_got_ref[kv_width:, :].astype(F32)
    ).astype(BF16)
    dnormed_ref[...] = (
        dot(wq_ref[...], dpre_ref[:width, :], 1, 0)
        + dot(wk_ref[...], dpre_ref[width : width + kv_width, :], 0, 0)
        + dot(wv_ref[...], dpre_ref[width + kv_width :, :], 0, 0)
    )
    norm_forward(x_ref, gain_ref, normed_ref)
    normed = normed_ref[...]
    return dot(normed, dpre_ref[:width, :], 1, 1), dot(dpre_ref[width:, :], normed, 1, 1)


def between_kernel(
    dq_ref, dkv_own_ref, dkv_got_ref, x_ref, grad_mid_ref,
    gain_ref, wq_ref, wk_ref, wv_ref, cos_ref, sin_ref,
    ffn1_ref, wg_refs, wu_refs, wd_refs, ffn2_ref, low2_ref, prod2_ref, gg2_ref, gu2_ref,
    dwq_ref, dwkv_ref, dgain_ref, gstream_ref, acc_ref, stack_refs,
    dpre_ref, dnormed_ref, low_ref,
):
    dwq_ref[...], dwkv_ref[...] = qkv_back(
        dq_ref, dkv_own_ref, dkv_got_ref, x_ref, gain_ref, wq_ref, wk_ref, wv_ref, cos_ref, sin_ref,
        dpre_ref, dnormed_ref, low_ref,
    )
    norm_backward(x_ref, gain_ref, dnormed_ref, grad_mid_ref, gstream_ref, dgain_ref)
    low_ref[...] = gstream_ref[...].astype(BF16)
    low = low_ref[...]
    ffn_in = ffn1_ref[...]
    width, half_hidden = wg_refs[0].shape
    acc_ref[...] = jnp.zeros(acc_ref.shape, F32)
    for part in range(2):
        stack = stack_refs[part]
        if stack.shape[0] > 3 * width:
            stack[3 * width :, :] = jnp.zeros((stack.shape[0] - 3 * width, half_hidden), BF16)
        for hidden in pieces(half_hidden, BLOCK):
            rows = slice(part * half_hidden + hidden.start, part * half_hidden + hidden.stop)
            gate = dot(wg_refs[part][:, hidden], ffn_in, 0, 0)
            up = dot(wu_refs[part][:, hidden], ffn_in, 0, 0)
            grad_product = dot(wd_refs[part][:, hidden], low, 0, 0)
            product, grad_gate, grad_up = ffn_terms(gate, up, grad_product)
            acc_ref[...] += dot(wg_refs[part][:, hidden], grad_gate, 1, 0) + dot(
                wu_refs[part][:, hidden], grad_up, 1, 0
            )
            stack[:width, hidden] = (
                dot(ffn_in, grad_gate, 1, 1) + dot(ffn2_ref[...], gg2_ref[rows, :], 1, 1)
            ).astype(BF16)
            stack[width : 2 * width, hidden] = (
                dot(ffn_in, grad_up, 1, 1) + dot(ffn2_ref[...], gu2_ref[rows, :], 1, 1)
            ).astype(BF16)
            stack[2 * width : 3 * width, hidden] = (
                dot(low, product, 1, 1) + dot(low2_ref[...], prod2_ref[rows, :], 1, 1)
            ).astype(BF16)


def out_kernel(
    acc_ref, gstream_ref, mid1_ref, ctx_low1_ref, wo_ref, ffn_gain_ref, dwo2_ref, dffn_gain2_ref,
    grad_mid1_ref, dwo_ref, grad_ctx_ref, dffn_gain_ref, low_ref,
):
    norm_backward(mid1_ref, ffn_gain_ref, acc_ref, gstream_ref, grad_mid1_ref, dffn_gain_ref)
    dffn_gain_ref[...] += dffn_gain2_ref[...]
    out_back(grad_mid1_ref, ctx_low1_ref, wo_ref, low_ref, dwo_ref, grad_ctx_ref, dwo2_ref)


def last_kernel(
    info_ref, dq_ref, dkv_own_ref, dkv_got_ref, x_low_ref, grad_mid_ref,
    gain_ref, wq_ref, wk_ref, wv_ref, cos_ref, sin_ref,
    dwq2_ref, dwkv2_ref, dwo_ref, dgain2_ref, dffn_gain_ref,
    out_refs, stack_own_ref, stack_other_ref,
    dpre_ref, dnormed_ref, normed_ref, x_ref, out_ref, dgain_ref, stack_ref,
):
    x_ref[...] = x_low_ref[...].astype(F32)
    width, rows = dwo_ref.shape[0], stack_ref.shape[1]
    dwq, dwkv = qkv_back(
        dq_ref, dkv_own_ref, dkv_got_ref, x_ref, gain_ref, wq_ref, wk_ref, wv_ref, cos_ref, sin_ref,
        dpre_ref, dnormed_ref, normed_ref,
    )
    norm_backward(x_ref, gain_ref, dnormed_ref, grad_mid_ref, out_ref, dgain_ref)
    cut = out_refs[0].shape[1]
    out_refs[0][...] = out_ref[:, :cut]
    out_refs[1][...] = out_ref[:, cut:]
    spare = stack_ref.shape[2] - width
    stack_ref[0, :width, :width] = (dwq + dwq2_ref[...]).astype(BF16)
    stack_ref[0, width:, :width] = dwo_ref[: rows - width, :].astype(BF16)
    left = 2 * width - rows
    stack_ref[1, :left, :width] = dwo_ref[rows - width :, :].astype(BF16)
    stack_ref[1, left:, :width] = (dwkv + dwkv2_ref[...]).astype(BF16)
    column = lax.broadcasted_iota(jnp.int32, (width, spare), 1)
    gains = jnp.where(
        column == 0,
        dgain_ref[...] + dgain2_ref[...],
        jnp.where(column == 1, dffn_gain_ref[...], 0.0),
    ).astype(BF16)
    for part in range(2):
        stack_ref[part, :width, width:] = gains
        stack_ref[part, width:, width:] = jnp.zeros((rows - width, spare), BF16)
    core = info_ref[0]
    stack_own_ref[...] = stack_ref[core]
    stack_other_ref[...] = stack_ref[1 - core]


def shape(dims, dtype):
    return jax.ShapeDtypeStruct(dims, dtype)


def run(kernel, args, outs, scratch=(), smem=0, name=None, us=5, limit=VMEM_LIMIT):
    leaves, tree = jax.tree.flatten(args)
    out_leaves, out_tree = jax.tree.flatten(outs)
    n_in, n_out = len(leaves), len(out_leaves)

    def body(*refs):
        ins = jax.tree.unflatten(tree, refs[:n_in])
        results = jax.tree.unflatten(out_tree, refs[n_in : n_in + n_out])
        kernel(*ins, *results, *refs[n_in + n_out :])

    in_specs = [
        pl.BlockSpec(memory_space=pltpu.SMEM if index < smem else pltpu.VMEM)
        for index in range(n_in)
    ]
    results = pl.pallas_call(
        body,
        out_shape=out_leaves,
        in_specs=in_specs,
        out_specs=[pl.BlockSpec(memory_space=pltpu.VMEM)] * n_out,
        scratch_shapes=list(scratch),
        compiler_params=pltpu.CompilerParams(vmem_limit_bytes=limit),
        cost_estimate=pl.CostEstimate(
            flops=int(us * 1e9), bytes_accessed=2**20, transcendentals=0
        ),
        name=name,
    )(*leaves)
    return jax.tree.unflatten(out_tree, results)


def swap(array):
    return lax.ppermute(array, "tensor", [(0, 1), (1, 0)])


def partners(sizes, flips):
    n, cores = sizes
    return [
        (place * cores + core, (place ^ flips[core]) * cores + core)
        for place in range(n)
        for core in range(cores)
    ]


class Plan:
    def __init__(self, sizes, place, core):
        n, _ = sizes
        bits = n.bit_length() - 1
        rounds = []
        bit = 0
        if bits >= 2:
            for one, two in ((0, 1), (1, 0)):
                own = jnp.where(core == 0, (place >> one) & 1, (place >> two) & 1)
                rounds.append((own, [1], [partners(sizes, (1 << one, 1 << two))]))
            bit = 2
        while bit < bits:
            wide = min(2, bits - bit)
            own = (place >> bit) & ((1 << wide) - 1)
            flips = list(range(1, 1 << wide))
            perms = [partners(sizes, (flip << bit, flip << bit)) for flip in flips]
            rounds.append((own, flips, perms))
            bit += wide
        self.n = n
        self.perms = [perms for _, _, perms in rounds]
        at = jnp.int32(0)
        scatter, bases = [], []
        for own, flips, _ in rounds:
            scatter.append((own, [own ^ flip for flip in flips]))
            bases.append(at * (len(flips) + 1))
            at = at * (len(flips) + 1) + own
        gather, size = [], 1
        for (own, flips, _), base in zip(reversed(rounds), reversed(bases)):
            gather.append(((base + own) * size, [(base + (own ^ flip)) * size for flip in flips]))
            size *= len(flips) + 1
        self.indices = (at, scatter, gather)


def take(array, start, count):
    return lax.dynamic_slice(
        array,
        (start,) + (0,) * (array.ndim - 1),
        (count,) + array.shape[1:],
        allow_negative_indices=False,
    )


def put(array, part, start):
    return lax.dynamic_update_slice(
        array, part, (start,) + (0,) * (array.ndim - 1), allow_negative_indices=False
    )


class Stream:
    def __init__(self, terms, plan):
        self.terms, self.plan = terms, plan
        self.round = 0
        if not plan.perms:
            self.all = self.total(lambda term: term)

    def total(self, cut):
        parts = [cut(term).astype(F32) for term in self.terms]
        result = parts[0]
        for part in parts[1:]:
            result = result + part
        return result.astype(BF16)

    def part(self, ways, index):
        def cut(term):
            parts = term.reshape((ways, -1) + term.shape[1:])
            return take(parts, index, 1)[0]

        return self.total(cut)

    def load(self):
        count = len(self.plan.perms)
        at, scatter, gather = self.plan.indices
        if self.round < count:
            own, others = scatter[self.round]
            ways = len(others) + 1
            sent = [self.part(ways, other) for other in others]
            self.terms = [self.part(ways, own)]
            return sent
        if self.round == count:
            chunk = self.total(lambda term: term)
            self.all = put(jnp.zeros((self.plan.n,) + chunk.shape[1:], BF16), chunk, at)
            self.size = 1
        own, others = gather[self.round - count]
        return [take(self.all, own, self.size)] * len(others)

    def move(self, sent):
        count = len(self.plan.perms)
        which = self.round if self.round < count else 2 * count - 1 - self.round
        got = [
            lax.ppermute(part, ("dp", "tensor"), perm)
            for part, perm in zip(sent, self.plan.perms[which])
        ]
        if self.round < count:
            self.terms = self.terms + got
        else:
            _, others = self.plan.indices[2][self.round - count]
            for other, part in zip(others, got):
                self.all = put(self.all, part, other)
            self.size *= len(got) + 1
        self.round += 1

    def split(self, columns):
        streams = []
        for cols in (slice(0, columns), slice(columns, None)):
            stream = Stream([term[..., cols] for term in self.terms], self.plan)
            stream.round = self.round
            streams.append(stream)
        return streams

    @property
    def done(self):
        return self.round == 2 * len(self.plan.perms)


def advance(streams, held):
    streams = [stream for stream in streams if not stream.done]
    sent = [stream.load() for stream in streams]
    sent, held = lax.optimization_barrier((sent, held))
    for stream, part in zip(streams, sent):
        stream.move(part)
    return held


def tie(*arrays):
    return lax.optimization_barrier(arrays)


def per_device(
    sizes, tokens, segments, cotangent, attn_gain, w_query, w_key, w_value, w_out, ffn_gain,
    w_gate, w_up, w_down,
):
    _, half, width = tokens.shape
    kv_width = KV_HEADS * HEAD_DIM
    hidden = w_gate.shape[1]
    n = sizes[0]
    core = lax.axis_index("tensor")
    cut = half // 2
    tokens, cotangent = tokens[0].T, cotangent[0].T
    w_key, w_value, w_down = w_key.T, w_value.T, w_down.T
    segments = segments[0]

    plan = Plan(sizes, lax.axis_index("dp"), core)
    tokens_got = swap(tokens)
    first_place, second_place = (tile * cut for tile in tile_places(core))
    place = jnp.concatenate([first_place + jnp.arange(cut), second_place + jnp.arange(cut)])
    inverse = 10000.0 ** (-2.0 * jnp.arange(HALF).astype(F32) / HEAD_DIM)
    angles = inverse[:, None] * place.astype(F32)[None, :]
    tables = (jnp.cos(angles), jnp.sin(angles))
    own_labels = jnp.concatenate(
        [lax.dynamic_slice_in_dim(segments, at, cut, 0) for at in (first_place, second_place)]
    )
    doc_start = jnp.sum((segments[:, None] < own_labels[None, :]).astype(jnp.int32), axis=0)
    info = jnp.concatenate([core[None], doc_start[::cut] // BLOCK]).astype(jnp.int32)
    doc_start = doc_start[None, :]
    is_first = core == 0
    tokens_got, info, doc_start, tables, is_first, plan.indices = lax.optimization_barrier(
        (tokens_got, info, doc_start, tables, is_first, plan.indices)
    )
    gain_col, ffn_gain_col = attn_gain[:, None], ffn_gain[:, None]
    projections = (w_query, w_key, w_value)

    act = shape((width, half), F32)
    low = shape((width, half), BF16)
    kv = shape((2 * kv_width, half), BF16)
    wide = shape((2 * hidden, half), BF16)
    column = shape((width, 1), F32)
    square = shape((width, width), F32)
    heads_f32 = pltpu.VMEM((HEADS, BLOCK, BLOCK), F32)
    heads_low = pltpu.VMEM((HEADS, BLOCK, BLOCK), BF16)
    key_scratch = [
        pltpu.VMEM((4, 2 * kv_width, BLOCK), BF16),
        pltpu.VMEM((2 * KV_HEADS, 4 * BLOCK, HEAD_DIM), BF16),
        pltpu.VMEM((BLOCK, BLOCK), F32),
        heads_f32,
    ]
    act_scratch = pltpu.VMEM((width, half), F32)
    low_scratch = pltpu.VMEM((width, half), BF16)

    def attend(query, kv_own, kv_other):
        return run(
            attend_kernel,
            (info, doc_start, query, kv_own, kv_other),
            (low, shape((16, half), F32)),
            key_scratch
            + [pltpu.VMEM((16, BLOCK), F32), pltpu.VMEM((16, BLOCK), F32),
               pltpu.VMEM((width, BLOCK), F32)],
            smem=1,
            name="attend",
            us=6,
        )

    def attend_back(query, kv_own, kv_other, ctx, lse, grad):
        return run(
            attend_back_kernel,
            (info, doc_start, query, kv_own, kv_other, ctx, lse, grad),
            (act, shape((2 * kv_width, half), F32), kv),
            key_scratch
            + [heads_low, heads_low, pltpu.VMEM((16, half), F32),
               pltpu.VMEM((4, 2 * kv_width, BLOCK), F32)],
            smem=1,
            name="attend_back",
            us=9,
        )

    x1, query1, kv1 = run(
        first_kernel,
        (tokens, tokens_got, gain_col) + projections + tables,
        (low, low, kv),
        [act_scratch, low_scratch],
        name="first",
        us=2,
    )
    kv1, w_gate, w_up, w_down, cot_sent = tie(kv1, w_gate, w_up, w_down, cotangent)
    kv1_other = swap(kv1)
    gate_pair = (w_gate, swap(w_gate))
    up_pair = (w_up, swap(w_up))
    down_pair = (w_down, swap(w_down))
    cot_got = swap(cot_sent)
    ctx1, lse1 = attend(query1, kv1, kv1_other)
    mid1, ffn1, x2, query2, kv2 = run(
        middle_kernel,
        (x1, ctx1, w_out, ffn_gain_col, gate_pair, up_pair, down_pair, gain_col)
        + projections + tables,
        (act, low, act, low, kv),
        [low_scratch],
        name="middle",
        us=6,
    )
    kv2_other = swap(kv2)
    ctx2, lse2 = attend(query2, kv2, kv2_other)
    tile_low = shape((width, cut), BF16)
    (
        (output, output_sent), cot, ffn2, prod2, gg2, gu2, grad_mid2, dwo2, grad_ctx2, dffn_gain2,
    ) = run(
        turn_kernel,
        (x2, ctx2, w_out, ffn_gain_col, gate_pair, up_pair, down_pair, cotangent, cot_got),
        ((tile_low, tile_low), low, low, wide, wide, wide, act, square, low, column),
        [act_scratch, act_scratch, low_scratch],
        name="turn",
        us=9,
    )
    dq2, dkv_own2, dkv_sent2 = attend_back(query2, kv2, kv2_other, ctx2, lse2, grad_ctx2)
    dkv_got2 = swap(dkv_sent2)
    pre_scratch = [
        pltpu.VMEM((width + 2 * kv_width, half), BF16), act_scratch, low_scratch
    ]
    pad = 16 * n
    stack_shape = shape((-(-3 * width // pad) * pad, hidden), BF16)
    dwq2, dwkv2, dgain2, gstream, dffn, (stack_own, stack_other) = run(
        between_kernel,
        (dq2, dkv_own2, dkv_got2, x2, grad_mid2, gain_col) + projections + tables
        + (ffn1, gate_pair, up_pair, down_pair, ffn2, cot, prod2, gg2, gu2),
        (square, shape((2 * kv_width, width), F32), column, act, act, (stack_shape, stack_shape)),
        pre_scratch,
        name="between",
        us=16,
    )
    stack_got = swap(stack_other)
    grad_mid1, dwo, grad_ctx1, dffn_gain = run(
        out_kernel,
        (dffn, gstream, mid1, ctx1, w_out, ffn_gain_col, dwo2, dffn_gain2),
        (act, square, low, column),
        [low_scratch],
        name="out",
        us=2,
    )
    def in_chunks(array):
        return array.reshape((n, -1) + array.shape[1:])

    ffn_stream = Stream([in_chunks(stack_own), in_chunks(stack_got)], plan)
    grad_ctx1 = advance([ffn_stream], grad_ctx1)
    dq1, dkv_own1, dkv_sent1 = attend_back(query1, kv1, kv1_other, ctx1, lse1, grad_ctx1)
    dkv_got1 = swap(dkv_sent1)
    dkv_got1 = advance([ffn_stream], dkv_got1)
    rows = (2 * width + 2 * kv_width) // 2
    lanes = -(-width // 128) * 128
    lanes = lanes if lanes - width >= 2 else lanes + 128
    half_stack = shape((rows, lanes), BF16)
    tile_act = shape((width, cut), F32)
    (grad_input, grad_input_sent), pack_own, pack_other = run(
        last_kernel,
        (info, dq1, dkv_own1, dkv_got1, x1, grad_mid1, gain_col) + projections + tables
        + (dwq2, dwkv2, dwo, dgain2, dffn_gain),
        ((tile_act, tile_act), half_stack, half_stack),
        pre_scratch
        + [act_scratch, act_scratch, pltpu.VMEM((width, 1), F32),
           pltpu.VMEM((2, rows, lanes), BF16)],
        smem=1,
        name="last",
        us=4,
    )
    one, two = ffn_stream.split(hidden // 2)
    pack_other = advance([one], pack_other)
    pack_stream = Stream([in_chunks(pack_own), in_chunks(swap(pack_other))], plan)
    advance([pack_stream], ())
    for streams in (
        [one, pack_stream], [two, one], [two, one], [two, pack_stream], [two, pack_stream],
        [pack_stream], [pack_stream],
    ):
        advance(streams, ())
    while not (one.done and two.done and pack_stream.done):
        advance([one, two, pack_stream], ())
    pack = pack_stream.all.reshape(rows, lanes)
    got = swap(pack)
    gains = pack[:width, width : width + 2].astype(F32)
    packed = jnp.where(
        is_first, jnp.concatenate([pack, got]), jnp.concatenate([got, pack])
    )[:, :width].astype(F32)
    ffn_sum = jnp.concatenate([one.all, two.all], axis=2).reshape(-1, hidden).astype(F32)
    output = jnp.concatenate([output, swap(output_sent)], axis=1)
    grad_input = jnp.concatenate([grad_input, swap(grad_input_sent)], axis=1)
    ends = (width, 2 * width, 2 * width + kv_width)
    return (
        output.T[None],
        grad_input.T[None],
        gains[:, 0],
        packed[: ends[0]],
        packed[ends[1] : ends[2]].T,
        packed[ends[2] :].T,
        packed[ends[0] : ends[1]],
        gains[:, 1],
        ffn_sum[:width],
        ffn_sum[width : 2 * width],
        ffn_sum[2 * width : 3 * width].T,
    )


def solution(mesh):
    sizes = (mesh.shape["dp"], mesh.shape["tensor"])

    def local(*args):
        return per_device(sizes, *args)

    split = P("dp", "tensor", None)
    in_specs = (
        split, P("dp", None), split, P(), P(), P(), P(), P(), P(),
        P(None, "tensor"), P(None, "tensor"), P("tensor", None),
    )
    out_specs = (
        split, split, P(), P(), P(), P(), P(), P(),
        P(None, "tensor"), P(None, "tensor"), P("tensor", None),
    )
    return jax.shard_map(
        local, mesh=mesh, in_specs=in_specs, out_specs=out_specs, check_vma=False
    )
```

```python
import jax
import jax.numpy as jnp
import numpy as np
from jax import lax
from jax.experimental import pallas as pl
from jax.experimental.pallas import tpu as pltpu
from jax.sharding import PartitionSpec as P

HEADS = 9
KV_HEADS = 3
GROUP = HEADS // KV_HEADS
HEAD_DIM = 64
HALF = HEAD_DIM // 2
EPSILON = 1e-05
MASKED = -1e30
BLOCK = 256
SCALE = HEAD_DIM ** (-0.5)
F32 = jnp.float32
BF16 = jnp.bfloat16
VMEM_LIMIT = 16 * 2**20


def dot(left, right, left_dim, right_dim):
    return lax.dot_general(
        left, right, (((left_dim,), (right_dim,)), ((), ())), preferred_element_type=F32
    )


def pieces(size, step):
    return [slice(start, start + step) for start in range(0, size, step)]


def inverse_rms(x_ref):
    total = None
    for rows in pieces(x_ref.shape[0], 64):
        x = x_ref[rows, :]
        part = jnp.sum(x * x, axis=0, keepdims=True)
        total = part if total is None else total + part
    return lax.rsqrt(total / x_ref.shape[0] + EPSILON)


def norm_forward(x_ref, gain_ref, out_ref):
    scale = inverse_rms(x_ref)
    for rows in pieces(x_ref.shape[0], 64):
        out_ref[rows, :] = (x_ref[rows, :] * scale * gain_ref[rows, :]).astype(BF16)


def norm_backward(x_ref, gain_ref, grad_ref, add_ref, out_ref, gain_grad_ref):
    scale = inverse_rms(x_ref)
    inner = None
    for rows in pieces(x_ref.shape[0], 64):
        x, e = x_ref[rows, :], grad_ref[rows, :]
        xe = x * e
        gain_grad_ref[rows, :] = jnp.sum(xe * scale, axis=1, keepdims=True)
        part = jnp.sum(xe * gain_ref[rows, :], axis=0, keepdims=True)
        inner = part if inner is None else inner + part
    cubed = scale * scale * scale * (inner / x_ref.shape[0])
    for rows in pieces(x_ref.shape[0], 64):
        out_ref[rows, :] = (
            add_ref[rows, :].astype(F32)
            + scale * gain_ref[rows, :] * grad_ref[rows, :]
            - x_ref[rows, :] * cubed
        )


def rotated(x, cos_table, sin_table):
    front, back = x[:HALF], x[HALF:]
    return jnp.concatenate(
        [front * cos_table - back * sin_table, back * cos_table + front * sin_table], axis=0
    )


def project_qkv(normed_ref, wq_ref, wk_ref, wv_ref, cos_ref, sin_ref, q_ref, kv_ref):
    normed = normed_ref[...]
    cos_table, sin_table = cos_ref[...], sin_ref[...]
    key = dot(wk_ref[...], normed, 1, 0)
    for head in pieces(KV_HEADS * HEAD_DIM, HEAD_DIM):
        kv_ref[head, :] = rotated(key[head], cos_table, sin_table).astype(BF16)
    kv_ref[KV_HEADS * HEAD_DIM :, :] = dot(wv_ref[...], normed, 1, 0).astype(BF16)
    query = dot(wq_ref[...], normed, 0, 0)
    for head in pieces(HEADS * HEAD_DIM, HEAD_DIM):
        q_ref[head, :] = (rotated(query[head], cos_table, sin_table) * SCALE).astype(BF16)


def first_kernel(
    tokens_hbm, got_hbm, wq_hbm, wk_hbm, wv_hbm, gains_ref, all_cos_ref, all_sin_ref,
    low_ref, normed_ref, q_ref, kv_ref, gain_ref, ffn_gain_ref, cos_ref, sin_ref,
    x_ref, tokens_ref, got_ref, wq_ref, wk_ref, wv_ref, sems,
):
    copies = [
        pltpu.make_async_copy(source, target, sems.at[index])
        for index, (source, target) in enumerate(
            (
                (tokens_hbm, tokens_ref), (got_hbm, got_ref), (wk_hbm, wk_ref), (wv_hbm, wv_ref),
                (wq_hbm, wq_ref),
            )
        )
    ]
    for copy in copies:
        copy.start()
    for at, column_ref in enumerate((gain_ref, ffn_gain_ref)):
        row = gains_ref[at : at + 1, :]
        column_ref[...] = jnp.broadcast_to(row, (128, row.shape[1])).T[:, :1]
    cut = got_ref.shape[1] // 2
    for local, tile in enumerate(tile_places(lax.axis_index("tensor"))):
        cols = slice(local * cut, (local + 1) * cut)
        cos_ref[:, cols] = all_cos_ref[:, tile_lanes(tile)]
        sin_ref[:, cols] = all_sin_ref[:, tile_lanes(tile)]
    copies[0].wait()
    copies[1].wait()
    low_ref[:, :cut] = tokens_ref[:, :cut]
    low_ref[:, cut:] = got_ref[:, cut:]
    x_ref[...] = low_ref[...].astype(F32)
    norm_forward(x_ref, gain_ref, normed_ref)
    for copy in copies[2:]:
        copy.wait()
    project_qkv(normed_ref, wq_ref, wk_ref, wv_ref, cos_ref, sin_ref, q_ref, kv_ref)


def tile_places(core):
    return 2 * core, 3 - 2 * core


def load_keys(core, own_ref, other_ref, all_ref, tok_ref):
    for which, ref in ((core, own_ref), (1 - core, other_ref)):
        for local, tile in enumerate(tile_places(which)):
            all_ref[tile] = ref[:, local * BLOCK : (local + 1) * BLOCK]
    for tile in range(4):
        for head in range(2 * KV_HEADS):
            rows = slice(head * HEAD_DIM, (head + 1) * HEAD_DIM)
            tok_ref[head, tile * BLOCK : (tile + 1) * BLOCK, :] = all_ref[tile, rows, :].T


def tile_lanes(tile):
    return pl.ds(pl.multiple_of(tile * BLOCK, BLOCK), BLOCK)


def set_labels(labels_ref, column_ref):
    column_ref[...] = jnp.broadcast_to(labels_ref[0:1, :], (8, labels_ref.shape[1])).T


def set_mask(bias_ref, labels_ref, column_ref, tile, kb):
    key_labels = column_ref[tile_lanes(kb), :1]
    key_place = kb * BLOCK + lax.broadcasted_iota(jnp.int32, (BLOCK, BLOCK), 0)
    place = tile * BLOCK + lax.broadcasted_iota(jnp.int32, (1, BLOCK), 1)
    allowed = (key_labels == labels_ref[0:1, tile_lanes(tile)]) & (key_place <= place)
    bias_ref[...] = jnp.where(allowed, 0.0, MASKED)


def first_block(segments_ref, tile):
    label = segments_ref[0, tile * BLOCK]
    count = jnp.int32(0)
    for kb in range(3):
        before = (kb < tile) & (segments_ref[0, kb * BLOCK + BLOCK - 1] < label)
        count = count + before.astype(jnp.int32)
    return count


def head_rows(head):
    return slice(head * HEAD_DIM, (head + 1) * HEAD_DIM)


def attend_kernel(
    segments_ref, labels_ref, q_ref, own_ref, other_ref, ctx_ref, lse_ref,
    all_ref, tok_ref, bias_ref, column_ref, scores_ref, m_ref, l_ref, acc_ref,
):
    core = lax.axis_index("tensor")
    load_keys(core, own_ref, other_ref, all_ref, tok_ref)
    set_labels(labels_ref, column_ref)
    for local, tile in enumerate(tile_places(core)):
        cols = slice(local * BLOCK, (local + 1) * BLOCK)
        m_ref[...] = jnp.full(m_ref.shape, MASKED, F32)
        l_ref[...] = jnp.zeros(l_ref.shape, F32)
        acc_ref[...] = jnp.zeros(acc_ref.shape, F32)

        def step(kb, carry):
            set_mask(bias_ref, labels_ref, column_ref, tile, kb)
            keys = pl.ds(pl.multiple_of(kb * BLOCK, BLOCK), BLOCK)
            for head in range(HEADS):
                key = tok_ref[head // GROUP, keys, :]
                scores_ref[head] = dot(key, q_ref[head_rows(head), cols], 1, 0) + bias_ref[...]
            for head in range(HEADS):
                rows = head_rows(head)
                m_old = m_ref[head : head + 1, :]
                m_new = jnp.maximum(m_old, jnp.max(scores_ref[head], axis=0, keepdims=True))
                m_ref[head : head + 1, :] = m_new
                fade = jnp.exp(m_old - m_new)
                probs = jnp.exp(scores_ref[head] - m_new)
                l_ref[head : head + 1, :] = l_ref[head : head + 1, :] * fade + jnp.sum(
                    probs, axis=0, keepdims=True
                )
                value = all_ref[kb, head_rows(KV_HEADS + head // GROUP), :]
                acc_ref[rows, :] = acc_ref[rows, :] * fade + dot(value, probs.astype(BF16), 1, 0)
            return carry

        lax.fori_loop(first_block(segments_ref, tile), tile + 1, step, 0)
        for head in range(HEADS):
            total = l_ref[head : head + 1, :]
            ctx_ref[head_rows(head), cols] = (acc_ref[head_rows(head), :] * (1.0 / total)).astype(
                BF16
            )
            lse_ref[head : head + 1, cols] = m_ref[head : head + 1, :] + jnp.log(total)


def attend_back_kernel(
    segments_ref, labels_ref, q_ref, own_ref, other_ref, ctx_ref, lse_ref, grad_ref,
    dq_ref, dkv_own_ref, dkv_other_ref,
    all_ref, tok_ref, bias_ref, column_ref, probs_ref, probs_low_ref, gs_ref, delta_ref, dkv_ref,
):
    core = lax.axis_index("tensor")
    load_keys(core, own_ref, other_ref, all_ref, tok_ref)
    set_labels(labels_ref, column_ref)
    dkv_ref[...] = jnp.zeros(dkv_ref.shape, F32)
    for head in range(HEADS):
        rows = head_rows(head)
        delta_ref[head : head + 1, :] = jnp.sum(
            grad_ref[rows, :].astype(F32) * ctx_ref[rows, :].astype(F32), axis=0, keepdims=True
        )
    for local, tile in enumerate(tile_places(core)):
        cols = slice(local * BLOCK, (local + 1) * BLOCK)
        dq_ref[:, cols] = jnp.zeros((HEADS * HEAD_DIM, BLOCK), F32)

        def step(kb, carry):
            set_mask(bias_ref, labels_ref, column_ref, tile, kb)
            keys = pl.ds(pl.multiple_of(kb * BLOCK, BLOCK), BLOCK)
            for head in range(HEADS):
                key = tok_ref[head // GROUP, keys, :]
                scores = dot(key, q_ref[head_rows(head), cols], 1, 0) + bias_ref[...]
                probs = jnp.exp(scores - lse_ref[head : head + 1, cols])
                probs_ref[head] = probs
                probs_low_ref[head] = probs.astype(BF16)
            for head in range(HEADS):
                value = tok_ref[KV_HEADS + head // GROUP, keys, :]
                grad_probs = dot(value, grad_ref[head_rows(head), cols], 1, 0)
                gs_ref[head] = (
                    probs_ref[head] * (grad_probs - delta_ref[head : head + 1, cols])
                ).astype(BF16)
            for group in range(KV_HEADS):
                rows = head_rows(KV_HEADS + group)
                dv = dkv_ref[kb, rows, :]
                for head in range(group * GROUP, (group + 1) * GROUP):
                    dv = dv + dot(grad_ref[head_rows(head), cols], probs_low_ref[head], 1, 1)
                dkv_ref[kb, rows, :] = dv
            for group in range(KV_HEADS):
                rows = head_rows(group)
                dk = dkv_ref[kb, rows, :]
                for head in range(group * GROUP, (group + 1) * GROUP):
                    dk = dk + dot(q_ref[head_rows(head), cols], gs_ref[head], 1, 1)
                dkv_ref[kb, rows, :] = dk
            for head in range(HEADS):
                key_cols = all_ref[kb, head_rows(head // GROUP), :]
                dq_ref[head_rows(head), cols] += dot(key_cols, gs_ref[head], 1, 0)
            return carry

        lax.fori_loop(first_block(segments_ref, tile), tile + 1, step, 0)
    for local, (own, other) in enumerate(zip(tile_places(core), tile_places(1 - core))):
        cols = slice(local * BLOCK, (local + 1) * BLOCK)
        dkv_own_ref[:, cols] = dkv_ref[own]
        dkv_other_ref[:, cols] = dkv_ref[other].astype(BF16)


def middle_kernel(
    low_ref, ctx_ref, wo_ref, ffn_gain_ref, wg_refs, wu_refs, wd_refs,
    gain_ref, wq_ref, wk_ref, wv_ref, cos_ref, sin_ref,
    mid_ref, ffn_ref, gate_ref, up_ref, x2_ref, normed_ref, q_ref, kv_ref,
):
    mid_ref[...] = low_ref[...].astype(F32) + dot(wo_ref[...], ctx_ref[...], 0, 0)
    norm_forward(mid_ref, ffn_gain_ref, ffn_ref)
    ffn_in = ffn_ref[...]
    x2_ref[...] = mid_ref[...]
    half_hidden = wg_refs[0].shape[1]
    for part in range(2):
        for hidden in pieces(half_hidden, BLOCK):
            gate = dot(wg_refs[part][:, hidden], ffn_in, 0, 0)
            up = dot(wu_refs[part][:, hidden], ffn_in, 0, 0)
            rows = slice(part * half_hidden + hidden.start, part * half_hidden + hidden.stop)
            gate_ref[rows, :] = gate.astype(BF16)
            up_ref[rows, :] = up.astype(BF16)
            product = (gate * jax.nn.sigmoid(gate) * up).astype(BF16)
            x2_ref[...] += dot(wd_refs[part][:, hidden], product, 1, 0)
    norm_forward(x2_ref, gain_ref, normed_ref)
    project_qkv(normed_ref, wq_ref, wk_ref, wv_ref, cos_ref, sin_ref, q_ref, kv_ref)


def ffn_terms(gate, up, grad_product):
    sig = jax.nn.sigmoid(gate)
    silu = gate * sig
    grad_gate = (grad_product * up * (sig + silu * (1.0 - sig))).astype(BF16)
    grad_up = (grad_product * silu).astype(BF16)
    return (silu * up).astype(BF16), grad_gate, grad_up


def turn_kernel(
    x_ref, ctx_ref, wo_ref, ffn_gain_ref, wg_refs, wu_refs, wd_refs, cotangent_ref, cot_got_ref,
    output_refs, cot_ref, ffn_ref, kept_own_refs, kept_other_refs,
    grad_mid_ref, grad_mid_low_ref, grad_ctx_ref, dgain_ref,
    mid_ref, acc_ref,
):
    mid_ref[...] = x_ref[...] + dot(wo_ref[...], ctx_ref[...], 0, 0)
    norm_forward(mid_ref, ffn_gain_ref, ffn_ref)
    ffn_in = ffn_ref[...]
    cut = cot_got_ref.shape[1] // 2
    cot_ref[:, :cut] = cotangent_ref[:, :cut]
    cot_ref[:, cut:] = cot_got_ref[:, cut:]
    grad_low = cot_ref[...]
    half_hidden = wg_refs[0].shape[1]
    acc_ref[...] = mid_ref[...]
    grad_mid_ref[...] = jnp.zeros(grad_mid_ref.shape, F32)
    for part in range(2):
        for hidden in pieces(half_hidden, BLOCK):
            gate = dot(wg_refs[part][:, hidden], ffn_in, 0, 0)
            up = dot(wu_refs[part][:, hidden], ffn_in, 0, 0)
            grad_product = dot(wd_refs[part][:, hidden], grad_low, 0, 0)
            product, grad_gate, grad_up = ffn_terms(gate, up, grad_product)
            kept = (kept_own_refs, kept_other_refs)[part]
            for ref, term in zip(kept, (product, grad_gate, grad_up)):
                ref[hidden, :] = term
            acc_ref[...] += dot(wd_refs[part][:, hidden], product, 1, 0)
            grad_mid_ref[...] += dot(wg_refs[part][:, hidden], grad_gate, 1, 0) + dot(
                wu_refs[part][:, hidden], grad_up, 1, 0
            )
    output_refs[0][...] = acc_ref[:, :cut].astype(BF16)
    output_refs[1][...] = acc_ref[:, cut:].astype(BF16)
    acc_ref[...] = grad_mid_ref[...]
    norm_backward(mid_ref, ffn_gain_ref, acc_ref, cot_ref, grad_mid_ref, dgain_ref)
    grad_mid_low_ref[...] = grad_mid_ref[...].astype(BF16)
    grad_ctx_ref[...] = dot(wo_ref[...], grad_mid_low_ref[...], 1, 0).astype(BF16)


def qkv_back(
    dq_ref, dkv_own_ref, dkv_got_ref, wq_ref, wk_ref, wv_ref, cos_ref, sin_ref, dpre_ref, dnormed_ref
):
    cos_table, sin_table = cos_ref[...], sin_ref[...]
    width, kv_width = HEADS * HEAD_DIM, KV_HEADS * HEAD_DIM
    for head in pieces(width, HEAD_DIM):
        dpre_ref[head, :] = rotated(dq_ref[head, :] * SCALE, cos_table, -sin_table).astype(BF16)
    for head in pieces(kv_width, HEAD_DIM):
        total = dkv_own_ref[head, :] + dkv_got_ref[head, :].astype(F32)
        rows = slice(width + head.start, width + head.stop)
        dpre_ref[rows, :] = rotated(total, cos_table, -sin_table).astype(BF16)
    dpre_ref[width + kv_width :, :] = (
        dkv_own_ref[kv_width:, :] + dkv_got_ref[kv_width:, :].astype(F32)
    ).astype(BF16)
    dnormed_ref[...] = (
        dot(wq_ref[...], dpre_ref[:width, :], 1, 0)
        + dot(wk_ref[...], dpre_ref[width : width + kv_width, :], 0, 0)
        + dot(wv_ref[...], dpre_ref[width + kv_width :, :], 0, 0)
    )


def weight_terms(stack, hidden, first, second, ffn1, ffn2, low1, low2):
    width = ffn1.shape[0]
    (product1, gate1, up1), (product2, gate2, up2) = first, second
    stack[:width, hidden] = (dot(ffn1, gate1, 1, 1) + dot(ffn2, gate2, 1, 1)).astype(BF16)
    stack[width : 2 * width, hidden] = (dot(ffn1, up1, 1, 1) + dot(ffn2, up2, 1, 1)).astype(BF16)
    stack[2 * width : 3 * width, hidden] = (
        dot(low1, product1, 1, 1) + dot(low2, product2, 1, 1)
    ).astype(BF16)


def fill_stack(stack, width):
    if stack.shape[0] > 3 * width:
        stack[3 * width :, :] = jnp.zeros((stack.shape[0] - 3 * width, stack.shape[1]), BF16)


def ffn_back(
    part, stack, low, ffn1, ffn2, low2, gate_ref, up_ref, wg_ref, wu_ref, wd_ref, kept2_refs, acc_ref
):
    half_hidden = wg_ref.shape[1]
    for hidden in pieces(half_hidden, BLOCK):
        rows = slice(part * half_hidden + hidden.start, part * half_hidden + hidden.stop)
        grad_product = dot(wd_ref[:, hidden], low, 0, 0)
        terms = ffn_terms(gate_ref[rows, :].astype(F32), up_ref[rows, :].astype(F32), grad_product)
        acc_ref[...] += dot(wg_ref[:, hidden], terms[1], 1, 0) + dot(
            wu_ref[:, hidden], terms[2], 1, 0
        )
        weight_terms(
            stack, hidden, terms, [ref[hidden, :] for ref in kept2_refs], ffn1, ffn2, low, low2
        )
    fill_stack(stack, ffn1.shape[0])


def other_kernel(
    dq_ref, dkv_own_ref, dkv_got_ref, x_ref, grad_mid_ref,
    gain_ref, wq_ref, wk_ref, wv_ref, cos_ref, sin_ref,
    ffn1_ref, gate_ref, up_ref, wg_ref, wu_ref, wd_ref, ffn2_ref, low2_ref, kept2_refs,
    dpre_ref, dgain_ref, low_ref, gstream_ref, acc_ref, stack, dnormed_ref,
):
    qkv_back(
        dq_ref, dkv_own_ref, dkv_got_ref, wq_ref, wk_ref, wv_ref, cos_ref, sin_ref,
        dpre_ref, dnormed_ref,
    )
    norm_backward(x_ref, gain_ref, dnormed_ref, grad_mid_ref, gstream_ref, dgain_ref)
    low_ref[...] = gstream_ref[...].astype(BF16)
    acc_ref[...] = jnp.zeros(acc_ref.shape, F32)
    ffn_back(
        1, stack, low_ref[...], ffn1_ref[...], ffn2_ref[...], low2_ref[...],
        gate_ref, up_ref, wg_ref, wu_ref, wd_ref, kept2_refs, acc_ref,
    )


def own_kernel(
    low_ref, gstream_ref, acc_in_ref,
    ffn1_ref, gate_ref, up_ref, wg_ref, wu_ref, wd_ref, ffn2_ref, low2_ref, kept2_refs,
    mid_ref, wo_ref, ffn_gain_ref, dffn_gain2_ref,
    stack, grad_mid_ref, grad_mid_low_ref, grad_ctx_ref, dffn_gain_ref, acc_ref,
):
    acc_ref[...] = acc_in_ref[...]
    ffn_back(
        0, stack, low_ref[...], ffn1_ref[...], ffn2_ref[...], low2_ref[...],
        gate_ref, up_ref, wg_ref, wu_ref, wd_ref, kept2_refs, acc_ref,
    )
    norm_backward(mid_ref, ffn_gain_ref, acc_ref, gstream_ref, grad_mid_ref, dffn_gain_ref)
    dffn_gain_ref[...] += dffn_gain2_ref[...]
    grad_mid_low_ref[...] = grad_mid_ref[...].astype(BF16)
    grad_ctx_ref[...] = dot(wo_ref[...], grad_mid_low_ref[...], 1, 0).astype(BF16)


def last_kernel(
    dq_ref, dkv_own_ref, dkv_got_ref, x_low_ref, grad_mid_ref,
    gain_ref, wq_ref, wk_ref, wv_ref, cos_ref, sin_ref,
    dpre2_ref, normed_refs, ctx_refs, grad_mid_low_refs, dgain2_ref, dffn_gain_ref,
    out_refs, stack_own_ref, stack_other_ref,
    dpre_ref, dnormed_ref, x_ref, out_ref, dgain_ref, stack_ref,
):
    x_ref[...] = x_low_ref[...].astype(F32)
    width, rows = x_ref.shape[0], stack_ref.shape[1]
    qkv_back(
        dq_ref, dkv_own_ref, dkv_got_ref, wq_ref, wk_ref, wv_ref, cos_ref, sin_ref,
        dpre_ref, dnormed_ref,
    )
    norm_backward(x_ref, gain_ref, dnormed_ref, grad_mid_ref, out_ref, dgain_ref)
    cut = out_refs[0].shape[1]
    out_refs[0][...] = out_ref[:, :cut]
    out_refs[1][...] = out_ref[:, cut:]
    normed1, normed2 = (ref[...] for ref in normed_refs)
    dwq = dot(normed1, dpre_ref[:width, :], 1, 1) + dot(normed2, dpre2_ref[:width, :], 1, 1)
    dwkv = dot(dpre_ref[width:, :], normed1, 1, 1) + dot(dpre2_ref[width:, :], normed2, 1, 1)
    dwo = dot(ctx_refs[0][...], grad_mid_low_refs[0][...], 1, 1) + dot(
        ctx_refs[1][...], grad_mid_low_refs[1][...], 1, 1
    )
    half_rows = width + dwkv.shape[0] // 2
    rest = half_rows - width
    stack_ref[0, :width, :width] = dwq.astype(BF16)
    stack_ref[0, width:half_rows, :width] = dwo[:rest].astype(BF16)
    stack_ref[1, : width - rest, :width] = dwo[rest:].astype(BF16)
    stack_ref[1, width - rest : half_rows, :width] = dwkv.astype(BF16)
    lanes = stack_ref.shape[2] - width
    column = lax.broadcasted_iota(jnp.int32, (width, lanes), 1)
    gains = jnp.where(
        column == 0,
        dgain_ref[...] + dgain2_ref[...],
        jnp.where(column == 1, dffn_gain_ref[...], 0.0),
    ).astype(BF16)
    for part in range(2):
        stack_ref[part, :width, width:] = gains
        stack_ref[part, width:, width:] = jnp.zeros((rows - width, lanes), BF16)
        if rows > half_rows:
            stack_ref[part, half_rows:, :width] = jnp.zeros((rows - half_rows, width), BF16)
    core = lax.axis_index("tensor")
    stack_own_ref[...] = stack_ref[core]
    stack_other_ref[...] = stack_ref[1 - core]


def shape(dims, dtype):
    return jax.ShapeDtypeStruct(dims, dtype)


def run(kernel, args, outs, scratch=(), smem=0, hbm=0, name=None, us=5, limit=VMEM_LIMIT):
    leaves, tree = jax.tree.flatten(args)
    out_leaves, out_tree = jax.tree.flatten(outs)
    n_in, n_out = len(leaves), len(out_leaves)

    def body(*refs):
        ins = jax.tree.unflatten(tree, refs[:n_in])
        results = jax.tree.unflatten(out_tree, refs[n_in : n_in + n_out])
        kernel(*ins, *results, *refs[n_in + n_out :])

    in_specs = [
        pl.BlockSpec(
            memory_space=pltpu.SMEM if index < smem else pltpu.HBM if index < hbm else pltpu.VMEM
        )
        for index in range(n_in)
    ]
    results = pl.pallas_call(
        body,
        out_shape=out_leaves,
        in_specs=in_specs,
        out_specs=[pl.BlockSpec(memory_space=pltpu.VMEM)] * n_out,
        scratch_shapes=list(scratch),
        compiler_params=pltpu.CompilerParams(vmem_limit_bytes=limit),
        cost_estimate=pl.CostEstimate(
            flops=int(us * 1e9) + 1, bytes_accessed=2**20 if us else 1, transcendentals=0
        ),
        name=name,
    )(*leaves)
    return jax.tree.unflatten(out_tree, results)


def swap(array):
    return lax.ppermute(array, "tensor", [(0, 1), (1, 0)])


def partners(sizes, bits):
    n, cores = sizes
    return [
        (place * cores + core, (place ^ (1 << bits[core])) * cores + core)
        for place in range(n)
        for core in range(cores)
    ]


def own_bit(bits):
    place, core = lax.axis_index("dp"), lax.axis_index("tensor")
    shift = jnp.where(core == 0, jnp.int32(bits[0]), jnp.int32(bits[1]))
    return lax.shift_right_logical(place.astype(jnp.int32), shift) & 1


def scatter_kernel(bits, terms, sent_ref, kept_ref):
    count = sent_ref.shape[0]
    own = own_bit(bits)

    def body(index, carry):
        for half, out_ref in ((1 - own, sent_ref), (own, kept_ref)):
            at = half * count + index
            total = terms[0][at].astype(F32)
            for term in terms[1:]:
                total = total + term[at].astype(F32)
            out_ref[index] = total.astype(BF16)
        return carry

    lax.fori_loop(0, count, body, 0)


def add_kernel(one_ref, two_ref, out_ref):
    out_ref[...] = (one_ref[...].astype(F32) + two_ref[...].astype(F32)).astype(BF16)


def join(bits, own_ref, got_ref, out_ref):
    count = own_ref.shape[0]
    own = own_bit(bits)

    def body(index, carry):
        out_ref[own * count + index] = own_ref[index]
        out_ref[(1 - own) * count + index] = got_ref[index]
        return carry

    lax.fori_loop(0, count, body, 0)


class Stream:
    def __init__(self, name, terms, sizes, orders):
        self.name, self.sizes = name, sizes
        self.bits = list(zip(*orders))
        self.halvings = len(self.bits) - 1
        self.chunks = 1 << self.halvings
        self.terms = [term.reshape((self.chunks, -1) + term.shape[1:]) for term in terms]
        self.rounds = 2 * self.halvings + 1
        self.round = 0

    def call(self, kernel, args, counts):
        rows, columns = self.terms[0].shape[1:]
        outs = tuple(shape((count, rows, columns), BF16) for count in counts)
        return run(kernel, args, outs, name=f"{self.name}_{self.round}", us=0)

    def load(self):
        if self.round < self.halvings:
            bits = self.bits[self.round]
            half = self.terms[0].shape[0] // 2

            def kernel(terms, *outs):
                scatter_kernel(bits, terms, *outs)

            sent, kept = self.call(kernel, (tuple(self.terms),), (half, half))
            self.terms = [kept]
            return sent
        if self.round == self.halvings or self.round == self.halvings + 1:
            (sent,) = self.call(add_kernel, tuple(self.terms), (1,))
            self.terms = [sent]
            return sent
        bits = self.bits[2 * self.halvings + 1 - self.round]

        def kernel(own_ref, got_ref, out_ref):
            join(bits, own_ref, got_ref, out_ref)

        (sent,) = self.call(kernel, tuple(self.terms), (2 * self.terms[0].shape[0],))
        self.terms = [sent]
        return sent

    def step(self, token):
        if self.done:
            return token
        self.terms, token = lax.optimization_barrier((self.terms, token))
        sent = self.load()
        which = self.round if self.round <= self.halvings else 2 * self.halvings - self.round
        got = lax.ppermute(sent, ("dp", "tensor"), partners(self.sizes, self.bits[which]))
        self.terms = self.terms + [got]
        self.round += 1
        return sent

    @property
    def done(self):
        return self.round == self.rounds

    def join(self, out_ref, own_ref, got_ref):
        join(self.bits[0], own_ref, got_ref, out_ref)


def finish_kernel(stream, pair, outs, all_ref):
    width = outs[0].shape[0]
    stream.join(all_ref, *pair)
    rows = all_ref.shape[1]
    for index, out_ref in enumerate(outs):
        at, end = index * width, (index + 1) * width
        while at < end:
            chunk, inside = divmod(at, rows)
            count = min(end - at, rows - inside)
            out_ref[at - index * width : at - index * width + count, :] = all_ref[
                chunk, inside : inside + count, :
            ].astype(F32)
            at += count


def pack_kernel(stream, own_ref, got_ref, out_ref, all_ref):
    stream.join(all_ref, own_ref, got_ref)
    rows = all_ref.shape[1]
    for chunk in range(all_ref.shape[0]):
        out_ref[chunk * rows : (chunk + 1) * rows, :] = all_ref[chunk]


def unpack_kernel(
    half_rows, pack_ref, pack_got_ref,
    gain_ref, ffn_gain_ref, dwq_ref, dwk_ref, dwv_ref, dwo_ref, all_ref,
):
    width, kv_width = dwq_ref.shape[0], dwk_ref.shape[0]
    core = lax.axis_index("tensor")
    for which, ref in ((core, pack_ref), (1 - core, pack_got_ref)):
        all_ref[which] = ref[:half_rows, :width].astype(F32)
    rest = half_rows - width
    dwq_ref[...] = all_ref[0, :width]
    dwo_ref[:rest, :] = all_ref[0, width:]
    dwo_ref[rest:, :] = all_ref[1, : width - rest]
    dwk_ref[...] = all_ref[1, width - rest : width - rest + kv_width]
    dwv_ref[...] = all_ref[1, width - rest + kv_width :]
    for at, ref in ((0, gain_ref), (1, ffn_gain_ref)):
        ref[...] = pack_ref[:width, width + at : width + at + 1].astype(F32)


def tie(*arrays):
    return lax.optimization_barrier(arrays)


def orders_of(n):
    bits = list(range(n.bit_length() - 1))
    if len(bits) < 3:
        return [(bits, bits)] * 2
    mixed = ([0, 2, 1] + bits[3:], [1, 0, 2] + bits[3:])
    near = (bits, [1, 0] + bits[2:])
    far = ([2, 0, 1] + bits[3:], [2, 1, 0] + bits[3:])
    return [mixed, far]


def position_tables(length):
    places = np.arange(length, dtype=np.float32)
    inverse = np.float32(10000.0) ** (np.arange(HALF, dtype=np.float32) * np.float32(-2.0 / HEAD_DIM))
    angles = inverse.astype(np.float32)[:, None] * places[None, :]
    return jnp.asarray(np.cos(angles)), jnp.asarray(np.sin(angles))


def per_device(
    sizes, tokens, segments, cotangent, attn_gain, w_query, w_key, w_value, w_out, ffn_gain,
    w_gate, w_up, w_down,
):
    _, half, width = tokens.shape
    kv_width = KV_HEADS * HEAD_DIM
    hidden = w_gate.shape[1]
    n = sizes[0]
    core = lax.axis_index("tensor")
    cut = half // 2
    tokens, cotangent = tokens[0].T, cotangent[0].T
    w_key, w_value, w_down = w_key.T, w_value.T, w_down.T

    tokens_got = swap(tokens)
    all_tables = position_tables(segments.shape[1])
    gains = jnp.stack([attn_gain, ffn_gain])
    where = (segments, segments)
    projections = (w_query, w_key, w_value)

    act = shape((width, half), F32)
    low = shape((width, half), BF16)
    kv = shape((2 * kv_width, half), BF16)
    wide = shape((2 * hidden, half), BF16)
    thin = shape((hidden, half), BF16)
    column = shape((width, 1), F32)
    square = shape((width, width), F32)
    heads_f32 = pltpu.VMEM((HEADS, BLOCK, BLOCK), F32)
    heads_low = pltpu.VMEM((HEADS, BLOCK, BLOCK), BF16)
    key_scratch = [
        pltpu.VMEM((4, 2 * kv_width, BLOCK), BF16),
        pltpu.VMEM((2 * KV_HEADS, 4 * BLOCK, HEAD_DIM), BF16),
        pltpu.VMEM((BLOCK, BLOCK), F32),
        pltpu.VMEM((4 * BLOCK, 8), jnp.int32),
        heads_f32,
    ]
    act_scratch = pltpu.VMEM((width, half), F32)
    low_scratch = pltpu.VMEM((width, half), BF16)

    def attend(query, kv_own, kv_other):
        return run(
            attend_kernel,
            where + (query, kv_own, kv_other),
            (low, shape((16, half), F32)),
            key_scratch
            + [pltpu.VMEM((16, BLOCK), F32), pltpu.VMEM((16, BLOCK), F32),
               pltpu.VMEM((width, BLOCK), F32)],
            smem=1,
            name="attend",
            us=6,
        )

    def attend_back(query, kv_own, kv_other, ctx, lse, grad, us=9):
        return run(
            attend_back_kernel,
            where + (query, kv_own, kv_other, ctx, lse, grad),
            (act, shape((2 * kv_width, half), F32), kv),
            key_scratch
            + [heads_low, heads_low, pltpu.VMEM((16, half), F32),
               pltpu.VMEM((4, 2 * kv_width, BLOCK), F32)],
            smem=1,
            name="attend_back",
            us=us,
        )

    weight_scratch = [
        pltpu.VMEM(weight.shape, BF16) for weight in (w_query, w_key, w_value)
    ]
    table = shape((HALF, half), F32)
    x1, normed1, query1, kv1, gain_col, ffn_gain_col, *tables = run(
        first_kernel,
        (tokens, tokens_got) + projections + (gains,) + all_tables,
        (low, low, low, kv, column, column, table, table),
        [act_scratch, low_scratch, low_scratch]
        + weight_scratch
        + [pltpu.SemaphoreType.DMA((5,))],
        hbm=5,
        name="first",
        us=2,
    )
    tables = tuple(tables)
    kv1, w_gate, w_up, w_down, cot_sent = tie(kv1, w_gate, w_up, w_down, cotangent)
    kv1_other = swap(kv1)
    gate_pair = (w_gate, swap(w_gate))
    up_pair = (w_up, swap(w_up))
    down_pair = (w_down, swap(w_down))
    cot_got = swap(cot_sent)
    ctx1, lse1 = attend(query1, kv1, kv1_other)
    mid1, ffn1, gate1, up1, x2, normed2, query2, kv2 = run(
        middle_kernel,
        (x1, ctx1, w_out, ffn_gain_col, gate_pair, up_pair, down_pair, gain_col)
        + projections + tables,
        (act, low, wide, wide, act, low, low, kv),
        name="middle",
        us=6,
    )
    kv2_other = swap(kv2)
    ctx2, lse2 = attend(query2, kv2, kv2_other)
    tile_low = shape((width, cut), BF16)
    (
        (output, output_sent), cot, ffn2, kept2_own, kept2_other, grad_mid2, grad_mid_low2,
        grad_ctx2, dffn_gain2,
    ) = run(
        turn_kernel,
        (x2, ctx2, w_out, ffn_gain_col, gate_pair, up_pair, down_pair, cotangent, cot_got),
        ((tile_low, tile_low), low, low, (thin,) * 3, (thin,) * 3, act, low, low, column),
        [act_scratch, act_scratch],
        name="turn",
        us=9,
    )
    dq2, dkv_own2, dkv_sent2 = attend_back(query2, kv2, kv2_other, ctx2, lse2, grad_ctx2)
    dkv_sent2, output_sent = tie(dkv_sent2, output_sent)
    dkv_got2 = swap(dkv_sent2)
    output_got = swap(output_sent)
    pad = 8 * n
    stack_rows = -(-3 * width // pad) * pad
    stack_shape = shape((stack_rows, hidden), BF16)
    pre = shape((width + 2 * kv_width, half), BF16)
    dpre2, dgain2, low1, gstream, dffn, stack_other = run(
        other_kernel,
        (dq2, dkv_own2, dkv_got2, x2, grad_mid2, gain_col) + projections + tables
        + (ffn1, gate1, up1, gate_pair[1], up_pair[1], down_pair[1], ffn2, cot, kept2_other),
        (pre, column, low, act, act, stack_shape),
        [act_scratch],
        name="other",
        us=8,
    )
    stack_got = swap(stack_other)
    stack_own, grad_mid1, grad_mid_low1, grad_ctx1, dffn_gain = run(
        own_kernel,
        (low1, gstream, dffn, ffn1, gate1, up1, gate_pair[0], up_pair[0], down_pair[0],
         ffn2, cot, kept2_own, mid1, w_out, ffn_gain_col, dffn_gain2),
        (stack_shape, act, low, low, column),
        [act_scratch],
        name="own",
        us=7,
    )
    ffn_orders, pack_orders = orders_of(n)
    ffn = Stream("ffn", (stack_own, stack_got), sizes, ffn_orders)
    token = ffn.step(stack_own)
    grad_ctx1, token = tie(grad_ctx1, token)
    dq1, dkv_own1, dkv_sent1 = attend_back(query1, kv1, kv1_other, ctx1, lse1, grad_ctx1, 0)
    dkv_got1 = swap(dkv_sent1)
    rows = -(-(2 * width + 2 * kv_width) // 2 // pad) * pad
    lanes = -(-width // 128) * 128
    lanes = lanes if lanes - width >= 2 else lanes + 128
    half_stack = shape((rows, lanes), BF16)
    tile_act = shape((width, cut), F32)
    (grad_input, grad_input_sent), pack_own, pack_other = run(
        last_kernel,
        (dq1, dkv_own1, dkv_got1, x1, grad_mid1, gain_col) + projections + tables
        + (dpre2, (normed1, normed2), (ctx1, ctx2), (grad_mid_low1, grad_mid_low2),
           dgain2, dffn_gain),
        ((tile_act, tile_act), half_stack, half_stack),
        [pltpu.VMEM(pre.shape, BF16), act_scratch, act_scratch, act_scratch,
         pltpu.VMEM((width, 1), F32), pltpu.VMEM((2, rows, lanes), BF16)],
        name="last",
        us=0,
    )
    pack_other, grad_input_sent = tie(pack_other, grad_input_sent)
    pack = Stream("pack", (pack_own, swap(pack_other)), sizes, pack_orders)
    grad_input_got = swap(grad_input_sent)
    token = pack_own
    for which in "fafafaafafafa":
        token = (ffn if which == "f" else pack).step(token)
    while not (ffn.done and pack.done):
        token = pack.step(ffn.step(token))

    def kernel(own_ref, got_ref, out_ref, all_ref):
        pack_kernel(pack, own_ref, got_ref, out_ref, all_ref)

    (pack_sum,) = run(
        kernel, tuple(pack.terms), (half_stack,),
        [pltpu.VMEM((pack.chunks, rows // pack.chunks, lanes), BF16)], name="pack_all", us=0,
    )
    half_rows = width + kv_width

    def kernel(*refs):
        unpack_kernel(half_rows, *refs)

    kv_square = shape((kv_width, width), F32)
    dgain, dffn_gain, dw_query, dw_key, dw_value, dw_out = run(
        kernel,
        (pack_sum, swap(pack_sum)),
        (column, column, square, kv_square, kv_square, square),
        [pltpu.VMEM((2, half_rows, width), F32)],
        name="unpack",
        us=0,
    )
    output = jnp.concatenate([output, output_got], axis=1)
    grad_input = jnp.concatenate([grad_input, grad_input_got], axis=1)
    dgain, dffn_gain = dgain[:, 0], dffn_gain[:, 0]
    pair, (output, grad_input, dgain, dffn_gain, dw_query, dw_key, dw_value, dw_out) = tie(
        tuple(ffn.terms),
        (output, grad_input, dgain, dffn_gain, dw_query, dw_key, dw_value, dw_out),
    )

    def kernel(pair, *refs):
        finish_kernel(ffn, pair, refs[:3], refs[3])

    dw_gate, dw_up, dw_down = run(
        kernel, (pair,), (shape((width, hidden), F32),) * 3,
        [pltpu.VMEM((ffn.chunks, stack_rows // ffn.chunks, hidden), BF16)], name="finish", us=0,
    )
    return (
        output.T[None],
        grad_input.T[None],
        dgain,
        dw_query,
        dw_key.T,
        dw_value.T,
        dw_out,
        dffn_gain,
        dw_gate,
        dw_up,
        dw_down.T,
    )


def solution(mesh):
    sizes = (mesh.shape["dp"], mesh.shape["tensor"])

    def local(*args):
        return per_device(sizes, *args)

    split = P("dp", "tensor", None)
    in_specs = (
        split, P("dp", None), split, P(), P(), P(), P(), P(), P(),
        P(None, "tensor"), P(None, "tensor"), P("tensor", None),
    )
    out_specs = (
        split, split, P(), P(), P(), P(), P(), P(),
        P(None, "tensor"), P(None, "tensor"), P("tensor", None),
    )
    return jax.shard_map(
        local, mesh=mesh, in_specs=in_specs, out_specs=out_specs, check_vma=False
    )
```

```python
import jax
import jax.numpy as jnp
import numpy as np
from jax import lax
from jax.experimental import pallas as pl
from jax.experimental.pallas import tpu as pltpu
from jax.sharding import PartitionSpec as P

HEADS = 9
KV_HEADS = 3
GROUP = HEADS // KV_HEADS
HEAD_DIM = 64
HALF = HEAD_DIM // 2
EPSILON = 1e-05
MASKED = -1e30
BLOCK = 256
SCALE = HEAD_DIM ** (-0.5)
F32 = jnp.float32
BF16 = jnp.bfloat16
VMEM_LIMIT = 16 * 2**20


def dot(left, right, left_dim, right_dim):
    return lax.dot_general(
        left, right, (((left_dim,), (right_dim,)), ((), ())), preferred_element_type=F32
    )


def pieces(size, step):
    return [slice(start, start + step) for start in range(0, size, step)]


def inverse_rms(x_ref):
    total = None
    for rows in pieces(x_ref.shape[0], 64):
        x = x_ref[rows, :]
        part = jnp.sum(x * x, axis=0, keepdims=True)
        total = part if total is None else total + part
    return lax.rsqrt(total / x_ref.shape[0] + EPSILON)


def norm_forward(x_ref, gain_ref, out_ref):
    scale = inverse_rms(x_ref)
    for rows in pieces(x_ref.shape[0], 64):
        out_ref[rows, :] = (x_ref[rows, :] * scale * gain_ref[rows, :]).astype(BF16)


def norm_backward(x_ref, gain_ref, grad_ref, add_ref, out_ref, gain_grad_ref):
    scale = inverse_rms(x_ref)
    inner = None
    for rows in pieces(x_ref.shape[0], 64):
        x, e = x_ref[rows, :], grad_ref[rows, :]
        xe = x * e
        gain_grad_ref[rows, :] = jnp.sum(xe * scale, axis=1, keepdims=True)
        part = jnp.sum(xe * gain_ref[rows, :], axis=0, keepdims=True)
        inner = part if inner is None else inner + part
    cubed = scale * scale * scale * (inner / x_ref.shape[0])
    for rows in pieces(x_ref.shape[0], 64):
        out_ref[rows, :] = (
            add_ref[rows, :].astype(F32)
            + scale * gain_ref[rows, :] * grad_ref[rows, :]
            - x_ref[rows, :] * cubed
        )


def rotated(x, cos_table, sin_table):
    front, back = x[:HALF], x[HALF:]
    return jnp.concatenate(
        [front * cos_table - back * sin_table, back * cos_table + front * sin_table], axis=0
    )


def project_qkv(normed_ref, wq_ref, wk_ref, wv_ref, cos_ref, sin_ref, q_ref, kv_ref):
    normed = normed_ref[...]
    cos_table, sin_table = cos_ref[...], sin_ref[...]
    key = dot(wk_ref[...], normed, 1, 0)
    for head in pieces(KV_HEADS * HEAD_DIM, HEAD_DIM):
        kv_ref[head, :] = rotated(key[head], cos_table, sin_table).astype(BF16)
    kv_ref[KV_HEADS * HEAD_DIM :, :] = dot(wv_ref[...], normed, 1, 0).astype(BF16)
    query = dot(wq_ref[...], normed, 0, 0)
    for head in pieces(HEADS * HEAD_DIM, HEAD_DIM):
        q_ref[head, :] = (rotated(query[head], cos_table, sin_table) * SCALE).astype(BF16)


def first_kernel(
    tokens_hbm, wq_hbm, wk_hbm, wv_hbm, cos_hbm, sin_hbm, gain_hbm, ffn_gain_hbm,
    low_ref, normed_ref, q_ref, kv_ref, gain_ref, ffn_gain_ref, cos_ref, sin_ref,
    wq_ref, wk_ref, wv_ref,
    x_ref, gain_in_ref, ffn_gain_in_ref, sems,
):
    cut = low_ref.shape[1]
    pairs = [
        (gain_hbm, gain_in_ref), (ffn_gain_hbm, ffn_gain_in_ref),
        (tokens_hbm.at[:, :cut], low_ref), (wk_hbm, wk_ref), (wv_hbm, wv_ref), (wq_hbm, wq_ref),
    ]
    for local, tile in enumerate(tile_places(lax.axis_index("tensor"))):
        cols = slice(local * cut, (local + 1) * cut)
        for source, target in ((cos_hbm, cos_ref), (sin_hbm, sin_ref)):
            pairs.append((source.at[:, tile_lanes(tile)], target.at[:, cols]))
    copies = [
        pltpu.make_async_copy(source, target, sems.at[index])
        for index, (source, target) in enumerate(pairs)
    ]
    for copy in copies:
        copy.start()
    copies[0].wait()
    copies[1].wait()
    for in_ref, column_ref in ((gain_in_ref, gain_ref), (ffn_gain_in_ref, ffn_gain_ref)):
        row = in_ref[...].reshape(1, -1)
        column_ref[...] = jnp.broadcast_to(row, (128, row.shape[1])).T[:, :1]
    copies[2].wait()
    x_ref[...] = low_ref[...].astype(F32)
    norm_forward(x_ref, gain_ref, normed_ref)
    for copy in copies[3:]:
        copy.wait()
    tables = (cos_ref.at[:, :cut], sin_ref.at[:, :cut])
    project_qkv(normed_ref, wq_ref, wk_ref, wv_ref, *tables, q_ref, kv_ref)


def second_kernel(
    got_ref, half_refs, gain_ref, cos_ref, sin_ref, wq_ref, wk_ref, wv_ref, full_refs, x_ref
):
    cut = x_ref.shape[1]
    for half_ref, full_ref in zip(half_refs, full_refs):
        full_ref[:, :cut] = half_ref[...]
    low_ref, normed_ref, q_ref, kv_ref = (ref.at[:, cut:] for ref in full_refs)
    low_ref[...] = got_ref[:, cut:]
    x_ref[...] = low_ref[...].astype(F32)
    norm_forward(x_ref, gain_ref, normed_ref)
    tables = (cos_ref.at[:, cut:], sin_ref.at[:, cut:])
    project_qkv(normed_ref, wq_ref, wk_ref, wv_ref, *tables, q_ref, kv_ref)


def tile_places(core):
    return 2 * core, 3 - 2 * core


def tile_lanes(tile):
    return pl.ds(pl.multiple_of(tile * BLOCK, BLOCK), BLOCK)


def set_labels(labels_ref, column_ref):
    column_ref[...] = jnp.broadcast_to(labels_ref[0:1, :], (8, labels_ref.shape[1])).T


def set_mask(bias_ref, labels_ref, column_ref, tile, kb):
    key_labels = column_ref[tile_lanes(kb), :1]
    key_place = kb * BLOCK + lax.broadcasted_iota(jnp.int32, (BLOCK, BLOCK), 0)
    place = tile * BLOCK + lax.broadcasted_iota(jnp.int32, (1, BLOCK), 1)
    allowed = (key_labels == labels_ref[0:1, tile_lanes(tile)]) & (key_place <= place)
    bias_ref[...] = jnp.where(allowed, 0.0, MASKED)


def first_block(segments_ref, tile):
    label = segments_ref[0, tile * BLOCK]
    count = jnp.int32(0)
    for kb in range(3):
        before = (kb < tile) & (segments_ref[0, kb * BLOCK + BLOCK - 1] < label)
        count = count + before.astype(jnp.int32)
    return count


def head_rows(head):
    return slice(head * HEAD_DIM, (head + 1) * HEAD_DIM)


def load_part(kv_ref, tok_ref):
    for head in range(2 * KV_HEADS):
        for cols in pieces(kv_ref.shape[1], BLOCK):
            tok_ref[head, cols, :] = kv_ref[head_rows(head), cols].T


def over_blocks(segments_ref, core, own, body):
    keys_of = tile_places(core if own else 1 - core)
    for local, tile in enumerate(tile_places(core)):
        cols = slice(local * BLOCK, (local + 1) * BLOCK)
        first = first_block(segments_ref, tile)

        def step(at, carry):
            kb = jnp.where(at == 0, keys_of[0], keys_of[1])

            @pl.when((kb >= first) & (kb <= tile))
            def _():
                body(tile, cols, kb, at)

            return carry

        lax.fori_loop(0, 2, step, 0)


def attend_kernel(
    own, segments_ref, labels_ref, q_ref, kv_ref, state_refs, out_refs,
    value_ref, bias_ref, column_ref, scores_ref,
):
    core = lax.axis_index("tensor")
    set_labels(labels_ref, column_ref)
    for at, cols in enumerate(pieces(kv_ref.shape[1], BLOCK)):
        for group in range(KV_HEADS):
            value_ref[at, group, :HEAD_DIM, :] = kv_ref[head_rows(KV_HEADS + group), cols]
            value_ref[at, group, HEAD_DIM:, :] = jnp.ones((16, BLOCK), BF16)
    m_ref, l_ref, acc_ref = out_refs if own else state_refs
    if own:
        m_ref[...] = jnp.full(m_ref.shape, MASKED, F32)
        l_ref[...] = jnp.zeros(l_ref.shape, F32)
        acc_ref[...] = jnp.zeros(acc_ref.shape, F32)

    def body(tile, cols, kb, at):
        set_mask(bias_ref, labels_ref, column_ref, tile, kb)
        keys = tile_lanes(at)

        def scores(group):
            key = kv_ref[head_rows(group), keys]
            for head in range(group * GROUP, (group + 1) * GROUP):
                scores_ref[head] = dot(key, q_ref[head_rows(head), cols], 0, 0) + bias_ref[...]

        def products(group):
            for head in range(group * GROUP, (group + 1) * GROUP):
                rows = head_rows(head)
                m_old = m_ref[head : head + 1, cols]
                m_new = jnp.maximum(m_old, jnp.max(scores_ref[head], axis=0, keepdims=True))
                m_ref[head : head + 1, cols] = m_new
                fade = jnp.exp(m_old - m_new)
                probs = jnp.exp(scores_ref[head] - m_new).astype(BF16)
                product = dot(value_ref[at, group], probs, 1, 0)
                l_ref[head : head + 1, cols] = (
                    l_ref[head : head + 1, cols] * fade + product[HEAD_DIM : HEAD_DIM + 1]
                )
                acc_ref[rows, cols] = acc_ref[rows, cols] * fade + product[:HEAD_DIM]

        scores(0)
        scores(1)
        products(0)
        scores(2)
        products(1)
        products(2)

    over_blocks(segments_ref, core, own, body)
    if not own:
        ctx_ref, lse_ref = out_refs
        for head in range(HEADS):
            total = l_ref[head : head + 1, :]
            ctx_ref[head_rows(head), :] = (acc_ref[head_rows(head), :] * (1.0 / total)).astype(BF16)
            lse_ref[head : head + 1, :] = m_ref[head : head + 1, :] + jnp.log(total)


def attend_back_kernel(
    own, segments_ref, labels_ref, q_ref, kv_ref, lse_ref, grad_ref, more_refs, out_refs,
    tok_ref, bias_ref, column_ref, probs_ref, probs_low_ref, gs_ref, dkv_ref,
):
    core = lax.axis_index("tensor")
    load_part(kv_ref, tok_ref)
    set_labels(labels_ref, column_ref)
    if own:
        dq_in_ref, delta_ref = more_refs
        dq_ref, dkv_out_ref = out_refs
        dq_ref[...] = dq_in_ref[...]
    else:
        (ctx_ref,) = more_refs
        dq_ref, delta_ref, dkv_out_ref = out_refs
        dq_ref[...] = jnp.zeros(dq_ref.shape, F32)
        for head in range(HEADS):
            rows = head_rows(head)
            delta_ref[head : head + 1, :] = jnp.sum(
                grad_ref[rows, :].astype(F32) * ctx_ref[rows, :].astype(F32), axis=0, keepdims=True
            )
    dkv_ref[...] = jnp.zeros(dkv_ref.shape, F32)

    def body(tile, cols, kb, at):
        set_mask(bias_ref, labels_ref, column_ref, tile, kb)
        keys = tile_lanes(at)
        for head in range(HEADS):
            key = tok_ref[head // GROUP, keys, :]
            scores = dot(key, q_ref[head_rows(head), cols], 1, 0) + bias_ref[...]
            probs = jnp.exp(scores - lse_ref[head : head + 1, cols])
            probs_ref[head] = probs
            probs_low_ref[head] = probs.astype(BF16)
        for head in range(HEADS):
            value = tok_ref[KV_HEADS + head // GROUP, keys, :]
            grad_probs = dot(value, grad_ref[head_rows(head), cols], 1, 0)
            gs_ref[head] = (
                probs_ref[head] * (grad_probs - delta_ref[head : head + 1, cols])
            ).astype(BF16)
        for group in range(KV_HEADS):
            dv = dkv_ref[at, head_rows(KV_HEADS + group), :]
            for head in range(group * GROUP, (group + 1) * GROUP):
                dv = dv + dot(grad_ref[head_rows(head), cols], probs_low_ref[head], 1, 1)
            dkv_ref[at, head_rows(KV_HEADS + group), :] = dv
        for group in range(KV_HEADS):
            dk = dkv_ref[at, head_rows(group), :]
            for head in range(group * GROUP, (group + 1) * GROUP):
                dk = dk + dot(q_ref[head_rows(head), cols], gs_ref[head], 1, 1)
            dkv_ref[at, head_rows(group), :] = dk
        for head in range(HEADS):
            key_cols = kv_ref[head_rows(head // GROUP), keys]
            dq_ref[head_rows(head), cols] += dot(key_cols, gs_ref[head], 1, 0)

    over_blocks(segments_ref, core, own, body)
    for at, cols in enumerate(pieces(dkv_out_ref.shape[1], BLOCK)):
        dkv_out_ref[:, cols] = dkv_ref[at].astype(dkv_out_ref.dtype)


def middle_kernel(
    low_ref, ctx_ref, wo_ref, ffn_gain_ref, wg_refs, wu_refs, wd_refs,
    gain_ref, wq_ref, wk_ref, wv_ref, cos_ref, sin_ref,
    mid_ref, ffn_ref, gate_ref, up_ref, x2_ref, normed_ref, q_ref, kv_ref, product_ref,
):
    mid_ref[...] = low_ref[...].astype(F32) + dot(wo_ref[...], ctx_ref[...], 0, 0)
    norm_forward(mid_ref, ffn_gain_ref, ffn_ref)
    ffn_in = ffn_ref[...]
    half_hidden = wg_refs[0].shape[1]
    for part in range(2):
        for hidden in pieces(half_hidden, BLOCK):
            gate = dot(wg_refs[part][:, hidden], ffn_in, 0, 0)
            up = dot(wu_refs[part][:, hidden], ffn_in, 0, 0)
            rows = slice(part * half_hidden + hidden.start, part * half_hidden + hidden.stop)
            gate_ref[rows, :] = gate.astype(BF16)
            up_ref[rows, :] = up.astype(BF16)
            product_ref[rows, :] = (gate * jax.nn.sigmoid(gate) * up).astype(BF16)
    x2_ref[...] = (
        mid_ref[...]
        + dot(wd_refs[0][...], product_ref[:half_hidden, :], 1, 0)
        + dot(wd_refs[1][...], product_ref[half_hidden:, :], 1, 0)
    )
    norm_forward(x2_ref, gain_ref, normed_ref)
    project_qkv(normed_ref, wq_ref, wk_ref, wv_ref, cos_ref, sin_ref, q_ref, kv_ref)


def ffn_terms(gate, up, grad_product):
    sig = jax.nn.sigmoid(gate)
    silu = gate * sig
    grad_gate = (grad_product * up * (sig + silu * (1.0 - sig))).astype(BF16)
    grad_up = (grad_product * silu).astype(BF16)
    return (silu * up).astype(BF16), grad_gate, grad_up


def turn_kernel(
    x_ref, ctx_ref, wo_ref, ffn_gain_ref, wg_refs, wu_refs, wd_refs, cotangent_ref, cot_got_ref,
    output_refs, cot_ref, ffn_ref, kept_own_refs, kept_other_refs,
    grad_mid_ref, grad_mid_low_ref, grad_ctx_ref, dgain_ref,
    mid_ref, acc_ref,
):
    mid_ref[...] = x_ref[...] + dot(wo_ref[...], ctx_ref[...], 0, 0)
    norm_forward(mid_ref, ffn_gain_ref, ffn_ref)
    ffn_in = ffn_ref[...]
    cut = cot_got_ref.shape[1] // 2
    cot_ref[:, :cut] = cotangent_ref[:, :cut]
    cot_ref[:, cut:] = cot_got_ref[:, cut:]
    grad_low = cot_ref[...]
    for part in range(2):
        for hidden in pieces(wg_refs[part].shape[1], BLOCK):
            gate = dot(wg_refs[part][:, hidden], ffn_in, 0, 0)
            up = dot(wu_refs[part][:, hidden], ffn_in, 0, 0)
            grad_product = dot(wd_refs[part][:, hidden], grad_low, 0, 0)
            kept = (kept_own_refs, kept_other_refs)[part]
            for ref, term in zip(kept, ffn_terms(gate, up, grad_product)):
                ref[hidden, :] = term
    acc_ref[...] = (
        mid_ref[...]
        + dot(wd_refs[0][...], kept_own_refs[0][...], 1, 0)
        + dot(wd_refs[1][...], kept_other_refs[0][...], 1, 0)
    )
    output_refs[0][...] = acc_ref[:, :cut].astype(BF16)
    output_refs[1][...] = acc_ref[:, cut:].astype(BF16)
    acc_ref[...] = (
        dot(wg_refs[0][...], kept_own_refs[1][...], 1, 0)
        + dot(wu_refs[0][...], kept_own_refs[2][...], 1, 0)
        + dot(wg_refs[1][...], kept_other_refs[1][...], 1, 0)
        + dot(wu_refs[1][...], kept_other_refs[2][...], 1, 0)
    )
    norm_backward(mid_ref, ffn_gain_ref, acc_ref, cot_ref, grad_mid_ref, dgain_ref)
    grad_mid_low_ref[...] = grad_mid_ref[...].astype(BF16)
    grad_ctx_ref[...] = dot(wo_ref[...], grad_mid_low_ref[...], 1, 0).astype(BF16)


def qkv_back(
    dq_ref, dkv_own_ref, dkv_got_ref, wq_ref, wk_ref, wv_ref, cos_ref, sin_ref, dpre_ref, dnormed_ref
):
    cos_table, sin_table = cos_ref[...], sin_ref[...]
    width, kv_width = HEADS * HEAD_DIM, KV_HEADS * HEAD_DIM
    for head in pieces(width, HEAD_DIM):
        dpre_ref[head, :] = rotated(dq_ref[head, :] * SCALE, cos_table, -sin_table).astype(BF16)
    for head in pieces(kv_width, HEAD_DIM):
        total = dkv_own_ref[head, :] + dkv_got_ref[head, :].astype(F32)
        rows = slice(width + head.start, width + head.stop)
        dpre_ref[rows, :] = rotated(total, cos_table, -sin_table).astype(BF16)
    dpre_ref[width + kv_width :, :] = (
        dkv_own_ref[kv_width:, :] + dkv_got_ref[kv_width:, :].astype(F32)
    ).astype(BF16)
    dnormed_ref[...] = (
        dot(wq_ref[...], dpre_ref[:width, :], 1, 0)
        + dot(wk_ref[...], dpre_ref[width : width + kv_width, :], 0, 0)
        + dot(wv_ref[...], dpre_ref[width + kv_width :, :], 0, 0)
    )


def fill_stack(stack, width):
    if stack.shape[0] > 3 * width:
        stack[3 * width :, :] = jnp.zeros((stack.shape[0] - 3 * width, stack.shape[1]), BF16)


def ffn_back(
    part, stack, low, ffn1, ffn2, low2, gate_ref, up_ref, wg_ref, wu_ref, wd_ref, kept2_refs,
    acc_ref, terms_ref,
):
    width, half_hidden = wg_ref.shape
    for hidden in pieces(half_hidden, BLOCK):
        rows = slice(part * half_hidden + hidden.start, part * half_hidden + hidden.stop)
        grad_product = dot(wd_ref[:, hidden], low, 0, 0)
        terms = ffn_terms(gate_ref[rows, :].astype(F32), up_ref[rows, :].astype(F32), grad_product)
        for at, term in enumerate(terms):
            terms_ref[at, hidden, :] = term
    acc_ref[...] += dot(wg_ref[...], terms_ref[1], 1, 0) + dot(wu_ref[...], terms_ref[2], 1, 0)
    for at, (left1, left2, which) in enumerate(((ffn1, ffn2, 1), (ffn1, ffn2, 2), (low, low2, 0))):
        stack[at * width : (at + 1) * width, :] = (
            dot(left1, terms_ref[which], 1, 1) + dot(left2, kept2_refs[which][...], 1, 1)
        ).astype(BF16)
    fill_stack(stack, width)


def other_kernel(
    dq_ref, dkv_own_ref, dkv_got_ref, x_ref, grad_mid_ref,
    gain_ref, wq_ref, wk_ref, wv_ref, cos_ref, sin_ref,
    ffn1_ref, gate_ref, up_ref, wg_ref, wu_ref, wd_ref, ffn2_ref, low2_ref, kept2_refs,
    dpre_ref, dgain_ref, low_ref, gstream_ref, acc_ref, stack, dnormed_ref, terms_ref,
):
    qkv_back(
        dq_ref, dkv_own_ref, dkv_got_ref, wq_ref, wk_ref, wv_ref, cos_ref, sin_ref,
        dpre_ref, dnormed_ref,
    )
    norm_backward(x_ref, gain_ref, dnormed_ref, grad_mid_ref, gstream_ref, dgain_ref)
    low_ref[...] = gstream_ref[...].astype(BF16)
    acc_ref[...] = jnp.zeros(acc_ref.shape, F32)
    ffn_back(
        1, stack, low_ref[...], ffn1_ref[...], ffn2_ref[...], low2_ref[...],
        gate_ref, up_ref, wg_ref, wu_ref, wd_ref, kept2_refs, acc_ref, terms_ref,
    )


def own_kernel(
    low_ref, gstream_ref, acc_in_ref,
    ffn1_ref, gate_ref, up_ref, wg_ref, wu_ref, wd_ref, ffn2_ref, low2_ref, kept2_refs,
    mid_ref, wo_ref, ffn_gain_ref, dffn_gain2_ref,
    stack, grad_mid_ref, grad_mid_low_ref, grad_ctx_ref, dffn_gain_ref, acc_ref, terms_ref,
):
    acc_ref[...] = acc_in_ref[...]
    ffn_back(
        0, stack, low_ref[...], ffn1_ref[...], ffn2_ref[...], low2_ref[...],
        gate_ref, up_ref, wg_ref, wu_ref, wd_ref, kept2_refs, acc_ref, terms_ref,
    )
    norm_backward(mid_ref, ffn_gain_ref, acc_ref, gstream_ref, grad_mid_ref, dffn_gain_ref)
    dffn_gain_ref[...] += dffn_gain2_ref[...]
    grad_mid_low_ref[...] = grad_mid_ref[...].astype(BF16)
    grad_ctx_ref[...] = dot(wo_ref[...], grad_mid_low_ref[...], 1, 0).astype(BF16)


def last_kernel(
    dq_ref, dkv_own_ref, dkv_got_ref, x_low_ref, grad_mid_ref,
    gain_ref, wq_ref, wk_ref, wv_ref, cos_ref, sin_ref,
    dpre2_ref, normed_refs, ctx_refs, grad_mid_low_refs, dgain2_ref, dffn_gain_ref,
    out_refs, stack_own_ref, stack_other_ref,
    dpre_ref, dnormed_ref, x_ref, out_ref, dgain_ref, stack_ref,
):
    x_ref[...] = x_low_ref[...].astype(F32)
    width, rows = x_ref.shape[0], stack_ref.shape[1]
    qkv_back(
        dq_ref, dkv_own_ref, dkv_got_ref, wq_ref, wk_ref, wv_ref, cos_ref, sin_ref,
        dpre_ref, dnormed_ref,
    )
    norm_backward(x_ref, gain_ref, dnormed_ref, grad_mid_ref, out_ref, dgain_ref)
    cut = out_refs[0].shape[1]
    out_refs[0][...] = out_ref[:, :cut]
    out_refs[1][...] = out_ref[:, cut:]
    normed1, normed2 = (ref[...] for ref in normed_refs)
    dwq = dot(normed1, dpre_ref[:width, :], 1, 1) + dot(normed2, dpre2_ref[:width, :], 1, 1)
    dwkv = dot(dpre_ref[width:, :], normed1, 1, 1) + dot(dpre2_ref[width:, :], normed2, 1, 1)
    dwo = dot(ctx_refs[0][...], grad_mid_low_refs[0][...], 1, 1) + dot(
        ctx_refs[1][...], grad_mid_low_refs[1][...], 1, 1
    )
    half_rows = width + dwkv.shape[0] // 2
    rest = half_rows - width
    stack_ref[0, :width, :width] = dwq.astype(BF16)
    stack_ref[0, width:half_rows, :width] = dwo[:rest].astype(BF16)
    stack_ref[1, : width - rest, :width] = dwo[rest:].astype(BF16)
    stack_ref[1, width - rest : half_rows, :width] = dwkv.astype(BF16)
    lanes = stack_ref.shape[2] - width
    column = lax.broadcasted_iota(jnp.int32, (width, lanes), 1)
    gains = jnp.where(
        column == 0,
        dgain_ref[...] + dgain2_ref[...],
        jnp.where(column == 1, dffn_gain_ref[...], 0.0),
    ).astype(BF16)
    for part in range(2):
        stack_ref[part, :width, width:] = gains
        stack_ref[part, width:, width:] = jnp.zeros((rows - width, lanes), BF16)
        if rows > half_rows:
            stack_ref[part, half_rows:, :width] = jnp.zeros((rows - half_rows, width), BF16)
    core = lax.axis_index("tensor")
    stack_own_ref[...] = stack_ref[core]
    stack_other_ref[...] = stack_ref[1 - core]


def shape(dims, dtype):
    return jax.ShapeDtypeStruct(dims, dtype)


def run(
    kernel, args, outs, scratch=(), smem=0, hbm=0, after=(), name=None, us=5, limit=VMEM_LIMIT
):
    leaves, tree = jax.tree.flatten(args)
    out_leaves, out_tree = jax.tree.flatten(outs)
    late = jax.tree.leaves(after)
    n_in, n_out = len(leaves), len(out_leaves)

    def body(*refs):
        ins = jax.tree.unflatten(tree, refs[:n_in])
        refs = refs[n_in + len(late) :]
        results = jax.tree.unflatten(out_tree, refs[:n_out])
        kernel(*ins, *results, *refs[n_out:])

    in_specs = [
        pl.BlockSpec(
            memory_space=pltpu.SMEM if index < smem else pltpu.HBM if index < hbm else pltpu.VMEM
        )
        for index in range(n_in)
    ] + [pl.BlockSpec(memory_space=pl.ANY)] * len(late)
    results = pl.pallas_call(
        body,
        out_shape=out_leaves,
        in_specs=in_specs,
        out_specs=[pl.BlockSpec(memory_space=pltpu.VMEM)] * n_out,
        scratch_shapes=list(scratch),
        compiler_params=pltpu.CompilerParams(vmem_limit_bytes=limit),
        cost_estimate=pl.CostEstimate(
            flops=int(us * 1e9) + 1, bytes_accessed=2**20 if us else 1, transcendentals=0
        ),
        name=name,
    )(*leaves, *late)
    return jax.tree.unflatten(out_tree, results)


def in_hbm(arrays):
    return tuple(pltpu.with_memory_space_constraint(array, pltpu.HBM) for array in arrays)


def swap(array):
    return lax.ppermute(array, "tensor", [(0, 1), (1, 0)])


def partners(sizes, bits):
    n, cores = sizes
    return [
        (place * cores + core, (place ^ (1 << bits[core])) * cores + core)
        for place in range(n)
        for core in range(cores)
    ]


def by_core(pair):
    return jnp.where(lax.axis_index("tensor") == 0, jnp.int32(pair[0]), jnp.int32(pair[1]))


def own_bit(bits):
    place = lax.axis_index("dp").astype(jnp.int32)
    return lax.shift_right_logical(place, by_core(bits)) & 1


def insert(index, rank, bit):
    low = index & (lax.shift_left(jnp.int32(1), rank) - 1)
    return lax.shift_left(index - low, jnp.int32(1)) + lax.shift_left(bit, rank) + low


def scatter_kernel(bits, ranks, terms, sent_ref, kept_ref):
    own, rank = own_bit(bits), by_core(ranks)

    def body(index, carry):
        for half, out_ref in ((1 - own, sent_ref), (own, kept_ref)):
            at = insert(index, rank, half)
            total = terms[0][at].astype(F32)
            for term in terms[1:]:
                total = total + term[at].astype(F32)
            out_ref[index] = total.astype(BF16)
        return carry

    lax.fori_loop(0, sent_ref.shape[0], body, 0)


def add_kernel(one_ref, two_ref, out_ref):
    out_ref[...] = (one_ref[...].astype(F32) + two_ref[...].astype(F32)).astype(BF16)


def join(bits, ranks, own_ref, got_ref, out_ref):
    own, rank = own_bit(bits), by_core(ranks)

    def body(index, carry):
        out_ref[insert(index, rank, own)] = own_ref[index]
        out_ref[insert(index, rank, 1 - own)] = got_ref[index]
        return carry

    lax.fori_loop(0, own_ref.shape[0], body, 0)


def ranks_of(dims, done):
    ranks = []
    for step in range(len(dims[0])):
        pair = []
        for order in dims:
            there = order[step + 1 :] if done == "after" else order[:step]
            pair.append(sum(other < order[step] for other in there))
        ranks.append(tuple(pair))
    return ranks


class Stream:
    def __init__(self, name, terms, sizes, orders):
        scatter, across, gather = orders
        self.name, self.sizes = name, sizes
        self.halvings = len(scatter[0])
        self.chunks = 1 << self.halvings
        self.bits = list(zip(*scatter)) + [(across, across)] + list(zip(*gather))
        self.ranks = ranks_of(scatter, "after") + [None] + ranks_of(gather, "before")
        self.terms = [term.reshape((self.chunks, -1) + term.shape[1:]) for term in terms]
        self.rounds = 2 * self.halvings + 1
        self.round = 0

    def call(self, kernel, args, counts, after):
        rows, columns = self.terms[0].shape[1:]
        outs = tuple(shape((count, rows, columns), BF16) for count in counts)
        return run(kernel, args, outs, after=after, name=f"{self.name}_{self.round}", us=0)

    def load(self, after):
        if self.round < self.halvings:
            half = self.terms[0].shape[0] // 2
            bits, ranks = self.bits[self.round], self.ranks[self.round]

            def kernel(terms, *outs):
                scatter_kernel(bits, ranks, terms, *outs)

            sent, kept = self.call(kernel, (tuple(self.terms),), (half, half), after)
            self.terms = [kept]
            return sent
        if self.round <= self.halvings + 1:
            (sent,) = self.call(add_kernel, tuple(self.terms), (1,), after)
        else:
            bits, ranks = self.bits[self.round - 1], self.ranks[self.round - 1]

            def kernel(*refs):
                join(bits, ranks, *refs)

            (sent,) = self.call(
                kernel, tuple(self.terms), (2 * self.terms[0].shape[0],), after
            )
        self.terms = [sent]
        return sent

    def step(self, token):
        if self.done:
            return token
        sent = self.load(token)
        got = lax.ppermute(sent, ("dp", "tensor"), partners(self.sizes, self.bits[self.round]))
        self.terms = self.terms + [got]
        self.round += 1
        return sent

    @property
    def done(self):
        return self.round == self.rounds

    def join(self, out_ref, own_ref, got_ref):
        join(self.bits[-1], self.ranks[-1], own_ref, got_ref, out_ref)


def finish_kernel(stream, pair, outs, all_ref):
    width = outs[0].shape[0]
    stream.join(all_ref, *pair)
    rows = all_ref.shape[1]
    for index, out_ref in enumerate(outs):
        at, end = index * width, (index + 1) * width
        while at < end:
            chunk, inside = divmod(at, rows)
            count = min(end - at, rows - inside)
            out_ref[at - index * width : at - index * width + count, :] = all_ref[
                chunk, inside : inside + count, :
            ].astype(F32)
            at += count


def pack_kernel(stream, own_ref, got_ref, out_ref, all_ref):
    stream.join(all_ref, own_ref, got_ref)
    rows = all_ref.shape[1]
    for chunk in range(all_ref.shape[0]):
        out_ref[chunk * rows : (chunk + 1) * rows, :] = all_ref[chunk]


def unpack_kernel(
    half_rows, pack_ref, pack_got_ref,
    gain_ref, ffn_gain_ref, dwq_ref, dwk_ref, dwv_ref, dwo_ref, all_ref,
):
    width, kv_width = dwq_ref.shape[0], dwk_ref.shape[0]
    core = lax.axis_index("tensor")
    for which, ref in ((core, pack_ref), (1 - core, pack_got_ref)):
        all_ref[which] = ref[:half_rows, :width].astype(F32)
    rest = half_rows - width
    dwq_ref[...] = all_ref[0, :width]
    dwo_ref[:rest, :] = all_ref[0, width:]
    dwo_ref[rest:, :] = all_ref[1, : width - rest]
    dwk_ref[...] = all_ref[1, width - rest : width - rest + kv_width]
    dwv_ref[...] = all_ref[1, width - rest + kv_width :]
    rows = pack_ref[:width, width:].astype(F32).T
    for at, ref in ((0, gain_ref), (1, ffn_gain_ref)):
        ref[...] = rows[at : at + 1, :].reshape(width)


def tie(*arrays):
    return lax.optimization_barrier(arrays)


def orders_of(n):
    bits = list(range(n.bit_length() - 1))
    across = bits[-1]
    halved = bits[:-1]
    if len(halved) < 3:
        return [((halved, halved), across, (halved, halved))] * 2
    rest = halved[3:]
    ffn = (([0, 2, 1] + rest, [1, 0, 2] + rest), across, (rest + [1, 2, 0], rest + [2, 0, 1]))
    attention = (([1, 0, 2] + rest,) * 2, across, (rest + [1, 0, 2],) * 2)
    return [ffn, attention]


def position_tables(length):
    places = np.arange(length, dtype=np.float32)
    inverse = np.float32(10000.0) ** (np.arange(HALF, dtype=np.float32) * np.float32(-2.0 / HEAD_DIM))
    angles = inverse.astype(np.float32)[:, None] * places[None, :]
    return jnp.asarray(np.cos(angles)), jnp.asarray(np.sin(angles))


def per_device(
    sizes, tokens, segments, cotangent, attn_gain, w_query, w_key, w_value, w_out, ffn_gain,
    w_gate, w_up, w_down,
):
    _, half, width = tokens.shape
    kv_width = KV_HEADS * HEAD_DIM
    hidden = w_gate.shape[1]
    n = sizes[0]
    core = lax.axis_index("tensor")
    cut = half // 2
    tokens, cotangent = tokens[0].T, cotangent[0].T
    w_key, w_value, w_down = w_key.T, w_value.T, w_down.T

    tokens_got = swap(tokens)
    all_tables = position_tables(segments.shape[1])
    where = (segments, segments)
    projections = (w_query, w_key, w_value)

    act = shape((width, half), F32)
    low = shape((width, half), BF16)
    kv = shape((2 * kv_width, half), BF16)
    kv_f32 = shape((2 * kv_width, half), F32)
    wide = shape((2 * hidden, half), BF16)
    thin = shape((hidden, half), BF16)
    column = shape((width, 1), F32)
    square = shape((width, width), F32)
    heads_f32 = pltpu.VMEM((HEADS, BLOCK, BLOCK), F32)
    heads_low = pltpu.VMEM((HEADS, BLOCK, BLOCK), BF16)
    key_scratch = pltpu.VMEM((2 * KV_HEADS, half, HEAD_DIM), BF16)
    mask_scratch = [
        pltpu.VMEM((BLOCK, BLOCK), F32), pltpu.VMEM((4 * BLOCK, 8), jnp.int32), heads_f32
    ]
    rows_f32 = shape((16, half), F32)
    act_scratch = pltpu.VMEM((width, half), F32)
    low_scratch = pltpu.VMEM((width, half), BF16)

    def attend(query, kv_own, kv_other):
        state = ()
        for own, kv_part in ((True, kv_own), (False, kv_other)):

            def kernel(*refs, own=own):
                attend_kernel(own, *refs)

            state = run(
                kernel,
                where + (query, kv_part, tuple(state)),
                ((rows_f32, rows_f32, act),) if own else ((low, rows_f32),),
                [pltpu.VMEM((2, KV_HEADS, HEAD_DIM + 16, BLOCK), BF16)]
                + mask_scratch,
                smem=1,
                name="attend_own" if own else "attend_other",
                us=4,
            )[0]
        return state

    def attend_back(query, kv_own, kv_other, ctx, lse, grad, us=5):
        more = (ctx,)
        for own, kv_part, dkv in ((False, kv_other, kv), (True, kv_own, kv_f32)):

            def kernel(*refs, own=own):
                attend_back_kernel(own, *refs)

            (outs,) = run(
                kernel,
                where + (query, kv_part, lse, grad, more),
                ((act, dkv),) if own else ((act, rows_f32, dkv),),
                [key_scratch] + mask_scratch
                + [heads_low, heads_low, pltpu.VMEM((2, 2 * kv_width, BLOCK), F32)],
                smem=1,
                name="attend_back_own" if own else "attend_back_other",
                us=us,
            )
            if not own:
                more = outs[:2]
                got = swap(outs[2])
        return outs[0], outs[1], got

    table = shape((HALF, half), F32)
    tile_low, tile_kv = shape((width, cut), BF16), shape((2 * kv_width, cut), BF16)
    x_half = pltpu.VMEM((width, cut), F32)
    *halves, gain_col, ffn_gain_col, cos_table, sin_table, wq, wk, wv = run(
        first_kernel,
        in_hbm((tokens,) + projections + all_tables + (attn_gain, ffn_gain)),
        (tile_low, tile_low, tile_low, tile_kv, column, column, table, table)
        + tuple(shape(weight.shape, BF16) for weight in projections),
        [x_half, pltpu.VMEM((width,), F32), pltpu.VMEM((width,), F32),
         pltpu.SemaphoreType.DMA((10,))],
        hbm=8,
        name="first",
        us=2,
    )
    projections, tables = (wq, wk, wv), (cos_table, sin_table)
    (x1, normed1, query1, kv1), = run(
        second_kernel,
        (tokens_got, tuple(halves), gain_col) + tables + projections,
        ((low, low, low, kv),),
        [x_half],
        name="second",
        us=1,
    )
    kv1, cot_sent = tie(kv1, cotangent)
    kv1_other = swap(kv1)
    gate_pair = (w_gate, swap(w_gate))
    up_pair = (w_up, swap(w_up))
    down_pair = (w_down, swap(w_down))
    cot_got = swap(cot_sent)
    ctx1, lse1 = attend(query1, kv1, kv1_other)
    mid1, ffn1, gate1, up1, x2, normed2, query2, kv2 = run(
        middle_kernel,
        (x1, ctx1, w_out, ffn_gain_col, gate_pair, up_pair, down_pair, gain_col)
        + projections + tables,
        (act, low, wide, wide, act, low, low, kv),
        [pltpu.VMEM(wide.shape, BF16)],
        name="middle",
        us=6,
    )
    kv2_other = swap(kv2)
    ctx2, lse2 = attend(query2, kv2, kv2_other)
    (
        (output, output_sent), cot, ffn2, kept2_own, kept2_other, grad_mid2, grad_mid_low2,
        grad_ctx2, dffn_gain2,
    ) = run(
        turn_kernel,
        (x2, ctx2, w_out, ffn_gain_col, gate_pair, up_pair, down_pair, cotangent, cot_got),
        ((tile_low, tile_low), low, low, (thin,) * 3, (thin,) * 3, act, low, low, column),
        [act_scratch, act_scratch],
        name="turn",
        us=9,
    )
    dq2, dkv_own2, dkv_got2 = attend_back(query2, kv2, kv2_other, ctx2, lse2, grad_ctx2)
    output_got = swap(output_sent)
    pad = 8 * n
    stack_rows = -(-3 * width // pad) * pad
    stack_shape = shape((stack_rows, hidden), BF16)
    pre = shape((width + 2 * kv_width, half), BF16)
    dpre2, dgain2, low1, gstream, dffn, stack_other = run(
        other_kernel,
        (dq2, dkv_own2, dkv_got2, x2, grad_mid2, gain_col) + projections + tables
        + (ffn1, gate1, up1, gate_pair[1], up_pair[1], down_pair[1], ffn2, cot, kept2_other),
        (pre, column, low, act, act, stack_shape),
        [act_scratch, pltpu.VMEM((3,) + thin.shape, BF16)],
        name="other",
        us=8,
    )
    stack_got = swap(stack_other)
    stack_own, grad_mid1, grad_mid_low1, grad_ctx1, dffn_gain = run(
        own_kernel,
        (low1, gstream, dffn, ffn1, gate1, up1, gate_pair[0], up_pair[0], down_pair[0],
         ffn2, cot, kept2_own, mid1, w_out, ffn_gain_col, dffn_gain2),
        (stack_shape, act, low, low, column),
        [act_scratch, pltpu.VMEM((3,) + thin.shape, BF16)],
        name="own",
        us=7,
    )
    ffn_orders, pack_orders = orders_of(n)
    ffn = Stream("ffn", (stack_own, stack_got), sizes, ffn_orders)
    token = ffn.step(stack_own)
    grad_ctx1, token = tie(grad_ctx1, token)
    dq1, dkv_own1, dkv_got1 = attend_back(query1, kv1, kv1_other, ctx1, lse1, grad_ctx1, 0)
    rows = -(-(2 * width + 2 * kv_width) // 2 // pad) * pad
    lanes = -(-width // 128) * 128
    lanes = lanes if lanes - width >= 2 else lanes + 128
    half_stack = shape((rows, lanes), BF16)
    tile_act = shape((width, cut), F32)
    (grad_input, grad_input_sent), pack_own, pack_other = run(
        last_kernel,
        (dq1, dkv_own1, dkv_got1, x1, grad_mid1, gain_col) + projections + tables
        + (dpre2, (normed1, normed2), (ctx1, ctx2), (grad_mid_low1, grad_mid_low2),
           dgain2, dffn_gain),
        ((tile_act, tile_act), half_stack, half_stack),
        [pltpu.VMEM(pre.shape, BF16), act_scratch, act_scratch, act_scratch,
         pltpu.VMEM((width, 1), F32), pltpu.VMEM((2, rows, lanes), BF16)],
        name="last",
        us=0,
    )
    pack_other, grad_input_sent = tie(pack_other, grad_input_sent)
    pack = Stream("pack", (pack_own, swap(pack_other)), sizes, pack_orders)
    grad_input_got = swap(grad_input_sent)
    token = pack_own
    for index, which in enumerate("fafafaafafafa"):
        token = (ffn if which == "f" else pack).step(token)
        if index == 5:
            output = jnp.concatenate([output, output_got], axis=1)
            grad_input = jnp.concatenate([grad_input, grad_input_got], axis=1)
            token = (token, output, grad_input)
    while not (ffn.done and pack.done):
        token = pack.step(ffn.step(token))

    def kernel(own_ref, got_ref, out_ref, all_ref):
        pack_kernel(pack, own_ref, got_ref, out_ref, all_ref)

    (pack_sum,) = run(
        kernel, tuple(pack.terms), (half_stack,),
        [pltpu.VMEM((pack.chunks, rows // pack.chunks, lanes), BF16)], name="pack_all", us=0,
    )
    half_rows = width + kv_width

    def kernel(*refs):
        unpack_kernel(half_rows, *refs)

    kv_square = shape((kv_width, width), F32)
    vector = shape((width,), F32)
    dgain, dffn_gain, dw_query, dw_key, dw_value, dw_out = run(
        kernel,
        (pack_sum, swap(pack_sum)),
        (vector, vector, square, kv_square, kv_square, square),
        [pltpu.VMEM((2, half_rows, width), F32)],
        name="unpack",
        us=0,
    )
    pair, (output, grad_input, dgain, dffn_gain, dw_query, dw_key, dw_value, dw_out) = tie(
        tuple(ffn.terms),
        (output, grad_input, dgain, dffn_gain, dw_query, dw_key, dw_value, dw_out),
    )

    def kernel(pair, *refs):
        finish_kernel(ffn, pair, refs[:3], refs[3])

    dw_gate, dw_up, dw_down = run(
        kernel, (pair,), (shape((width, hidden), F32),) * 3,
        [pltpu.VMEM((ffn.chunks, stack_rows // ffn.chunks, hidden), BF16)], name="finish", us=0,
    )
    return (
        output.T[None],
        grad_input.T[None],
        dgain,
        dw_query,
        dw_key.T,
        dw_value.T,
        dw_out,
        dffn_gain,
        dw_gate,
        dw_up,
        dw_down.T,
    )


def solution(mesh):
    sizes = (mesh.shape["dp"], mesh.shape["tensor"])

    def local(*args):
        return per_device(sizes, *args)

    split = P("dp", "tensor", None)
    in_specs = (
        split, P("dp", None), split, P(), P(), P(), P(), P(), P(),
        P(None, "tensor"), P(None, "tensor"), P("tensor", None),
    )
    out_specs = (
        split, split, P(), P(), P(), P(), P(), P(),
        P(None, "tensor"), P(None, "tensor"), P("tensor", None),
    )
    return jax.shard_map(
        local, mesh=mesh, in_specs=in_specs, out_specs=out_specs, check_vma=False
    )
```

```python
import jax
import jax.numpy as jnp
import numpy as np
from jax import lax
from jax.experimental import pallas as pl
from jax.experimental.pallas import tpu as pltpu
from jax.sharding import PartitionSpec as P

HEADS = 9
KV_HEADS = 3
GROUP = HEADS // KV_HEADS
HEAD_DIM = 64
HALF = HEAD_DIM // 2
EPSILON = 1e-05
MASKED = -1e30
BLOCK = 256
SCALE = HEAD_DIM ** (-0.5)
F32 = jnp.float32
BF16 = jnp.bfloat16
VMEM_LIMIT = 16 * 2**20


def dot(left, right, left_dim, right_dim):
    return lax.dot_general(
        left, right, (((left_dim,), (right_dim,)), ((), ())), preferred_element_type=F32
    )


def pieces(size, step):
    return [slice(start, start + step) for start in range(0, size, step)]


def inverse_rms(x_ref):
    total = None
    for rows in pieces(x_ref.shape[0], 64):
        x = x_ref[rows, :]
        part = jnp.sum(x * x, axis=0, keepdims=True)
        total = part if total is None else total + part
    return lax.rsqrt(total / x_ref.shape[0] + EPSILON)


def norm_forward(x_ref, gain_ref, out_ref):
    scale = inverse_rms(x_ref)
    for rows in pieces(x_ref.shape[0], 64):
        out_ref[rows, :] = (x_ref[rows, :] * scale * gain_ref[rows, :]).astype(BF16)


def norm_backward(x_ref, gain_ref, grad_ref, add_ref, out_ref, gain_grad_ref):
    scale = inverse_rms(x_ref)
    inner = None
    for rows in pieces(x_ref.shape[0], 64):
        x, e = x_ref[rows, :], grad_ref[rows, :]
        xe = x * e
        gain_grad_ref[rows, :] = jnp.sum(xe * scale, axis=1, keepdims=True)
        part = jnp.sum(xe * gain_ref[rows, :], axis=0, keepdims=True)
        inner = part if inner is None else inner + part
    cubed = scale * scale * scale * (inner / x_ref.shape[0])
    for rows in pieces(x_ref.shape[0], 64):
        out_ref[rows, :] = (
            add_ref[rows, :].astype(F32)
            + scale * gain_ref[rows, :] * grad_ref[rows, :]
            - x_ref[rows, :] * cubed
        )


def rotated(x, cos_table, sin_table):
    front, back = x[:HALF], x[HALF:]
    return jnp.concatenate(
        [front * cos_table - back * sin_table, back * cos_table + front * sin_table], axis=0
    )


def project_qkv(normed_ref, wq_ref, wk_ref, wv_ref, cos_ref, sin_ref, q_ref, kv_ref):
    normed = normed_ref[...]
    cos_table, sin_table = cos_ref[...], sin_ref[...]
    key = dot(wk_ref[...], normed, 1, 0)
    for head in pieces(KV_HEADS * HEAD_DIM, HEAD_DIM):
        kv_ref[head, :] = rotated(key[head], cos_table, sin_table).astype(BF16)
    kv_ref[KV_HEADS * HEAD_DIM :, :] = dot(wv_ref[...], normed, 1, 0).astype(BF16)
    query = dot(wq_ref[...], normed, 0, 0)
    for head in pieces(HEADS * HEAD_DIM, HEAD_DIM):
        q_ref[head, :] = (rotated(query[head], cos_table, sin_table) * SCALE).astype(BF16)


def first_kernel(
    tokens_hbm, wq_hbm, wk_hbm, wv_hbm, cos_hbm, sin_hbm, gain_hbm, ffn_gain_hbm,
    low_ref, normed_ref, q_ref, kv_ref, gain_ref, ffn_gain_ref, cos_ref, sin_ref,
    wq_ref, wk_ref, wv_ref,
    x_ref, gain_in_ref, ffn_gain_in_ref, sems,
):
    cut = low_ref.shape[1]
    pairs = [
        (gain_hbm, gain_in_ref), (ffn_gain_hbm, ffn_gain_in_ref),
        (tokens_hbm.at[:, :cut], low_ref), (wk_hbm, wk_ref), (wv_hbm, wv_ref), (wq_hbm, wq_ref),
    ]
    for local, tile in enumerate(tile_places(lax.axis_index("tensor"))):
        cols = slice(local * cut, (local + 1) * cut)
        for source, target in ((cos_hbm, cos_ref), (sin_hbm, sin_ref)):
            pairs.append((source.at[:, tile_lanes(tile)], target.at[:, cols]))
    copies = [
        pltpu.make_async_copy(source, target, sems.at[index])
        for index, (source, target) in enumerate(pairs)
    ]
    for copy in copies:
        copy.start()
    copies[0].wait()
    copies[1].wait()
    for in_ref, column_ref in ((gain_in_ref, gain_ref), (ffn_gain_in_ref, ffn_gain_ref)):
        row = in_ref[...].reshape(1, -1)
        column_ref[...] = jnp.broadcast_to(row, (128, row.shape[1])).T[:, :1]
    copies[2].wait()
    x_ref[...] = low_ref[...].astype(F32)
    norm_forward(x_ref, gain_ref, normed_ref)
    for copy in copies[3:]:
        copy.wait()
    tables = (cos_ref.at[:, :cut], sin_ref.at[:, :cut])
    project_qkv(normed_ref, wq_ref, wk_ref, wv_ref, *tables, q_ref, kv_ref)


def second_kernel(
    got_ref, half_refs, gain_ref, cos_ref, sin_ref, wq_ref, wk_ref, wv_ref, full_refs, x_ref
):
    cut = x_ref.shape[1]
    for half_ref, full_ref in zip(half_refs, full_refs):
        full_ref[:, :cut] = half_ref[...]
    low_ref, normed_ref, q_ref, kv_ref = (ref.at[:, cut:] for ref in full_refs)
    low_ref[...] = got_ref[:, cut:]
    x_ref[...] = low_ref[...].astype(F32)
    norm_forward(x_ref, gain_ref, normed_ref)
    tables = (cos_ref.at[:, cut:], sin_ref.at[:, cut:])
    project_qkv(normed_ref, wq_ref, wk_ref, wv_ref, *tables, q_ref, kv_ref)


def tile_places(core):
    return 2 * core, 3 - 2 * core


def tile_lanes(tile):
    return pl.ds(pl.multiple_of(tile * BLOCK, BLOCK), BLOCK)


def set_labels(labels_ref, column_ref):
    column_ref[...] = jnp.broadcast_to(labels_ref[0:1, :], (8, labels_ref.shape[1])).T


def set_mask(bias_ref, labels_ref, column_ref, tile, kb):
    key_labels = column_ref[tile_lanes(kb), :1]
    key_place = kb * BLOCK + lax.broadcasted_iota(jnp.int32, (BLOCK, BLOCK), 0)
    place = tile * BLOCK + lax.broadcasted_iota(jnp.int32, (1, BLOCK), 1)
    allowed = (key_labels == labels_ref[0:1, tile_lanes(tile)]) & (key_place <= place)
    bias_ref[...] = jnp.where(allowed, 0.0, MASKED)


def first_block(segments_ref, tile):
    label = segments_ref[0, tile * BLOCK]
    count = jnp.int32(0)
    for kb in range(3):
        before = (kb < tile) & (segments_ref[0, kb * BLOCK + BLOCK - 1] < label)
        count = count + before.astype(jnp.int32)
    return count


def head_rows(head):
    return slice(head * HEAD_DIM, (head + 1) * HEAD_DIM)


def load_part(kv_ref, tok_ref):
    for head in range(2 * KV_HEADS):
        for cols in pieces(kv_ref.shape[1], BLOCK):
            tok_ref[head, cols, :] = kv_ref[head_rows(head), cols].T


def over_blocks(segments_ref, core, own, body):
    keys_of = tile_places(core if own else 1 - core)
    for local, tile in enumerate(tile_places(core)):
        cols = slice(local * BLOCK, (local + 1) * BLOCK)
        first = first_block(segments_ref, tile)

        def step(at, carry):
            kb = jnp.where(at == 0, keys_of[0], keys_of[1])

            @pl.when((kb >= first) & (kb <= tile))
            def _():
                body(local, tile, cols, kb, at)

            return carry

        lax.fori_loop(0, 2, step, 0)


def attend_kernel(
    own, segments_ref, labels_ref, q_ref, kv_ref, state_refs, mask_in_refs, out_refs, mask_out_refs,
    value_ref, column_ref, scores_ref,
):
    core = lax.axis_index("tensor")
    if mask_out_refs:
        set_labels(labels_ref, column_ref)
    (masks_ref,) = mask_in_refs or mask_out_refs
    for at, cols in enumerate(pieces(kv_ref.shape[1], BLOCK)):
        for group in range(KV_HEADS):
            value_ref[at, group, :HEAD_DIM, :] = kv_ref[head_rows(KV_HEADS + group), cols]
            value_ref[at, group, HEAD_DIM:, :] = jnp.ones((16, BLOCK), BF16)
    m_ref, l_ref, acc_ref = out_refs if own else state_refs
    if own:
        m_ref[...] = jnp.full(m_ref.shape, MASKED, F32)
        l_ref[...] = jnp.zeros(l_ref.shape, F32)
        acc_ref[...] = jnp.zeros(acc_ref.shape, F32)

    def body(local, tile, cols, kb, at):
        bias_ref = masks_ref.at[local, at]
        if mask_out_refs:
            set_mask(bias_ref, labels_ref, column_ref, tile, kb)
        keys = tile_lanes(at)

        def scores(group):
            key = kv_ref[head_rows(group), keys]
            for head in range(group * GROUP, (group + 1) * GROUP):
                scores_ref[head] = dot(key, q_ref[head_rows(head), cols], 0, 0) + bias_ref[...]

        def products(group):
            for head in range(group * GROUP, (group + 1) * GROUP):
                rows = head_rows(head)
                m_old = m_ref[head : head + 1, cols]
                m_new = jnp.maximum(m_old, jnp.max(scores_ref[head], axis=0, keepdims=True))
                m_ref[head : head + 1, cols] = m_new
                fade = jnp.exp(m_old - m_new)
                probs = jnp.exp(scores_ref[head] - m_new).astype(BF16)
                product = dot(value_ref[at, group], probs, 1, 0)
                l_ref[head : head + 1, cols] = (
                    l_ref[head : head + 1, cols] * fade + product[HEAD_DIM : HEAD_DIM + 1]
                )
                acc_ref[rows, cols] = acc_ref[rows, cols] * fade + product[:HEAD_DIM]

        scores(0)
        scores(1)
        products(0)
        scores(2)
        products(1)
        products(2)

    over_blocks(segments_ref, core, own, body)
    if not own:
        ctx_ref, lse_ref = out_refs
        for head in range(HEADS):
            total = l_ref[head : head + 1, :]
            ctx_ref[head_rows(head), :] = (acc_ref[head_rows(head), :] * (1.0 / total)).astype(BF16)
            lse_ref[head : head + 1, :] = m_ref[head : head + 1, :] + jnp.log(total)


def attend_back_kernel(
    own, segments_ref, q_ref, kv_ref, masks_ref, lse_ref, grad_ref, more_refs, out_refs,
    tok_ref, probs_ref, probs_low_ref, gs_ref, dkv_ref,
):
    core = lax.axis_index("tensor")
    load_part(kv_ref, tok_ref)
    if own:
        dq_in_ref, delta_ref = more_refs
        dq_ref, dkv_out_ref = out_refs
        dq_ref[...] = dq_in_ref[...]
    else:
        (ctx_ref,) = more_refs
        dq_ref, delta_ref, dkv_out_ref = out_refs
        dq_ref[...] = jnp.zeros(dq_ref.shape, F32)
        for head in range(HEADS):
            rows = head_rows(head)
            delta_ref[head : head + 1, :] = jnp.sum(
                grad_ref[rows, :].astype(F32) * ctx_ref[rows, :].astype(F32), axis=0, keepdims=True
            )
    dkv_ref[...] = jnp.zeros(dkv_ref.shape, F32)

    def body(local, tile, cols, kb, at):
        bias_ref = masks_ref.at[local, at]
        keys = tile_lanes(at)
        for head in range(HEADS):
            key = tok_ref[head // GROUP, keys, :]
            scores = dot(key, q_ref[head_rows(head), cols], 1, 0) + bias_ref[...]
            probs = jnp.exp(scores - lse_ref[head : head + 1, cols])
            probs_ref[head] = probs
            probs_low_ref[head] = probs.astype(BF16)
        for head in range(HEADS):
            value = tok_ref[KV_HEADS + head // GROUP, keys, :]
            grad_probs = dot(value, grad_ref[head_rows(head), cols], 1, 0)
            gs_ref[head] = (
                probs_ref[head] * (grad_probs - delta_ref[head : head + 1, cols])
            ).astype(BF16)
        for group in range(KV_HEADS):
            dv = dkv_ref[at, head_rows(KV_HEADS + group), :]
            for head in range(group * GROUP, (group + 1) * GROUP):
                dv = dv + dot(grad_ref[head_rows(head), cols], probs_low_ref[head], 1, 1)
            dkv_ref[at, head_rows(KV_HEADS + group), :] = dv
        for group in range(KV_HEADS):
            dk = dkv_ref[at, head_rows(group), :]
            for head in range(group * GROUP, (group + 1) * GROUP):
                dk = dk + dot(q_ref[head_rows(head), cols], gs_ref[head], 1, 1)
            dkv_ref[at, head_rows(group), :] = dk
        for head in range(HEADS):
            key_cols = kv_ref[head_rows(head // GROUP), keys]
            dq_ref[head_rows(head), cols] += dot(key_cols, gs_ref[head], 1, 0)

    over_blocks(segments_ref, core, own, body)
    for at, cols in enumerate(pieces(dkv_out_ref.shape[1], BLOCK)):
        dkv_out_ref[:, cols] = dkv_ref[at].astype(dkv_out_ref.dtype)


def middle_kernel(
    low_ref, ctx_ref, wo_ref, ffn_gain_ref, wg_refs, wu_refs, wd_refs,
    gain_ref, wq_ref, wk_ref, wv_ref, cos_ref, sin_ref,
    mid_ref, ffn_ref, gate_ref, up_ref, x2_ref, normed_ref, q_ref, kv_ref, product_ref,
):
    mid_ref[...] = low_ref[...].astype(F32) + dot(wo_ref[...], ctx_ref[...], 0, 0)
    norm_forward(mid_ref, ffn_gain_ref, ffn_ref)
    ffn_in = ffn_ref[...]
    half_hidden = wg_refs[0].shape[1]
    for part in range(2):
        for hidden in pieces(half_hidden, BLOCK):
            gate = dot(wg_refs[part][:, hidden], ffn_in, 0, 0)
            up = dot(wu_refs[part][:, hidden], ffn_in, 0, 0)
            rows = slice(part * half_hidden + hidden.start, part * half_hidden + hidden.stop)
            gate_ref[rows, :] = gate.astype(BF16)
            up_ref[rows, :] = up.astype(BF16)
            product_ref[rows, :] = (gate * jax.nn.sigmoid(gate) * up).astype(BF16)
    x2_ref[...] = (
        mid_ref[...]
        + dot(wd_refs[0][...], product_ref[:half_hidden, :], 1, 0)
        + dot(wd_refs[1][...], product_ref[half_hidden:, :], 1, 0)
    )
    norm_forward(x2_ref, gain_ref, normed_ref)
    project_qkv(normed_ref, wq_ref, wk_ref, wv_ref, cos_ref, sin_ref, q_ref, kv_ref)


def ffn_terms(gate, up, grad_product):
    sig = jax.nn.sigmoid(gate)
    silu = gate * sig
    grad_gate = (grad_product * up * (sig + silu * (1.0 - sig))).astype(BF16)
    grad_up = (grad_product * silu).astype(BF16)
    return (silu * up).astype(BF16), grad_gate, grad_up


def turn_kernel(
    x_ref, ctx_ref, wo_ref, ffn_gain_ref, wg_refs, wu_refs, wd_refs, cotangent_ref, cot_got_ref,
    output_refs, cot_ref, ffn_ref, kept_own_refs, kept_other_refs,
    grad_mid_ref, grad_mid_low_ref, grad_ctx_ref, dgain_ref,
    mid_ref, acc_ref,
):
    mid_ref[...] = x_ref[...] + dot(wo_ref[...], ctx_ref[...], 0, 0)
    norm_forward(mid_ref, ffn_gain_ref, ffn_ref)
    ffn_in = ffn_ref[...]
    cut = cot_got_ref.shape[1] // 2
    cot_ref[:, :cut] = cotangent_ref[:, :cut]
    cot_ref[:, cut:] = cot_got_ref[:, cut:]
    grad_low = cot_ref[...]
    for part in range(2):
        for hidden in pieces(wg_refs[part].shape[1], BLOCK):
            gate = dot(wg_refs[part][:, hidden], ffn_in, 0, 0)
            up = dot(wu_refs[part][:, hidden], ffn_in, 0, 0)
            grad_product = dot(wd_refs[part][:, hidden], grad_low, 0, 0)
            kept = (kept_own_refs, kept_other_refs)[part]
            for ref, term in zip(kept, ffn_terms(gate, up, grad_product)):
                ref[hidden, :] = term
    acc_ref[...] = (
        mid_ref[...]
        + dot(wd_refs[0][...], kept_own_refs[0][...], 1, 0)
        + dot(wd_refs[1][...], kept_other_refs[0][...], 1, 0)
    )
    output_refs[0][...] = acc_ref[:, :cut].astype(BF16)
    output_refs[1][...] = acc_ref[:, cut:].astype(BF16)
    acc_ref[...] = (
        dot(wg_refs[0][...], kept_own_refs[1][...], 1, 0)
        + dot(wu_refs[0][...], kept_own_refs[2][...], 1, 0)
        + dot(wg_refs[1][...], kept_other_refs[1][...], 1, 0)
        + dot(wu_refs[1][...], kept_other_refs[2][...], 1, 0)
    )
    norm_backward(mid_ref, ffn_gain_ref, acc_ref, cot_ref, grad_mid_ref, dgain_ref)
    grad_mid_low_ref[...] = grad_mid_ref[...].astype(BF16)
    grad_ctx_ref[...] = dot(wo_ref[...], grad_mid_low_ref[...], 1, 0).astype(BF16)


def qkv_back(
    dq_ref, dkv_own_ref, dkv_got_ref, wq_ref, wk_ref, wv_ref, cos_ref, sin_ref, dpre_ref, dnormed_ref
):
    cos_table, sin_table = cos_ref[...], sin_ref[...]
    width, kv_width = HEADS * HEAD_DIM, KV_HEADS * HEAD_DIM
    for head in pieces(width, HEAD_DIM):
        dpre_ref[head, :] = rotated(dq_ref[head, :] * SCALE, cos_table, -sin_table).astype(BF16)
    for head in pieces(kv_width, HEAD_DIM):
        total = dkv_own_ref[head, :] + dkv_got_ref[head, :].astype(F32)
        rows = slice(width + head.start, width + head.stop)
        dpre_ref[rows, :] = rotated(total, cos_table, -sin_table).astype(BF16)
    dpre_ref[width + kv_width :, :] = (
        dkv_own_ref[kv_width:, :] + dkv_got_ref[kv_width:, :].astype(F32)
    ).astype(BF16)
    dnormed_ref[...] = (
        dot(wq_ref[...], dpre_ref[:width, :], 1, 0)
        + dot(wk_ref[...], dpre_ref[width : width + kv_width, :], 0, 0)
        + dot(wv_ref[...], dpre_ref[width + kv_width :, :], 0, 0)
    )


def fill_stack(stack, width):
    if stack.shape[0] > 3 * width:
        stack[3 * width :, :] = jnp.zeros((stack.shape[0] - 3 * width, stack.shape[1]), BF16)


def ffn_back(
    part, stack, low, ffn1, ffn2, low2, gate_ref, up_ref, wg_ref, wu_ref, wd_ref, kept2_refs,
    acc_ref, terms_ref,
):
    width, half_hidden = wg_ref.shape
    for hidden in pieces(half_hidden, BLOCK):
        rows = slice(part * half_hidden + hidden.start, part * half_hidden + hidden.stop)
        grad_product = dot(wd_ref[:, hidden], low, 0, 0)
        terms = ffn_terms(gate_ref[rows, :].astype(F32), up_ref[rows, :].astype(F32), grad_product)
        for at, term in enumerate(terms):
            terms_ref[at, hidden, :] = term
    acc_ref[...] += dot(wg_ref[...], terms_ref[1], 1, 0) + dot(wu_ref[...], terms_ref[2], 1, 0)
    for at, (left1, left2, which) in enumerate(((ffn1, ffn2, 1), (ffn1, ffn2, 2), (low, low2, 0))):
        stack[at * width : (at + 1) * width, :] = (
            dot(left1, terms_ref[which], 1, 1) + dot(left2, kept2_refs[which][...], 1, 1)
        ).astype(BF16)
    fill_stack(stack, width)


def other_kernel(
    dq_ref, dkv_own_ref, dkv_got_ref, x_ref, grad_mid_ref,
    gain_ref, wq_ref, wk_ref, wv_ref, cos_ref, sin_ref,
    ffn1_ref, gate_ref, up_ref, wg_ref, wu_ref, wd_ref, ffn2_ref, low2_ref, kept2_refs,
    dpre_ref, dgain_ref, low_ref, gstream_ref, acc_ref, stack, dnormed_ref, terms_ref,
):
    qkv_back(
        dq_ref, dkv_own_ref, dkv_got_ref, wq_ref, wk_ref, wv_ref, cos_ref, sin_ref,
        dpre_ref, dnormed_ref,
    )
    norm_backward(x_ref, gain_ref, dnormed_ref, grad_mid_ref, gstream_ref, dgain_ref)
    low_ref[...] = gstream_ref[...].astype(BF16)
    acc_ref[...] = jnp.zeros(acc_ref.shape, F32)
    ffn_back(
        1, stack, low_ref[...], ffn1_ref[...], ffn2_ref[...], low2_ref[...],
        gate_ref, up_ref, wg_ref, wu_ref, wd_ref, kept2_refs, acc_ref, terms_ref,
    )


def own_kernel(
    low_ref, gstream_ref, acc_in_ref,
    ffn1_ref, gate_ref, up_ref, wg_ref, wu_ref, wd_ref, ffn2_ref, low2_ref, kept2_refs,
    mid_ref, wo_ref, ffn_gain_ref, dffn_gain2_ref,
    stack, grad_mid_ref, grad_mid_low_ref, grad_ctx_ref, dffn_gain_ref, acc_ref, terms_ref,
):
    acc_ref[...] = acc_in_ref[...]
    ffn_back(
        0, stack, low_ref[...], ffn1_ref[...], ffn2_ref[...], low2_ref[...],
        gate_ref, up_ref, wg_ref, wu_ref, wd_ref, kept2_refs, acc_ref, terms_ref,
    )
    norm_backward(mid_ref, ffn_gain_ref, acc_ref, gstream_ref, grad_mid_ref, dffn_gain_ref)
    dffn_gain_ref[...] += dffn_gain2_ref[...]
    grad_mid_low_ref[...] = grad_mid_ref[...].astype(BF16)
    grad_ctx_ref[...] = dot(wo_ref[...], grad_mid_low_ref[...], 1, 0).astype(BF16)


def last_kernel(
    dq_ref, dkv_own_ref, dkv_got_ref, x_low_ref, grad_mid_ref,
    gain_ref, wq_ref, wk_ref, wv_ref, cos_ref, sin_ref,
    dpre2_ref, normed_refs, ctx_refs, grad_mid_low_refs, dgain2_ref, dffn_gain_ref,
    out_refs, stack_own_ref, stack_other_ref,
    dpre_ref, dnormed_ref, x_ref, out_ref, dgain_ref, stack_ref,
):
    x_ref[...] = x_low_ref[...].astype(F32)
    width, rows = x_ref.shape[0], stack_ref.shape[1]
    qkv_back(
        dq_ref, dkv_own_ref, dkv_got_ref, wq_ref, wk_ref, wv_ref, cos_ref, sin_ref,
        dpre_ref, dnormed_ref,
    )
    norm_backward(x_ref, gain_ref, dnormed_ref, grad_mid_ref, out_ref, dgain_ref)
    cut = out_refs[0].shape[1]
    out_refs[0][...] = out_ref[:, :cut]
    out_refs[1][...] = out_ref[:, cut:]
    normed1, normed2 = (ref[...] for ref in normed_refs)
    dwq = dot(normed1, dpre_ref[:width, :], 1, 1) + dot(normed2, dpre2_ref[:width, :], 1, 1)
    dwkv = dot(dpre_ref[width:, :], normed1, 1, 1) + dot(dpre2_ref[width:, :], normed2, 1, 1)
    dwo = dot(ctx_refs[0][...], grad_mid_low_refs[0][...], 1, 1) + dot(
        ctx_refs[1][...], grad_mid_low_refs[1][...], 1, 1
    )
    half_rows = width + dwkv.shape[0] // 2
    rest = half_rows - width
    stack_ref[0, :width, :width] = dwq.astype(BF16)
    stack_ref[0, width:half_rows, :width] = dwo[:rest].astype(BF16)
    stack_ref[1, : width - rest, :width] = dwo[rest:].astype(BF16)
    stack_ref[1, width - rest : half_rows, :width] = dwkv.astype(BF16)
    lanes = stack_ref.shape[2] - width
    column = lax.broadcasted_iota(jnp.int32, (width, lanes), 1)
    gains = jnp.where(
        column == 0,
        dgain_ref[...] + dgain2_ref[...],
        jnp.where(column == 1, dffn_gain_ref[...], 0.0),
    ).astype(BF16)
    for part in range(2):
        stack_ref[part, :width, width:] = gains
        stack_ref[part, width:, width:] = jnp.zeros((rows - width, lanes), BF16)
        if rows > half_rows:
            stack_ref[part, half_rows:, :width] = jnp.zeros((rows - half_rows, width), BF16)
    core = lax.axis_index("tensor")
    stack_own_ref[...] = stack_ref[core]
    stack_other_ref[...] = stack_ref[1 - core]


def shape(dims, dtype):
    return jax.ShapeDtypeStruct(dims, dtype)


def run(
    kernel, args, outs, scratch=(), smem=0, hbm=0, after=(), name=None, us=5, limit=VMEM_LIMIT,
    hbm_outs=False, update=(),
):
    leaves, tree = jax.tree.flatten(args)
    out_leaves, out_tree = jax.tree.flatten(outs)
    late = jax.tree.leaves(after) + list(update)
    n_in, n_out = len(leaves), len(out_leaves)

    def body(*refs):
        ins = jax.tree.unflatten(tree, refs[:n_in])
        refs = refs[n_in + len(late) :]
        results = jax.tree.unflatten(out_tree, refs[:n_out])
        kernel(*ins, *results, *refs[n_out:])

    in_specs = [
        pl.BlockSpec(
            memory_space=pltpu.SMEM if index < smem else pltpu.HBM if index < hbm else pltpu.VMEM
        )
        for index in range(n_in)
    ] + [pl.BlockSpec(memory_space=pl.ANY)] * len(late)
    results = pl.pallas_call(
        body,
        out_shape=out_leaves,
        in_specs=in_specs,
        out_specs=[pl.BlockSpec(memory_space=pltpu.HBM if hbm_outs else pltpu.VMEM)] * n_out,
        scratch_shapes=list(scratch),
        input_output_aliases={
            n_in + len(late) - len(update) + index: index for index in range(len(update))
        },
        compiler_params=pltpu.CompilerParams(vmem_limit_bytes=limit),
        cost_estimate=pl.CostEstimate(
            flops=int(us * 1e9) + 1, bytes_accessed=2**20 if us else 1, transcendentals=0
        ),
        name=name,
    )(*leaves, *late)
    return jax.tree.unflatten(out_tree, results)


def in_hbm(arrays):
    return tuple(pltpu.with_memory_space_constraint(array, pltpu.HBM) for array in arrays)


def swap(array):
    return lax.ppermute(array, "tensor", [(0, 1), (1, 0)])


def partners(sizes, bits):
    n, cores = sizes
    return [
        (place * cores + core, (place ^ (1 << bits[core])) * cores + core)
        for place in range(n)
        for core in range(cores)
    ]


def by_core(pair):
    return jnp.where(lax.axis_index("tensor") == 0, jnp.int32(pair[0]), jnp.int32(pair[1]))


def own_bit(bits):
    place = lax.axis_index("dp").astype(jnp.int32)
    return lax.shift_right_logical(place, by_core(bits)) & 1


def insert(index, rank, bit):
    low = index & (lax.shift_left(jnp.int32(1), rank) - 1)
    return lax.shift_left(index - low, jnp.int32(1)) + lax.shift_left(bit, rank) + low


def scatter_kernel(bits, ranks, sent, terms, out_ref):
    own, rank = own_bit(bits), by_core(ranks)
    half = 1 - own if sent else own

    def body(index, carry):
        at = insert(index, rank, half)
        total = terms[0][at].astype(F32)
        for term in terms[1:]:
            total = total + term[at].astype(F32)
        out_ref[index] = total.astype(BF16)
        return carry

    lax.fori_loop(0, out_ref.shape[0], body, 0)


def add_kernel(one_ref, two_ref, out_ref):
    out_ref[...] = (one_ref[...].astype(F32) + two_ref[...].astype(F32)).astype(BF16)


def join(bits, ranks, own_ref, got_ref, out_ref):
    own, rank = own_bit(bits), by_core(ranks)

    def body(index, carry):
        out_ref[insert(index, rank, own)] = own_ref[index]
        out_ref[insert(index, rank, 1 - own)] = got_ref[index]
        return carry

    lax.fori_loop(0, own_ref.shape[0], body, 0)


def ranks_of(dims, done):
    ranks = []
    for step in range(len(dims[0])):
        pair = []
        for order in dims:
            there = order[step + 1 :] if done == "after" else order[:step]
            pair.append(sum(other < order[step] for other in there))
        ranks.append(tuple(pair))
    return ranks


class Stream:
    def __init__(self, name, terms, sizes, orders):
        scatter, across, gather = orders
        self.name, self.sizes = name, sizes
        self.halvings = len(scatter[0])
        self.chunks = 1 << self.halvings
        self.bits = list(zip(*scatter)) + [(across, across)] + list(zip(*gather))
        self.ranks = ranks_of(scatter, "after") + [None] + ranks_of(gather, "before")
        self.terms = [term.reshape((self.chunks, -1) + term.shape[1:]) for term in terms]
        self.rounds = 2 * self.halvings + 1
        self.round = 0

    def call(self, kernel, args, counts, after):
        rows, columns = self.terms[0].shape[1:]
        outs = tuple(shape((count, rows, columns), BF16) for count in counts)
        return run(kernel, args, outs, after=after, name=f"{self.name}_{self.round}", us=0)

    def load(self, after):
        if self.round < self.halvings:
            half = self.terms[0].shape[0] // 2
            bits, ranks = self.bits[self.round], self.ranks[self.round]

            terms = tuple(self.terms)

            def part(which, after):
                def kernel(terms, out_ref):
                    scatter_kernel(bits, ranks, which, terms, out_ref)

                return self.call(kernel, (terms,), (half,), after)[0]

            sent = part(True, after)
            self.terms = [part(False, sent)]
            return sent
        if self.round <= self.halvings + 1:
            (sent,) = self.call(add_kernel, tuple(self.terms), (1,), after)
        else:
            bits, ranks = self.bits[self.round - 1], self.ranks[self.round - 1]

            def kernel(*refs):
                join(bits, ranks, *refs)

            (sent,) = self.call(
                kernel, tuple(self.terms), (2 * self.terms[0].shape[0],), after
            )
        self.terms = [sent]
        return sent

    def step(self, token):
        if self.done:
            return token
        sent = self.load(token)
        got = lax.ppermute(sent, ("dp", "tensor"), partners(self.sizes, self.bits[self.round]))
        self.terms = self.terms + [got]
        self.round += 1
        return sent

    @property
    def done(self):
        return self.round == self.rounds

    def join(self, out_ref, own_ref, got_ref):
        join(self.bits[-1], self.ranks[-1], own_ref, got_ref, out_ref)


def finish_kernel(stream, mine, part_ref, outs, wide_ref, sems):
    count, rows = part_ref.shape[:2]
    for index in range(count):
        wide_ref[index] = part_ref[index].astype(F32)
    width = outs[0].shape[0]
    own, core = own_bit(stream.bits[-1]), lax.axis_index("tensor")
    half = own if mine else 1 - own

    def copies(chunk, index):
        at, end, found = chunk * rows, (chunk + 1) * rows, []
        while at < end:
            which, inside = divmod(at, width)
            size = min(end - at, width - inside)
            if which == len(outs):
                break
            found.append(
                pltpu.make_async_copy(
                    wide_ref.at[index, at - chunk * rows : at - chunk * rows + size, :],
                    outs[which].at[inside : inside + size, :],
                    sems.at[index, len(found)],
                )
            )
            at += size
        return found

    for act in ("start", "wait"):
        for which, rank in enumerate(stream.ranks[-1]):
            for chunk in range(2 * count):
                bit, low = (chunk >> rank) & 1, chunk & ((1 << rank) - 1)
                index = ((chunk >> (rank + 1)) << rank) + low

                @pl.when((core == which) & (half == bit))
                def _():
                    for copy in copies(chunk, index):
                        getattr(copy, act)()


def pack_kernel(stream, own_ref, got_ref, out_ref, all_ref):
    stream.join(all_ref, own_ref, got_ref)
    rows = all_ref.shape[1]
    for chunk in range(all_ref.shape[0]):
        out_ref[chunk * rows : (chunk + 1) * rows, :] = all_ref[chunk]


def unpack_kernel(
    half_rows, pack_ref, pack_got_ref,
    gain_ref, ffn_gain_ref, dwq_ref, dwk_ref, dwv_ref, dwo_ref, all_ref,
):
    width, kv_width = dwq_ref.shape[0], dwk_ref.shape[0]
    core = lax.axis_index("tensor")
    for which, ref in ((core, pack_ref), (1 - core, pack_got_ref)):
        all_ref[which] = ref[:half_rows, :width].astype(F32)
    rest = half_rows - width
    dwq_ref[...] = all_ref[0, :width]
    dwo_ref[:rest, :] = all_ref[0, width:]
    dwo_ref[rest:, :] = all_ref[1, : width - rest]
    dwk_ref[...] = all_ref[1, width - rest : width - rest + kv_width]
    dwv_ref[...] = all_ref[1, width - rest + kv_width :]
    rows = pack_ref[:width, width:].astype(F32).T
    for at, ref in ((0, gain_ref), (1, ffn_gain_ref)):
        ref[...] = rows[at : at + 1, :].reshape(width)


def tie(*arrays):
    return lax.optimization_barrier(arrays)


def orders_of(n):
    bits = list(range(n.bit_length() - 1))
    across = bits[-1]
    halved = bits[:-1]
    if len(halved) < 3:
        return [((halved, halved), across, (halved, halved))] * 2
    rest = halved[3:]
    ffn = (([0, 2, 1] + rest, [1, 0, 2] + rest), across, (rest + [1, 2, 0], rest + [2, 0, 1]))
    attention = (([1, 0, 2] + rest,) * 2, across, (rest + [1, 0, 2],) * 2)
    return [ffn, attention]


def position_tables(length):
    places = np.arange(length, dtype=np.float32)
    inverse = np.float32(10000.0) ** (np.arange(HALF, dtype=np.float32) * np.float32(-2.0 / HEAD_DIM))
    angles = inverse.astype(np.float32)[:, None] * places[None, :]
    return jnp.asarray(np.cos(angles)), jnp.asarray(np.sin(angles))


def per_device(
    sizes, tokens, segments, cotangent, attn_gain, w_query, w_key, w_value, w_out, ffn_gain,
    w_gate, w_up, w_down,
):
    _, half, width = tokens.shape
    kv_width = KV_HEADS * HEAD_DIM
    hidden = w_gate.shape[1]
    n = sizes[0]
    core = lax.axis_index("tensor")
    cut = half // 2
    tokens, cotangent = tokens[0].T, cotangent[0].T
    w_key, w_value, w_down = w_key.T, w_value.T, w_down.T

    tokens_got = swap(tokens)
    all_tables = position_tables(segments.shape[1])
    where = (segments, segments)
    projections = (w_query, w_key, w_value)

    act = shape((width, half), F32)
    low = shape((width, half), BF16)
    kv = shape((2 * kv_width, half), BF16)
    kv_f32 = shape((2 * kv_width, half), F32)
    wide = shape((2 * hidden, half), BF16)
    thin = shape((hidden, half), BF16)
    column = shape((width, 1), F32)
    square = shape((width, width), F32)
    heads_f32 = pltpu.VMEM((HEADS, BLOCK, BLOCK), F32)
    heads_low = pltpu.VMEM((HEADS, BLOCK, BLOCK), BF16)
    key_scratch = pltpu.VMEM((2 * KV_HEADS, half, HEAD_DIM), BF16)
    masks_shape = shape((2, 2, BLOCK, BLOCK), F32)
    rows_f32 = shape((16, half), F32)
    act_scratch = pltpu.VMEM((width, half), F32)
    low_scratch = pltpu.VMEM((width, half), BF16)

    def attend(query, kv_own, kv_other, masks=None):
        state, made = (), []
        for own, kv_part in ((True, kv_own), (False, kv_other)):

            def kernel(*refs, own=own):
                attend_kernel(own, *refs)

            state, new = run(
                kernel,
                where + (query, kv_part, tuple(state), () if masks is None else (masks[len(made)],)),
                ((rows_f32, rows_f32, act) if own else (low, rows_f32),
                 (masks_shape,) if masks is None else ()),
                [pltpu.VMEM((2, KV_HEADS, HEAD_DIM + 16, BLOCK), BF16),
                 pltpu.VMEM((4 * BLOCK, 8), jnp.int32), heads_f32],
                smem=1,
                name="attend_own" if own else "attend_other",
                us=4,
            )
            made.append(new[0] if masks is None else masks[len(made)])
        return (*state, made)

    def attend_back(query, kv_own, kv_other, masks, ctx, lse, grad, us=5):
        more = (ctx,)
        for own, kv_part, dkv in ((False, kv_other, kv), (True, kv_own, kv_f32)):

            def kernel(*refs, own=own):
                attend_back_kernel(own, *refs)

            (outs,) = run(
                kernel,
                (segments, query, kv_part, masks[0 if own else 1], lse, grad, more),
                ((act, dkv),) if own else ((act, rows_f32, dkv),),
                [key_scratch, heads_f32, heads_low, heads_low,
                 pltpu.VMEM((2, 2 * kv_width, BLOCK), F32)],
                smem=1,
                name="attend_back_own" if own else "attend_back_other",
                us=us,
            )
            if not own:
                more = outs[:2]
                got = swap(outs[2])
        return outs[0], outs[1], got

    table = shape((HALF, half), F32)
    tile_low, tile_kv = shape((width, cut), BF16), shape((2 * kv_width, cut), BF16)
    x_half = pltpu.VMEM((width, cut), F32)
    *halves, gain_col, ffn_gain_col, cos_table, sin_table, wq, wk, wv = run(
        first_kernel,
        in_hbm((tokens,) + projections + all_tables + (attn_gain, ffn_gain)),
        (tile_low, tile_low, tile_low, tile_kv, column, column, table, table)
        + tuple(shape(weight.shape, BF16) for weight in projections),
        [x_half, pltpu.VMEM((width,), F32), pltpu.VMEM((width,), F32),
         pltpu.SemaphoreType.DMA((10,))],
        hbm=8,
        name="first",
        us=2,
    )
    projections, tables = (wq, wk, wv), (cos_table, sin_table)
    (x1, normed1, query1, kv1), = run(
        second_kernel,
        (tokens_got, tuple(halves), gain_col) + tables + projections,
        ((low, low, low, kv),),
        [x_half],
        name="second",
        us=1,
    )
    kv1, cot_sent = tie(kv1, cotangent)
    kv1_other = swap(kv1)
    gate_pair = (w_gate, swap(w_gate))
    up_pair = (w_up, swap(w_up))
    down_pair = (w_down, swap(w_down))
    cot_got = swap(cot_sent)
    ctx1, lse1, masks = attend(query1, kv1, kv1_other)
    mid1, ffn1, gate1, up1, x2, normed2, query2, kv2 = run(
        middle_kernel,
        (x1, ctx1, w_out, ffn_gain_col, gate_pair, up_pair, down_pair, gain_col)
        + projections + tables,
        (act, low, wide, wide, act, low, low, kv),
        [pltpu.VMEM(wide.shape, BF16)],
        name="middle",
        us=6,
    )
    kv2_other = swap(kv2)
    ctx2, lse2, _ = attend(query2, kv2, kv2_other, masks)
    (
        (output, output_sent), cot, ffn2, kept2_own, kept2_other, grad_mid2, grad_mid_low2,
        grad_ctx2, dffn_gain2,
    ) = run(
        turn_kernel,
        (x2, ctx2, w_out, ffn_gain_col, gate_pair, up_pair, down_pair, cotangent, cot_got),
        ((tile_low, tile_low), low, low, (thin,) * 3, (thin,) * 3, act, low, low, column),
        [act_scratch, act_scratch],
        name="turn",
        us=9,
    )
    dq2, dkv_own2, dkv_got2 = attend_back(query2, kv2, kv2_other, masks, ctx2, lse2, grad_ctx2)
    output_got = swap(output_sent)
    pad = 8 * max(n // 2, 1)
    stack_rows = -(-3 * width // pad) * pad
    stack_shape = shape((stack_rows, hidden), BF16)
    pre = shape((width + 2 * kv_width, half), BF16)
    dpre2, dgain2, low1, gstream, dffn, stack_other = run(
        other_kernel,
        (dq2, dkv_own2, dkv_got2, x2, grad_mid2, gain_col) + projections + tables
        + (ffn1, gate1, up1, gate_pair[1], up_pair[1], down_pair[1], ffn2, cot, kept2_other),
        (pre, column, low, act, act, stack_shape),
        [act_scratch, pltpu.VMEM((3,) + thin.shape, BF16)],
        name="other",
        us=8,
    )
    stack_got = swap(stack_other)
    stack_own, grad_mid1, grad_mid_low1, grad_ctx1, dffn_gain = run(
        own_kernel,
        (low1, gstream, dffn, ffn1, gate1, up1, gate_pair[0], up_pair[0], down_pair[0],
         ffn2, cot, kept2_own, mid1, w_out, ffn_gain_col, dffn_gain2),
        (stack_shape, act, low, low, column),
        [act_scratch, pltpu.VMEM((3,) + thin.shape, BF16)],
        name="own",
        us=7,
    )
    ffn_orders, pack_orders = orders_of(n)
    ffn = Stream("ffn", (stack_own, stack_got), sizes, ffn_orders)
    token = ffn.step(stack_own)
    grad_ctx1, token = tie(grad_ctx1, token)
    dq1, dkv_own1, dkv_got1 = attend_back(query1, kv1, kv1_other, masks, ctx1, lse1, grad_ctx1, 0)
    rows = -(-(2 * width + 2 * kv_width) // 2 // pad) * pad
    lanes = -(-width // 128) * 128
    lanes = lanes if lanes - width >= 2 else lanes + 128
    half_stack = shape((rows, lanes), BF16)
    tile_act = shape((width, cut), F32)
    (grad_input, grad_input_sent), pack_own, pack_other = run(
        last_kernel,
        (dq1, dkv_own1, dkv_got1, x1, grad_mid1, gain_col) + projections + tables
        + (dpre2, (normed1, normed2), (ctx1, ctx2), (grad_mid_low1, grad_mid_low2),
           dgain2, dffn_gain),
        ((tile_act, tile_act), half_stack, half_stack),
        [pltpu.VMEM(pre.shape, BF16), act_scratch, act_scratch, act_scratch,
         pltpu.VMEM((width, 1), F32), pltpu.VMEM((2, rows, lanes), BF16)],
        name="last",
        us=0,
    )
    pack_other, grad_input_sent = tie(pack_other, grad_input_sent)
    pack = Stream("pack", (pack_own, swap(pack_other)), sizes, pack_orders)
    grad_input_got = swap(grad_input_sent)
    token = pack_own
    for index, which in enumerate("fafafaafafafa"):
        token = (ffn if which == "f" else pack).step(token)
        if index == 5:
            output = jnp.concatenate([output, output_got], axis=1)
            grad_input = jnp.concatenate([grad_input, grad_input_got], axis=1)
            token = (token, output, grad_input)
    while not (ffn.done and pack.done):
        token = pack.step(ffn.step(token))

    def kernel(own_ref, got_ref, out_ref, all_ref):
        pack_kernel(pack, own_ref, got_ref, out_ref, all_ref)

    (pack_sum,) = run(
        kernel, tuple(pack.terms), (half_stack,),
        [pltpu.VMEM((pack.chunks, rows // pack.chunks, lanes), BF16)], name="pack_all", us=0,
    )
    def finish(mine, part, after, update):
        def kernel(part_ref, *refs):
            finish_kernel(ffn, mine, part_ref, refs[:3], *refs[3:])

        count, rows, columns = part.shape
        return run(
            kernel, (part,), (shape((width, hidden), F32),) * 3,
            [pltpu.VMEM(part.shape, F32), pltpu.SemaphoreType.DMA((count, rows // width + 2))],
            after=after, name="finish", us=2, hbm_outs=True, update=update,
        )

    finished = finish(True, ffn.terms[0], pack_sum, ())
    half_rows = width + kv_width

    def kernel(*refs):
        unpack_kernel(half_rows, *refs)

    kv_square = shape((kv_width, width), F32)
    vector = shape((width,), F32)
    dgain, dffn_gain, dw_query, dw_key, dw_value, dw_out = run(
        kernel,
        (pack_sum, swap(pack_sum)),
        (vector, vector, square, kv_square, kv_square, square),
        [pltpu.VMEM((2, half_rows, width), F32)],
        name="unpack",
        us=0,
    )
    got, (output, grad_input, dgain, dffn_gain, dw_query, dw_key, dw_value, dw_out) = tie(
        ffn.terms[1],
        (output, grad_input, dgain, dffn_gain, dw_query, dw_key, dw_value, dw_out),
    )
    dw_gate, dw_up, dw_down = finish(False, got, (), finished)
    return (
        output.T[None],
        grad_input.T[None],
        dgain,
        dw_query,
        dw_key.T,
        dw_value.T,
        dw_out,
        dffn_gain,
        dw_gate,
        dw_up,
        dw_down.T,
    )


def solution(mesh):
    sizes = (mesh.shape["dp"], mesh.shape["tensor"])

    def local(*args):
        return per_device(sizes, *args)

    split = P("dp", "tensor", None)
    in_specs = (
        split, P("dp", None), split, P(), P(), P(), P(), P(), P(),
        P(None, "tensor"), P(None, "tensor"), P("tensor", None),
    )
    out_specs = (
        split, split, P(), P(), P(), P(), P(), P(),
        P(None, "tensor"), P(None, "tensor"), P("tensor", None),
    )
    return jax.shard_map(
        local, mesh=mesh, in_specs=in_specs, out_specs=out_specs, check_vma=False
    )
```

```python
import jax
import jax.numpy as jnp
import numpy as np
from jax import lax
from jax.experimental import pallas as pl
from jax.experimental.pallas import tpu as pltpu
from jax.sharding import PartitionSpec as P

HEADS = 9
KV_HEADS = 3
GROUP = HEADS // KV_HEADS
HEAD_DIM = 64
HALF = HEAD_DIM // 2
EPSILON = 1e-05
MASKED = -1e30
BLOCK = 256
SCALE = HEAD_DIM ** (-0.5)
F32 = jnp.float32
BF16 = jnp.bfloat16
VMEM_LIMIT = 16 * 2**20


def dot(left, right, left_dim, right_dim):
    return lax.dot_general(
        left, right, (((left_dim,), (right_dim,)), ((), ())), preferred_element_type=F32
    )


def pieces(size, step):
    return [slice(start, start + step) for start in range(0, size, step)]


def inverse_rms(x_ref):
    total = None
    for rows in pieces(x_ref.shape[0], 64):
        x = x_ref[rows, :]
        part = jnp.sum(x * x, axis=0, keepdims=True)
        total = part if total is None else total + part
    return lax.rsqrt(total / x_ref.shape[0] + EPSILON)


def norm_forward(x_ref, gain_ref, out_ref):
    scale = inverse_rms(x_ref)
    for rows in pieces(x_ref.shape[0], 64):
        out_ref[rows, :] = (x_ref[rows, :] * scale * gain_ref[rows, :]).astype(BF16)


def norm_backward(x_ref, gain_ref, grad_ref, add_ref, out_ref, gain_grad_ref):
    scale = inverse_rms(x_ref)
    inner = None
    for rows in pieces(x_ref.shape[0], 64):
        x, e = x_ref[rows, :], grad_ref[rows, :]
        xe = x * e
        gain_grad_ref[rows, :] = jnp.sum(xe * scale, axis=1, keepdims=True)
        part = jnp.sum(xe * gain_ref[rows, :], axis=0, keepdims=True)
        inner = part if inner is None else inner + part
    cubed = scale * scale * scale * (inner / x_ref.shape[0])
    for rows in pieces(x_ref.shape[0], 64):
        out_ref[rows, :] = (
            add_ref[rows, :].astype(F32)
            + scale * gain_ref[rows, :] * grad_ref[rows, :]
            - x_ref[rows, :] * cubed
        )


def gain_backward(x_ref, grad_ref, gain_grad_ref):
    scale = inverse_rms(x_ref)
    for rows in pieces(x_ref.shape[0], 64):
        gain_grad_ref[rows, :] = jnp.sum(
            x_ref[rows, :] * grad_ref[rows, :] * scale, axis=1, keepdims=True
        )


def rotated(x, cos_table, sin_table):
    front, back = x[:HALF], x[HALF:]
    return jnp.concatenate(
        [front * cos_table - back * sin_table, back * cos_table + front * sin_table], axis=0
    )


def project_qkv(normed_ref, wq_ref, wk_ref, wv_ref, cos_ref, sin_ref, q_ref, kv_ref):
    normed = normed_ref[...]
    cos_table, sin_table = cos_ref[...], sin_ref[...]
    key = dot(wk_ref[...], normed, 1, 0)
    for head in pieces(KV_HEADS * HEAD_DIM, HEAD_DIM):
        kv_ref[head, :] = rotated(key[head], cos_table, sin_table).astype(BF16)
    kv_ref[KV_HEADS * HEAD_DIM :, :] = dot(wv_ref[...], normed, 1, 0).astype(BF16)
    query = dot(wq_ref[...], normed, 0, 0)
    for head in pieces(HEADS * HEAD_DIM, HEAD_DIM):
        q_ref[head, :] = (rotated(query[head], cos_table, sin_table) * SCALE).astype(BF16)


def first_kernel(
    tokens_hbm, wq_hbm, wk_hbm, wv_hbm, cos_hbm, sin_hbm, gain_hbm, ffn_gain_hbm,
    low_ref, normed_ref, q_ref, kv_ref, gain_ref, ffn_gain_ref, cos_ref, sin_ref,
    wq_ref, wk_ref, wv_ref,
    x_ref, gain_in_ref, ffn_gain_in_ref, sems,
):
    cut = low_ref.shape[1]
    pairs = [
        (gain_hbm, gain_in_ref), (ffn_gain_hbm, ffn_gain_in_ref),
        (tokens_hbm.at[:, :cut], low_ref), (wk_hbm, wk_ref), (wv_hbm, wv_ref), (wq_hbm, wq_ref),
    ]
    for local, tile in enumerate(tile_places(lax.axis_index("tensor"))):
        cols = slice(local * cut, (local + 1) * cut)
        for source, target in ((cos_hbm, cos_ref), (sin_hbm, sin_ref)):
            pairs.append((source.at[:, tile_lanes(tile)], target.at[:, cols]))
    copies = [
        pltpu.make_async_copy(source, target, sems.at[index])
        for index, (source, target) in enumerate(pairs)
    ]
    for copy in copies:
        copy.start()
    copies[0].wait()
    copies[1].wait()
    for in_ref, column_ref in ((gain_in_ref, gain_ref), (ffn_gain_in_ref, ffn_gain_ref)):
        row = in_ref[...].reshape(1, -1)
        column_ref[...] = jnp.broadcast_to(row, (128, row.shape[1])).T[:, :1]
    copies[2].wait()
    x_ref[...] = low_ref[...].astype(F32)
    norm_forward(x_ref, gain_ref, normed_ref)
    for copy in copies[3:]:
        copy.wait()
    tables = (cos_ref.at[:, :cut], sin_ref.at[:, :cut])
    project_qkv(normed_ref, wq_ref, wk_ref, wv_ref, *tables, q_ref, kv_ref)


def second_kernel(
    got_ref, half_refs, gain_ref, cos_ref, sin_ref, wq_ref, wk_ref, wv_ref, full_refs, x_ref
):
    cut = x_ref.shape[1]
    for half_ref, full_ref in zip(half_refs, full_refs):
        full_ref[:, :cut] = half_ref[...]
    low_ref, normed_ref, q_ref, kv_ref = (ref.at[:, cut:] for ref in full_refs)
    low_ref[...] = got_ref[:, cut:]
    x_ref[...] = low_ref[...].astype(F32)
    norm_forward(x_ref, gain_ref, normed_ref)
    tables = (cos_ref.at[:, cut:], sin_ref.at[:, cut:])
    project_qkv(normed_ref, wq_ref, wk_ref, wv_ref, *tables, q_ref, kv_ref)


def tile_places(core):
    return 2 * core, 3 - 2 * core


def tile_lanes(tile):
    return pl.ds(pl.multiple_of(tile * BLOCK, BLOCK), BLOCK)


def set_labels(labels_ref, column_ref):
    column_ref[...] = jnp.broadcast_to(labels_ref[0:1, :], (8, labels_ref.shape[1])).T


def set_mask(bias_ref, labels_ref, column_ref, tile, kb):
    key_labels = column_ref[tile_lanes(kb), :1]
    key_place = kb * BLOCK + lax.broadcasted_iota(jnp.int32, (BLOCK, BLOCK), 0)
    place = tile * BLOCK + lax.broadcasted_iota(jnp.int32, (1, BLOCK), 1)
    allowed = (key_labels == labels_ref[0:1, tile_lanes(tile)]) & (key_place <= place)
    bias_ref[...] = jnp.where(allowed, 0.0, MASKED)


def first_block(segments_ref, tile):
    label = segments_ref[0, tile * BLOCK]
    count = jnp.int32(0)
    for kb in range(3):
        before = (kb < tile) & (segments_ref[0, kb * BLOCK + BLOCK - 1] < label)
        count = count + before.astype(jnp.int32)
    return count


def head_rows(head):
    return slice(head * HEAD_DIM, (head + 1) * HEAD_DIM)


def load_part(kv_ref, tok_ref):
    for head in range(2 * KV_HEADS):
        for cols in pieces(kv_ref.shape[1], BLOCK):
            tok_ref[head, cols, :] = kv_ref[head_rows(head), cols].T


def over_blocks(segments_ref, core, own, body):
    keys_of = tile_places(core if own else 1 - core)
    for local, tile in enumerate(tile_places(core)):
        cols = slice(local * BLOCK, (local + 1) * BLOCK)
        first = first_block(segments_ref, tile)

        def step(at, carry):
            kb = jnp.where(at == 0, keys_of[0], keys_of[1])

            @pl.when((kb >= first) & (kb <= tile))
            def _():
                body(local, tile, cols, kb, at)

            return carry

        lax.fori_loop(0, 2, step, 0)


def attend_kernel(
    own, segments_ref, labels_ref, q_ref, kv_ref, state_refs, mask_in_refs, out_refs, mask_out_refs,
    value_ref, column_ref, scores_ref,
):
    core = lax.axis_index("tensor")
    if mask_out_refs:
        set_labels(labels_ref, column_ref)
    (masks_ref,) = mask_in_refs or mask_out_refs
    for at, cols in enumerate(pieces(kv_ref.shape[1], BLOCK)):
        for group in range(KV_HEADS):
            value_ref[at, group, :HEAD_DIM, :] = kv_ref[head_rows(KV_HEADS + group), cols]
            value_ref[at, group, HEAD_DIM:, :] = jnp.ones((16, BLOCK), BF16)
    m_ref, l_ref, acc_ref = out_refs if own else state_refs
    if own:
        m_ref[...] = jnp.full(m_ref.shape, MASKED, F32)
        l_ref[...] = jnp.zeros(l_ref.shape, F32)
        acc_ref[...] = jnp.zeros(acc_ref.shape, F32)

    def body(local, tile, cols, kb, at):
        bias_ref = masks_ref.at[local, at]
        if mask_out_refs:
            set_mask(bias_ref, labels_ref, column_ref, tile, kb)
        keys = tile_lanes(at)

        def scores(group):
            key = kv_ref[head_rows(group), keys]
            for head in range(group * GROUP, (group + 1) * GROUP):
                scores_ref[head] = dot(key, q_ref[head_rows(head), cols], 0, 0) + bias_ref[...]

        def products(group):
            for head in range(group * GROUP, (group + 1) * GROUP):
                rows = head_rows(head)
                m_old = m_ref[head : head + 1, cols]
                m_new = jnp.maximum(m_old, jnp.max(scores_ref[head], axis=0, keepdims=True))
                m_ref[head : head + 1, cols] = m_new
                fade = jnp.exp(m_old - m_new)
                probs = jnp.exp(scores_ref[head] - m_new).astype(BF16)
                product = dot(value_ref[at, group], probs, 1, 0)
                l_ref[head : head + 1, cols] = (
                    l_ref[head : head + 1, cols] * fade + product[HEAD_DIM : HEAD_DIM + 1]
                )
                acc_ref[rows, cols] = acc_ref[rows, cols] * fade + product[:HEAD_DIM]

        scores(0)
        scores(1)
        products(0)
        scores(2)
        products(1)
        products(2)

    over_blocks(segments_ref, core, own, body)
    if not own:
        ctx_ref, lse_ref = out_refs
        for head in range(HEADS):
            total = l_ref[head : head + 1, :]
            ctx_ref[head_rows(head), :] = (acc_ref[head_rows(head), :] * (1.0 / total)).astype(BF16)
            lse_ref[head : head + 1, :] = m_ref[head : head + 1, :] + jnp.log(total)


def attend_back_kernel(
    own, segments_ref, q_ref, kv_ref, masks_ref, lse_ref, grad_ref, more_refs, out_refs,
    tok_ref, probs_ref, probs_low_ref, gs_ref, dkv_ref,
):
    core = lax.axis_index("tensor")
    load_part(kv_ref, tok_ref)
    if own:
        dq_in_ref, delta_ref = more_refs
        dq_ref, dkv_out_ref = out_refs
        dq_ref[...] = dq_in_ref[...]
    else:
        (ctx_ref,) = more_refs
        dq_ref, delta_ref, dkv_out_ref = out_refs
        dq_ref[...] = jnp.zeros(dq_ref.shape, F32)
        for head in range(HEADS):
            rows = head_rows(head)
            delta_ref[head : head + 1, :] = jnp.sum(
                grad_ref[rows, :].astype(F32) * ctx_ref[rows, :].astype(F32), axis=0, keepdims=True
            )
    dkv_ref[...] = jnp.zeros(dkv_ref.shape, F32)

    def body(local, tile, cols, kb, at):
        bias_ref = masks_ref.at[local, at]
        keys = tile_lanes(at)
        for head in range(HEADS):
            key = tok_ref[head // GROUP, keys, :]
            scores = dot(key, q_ref[head_rows(head), cols], 1, 0) + bias_ref[...]
            probs = jnp.exp(scores - lse_ref[head : head + 1, cols])
            probs_ref[head] = probs
            probs_low_ref[head] = probs.astype(BF16)
        for head in range(HEADS):
            value = tok_ref[KV_HEADS + head // GROUP, keys, :]
            grad_probs = dot(value, grad_ref[head_rows(head), cols], 1, 0)
            gs_ref[head] = (
                probs_ref[head] * (grad_probs - delta_ref[head : head + 1, cols])
            ).astype(BF16)
        for group in range(KV_HEADS):
            dv = dkv_ref[at, head_rows(KV_HEADS + group), :]
            for head in range(group * GROUP, (group + 1) * GROUP):
                dv = dv + dot(grad_ref[head_rows(head), cols], probs_low_ref[head], 1, 1)
            dkv_ref[at, head_rows(KV_HEADS + group), :] = dv
        for group in range(KV_HEADS):
            dk = dkv_ref[at, head_rows(group), :]
            for head in range(group * GROUP, (group + 1) * GROUP):
                dk = dk + dot(q_ref[head_rows(head), cols], gs_ref[head], 1, 1)
            dkv_ref[at, head_rows(group), :] = dk
        for head in range(HEADS):
            key_cols = kv_ref[head_rows(head // GROUP), keys]
            dq_ref[head_rows(head), cols] += dot(key_cols, gs_ref[head], 1, 0)

    over_blocks(segments_ref, core, own, body)
    for at, cols in enumerate(pieces(dkv_out_ref.shape[1], BLOCK)):
        dkv_out_ref[:, cols] = dkv_ref[at].astype(dkv_out_ref.dtype)


def middle_kernel(
    low_ref, ctx_ref, wo_ref, ffn_gain_ref, wg_refs, wu_refs, wd_refs,
    gain_ref, wq_ref, wk_ref, wv_ref, cos_ref, sin_ref,
    mid_ref, ffn_ref, gate_ref, up_ref, x2_ref, normed_ref, q_ref, kv_ref, product_ref,
):
    mid_ref[...] = low_ref[...].astype(F32) + dot(wo_ref[...], ctx_ref[...], 0, 0)
    norm_forward(mid_ref, ffn_gain_ref, ffn_ref)
    ffn_in = ffn_ref[...]
    half_hidden = wg_refs[0].shape[1]
    for part in range(2):
        for hidden in pieces(half_hidden, BLOCK):
            gate = dot(wg_refs[part][:, hidden], ffn_in, 0, 0)
            up = dot(wu_refs[part][:, hidden], ffn_in, 0, 0)
            rows = slice(part * half_hidden + hidden.start, part * half_hidden + hidden.stop)
            gate_ref[rows, :] = gate.astype(BF16)
            up_ref[rows, :] = up.astype(BF16)
            product_ref[rows, :] = (gate * jax.nn.sigmoid(gate) * up).astype(BF16)
    x2_ref[...] = (
        mid_ref[...]
        + dot(wd_refs[0][...], product_ref[:half_hidden, :], 1, 0)
        + dot(wd_refs[1][...], product_ref[half_hidden:, :], 1, 0)
    )
    norm_forward(x2_ref, gain_ref, normed_ref)
    project_qkv(normed_ref, wq_ref, wk_ref, wv_ref, cos_ref, sin_ref, q_ref, kv_ref)


def ffn_terms(gate, up, grad_product):
    sig = jax.nn.sigmoid(gate)
    silu = gate * sig
    grad_gate = (grad_product * up * (sig + silu * (1.0 - sig))).astype(BF16)
    grad_up = (grad_product * silu).astype(BF16)
    return (silu * up).astype(BF16), grad_gate, grad_up


def turn_kernel(
    x_ref, ctx_ref, wo_ref, ffn_gain_ref, wg_refs, wu_refs, wd_refs, cotangent_ref, cot_got_ref,
    mid_ref, cot_ref, ffn_ref, kept_own_refs, kept_other_refs,
    grad_mid_ref, grad_mid_low_ref, grad_ctx_ref, dgain_ref,
    acc_ref,
):
    mid_ref[...] = x_ref[...] + dot(wo_ref[...], ctx_ref[...], 0, 0)
    norm_forward(mid_ref, ffn_gain_ref, ffn_ref)
    ffn_in = ffn_ref[...]
    cut = cot_got_ref.shape[1] // 2
    cot_ref[:, :cut] = cotangent_ref[:, :cut]
    cot_ref[:, cut:] = cot_got_ref[:, cut:]
    grad_low = cot_ref[...]
    for part in range(2):
        for hidden in pieces(wg_refs[part].shape[1], BLOCK):
            gate = dot(wg_refs[part][:, hidden], ffn_in, 0, 0)
            up = dot(wu_refs[part][:, hidden], ffn_in, 0, 0)
            grad_product = dot(wd_refs[part][:, hidden], grad_low, 0, 0)
            kept = (kept_own_refs, kept_other_refs)[part]
            for ref, term in zip(kept, ffn_terms(gate, up, grad_product)):
                ref[hidden, :] = term
    acc_ref[...] = (
        dot(wg_refs[0][...], kept_own_refs[1][...], 1, 0)
        + dot(wu_refs[0][...], kept_own_refs[2][...], 1, 0)
        + dot(wg_refs[1][...], kept_other_refs[1][...], 1, 0)
        + dot(wu_refs[1][...], kept_other_refs[2][...], 1, 0)
    )
    norm_backward(mid_ref, ffn_gain_ref, acc_ref, cot_ref, grad_mid_ref, dgain_ref)
    grad_mid_low_ref[...] = grad_mid_ref[...].astype(BF16)
    grad_ctx_ref[...] = dot(wo_ref[...], grad_mid_low_ref[...], 1, 0).astype(BF16)


def result_kernel(mid_ref, product_refs, wd_refs, out_refs):
    result = (
        mid_ref[...]
        + dot(wd_refs[0][...], product_refs[0][...], 1, 0)
        + dot(wd_refs[1][...], product_refs[1][...], 1, 0)
    )
    cut = out_refs[0].shape[1]
    out_refs[0][...] = result[:, :cut].astype(BF16)
    out_refs[1][...] = result[:, cut:].astype(BF16)


def input_kernel(
    x_low_ref, gain_ref, dnormed_ref, grad_mid_ref, out_refs, x_ref, out_ref, dgain_ref
):
    x_ref[...] = x_low_ref[...].astype(F32)
    norm_backward(x_ref, gain_ref, dnormed_ref, grad_mid_ref, out_ref, dgain_ref)
    cut = out_refs[0].shape[1]
    out_refs[0][...] = out_ref[:, :cut]
    out_refs[1][...] = out_ref[:, cut:]


def qkv_back(
    dq_ref, dkv_own_ref, dkv_got_ref, wq_ref, wk_ref, wv_ref, cos_ref, sin_ref, dpre_ref, dnormed_ref
):
    cos_table, sin_table = cos_ref[...], sin_ref[...]
    width, kv_width = HEADS * HEAD_DIM, KV_HEADS * HEAD_DIM
    for head in pieces(width, HEAD_DIM):
        dpre_ref[head, :] = rotated(dq_ref[head, :] * SCALE, cos_table, -sin_table).astype(BF16)
    for head in pieces(kv_width, HEAD_DIM):
        total = dkv_own_ref[head, :] + dkv_got_ref[head, :].astype(F32)
        rows = slice(width + head.start, width + head.stop)
        dpre_ref[rows, :] = rotated(total, cos_table, -sin_table).astype(BF16)
    dpre_ref[width + kv_width :, :] = (
        dkv_own_ref[kv_width:, :] + dkv_got_ref[kv_width:, :].astype(F32)
    ).astype(BF16)
    dnormed_ref[...] = (
        dot(wq_ref[...], dpre_ref[:width, :], 1, 0)
        + dot(wk_ref[...], dpre_ref[width : width + kv_width, :], 0, 0)
        + dot(wv_ref[...], dpre_ref[width + kv_width :, :], 0, 0)
    )


def fill_stack(stack, width):
    if stack.shape[0] > 3 * width:
        stack[3 * width :, :] = jnp.zeros((stack.shape[0] - 3 * width, stack.shape[1]), BF16)


def ffn_back(
    part, stack, low, ffn1, ffn2, low2, gate_ref, up_ref, wg_ref, wu_ref, wd_ref, kept2_refs,
    acc_ref, terms_ref,
):
    width, half_hidden = wg_ref.shape
    for hidden in pieces(half_hidden, BLOCK):
        rows = slice(part * half_hidden + hidden.start, part * half_hidden + hidden.stop)
        grad_product = dot(wd_ref[:, hidden], low, 0, 0)
        terms = ffn_terms(gate_ref[rows, :].astype(F32), up_ref[rows, :].astype(F32), grad_product)
        for at, term in enumerate(terms):
            terms_ref[at, hidden, :] = term
    acc_ref[...] += dot(wg_ref[...], terms_ref[1], 1, 0) + dot(wu_ref[...], terms_ref[2], 1, 0)
    for at, (left1, left2, which) in enumerate(((ffn1, ffn2, 1), (ffn1, ffn2, 2), (low, low2, 0))):
        stack[at * width : (at + 1) * width, :] = (
            dot(left1, terms_ref[which], 1, 1) + dot(left2, kept2_refs[which][...], 1, 1)
        ).astype(BF16)
    fill_stack(stack, width)


def other_kernel(
    dq_ref, dkv_own_ref, dkv_got_ref, x_ref, grad_mid_ref,
    gain_ref, wq_ref, wk_ref, wv_ref, cos_ref, sin_ref,
    ffn1_ref, gate_ref, up_ref, wg_ref, wu_ref, wd_ref, ffn2_ref, low2_ref, kept2_refs,
    dpre_ref, dgain_ref, low_ref, gstream_ref, acc_ref, stack, dnormed_ref, terms_ref,
):
    qkv_back(
        dq_ref, dkv_own_ref, dkv_got_ref, wq_ref, wk_ref, wv_ref, cos_ref, sin_ref,
        dpre_ref, dnormed_ref,
    )
    norm_backward(x_ref, gain_ref, dnormed_ref, grad_mid_ref, gstream_ref, dgain_ref)
    low_ref[...] = gstream_ref[...].astype(BF16)
    acc_ref[...] = jnp.zeros(acc_ref.shape, F32)
    ffn_back(
        1, stack, low_ref[...], ffn1_ref[...], ffn2_ref[...], low2_ref[...],
        gate_ref, up_ref, wg_ref, wu_ref, wd_ref, kept2_refs, acc_ref, terms_ref,
    )


def own_kernel(
    low_ref, gstream_ref, acc_in_ref,
    ffn1_ref, gate_ref, up_ref, wg_ref, wu_ref, wd_ref, ffn2_ref, low2_ref, kept2_refs,
    mid_ref, wo_ref, ffn_gain_ref, dffn_gain2_ref,
    stack, grad_mid_ref, grad_mid_low_ref, grad_ctx_ref, dffn_gain_ref, acc_ref, terms_ref,
):
    acc_ref[...] = acc_in_ref[...]
    ffn_back(
        0, stack, low_ref[...], ffn1_ref[...], ffn2_ref[...], low2_ref[...],
        gate_ref, up_ref, wg_ref, wu_ref, wd_ref, kept2_refs, acc_ref, terms_ref,
    )
    norm_backward(mid_ref, ffn_gain_ref, acc_ref, gstream_ref, grad_mid_ref, dffn_gain_ref)
    dffn_gain_ref[...] += dffn_gain2_ref[...]
    grad_mid_low_ref[...] = grad_mid_ref[...].astype(BF16)
    grad_ctx_ref[...] = dot(wo_ref[...], grad_mid_low_ref[...], 1, 0).astype(BF16)


def last_kernel(
    dq_ref, dkv_own_ref, dkv_got_ref, x_low_ref, wq_ref, wk_ref, wv_ref, cos_ref, sin_ref,
    dpre2_ref, normed_refs, ctx_refs, grad_mid_low_refs, dgain2_ref, dffn_gain_ref,
    dnormed_ref, stack_own_ref, stack_other_ref,
    dpre_ref, x_ref, dgain_ref, stack_ref,
):
    x_ref[...] = x_low_ref[...].astype(F32)
    width, rows = x_ref.shape[0], stack_ref.shape[1]
    qkv_back(
        dq_ref, dkv_own_ref, dkv_got_ref, wq_ref, wk_ref, wv_ref, cos_ref, sin_ref,
        dpre_ref, dnormed_ref,
    )
    gain_backward(x_ref, dnormed_ref, dgain_ref)
    normed1, normed2 = (ref[...] for ref in normed_refs)
    dwq = dot(normed1, dpre_ref[:width, :], 1, 1) + dot(normed2, dpre2_ref[:width, :], 1, 1)
    dwkv = dot(dpre_ref[width:, :], normed1, 1, 1) + dot(dpre2_ref[width:, :], normed2, 1, 1)
    dwo = dot(ctx_refs[0][...], grad_mid_low_refs[0][...], 1, 1) + dot(
        ctx_refs[1][...], grad_mid_low_refs[1][...], 1, 1
    )
    half_rows = width + dwkv.shape[0] // 2
    rest = half_rows - width
    stack_ref[0, :width, :width] = dwq.astype(BF16)
    stack_ref[0, width:half_rows, :width] = dwo[:rest].astype(BF16)
    stack_ref[1, : width - rest, :width] = dwo[rest:].astype(BF16)
    stack_ref[1, width - rest : half_rows, :width] = dwkv.astype(BF16)
    lanes = stack_ref.shape[2] - width
    column = lax.broadcasted_iota(jnp.int32, (width, lanes), 1)
    gains = jnp.where(
        column == 0,
        dgain_ref[...] + dgain2_ref[...],
        jnp.where(column == 1, dffn_gain_ref[...], 0.0),
    ).astype(BF16)
    for part in range(2):
        stack_ref[part, :width, width:] = gains
        stack_ref[part, width:, width:] = jnp.zeros((rows - width, lanes), BF16)
        if rows > half_rows:
            stack_ref[part, half_rows:, :width] = jnp.zeros((rows - half_rows, width), BF16)
    core = lax.axis_index("tensor")
    stack_own_ref[...] = stack_ref[core]
    stack_other_ref[...] = stack_ref[1 - core]


def shape(dims, dtype):
    return jax.ShapeDtypeStruct(dims, dtype)


def run(
    kernel, args, outs, scratch=(), smem=0, hbm=0, after=(), name=None, us=5, limit=VMEM_LIMIT,
    hbm_outs=False, update=(),
):
    leaves, tree = jax.tree.flatten(args)
    out_leaves, out_tree = jax.tree.flatten(outs)
    late = jax.tree.leaves(after) + list(update)
    n_in, n_out = len(leaves), len(out_leaves)

    def body(*refs):
        ins = jax.tree.unflatten(tree, refs[:n_in])
        refs = refs[n_in + len(late) :]
        results = jax.tree.unflatten(out_tree, refs[:n_out])
        kernel(*ins, *results, *refs[n_out:])

    in_specs = [
        pl.BlockSpec(
            memory_space=pltpu.SMEM if index < smem else pltpu.HBM if index < hbm else pltpu.VMEM
        )
        for index in range(n_in)
    ] + [pl.BlockSpec(memory_space=pl.ANY)] * len(late)
    results = pl.pallas_call(
        body,
        out_shape=out_leaves,
        in_specs=in_specs,
        out_specs=[pl.BlockSpec(memory_space=pltpu.HBM if hbm_outs else pltpu.VMEM)] * n_out,
        scratch_shapes=list(scratch),
        input_output_aliases={
            n_in + len(late) - len(update) + index: index for index in range(len(update))
        },
        compiler_params=pltpu.CompilerParams(vmem_limit_bytes=limit),
        cost_estimate=pl.CostEstimate(
            flops=int(us * 1e9) + 1, bytes_accessed=2**20 if us else 1, transcendentals=0
        ),
        name=name,
    )(*leaves, *late)
    return jax.tree.unflatten(out_tree, results)


def in_hbm(arrays):
    return tuple(pltpu.with_memory_space_constraint(array, pltpu.HBM) for array in arrays)


def swap(array):
    return lax.ppermute(array, "tensor", [(0, 1), (1, 0)])


def partners(sizes, bits):
    n, cores = sizes
    return [
        (place * cores + core, (place ^ (1 << bits[core])) * cores + core)
        for place in range(n)
        for core in range(cores)
    ]


def by_core(pair):
    return jnp.where(lax.axis_index("tensor") == 0, jnp.int32(pair[0]), jnp.int32(pair[1]))


def own_bit(bits):
    place = lax.axis_index("dp").astype(jnp.int32)
    return lax.shift_right_logical(place, by_core(bits)) & 1


def insert(index, rank, bit):
    low = index & (lax.shift_left(jnp.int32(1), rank) - 1)
    return lax.shift_left(index - low, jnp.int32(1)) + lax.shift_left(bit, rank) + low


def scatter_kernel(bits, ranks, sent, terms, out_ref):
    own, rank = own_bit(bits), by_core(ranks)
    half = 1 - own if sent else own

    def body(index, carry):
        at = insert(index, rank, half)
        total = terms[0][at].astype(F32)
        for term in terms[1:]:
            total = total + term[at].astype(F32)
        out_ref[index] = total.astype(BF16)
        return carry

    lax.fori_loop(0, out_ref.shape[0], body, 0)


def add_kernel(one_ref, two_ref, out_ref):
    out_ref[...] = (one_ref[...].astype(F32) + two_ref[...].astype(F32)).astype(BF16)


def join(bits, ranks, own_ref, got_ref, out_ref):
    own, rank = own_bit(bits), by_core(ranks)

    def body(index, carry):
        out_ref[insert(index, rank, own)] = own_ref[index]
        out_ref[insert(index, rank, 1 - own)] = got_ref[index]
        return carry

    lax.fori_loop(0, own_ref.shape[0], body, 0)


def ranks_of(dims, done):
    ranks = []
    for step in range(len(dims[0])):
        pair = []
        for order in dims:
            there = order[step + 1 :] if done == "after" else order[:step]
            pair.append(sum(other < order[step] for other in there))
        ranks.append(tuple(pair))
    return ranks


class Stream:
    def __init__(self, name, terms, sizes, orders):
        scatter, across, gather = orders
        self.name, self.sizes = name, sizes
        self.halvings = len(scatter[0])
        self.chunks = 1 << self.halvings
        self.bits = list(zip(*scatter)) + [(across, across)] + list(zip(*gather))
        self.ranks = ranks_of(scatter, "after") + [None] + ranks_of(gather, "before")
        self.terms = [term.reshape((self.chunks, -1) + term.shape[1:]) for term in terms]
        self.rounds = 2 * self.halvings + 1
        self.round = 0

    def call(self, kernel, args, counts, after):
        rows, columns = self.terms[0].shape[1:]
        outs = tuple(shape((count, rows, columns), BF16) for count in counts)
        return run(kernel, args, outs, after=after, name=f"{self.name}_{self.round}", us=0)

    def load(self, after):
        if self.round < self.halvings:
            half = self.terms[0].shape[0] // 2
            bits, ranks = self.bits[self.round], self.ranks[self.round]

            terms = tuple(self.terms)

            def part(which, after):
                def kernel(terms, out_ref):
                    scatter_kernel(bits, ranks, which, terms, out_ref)

                return self.call(kernel, (terms,), (half,), after)[0]

            sent = part(True, after)
            self.terms = [part(False, sent)]
            return sent
        if self.round <= self.halvings + 1:
            (sent,) = self.call(add_kernel, tuple(self.terms), (1,), after)
        else:
            bits, ranks = self.bits[self.round - 1], self.ranks[self.round - 1]

            def kernel(*refs):
                join(bits, ranks, *refs)

            (sent,) = self.call(
                kernel, tuple(self.terms), (2 * self.terms[0].shape[0],), after
            )
        self.terms = [sent]
        return sent

    def step(self, token):
        if self.done:
            return token
        sent = self.load(token)
        got = lax.ppermute(sent, ("dp", "tensor"), partners(self.sizes, self.bits[self.round]))
        self.terms = self.terms + [got]
        self.round += 1
        return sent

    @property
    def done(self):
        return self.round == self.rounds

    def join(self, out_ref, own_ref, got_ref):
        join(self.bits[-1], self.ranks[-1], own_ref, got_ref, out_ref)


def finish_kernel(stream, mine, part_ref, outs, wide_ref, sems):
    count, rows = part_ref.shape[:2]
    for index in range(count):
        wide_ref[index] = part_ref[index].astype(F32)
    width = outs[0].shape[0]
    own, core = own_bit(stream.bits[-1]), lax.axis_index("tensor")
    half = own if mine else 1 - own

    def copies(chunk, index):
        at, end, found = chunk * rows, (chunk + 1) * rows, []
        while at < end:
            which, inside = divmod(at, width)
            size = min(end - at, width - inside)
            if which == len(outs):
                break
            found.append(
                pltpu.make_async_copy(
                    wide_ref.at[index, at - chunk * rows : at - chunk * rows + size, :],
                    outs[which].at[inside : inside + size, :],
                    sems.at[index, len(found)],
                )
            )
            at += size
        return found

    for act in ("start", "wait"):
        for which, rank in enumerate(stream.ranks[-1]):
            for chunk in range(2 * count):
                bit, low = (chunk >> rank) & 1, chunk & ((1 << rank) - 1)
                index = ((chunk >> (rank + 1)) << rank) + low

                @pl.when((core == which) & (half == bit))
                def _():
                    for copy in copies(chunk, index):
                        getattr(copy, act)()


def pack_kernel(stream, own_ref, got_ref, out_ref, all_ref):
    stream.join(all_ref, own_ref, got_ref)
    rows = all_ref.shape[1]
    for chunk in range(all_ref.shape[0]):
        out_ref[chunk * rows : (chunk + 1) * rows, :] = all_ref[chunk]


def unpack_kernel(
    half_rows, pack_ref, pack_got_ref,
    gain_ref, ffn_gain_ref, dwq_ref, dwk_ref, dwv_ref, dwo_ref, all_ref,
):
    width, kv_width = dwq_ref.shape[0], dwk_ref.shape[0]
    core = lax.axis_index("tensor")
    for which, ref in ((core, pack_ref), (1 - core, pack_got_ref)):
        all_ref[which] = ref[:half_rows, :width].astype(F32)
    rest = half_rows - width
    dwq_ref[...] = all_ref[0, :width]
    dwo_ref[:rest, :] = all_ref[0, width:]
    dwo_ref[rest:, :] = all_ref[1, : width - rest]
    dwk_ref[...] = all_ref[1, width - rest : width - rest + kv_width]
    dwv_ref[...] = all_ref[1, width - rest + kv_width :]
    rows = pack_ref[:width, width:].astype(F32).T
    for at, ref in ((0, gain_ref), (1, ffn_gain_ref)):
        ref[...] = rows[at : at + 1, :].reshape(width)


def tie(*arrays):
    return lax.optimization_barrier(arrays)


def orders_of(n):
    bits = list(range(n.bit_length() - 1))
    across = bits[-1]
    halved = bits[:-1]
    if len(halved) < 3:
        return [((halved, halved), across, (halved, halved))] * 2
    rest = halved[3:]
    ffn = (([0, 2, 1] + rest, [1, 0, 2] + rest), across, (rest + [1, 2, 0], rest + [2, 0, 1]))
    attention = (([1, 0, 2] + rest,) * 2, across, (rest + [1, 0, 2],) * 2)
    return [ffn, attention]


def position_tables(length):
    places = np.arange(length, dtype=np.float32)
    inverse = np.float32(10000.0) ** (np.arange(HALF, dtype=np.float32) * np.float32(-2.0 / HEAD_DIM))
    angles = inverse.astype(np.float32)[:, None] * places[None, :]
    return jnp.asarray(np.cos(angles)), jnp.asarray(np.sin(angles))


def per_device(
    sizes, tokens, segments, cotangent, attn_gain, w_query, w_key, w_value, w_out, ffn_gain,
    w_gate, w_up, w_down,
):
    _, half, width = tokens.shape
    kv_width = KV_HEADS * HEAD_DIM
    hidden = w_gate.shape[1]
    n = sizes[0]
    core = lax.axis_index("tensor")
    cut = half // 2
    tokens, cotangent = tokens[0].T, cotangent[0].T
    w_key, w_value, w_down = w_key.T, w_value.T, w_down.T

    tokens_got = swap(tokens)
    all_tables = position_tables(segments.shape[1])
    where = (segments, segments)
    projections = (w_query, w_key, w_value)

    act = shape((width, half), F32)
    low = shape((width, half), BF16)
    kv = shape((2 * kv_width, half), BF16)
    kv_f32 = shape((2 * kv_width, half), F32)
    wide = shape((2 * hidden, half), BF16)
    thin = shape((hidden, half), BF16)
    column = shape((width, 1), F32)
    square = shape((width, width), F32)
    heads_f32 = pltpu.VMEM((HEADS, BLOCK, BLOCK), F32)
    heads_low = pltpu.VMEM((HEADS, BLOCK, BLOCK), BF16)
    key_scratch = pltpu.VMEM((2 * KV_HEADS, half, HEAD_DIM), BF16)
    masks_shape = shape((2, 2, BLOCK, BLOCK), F32)
    rows_f32 = shape((16, half), F32)
    act_scratch = pltpu.VMEM((width, half), F32)
    low_scratch = pltpu.VMEM((width, half), BF16)

    def attend(query, kv_own, kv_other, masks=None):
        state, made = (), []
        for own, kv_part in ((True, kv_own), (False, kv_other)):

            def kernel(*refs, own=own):
                attend_kernel(own, *refs)

            state, new = run(
                kernel,
                where + (query, kv_part, tuple(state), () if masks is None else (masks[len(made)],)),
                ((rows_f32, rows_f32, act) if own else (low, rows_f32),
                 (masks_shape,) if masks is None else ()),
                [pltpu.VMEM((2, KV_HEADS, HEAD_DIM + 16, BLOCK), BF16),
                 pltpu.VMEM((4 * BLOCK, 8), jnp.int32), heads_f32],
                smem=1,
                name="attend_own" if own else "attend_other",
                us=4,
            )
            made.append(new[0] if masks is None else masks[len(made)])
        return (*state, made)

    def attend_back(query, kv_own, kv_other, masks, ctx, lse, grad, us=5):
        more = (ctx,)
        for own, kv_part, dkv in ((False, kv_other, kv), (True, kv_own, kv_f32)):

            def kernel(*refs, own=own):
                attend_back_kernel(own, *refs)

            (outs,) = run(
                kernel,
                (segments, query, kv_part, masks[0 if own else 1], lse, grad, more),
                ((act, dkv),) if own else ((act, rows_f32, dkv),),
                [key_scratch, heads_f32, heads_low, heads_low,
                 pltpu.VMEM((2, 2 * kv_width, BLOCK), F32)],
                smem=1,
                name="attend_back_own" if own else "attend_back_other",
                us=us,
            )
            if not own:
                more = outs[:2]
                got = swap(outs[2])
        return outs[0], outs[1], got

    table = shape((HALF, half), F32)
    tile_low, tile_kv = shape((width, cut), BF16), shape((2 * kv_width, cut), BF16)
    x_half = pltpu.VMEM((width, cut), F32)
    *halves, gain_col, ffn_gain_col, cos_table, sin_table, wq, wk, wv = run(
        first_kernel,
        in_hbm((tokens,) + projections + all_tables + (attn_gain, ffn_gain)),
        (tile_low, tile_low, tile_low, tile_kv, column, column, table, table)
        + tuple(shape(weight.shape, BF16) for weight in projections),
        [x_half, pltpu.VMEM((width,), F32), pltpu.VMEM((width,), F32),
         pltpu.SemaphoreType.DMA((10,))],
        hbm=8,
        name="first",
        us=2,
    )
    projections, tables = (wq, wk, wv), (cos_table, sin_table)
    (x1, normed1, query1, kv1), = run(
        second_kernel,
        (tokens_got, tuple(halves), gain_col) + tables + projections,
        ((low, low, low, kv),),
        [x_half],
        name="second",
        us=1,
    )
    kv1, cot_sent = tie(kv1, cotangent)
    kv1_other = swap(kv1)
    gate_pair = (w_gate, swap(w_gate))
    up_pair = (w_up, swap(w_up))
    down_pair = (w_down, swap(w_down))
    cot_got = swap(cot_sent)
    ctx1, lse1, masks = attend(query1, kv1, kv1_other)
    mid1, ffn1, gate1, up1, x2, normed2, query2, kv2 = run(
        middle_kernel,
        (x1, ctx1, w_out, ffn_gain_col, gate_pair, up_pair, down_pair, gain_col)
        + projections + tables,
        (act, low, wide, wide, act, low, low, kv),
        [pltpu.VMEM(wide.shape, BF16)],
        name="middle",
        us=6,
    )
    kv2_other = swap(kv2)
    ctx2, lse2, _ = attend(query2, kv2, kv2_other, masks)
    (
        mid2, cot, ffn2, kept2_own, kept2_other, grad_mid2, grad_mid_low2, grad_ctx2, dffn_gain2,
    ) = run(
        turn_kernel,
        (x2, ctx2, w_out, ffn_gain_col, gate_pair, up_pair, down_pair, cotangent, cot_got),
        (act, low, low, (thin,) * 3, (thin,) * 3, act, low, low, column),
        [act_scratch],
        name="turn",
        us=9,
    )
    dq2, dkv_own2, dkv_got2 = attend_back(query2, kv2, kv2_other, masks, ctx2, lse2, grad_ctx2)
    pad = 8 * max(n // 2, 1)
    stack_rows = -(-3 * width // pad) * pad
    stack_shape = shape((stack_rows, hidden), BF16)
    pre = shape((width + 2 * kv_width, half), BF16)
    dpre2, dgain2, low1, gstream, dffn, stack_other = run(
        other_kernel,
        (dq2, dkv_own2, dkv_got2, x2, grad_mid2, gain_col) + projections + tables
        + (ffn1, gate1, up1, gate_pair[1], up_pair[1], down_pair[1], ffn2, cot, kept2_other),
        (pre, column, low, act, act, stack_shape),
        [act_scratch, pltpu.VMEM((3,) + thin.shape, BF16)],
        name="other",
        us=8,
    )
    stack_got = swap(stack_other)
    stack_own, grad_mid1, grad_mid_low1, grad_ctx1, dffn_gain = run(
        own_kernel,
        (low1, gstream, dffn, ffn1, gate1, up1, gate_pair[0], up_pair[0], down_pair[0],
         ffn2, cot, kept2_own, mid1, w_out, ffn_gain_col, dffn_gain2),
        (stack_shape, act, low, low, column),
        [act_scratch, pltpu.VMEM((3,) + thin.shape, BF16)],
        name="own",
        us=7,
    )
    ffn_orders, pack_orders = orders_of(n)
    ffn = Stream("ffn", (stack_own, stack_got), sizes, ffn_orders)
    token = ffn.step(stack_own)
    grad_ctx1, token = tie(grad_ctx1, token)
    dq1, dkv_own1, dkv_got1 = attend_back(query1, kv1, kv1_other, masks, ctx1, lse1, grad_ctx1, 0)
    rows = -(-(2 * width + 2 * kv_width) // 2 // pad) * pad
    lanes = -(-width // 128) * 128
    lanes = lanes if lanes - width >= 2 else lanes + 128
    half_stack = shape((rows, lanes), BF16)
    tile_act = shape((width, cut), F32)
    dnormed1, pack_own, pack_other = run(
        last_kernel,
        (dq1, dkv_own1, dkv_got1, x1) + projections + tables
        + (dpre2, (normed1, normed2), (ctx1, ctx2), (grad_mid_low1, grad_mid_low2),
           dgain2, dffn_gain),
        (act, half_stack, half_stack),
        [pltpu.VMEM(pre.shape, BF16), act_scratch,
         pltpu.VMEM((width, 1), F32), pltpu.VMEM((2, rows, lanes), BF16)],
        name="last",
        us=0,
    )
    pack = Stream("pack", (pack_own, swap(pack_other)), sizes, pack_orders)
    token = pack_own
    for index, which in enumerate("fafafaafafafa"):
        token = (ffn if which == "f" else pack).step(token)
        if index == 1:
            ((output, output_sent),) = run(
                result_kernel,
                (mid2, (kept2_own[0], kept2_other[0]), down_pair),
                ((tile_low, tile_low),), after=token, name="result", us=0,
            )
            token = (token, output)
        if index == 3:
            ((grad_input, grad_input_sent),) = run(
                input_kernel,
                (x1, gain_col, dnormed1, grad_mid1), ((tile_act, tile_act),),
                [act_scratch, act_scratch, pltpu.VMEM((width, 1), F32)],
                after=token, name="input", us=0,
            )
            token = (token, grad_input)
        if index == 7:
            output = jnp.concatenate([output, swap(output_sent)], axis=1)
            grad_input = jnp.concatenate([grad_input, swap(grad_input_sent)], axis=1)
            token = (token, output, grad_input)
    while not (ffn.done and pack.done):
        token = pack.step(ffn.step(token))

    def kernel(own_ref, got_ref, out_ref, all_ref):
        pack_kernel(pack, own_ref, got_ref, out_ref, all_ref)

    (pack_sum,) = run(
        kernel, tuple(pack.terms), (half_stack,),
        [pltpu.VMEM((pack.chunks, rows // pack.chunks, lanes), BF16)], name="pack_all", us=0,
    )
    def finish(mine, part, after, update):
        def kernel(part_ref, *refs):
            finish_kernel(ffn, mine, part_ref, refs[:3], *refs[3:])

        count, rows, columns = part.shape
        return run(
            kernel, (part,), (shape((width, hidden), F32),) * 3,
            [pltpu.VMEM(part.shape, F32), pltpu.SemaphoreType.DMA((count, rows // width + 2))],
            after=after, name="finish", us=2, hbm_outs=True, update=update,
        )

    finished = finish(True, ffn.terms[0], pack_sum, ())
    half_rows = width + kv_width

    def kernel(*refs):
        unpack_kernel(half_rows, *refs)

    kv_square = shape((kv_width, width), F32)
    vector = shape((width,), F32)
    dgain, dffn_gain, dw_query, dw_key, dw_value, dw_out = run(
        kernel,
        (pack_sum, swap(pack_sum)),
        (vector, vector, square, kv_square, kv_square, square),
        [pltpu.VMEM((2, half_rows, width), F32)],
        name="unpack",
        us=0,
    )
    got, (output, grad_input, dgain, dffn_gain, dw_query, dw_key, dw_value, dw_out) = tie(
        ffn.terms[1],
        (output, grad_input, dgain, dffn_gain, dw_query, dw_key, dw_value, dw_out),
    )
    dw_gate, dw_up, dw_down = finish(False, got, (), finished)
    return (
        output.T[None],
        grad_input.T[None],
        dgain,
        dw_query,
        dw_key.T,
        dw_value.T,
        dw_out,
        dffn_gain,
        dw_gate,
        dw_up,
        dw_down.T,
    )


def solution(mesh):
    sizes = (mesh.shape["dp"], mesh.shape["tensor"])

    def local(*args):
        return per_device(sizes, *args)

    split = P("dp", "tensor", None)
    in_specs = (
        split, P("dp", None), split, P(), P(), P(), P(), P(), P(),
        P(None, "tensor"), P(None, "tensor"), P("tensor", None),
    )
    out_specs = (
        split, split, P(), P(), P(), P(), P(), P(),
        P(None, "tensor"), P(None, "tensor"), P("tensor", None),
    )
    return jax.shard_map(
        local, mesh=mesh, in_specs=in_specs, out_specs=out_specs, check_vma=False
    )
```

```python
import jax
import jax.numpy as jnp
import numpy as np
from jax import lax
from jax.experimental import pallas as pl
from jax.experimental.pallas import tpu as pltpu
from jax.sharding import PartitionSpec as P

HEADS = 9
KV_HEADS = 3
GROUP = HEADS // KV_HEADS
HEAD_DIM = 64
HALF = HEAD_DIM // 2
EPSILON = 1e-05
MASKED = -1e30
BLOCK = 256
SCALE = HEAD_DIM ** (-0.5)
F32 = jnp.float32
BF16 = jnp.bfloat16
VMEM_LIMIT = 16 * 2**20


def dot(left, right, left_dim, right_dim):
    return lax.dot_general(
        left, right, (((left_dim,), (right_dim,)), ((), ())), preferred_element_type=F32
    )


def pieces(size, step):
    return [slice(start, start + step) for start in range(0, size, step)]


def inverse_rms(x_ref):
    total = None
    for rows in pieces(x_ref.shape[0], 64):
        x = x_ref[rows, :]
        part = jnp.sum(x * x, axis=0, keepdims=True)
        total = part if total is None else total + part
    return lax.rsqrt(total / x_ref.shape[0] + EPSILON)


def norm_forward(x_ref, gain_ref, out_ref):
    scale = inverse_rms(x_ref)
    for rows in pieces(x_ref.shape[0], 64):
        out_ref[rows, :] = (x_ref[rows, :] * scale * gain_ref[rows, :]).astype(BF16)


def norm_backward(x_ref, gain_ref, grad_ref, add_ref, out_ref, gain_grad_ref):
    scale = inverse_rms(x_ref)
    inner = None
    for rows in pieces(x_ref.shape[0], 64):
        x, e = x_ref[rows, :], grad_ref[rows, :]
        xe = x * e
        gain_grad_ref[rows, :] = jnp.sum(xe * scale, axis=1, keepdims=True)
        part = jnp.sum(xe * gain_ref[rows, :], axis=0, keepdims=True)
        inner = part if inner is None else inner + part
    cubed = scale * scale * scale * (inner / x_ref.shape[0])
    for rows in pieces(x_ref.shape[0], 64):
        out_ref[rows, :] = (
            add_ref[rows, :].astype(F32)
            + scale * gain_ref[rows, :] * grad_ref[rows, :]
            - x_ref[rows, :] * cubed
        )


def gain_backward(x_ref, grad_ref, gain_grad_ref):
    scale = inverse_rms(x_ref)
    for rows in pieces(x_ref.shape[0], 64):
        gain_grad_ref[rows, :] = jnp.sum(
            x_ref[rows, :] * grad_ref[rows, :] * scale, axis=1, keepdims=True
        )


def rotated(x, cos_table, sin_table):
    front, back = x[:HALF], x[HALF:]
    return jnp.concatenate(
        [front * cos_table - back * sin_table, back * cos_table + front * sin_table], axis=0
    )


def project_qkv(normed_ref, wq_ref, wk_ref, wv_ref, cos_ref, sin_ref, q_ref, kv_ref):
    normed = normed_ref[...]
    cos_table, sin_table = cos_ref[...], sin_ref[...]
    key = dot(wk_ref[...], normed, 1, 0)
    for head in pieces(KV_HEADS * HEAD_DIM, HEAD_DIM):
        kv_ref[head, :] = rotated(key[head], cos_table, sin_table).astype(BF16)
    kv_ref[KV_HEADS * HEAD_DIM :, :] = dot(wv_ref[...], normed, 1, 0).astype(BF16)
    query = dot(wq_ref[...], normed, 0, 0)
    for head in pieces(HEADS * HEAD_DIM, HEAD_DIM):
        q_ref[head, :] = (rotated(query[head], cos_table, sin_table) * SCALE).astype(BF16)


def first_kernel(
    tokens_hbm, wq_hbm, wk_hbm, wv_hbm, cos_hbm, sin_hbm, gain_hbm, ffn_gain_hbm,
    low_ref, normed_ref, q_ref, kv_ref, gain_ref, ffn_gain_ref, cos_ref, sin_ref,
    wq_ref, wk_ref, wv_ref,
    x_ref, gain_in_ref, ffn_gain_in_ref, sems,
):
    cut = low_ref.shape[1]
    pairs = [
        (gain_hbm, gain_in_ref), (ffn_gain_hbm, ffn_gain_in_ref),
        (tokens_hbm.at[:, :cut], low_ref), (wk_hbm, wk_ref), (wv_hbm, wv_ref), (wq_hbm, wq_ref),
    ]
    for local, tile in enumerate(tile_places(lax.axis_index("tensor"))):
        cols = slice(local * cut, (local + 1) * cut)
        for source, target in ((cos_hbm, cos_ref), (sin_hbm, sin_ref)):
            pairs.append((source.at[:, tile_lanes(tile)], target.at[:, cols]))
    copies = [
        pltpu.make_async_copy(source, target, sems.at[index])
        for index, (source, target) in enumerate(pairs)
    ]
    for copy in copies:
        copy.start()
    copies[0].wait()
    copies[1].wait()
    for in_ref, column_ref in ((gain_in_ref, gain_ref), (ffn_gain_in_ref, ffn_gain_ref)):
        row = in_ref[...].reshape(1, -1)
        column_ref[...] = jnp.broadcast_to(row, (128, row.shape[1])).T[:, :1]
    copies[2].wait()
    x_ref[...] = low_ref[...].astype(F32)
    norm_forward(x_ref, gain_ref, normed_ref)
    for copy in copies[3:]:
        copy.wait()
    tables = (cos_ref.at[:, :cut], sin_ref.at[:, :cut])
    project_qkv(normed_ref, wq_ref, wk_ref, wv_ref, *tables, q_ref, kv_ref)


def second_kernel(
    got_ref, half_refs, gain_ref, cos_ref, sin_ref, wq_ref, wk_ref, wv_ref, full_refs, x_ref
):
    cut = x_ref.shape[1]
    for half_ref, full_ref in zip(half_refs, full_refs):
        full_ref[:, :cut] = half_ref[...]
    low_ref, normed_ref, q_ref, kv_ref = (ref.at[:, cut:] for ref in full_refs)
    low_ref[...] = got_ref[:, cut:]
    x_ref[...] = low_ref[...].astype(F32)
    norm_forward(x_ref, gain_ref, normed_ref)
    tables = (cos_ref.at[:, cut:], sin_ref.at[:, cut:])
    project_qkv(normed_ref, wq_ref, wk_ref, wv_ref, *tables, q_ref, kv_ref)


def tile_places(core):
    return 2 * core, 3 - 2 * core


def tile_lanes(tile):
    return pl.ds(pl.multiple_of(tile * BLOCK, BLOCK), BLOCK)


def set_labels(labels_ref, column_ref):
    column_ref[...] = jnp.broadcast_to(labels_ref[0:1, :], (8, labels_ref.shape[1])).T


def set_mask(bias_ref, labels_ref, column_ref, tile, kb):
    key_labels = column_ref[tile_lanes(kb), :1]
    key_place = kb * BLOCK + lax.broadcasted_iota(jnp.int32, (BLOCK, BLOCK), 0)
    place = tile * BLOCK + lax.broadcasted_iota(jnp.int32, (1, BLOCK), 1)
    allowed = (key_labels == labels_ref[0:1, tile_lanes(tile)]) & (key_place <= place)
    bias_ref[...] = jnp.where(allowed, 0.0, MASKED)


def first_block(segments_ref, tile):
    label = segments_ref[0, tile * BLOCK]
    count = jnp.int32(0)
    for kb in range(3):
        before = (kb < tile) & (segments_ref[0, kb * BLOCK + BLOCK - 1] < label)
        count = count + before.astype(jnp.int32)
    return count


def head_rows(head):
    return slice(head * HEAD_DIM, (head + 1) * HEAD_DIM)


def load_part(kv_ref, tok_ref):
    for head in range(2 * KV_HEADS):
        for cols in pieces(kv_ref.shape[1], BLOCK):
            tok_ref[head, cols, :] = kv_ref[head_rows(head), cols].T


def over_blocks(segments_ref, core, own, body):
    keys_of = tile_places(core if own else 1 - core)
    for local, tile in enumerate(tile_places(core)):
        cols = slice(local * BLOCK, (local + 1) * BLOCK)
        first = first_block(segments_ref, tile)

        def step(at, carry):
            kb = jnp.where(at == 0, keys_of[0], keys_of[1])

            @pl.when((kb >= first) & (kb <= tile))
            def _():
                body(local, tile, cols, kb, at)

            return carry

        lax.fori_loop(0, 2, step, 0)


def attend_kernel(
    own, segments_ref, labels_ref, q_ref, kv_ref, state_refs, mask_in_refs, out_refs, mask_out_refs,
    value_ref, column_ref, scores_ref,
):
    core = lax.axis_index("tensor")
    if mask_out_refs:
        set_labels(labels_ref, column_ref)
    (masks_ref,) = mask_in_refs or mask_out_refs
    for at, cols in enumerate(pieces(kv_ref.shape[1], BLOCK)):
        for group in range(KV_HEADS):
            value_ref[at, group, :HEAD_DIM, :] = kv_ref[head_rows(KV_HEADS + group), cols]
            value_ref[at, group, HEAD_DIM:, :] = jnp.ones((16, BLOCK), BF16)
    m_ref, l_ref, acc_ref = out_refs if own else state_refs
    if own:
        m_ref[...] = jnp.full(m_ref.shape, MASKED, F32)
        l_ref[...] = jnp.zeros(l_ref.shape, F32)
        acc_ref[...] = jnp.zeros(acc_ref.shape, F32)

    def body(local, tile, cols, kb, at):
        bias_ref = masks_ref.at[local, at]
        if mask_out_refs:
            set_mask(bias_ref, labels_ref, column_ref, tile, kb)
        keys = tile_lanes(at)

        def scores(group):
            key = kv_ref[head_rows(group), keys]
            for head in range(group * GROUP, (group + 1) * GROUP):
                scores_ref[head] = dot(key, q_ref[head_rows(head), cols], 0, 0) + bias_ref[...]

        def products(group):
            for head in range(group * GROUP, (group + 1) * GROUP):
                rows = head_rows(head)
                m_old = m_ref[head : head + 1, cols]
                m_new = jnp.maximum(m_old, jnp.max(scores_ref[head], axis=0, keepdims=True))
                m_ref[head : head + 1, cols] = m_new
                fade = jnp.exp(m_old - m_new)
                probs = jnp.exp(scores_ref[head] - m_new).astype(BF16)
                product = dot(value_ref[at, group], probs, 1, 0)
                l_ref[head : head + 1, cols] = (
                    l_ref[head : head + 1, cols] * fade + product[HEAD_DIM : HEAD_DIM + 1]
                )
                acc_ref[rows, cols] = acc_ref[rows, cols] * fade + product[:HEAD_DIM]

        scores(0)
        scores(1)
        products(0)
        scores(2)
        products(1)
        products(2)

    over_blocks(segments_ref, core, own, body)
    if not own:
        ctx_ref, lse_ref = out_refs
        for head in range(HEADS):
            total = l_ref[head : head + 1, :]
            ctx_ref[head_rows(head), :] = (acc_ref[head_rows(head), :] * (1.0 / total)).astype(BF16)
            lse_ref[head : head + 1, :] = m_ref[head : head + 1, :] + jnp.log(total)


def attend_back_kernel(
    own, segments_ref, q_ref, kv_ref, masks_ref, lse_ref, grad_ref, more_refs, out_refs,
    tok_ref, probs_ref, probs_low_ref, gs_ref, dkv_ref,
):
    core = lax.axis_index("tensor")
    load_part(kv_ref, tok_ref)
    if own:
        dq_in_ref, delta_ref = more_refs
        dq_ref, dkv_out_ref = out_refs
        dq_ref[...] = dq_in_ref[...]
    else:
        (ctx_ref,) = more_refs
        dq_ref, delta_ref, dkv_out_ref = out_refs
        dq_ref[...] = jnp.zeros(dq_ref.shape, F32)
        for head in range(HEADS):
            rows = head_rows(head)
            delta_ref[head : head + 1, :] = jnp.sum(
                grad_ref[rows, :].astype(F32) * ctx_ref[rows, :].astype(F32), axis=0, keepdims=True
            )
    dkv_ref[...] = jnp.zeros(dkv_ref.shape, F32)

    def body(local, tile, cols, kb, at):
        bias_ref = masks_ref.at[local, at]
        keys = tile_lanes(at)
        for head in range(HEADS):
            key = tok_ref[head // GROUP, keys, :]
            scores = dot(key, q_ref[head_rows(head), cols], 1, 0) + bias_ref[...]
            probs = jnp.exp(scores - lse_ref[head : head + 1, cols])
            probs_ref[head] = probs
            probs_low_ref[head] = probs.astype(BF16)
        for head in range(HEADS):
            value = tok_ref[KV_HEADS + head // GROUP, keys, :]
            grad_probs = dot(value, grad_ref[head_rows(head), cols], 1, 0)
            gs_ref[head] = (
                probs_ref[head] * (grad_probs - delta_ref[head : head + 1, cols])
            ).astype(BF16)
        for group in range(KV_HEADS):
            dv = dkv_ref[at, head_rows(KV_HEADS + group), :]
            for head in range(group * GROUP, (group + 1) * GROUP):
                dv = dv + dot(grad_ref[head_rows(head), cols], probs_low_ref[head], 1, 1)
            dkv_ref[at, head_rows(KV_HEADS + group), :] = dv
        for group in range(KV_HEADS):
            dk = dkv_ref[at, head_rows(group), :]
            for head in range(group * GROUP, (group + 1) * GROUP):
                dk = dk + dot(q_ref[head_rows(head), cols], gs_ref[head], 1, 1)
            dkv_ref[at, head_rows(group), :] = dk
        for head in range(HEADS):
            key_cols = kv_ref[head_rows(head // GROUP), keys]
            dq_ref[head_rows(head), cols] += dot(key_cols, gs_ref[head], 1, 0)

    over_blocks(segments_ref, core, own, body)
    for at, cols in enumerate(pieces(dkv_out_ref.shape[1], BLOCK)):
        dkv_out_ref[:, cols] = dkv_ref[at].astype(dkv_out_ref.dtype)


def middle_kernel(
    low_ref, ctx_ref, wo_ref, ffn_gain_ref, wg_refs, wu_refs, wd_refs,
    gain_ref, wq_ref, wk_ref, wv_ref, cos_ref, sin_ref,
    mid_ref, ffn_ref, gate_ref, up_ref, x2_ref, normed_ref, q_ref, kv_ref, product_ref,
):
    mid_ref[...] = low_ref[...].astype(F32) + dot(wo_ref[...], ctx_ref[...], 0, 0)
    norm_forward(mid_ref, ffn_gain_ref, ffn_ref)
    ffn_in = ffn_ref[...]
    half_hidden = wg_refs[0].shape[1]
    for part in range(2):
        for hidden in pieces(half_hidden, BLOCK):
            gate = dot(wg_refs[part][:, hidden], ffn_in, 0, 0)
            up = dot(wu_refs[part][:, hidden], ffn_in, 0, 0)
            rows = slice(part * half_hidden + hidden.start, part * half_hidden + hidden.stop)
            gate_ref[rows, :] = gate.astype(BF16)
            up_ref[rows, :] = up.astype(BF16)
            product_ref[rows, :] = (gate * jax.nn.sigmoid(gate) * up).astype(BF16)
    x2_ref[...] = (
        mid_ref[...]
        + dot(wd_refs[0][...], product_ref[:half_hidden, :], 1, 0)
        + dot(wd_refs[1][...], product_ref[half_hidden:, :], 1, 0)
    )
    norm_forward(x2_ref, gain_ref, normed_ref)
    project_qkv(normed_ref, wq_ref, wk_ref, wv_ref, cos_ref, sin_ref, q_ref, kv_ref)


def ffn_terms(gate, up, grad_product):
    sig = jax.nn.sigmoid(gate)
    silu = gate * sig
    grad_gate = (grad_product * up * (sig + silu * (1.0 - sig))).astype(BF16)
    grad_up = (grad_product * silu).astype(BF16)
    return (silu * up).astype(BF16), grad_gate, grad_up


def turn_kernel(
    x_ref, ctx_ref, wo_ref, ffn_gain_ref, wg_refs, wu_refs, wd_refs, cotangent_ref, cot_got_ref,
    mid_ref, cot_ref, ffn_ref, kept_own_refs, kept_other_refs,
    grad_mid_ref, grad_mid_low_ref, grad_ctx_ref, dgain_ref,
    acc_ref,
):
    mid_ref[...] = x_ref[...] + dot(wo_ref[...], ctx_ref[...], 0, 0)
    norm_forward(mid_ref, ffn_gain_ref, ffn_ref)
    ffn_in = ffn_ref[...]
    cut = cot_got_ref.shape[1] // 2
    cot_ref[:, :cut] = cotangent_ref[:, :cut]
    cot_ref[:, cut:] = cot_got_ref[:, cut:]
    grad_low = cot_ref[...]
    for part in range(2):
        for hidden in pieces(wg_refs[part].shape[1], BLOCK):
            gate = dot(wg_refs[part][:, hidden], ffn_in, 0, 0)
            up = dot(wu_refs[part][:, hidden], ffn_in, 0, 0)
            grad_product = dot(wd_refs[part][:, hidden], grad_low, 0, 0)
            kept = (kept_own_refs, kept_other_refs)[part]
            for ref, term in zip(kept, ffn_terms(gate, up, grad_product)):
                ref[hidden, :] = term
    acc_ref[...] = (
        dot(wg_refs[0][...], kept_own_refs[1][...], 1, 0)
        + dot(wu_refs[0][...], kept_own_refs[2][...], 1, 0)
        + dot(wg_refs[1][...], kept_other_refs[1][...], 1, 0)
        + dot(wu_refs[1][...], kept_other_refs[2][...], 1, 0)
    )
    norm_backward(mid_ref, ffn_gain_ref, acc_ref, cot_ref, grad_mid_ref, dgain_ref)
    grad_mid_low_ref[...] = grad_mid_ref[...].astype(BF16)
    grad_ctx_ref[...] = dot(wo_ref[...], grad_mid_low_ref[...], 1, 0).astype(BF16)


def result_kernel(mid_ref, product_refs, wd_refs, out_refs):
    result = (
        mid_ref[...]
        + dot(wd_refs[0][...], product_refs[0][...], 1, 0)
        + dot(wd_refs[1][...], product_refs[1][...], 1, 0)
    )
    cut = out_refs[0].shape[1]
    out_refs[0][...] = result[:, :cut].astype(BF16)
    out_refs[1][...] = result[:, cut:].astype(BF16)


def input_kernel(
    x_low_ref, gain_ref, dnormed_ref, grad_mid_ref, out_refs, x_ref, out_ref, dgain_ref
):
    x_ref[...] = x_low_ref[...].astype(F32)
    norm_backward(x_ref, gain_ref, dnormed_ref, grad_mid_ref, out_ref, dgain_ref)
    cut = out_refs[0].shape[1]
    out_refs[0][...] = out_ref[:, :cut]
    out_refs[1][...] = out_ref[:, cut:]


def qkv_back(
    dq_ref, dkv_own_ref, dkv_got_ref, wq_ref, wk_ref, wv_ref, cos_ref, sin_ref, dpre_ref, dnormed_ref
):
    cos_table, sin_table = cos_ref[...], sin_ref[...]
    width, kv_width = HEADS * HEAD_DIM, KV_HEADS * HEAD_DIM
    for head in pieces(width, HEAD_DIM):
        dpre_ref[head, :] = rotated(dq_ref[head, :] * SCALE, cos_table, -sin_table).astype(BF16)
    for head in pieces(kv_width, HEAD_DIM):
        total = dkv_own_ref[head, :] + dkv_got_ref[head, :].astype(F32)
        rows = slice(width + head.start, width + head.stop)
        dpre_ref[rows, :] = rotated(total, cos_table, -sin_table).astype(BF16)
    dpre_ref[width + kv_width :, :] = (
        dkv_own_ref[kv_width:, :] + dkv_got_ref[kv_width:, :].astype(F32)
    ).astype(BF16)
    dnormed_ref[...] = (
        dot(wq_ref[...], dpre_ref[:width, :], 1, 0)
        + dot(wk_ref[...], dpre_ref[width : width + kv_width, :], 0, 0)
        + dot(wv_ref[...], dpre_ref[width + kv_width :, :], 0, 0)
    )


def fill_stack(stack, width):
    if stack.shape[0] > 3 * width:
        stack[3 * width :, :] = jnp.zeros((stack.shape[0] - 3 * width, stack.shape[1]), BF16)


def ffn_back(
    part, stack, low, ffn1, ffn2, low2, gate_ref, up_ref, wg_ref, wu_ref, wd_ref, kept2_refs,
    acc_ref, terms_ref,
):
    width, half_hidden = wg_ref.shape
    for hidden in pieces(half_hidden, BLOCK):
        rows = slice(part * half_hidden + hidden.start, part * half_hidden + hidden.stop)
        grad_product = dot(wd_ref[:, hidden], low, 0, 0)
        terms = ffn_terms(gate_ref[rows, :].astype(F32), up_ref[rows, :].astype(F32), grad_product)
        for at, term in enumerate(terms):
            terms_ref[at, hidden, :] = term
    acc_ref[...] += dot(wg_ref[...], terms_ref[1], 1, 0) + dot(wu_ref[...], terms_ref[2], 1, 0)
    for at, (left1, left2, which) in enumerate(((ffn1, ffn2, 1), (ffn1, ffn2, 2), (low, low2, 0))):
        stack[at * width : (at + 1) * width, :] = (
            dot(left1, terms_ref[which], 1, 1) + dot(left2, kept2_refs[which][...], 1, 1)
        ).astype(BF16)
    fill_stack(stack, width)


def other_kernel(
    dq_ref, dkv_own_ref, dkv_got_ref, x_ref, grad_mid_ref,
    gain_ref, wq_ref, wk_ref, wv_ref, cos_ref, sin_ref,
    ffn1_ref, gate_ref, up_ref, wg_ref, wu_ref, wd_ref, ffn2_ref, low2_ref, kept2_refs,
    dpre_ref, dgain_ref, low_ref, gstream_ref, acc_ref, stack, dnormed_ref, terms_ref,
):
    qkv_back(
        dq_ref, dkv_own_ref, dkv_got_ref, wq_ref, wk_ref, wv_ref, cos_ref, sin_ref,
        dpre_ref, dnormed_ref,
    )
    norm_backward(x_ref, gain_ref, dnormed_ref, grad_mid_ref, gstream_ref, dgain_ref)
    low_ref[...] = gstream_ref[...].astype(BF16)
    acc_ref[...] = jnp.zeros(acc_ref.shape, F32)
    ffn_back(
        1, stack, low_ref[...], ffn1_ref[...], ffn2_ref[...], low2_ref[...],
        gate_ref, up_ref, wg_ref, wu_ref, wd_ref, kept2_refs, acc_ref, terms_ref,
    )


def own_kernel(
    low_ref, gstream_ref, acc_in_ref,
    ffn1_ref, gate_ref, up_ref, wg_ref, wu_ref, wd_ref, ffn2_ref, low2_ref, kept2_refs,
    mid_ref, wo_ref, ffn_gain_ref, dffn_gain2_ref,
    stack, grad_mid_ref, grad_mid_low_ref, grad_ctx_ref, dffn_gain_ref, acc_ref, terms_ref,
):
    acc_ref[...] = acc_in_ref[...]
    ffn_back(
        0, stack, low_ref[...], ffn1_ref[...], ffn2_ref[...], low2_ref[...],
        gate_ref, up_ref, wg_ref, wu_ref, wd_ref, kept2_refs, acc_ref, terms_ref,
    )
    norm_backward(mid_ref, ffn_gain_ref, acc_ref, gstream_ref, grad_mid_ref, dffn_gain_ref)
    dffn_gain_ref[...] += dffn_gain2_ref[...]
    grad_mid_low_ref[...] = grad_mid_ref[...].astype(BF16)
    grad_ctx_ref[...] = dot(wo_ref[...], grad_mid_low_ref[...], 1, 0).astype(BF16)


def last_kernel(
    dq_ref, dkv_own_ref, dkv_got_ref, x_low_ref, wq_ref, wk_ref, wv_ref, cos_ref, sin_ref,
    dpre2_ref, normed_refs, ctx_refs, grad_mid_low_refs, dgain2_ref, dffn_gain_ref,
    dnormed_ref, stack_own_ref, stack_other_ref,
    dpre_ref, x_ref, dgain_ref, stack_ref,
):
    x_ref[...] = x_low_ref[...].astype(F32)
    width, rows = x_ref.shape[0], stack_ref.shape[1]
    qkv_back(
        dq_ref, dkv_own_ref, dkv_got_ref, wq_ref, wk_ref, wv_ref, cos_ref, sin_ref,
        dpre_ref, dnormed_ref,
    )
    gain_backward(x_ref, dnormed_ref, dgain_ref)
    normed1, normed2 = (ref[...] for ref in normed_refs)
    dwq = dot(normed1, dpre_ref[:width, :], 1, 1) + dot(normed2, dpre2_ref[:width, :], 1, 1)
    dwkv = dot(dpre_ref[width:, :], normed1, 1, 1) + dot(dpre2_ref[width:, :], normed2, 1, 1)
    dwo = dot(ctx_refs[0][...], grad_mid_low_refs[0][...], 1, 1) + dot(
        ctx_refs[1][...], grad_mid_low_refs[1][...], 1, 1
    )
    half_rows = width + dwkv.shape[0] // 2
    rest = half_rows - width
    stack_ref[0, :width, :width] = dwq.astype(BF16)
    stack_ref[0, width:half_rows, :width] = dwo[:rest].astype(BF16)
    stack_ref[1, : width - rest, :width] = dwo[rest:].astype(BF16)
    stack_ref[1, width - rest : half_rows, :width] = dwkv.astype(BF16)
    lanes = stack_ref.shape[2] - width
    column = lax.broadcasted_iota(jnp.int32, (width, lanes), 1)
    gains = jnp.where(
        column == 0,
        dgain_ref[...] + dgain2_ref[...],
        jnp.where(column == 1, dffn_gain_ref[...], 0.0),
    ).astype(BF16)
    for part in range(2):
        stack_ref[part, :width, width:] = gains
        stack_ref[part, width:, width:] = jnp.zeros((rows - width, lanes), BF16)
        if rows > half_rows:
            stack_ref[part, half_rows:, :width] = jnp.zeros((rows - half_rows, width), BF16)
    core = lax.axis_index("tensor")
    stack_own_ref[...] = stack_ref[core]
    stack_other_ref[...] = stack_ref[1 - core]


def shape(dims, dtype):
    return jax.ShapeDtypeStruct(dims, dtype)


def run(
    kernel, args, outs, scratch=(), smem=0, hbm=0, after=(), name=None, us=5, limit=VMEM_LIMIT,
    hbm_outs=0, update=(),
):
    leaves, tree = jax.tree.flatten(args)
    out_leaves, out_tree = jax.tree.flatten(outs)
    late = jax.tree.leaves(after) + list(update)
    n_in, n_out = len(leaves), len(out_leaves)

    def body(*refs):
        ins = jax.tree.unflatten(tree, refs[:n_in])
        refs = refs[n_in + len(late) :]
        results = jax.tree.unflatten(out_tree, refs[:n_out])
        kernel(*ins, *results, *refs[n_out:])

    in_specs = [
        pl.BlockSpec(
            memory_space=pltpu.SMEM if index < smem else pltpu.HBM if index < hbm else pltpu.VMEM
        )
        for index in range(n_in)
    ] + [pl.BlockSpec(memory_space=pl.ANY)] * len(late)
    results = pl.pallas_call(
        body,
        out_shape=out_leaves,
        in_specs=in_specs,
        out_specs=[pl.BlockSpec(memory_space=pltpu.HBM if index < hbm_outs else pltpu.VMEM)
            for index in range(n_out)
        ],
        scratch_shapes=list(scratch),
        input_output_aliases={
            n_in + len(late) - len(update) + index: index for index in range(len(update))
        },
        compiler_params=pltpu.CompilerParams(vmem_limit_bytes=limit),
        cost_estimate=pl.CostEstimate(
            flops=int(us * 1e9) + 1, bytes_accessed=2**20 if us else 1, transcendentals=0
        ),
        name=name,
    )(*leaves, *late)
    return jax.tree.unflatten(out_tree, results)


def in_hbm(arrays):
    return tuple(pltpu.with_memory_space_constraint(array, pltpu.HBM) for array in arrays)


def swap(array):
    return lax.ppermute(array, "tensor", [(0, 1), (1, 0)])


def partners(sizes, bits):
    n, cores = sizes
    return [
        (place * cores + core, (place ^ (1 << bits[core])) * cores + core)
        for place in range(n)
        for core in range(cores)
    ]


def by_core(pair):
    return jnp.where(lax.axis_index("tensor") == 0, jnp.int32(pair[0]), jnp.int32(pair[1]))


def own_bit(bits):
    place = lax.axis_index("dp").astype(jnp.int32)
    return lax.shift_right_logical(place, by_core(bits)) & 1


def insert(index, rank, bit):
    low = index & (lax.shift_left(jnp.int32(1), rank) - 1)
    return lax.shift_left(index - low, jnp.int32(1)) + lax.shift_left(bit, rank) + low


def scatter_kernel(bits, ranks, sent, terms, out_ref):
    own, rank = own_bit(bits), by_core(ranks)
    half = 1 - own if sent else own

    def body(index, carry):
        at = insert(index, rank, half)
        total = terms[0][at].astype(F32)
        for term in terms[1:]:
            total = total + term[at].astype(F32)
        out_ref[index] = total.astype(BF16)
        return carry

    lax.fori_loop(0, out_ref.shape[0], body, 0)


def add_kernel(one_ref, two_ref, out_ref):
    out_ref[...] = (one_ref[...].astype(F32) + two_ref[...].astype(F32)).astype(BF16)


def join(bits, ranks, own_ref, got_ref, out_ref):
    own, rank = own_bit(bits), by_core(ranks)

    def body(index, carry):
        out_ref[insert(index, rank, own)] = own_ref[index]
        out_ref[insert(index, rank, 1 - own)] = got_ref[index]
        return carry

    lax.fori_loop(0, own_ref.shape[0], body, 0)


def ranks_of(dims, done):
    ranks = []
    for step in range(len(dims[0])):
        pair = []
        for order in dims:
            there = order[step + 1 :] if done == "after" else order[:step]
            pair.append(sum(other < order[step] for other in there))
        ranks.append(tuple(pair))
    return ranks


class Stream:
    def __init__(self, name, terms, sizes, orders):
        scatter, across, gather = orders
        self.name, self.sizes = name, sizes
        self.halvings = len(scatter[0])
        self.chunks = 1 << self.halvings
        self.bits = list(zip(*scatter)) + [(across, across)] + list(zip(*gather))
        self.ranks = ranks_of(scatter, "after") + [None] + ranks_of(gather, "before")
        self.terms = [term.reshape((self.chunks, -1) + term.shape[1:]) for term in terms]
        self.rounds = 2 * self.halvings + 1
        self.round = 0

    def call(self, kernel, args, counts, after):
        rows, columns = self.terms[0].shape[1:]
        outs = tuple(shape((count, rows, columns), BF16) for count in counts)
        return run(kernel, args, outs, after=after, name=f"{self.name}_{self.round}", us=0)

    def load(self, after):
        if self.round < self.halvings:
            half = self.terms[0].shape[0] // 2
            bits, ranks = self.bits[self.round], self.ranks[self.round]

            terms = tuple(self.terms)

            def part(which, after):
                def kernel(terms, out_ref):
                    scatter_kernel(bits, ranks, which, terms, out_ref)

                return self.call(kernel, (terms,), (half,), after)[0]

            sent = part(True, after)
            self.terms = [part(False, sent)]
            return sent
        if self.round <= self.halvings + 1:
            (sent,) = self.call(add_kernel, tuple(self.terms), (1,), after)
        else:
            bits, ranks = self.bits[self.round - 1], self.ranks[self.round - 1]

            def kernel(*refs):
                join(bits, ranks, *refs)

            (sent,) = self.call(
                kernel, tuple(self.terms), (2 * self.terms[0].shape[0],), after
            )
        self.terms = [sent]
        return sent

    def step(self, token):
        if self.done:
            return token
        sent = self.load(token)
        got = lax.ppermute(sent, ("dp", "tensor"), partners(self.sizes, self.bits[self.round]))
        self.terms = self.terms + [got]
        self.round += 1
        return sent

    @property
    def done(self):
        return self.round == self.rounds

    def join(self, out_ref, own_ref, got_ref):
        join(self.bits[-1], self.ranks[-1], own_ref, got_ref, out_ref)


def finish_kernel(stream, mine, part_ref, outs, token_ref, wide_ref, sems):
    count, rows = part_ref.shape[:2]
    token_ref[...] = jnp.zeros(token_ref.shape, F32)
    for index in range(count):
        wide_ref[index] = part_ref[index].astype(F32)
    width = outs[0].shape[0]
    own, core = own_bit(stream.bits[-1]), lax.axis_index("tensor")
    half = own if mine else 1 - own

    def copies(chunk, index):
        at, end, found = chunk * rows, (chunk + 1) * rows, []
        while at < end:
            which, inside = divmod(at, width)
            size = min(end - at, width - inside)
            if which == len(outs):
                break
            found.append(
                pltpu.make_async_copy(
                    wide_ref.at[index, at - chunk * rows : at - chunk * rows + size, :],
                    outs[which].at[inside : inside + size, :],
                    sems.at[index, len(found)],
                )
            )
            at += size
        return found

    for act in ("start", "wait"):
        for which, rank in enumerate(stream.ranks[-1]):
            for chunk in range(2 * count):
                bit, low = (chunk >> rank) & 1, chunk & ((1 << rank) - 1)
                index = ((chunk >> (rank + 1)) << rank) + low

                @pl.when((core == which) & (half == bit))
                def _():
                    for copy in copies(chunk, index):
                        getattr(copy, act)()


def pack_kernel(stream, own_ref, got_ref, out_ref, all_ref):
    stream.join(all_ref, own_ref, got_ref)
    rows = all_ref.shape[1]
    for chunk in range(all_ref.shape[0]):
        out_ref[chunk * rows : (chunk + 1) * rows, :] = all_ref[chunk]


def unpack_kernel(
    half_rows, pack_ref, pack_got_ref,
    gain_ref, ffn_gain_ref, dwq_ref, dwk_ref, dwv_ref, dwo_ref, all_ref,
):
    width, kv_width = dwq_ref.shape[0], dwk_ref.shape[0]
    core = lax.axis_index("tensor")
    for which, ref in ((core, pack_ref), (1 - core, pack_got_ref)):
        all_ref[which] = ref[:half_rows, :width].astype(F32)
    rest = half_rows - width
    dwq_ref[...] = all_ref[0, :width]
    dwo_ref[:rest, :] = all_ref[0, width:]
    dwo_ref[rest:, :] = all_ref[1, : width - rest]
    dwk_ref[...] = all_ref[1, width - rest : width - rest + kv_width]
    dwv_ref[...] = all_ref[1, width - rest + kv_width :]
    rows = pack_ref[:width, width:].astype(F32).T
    for at, ref in ((0, gain_ref), (1, ffn_gain_ref)):
        ref[...] = rows[at : at + 1, :].reshape(width)


def tie(*arrays):
    return lax.optimization_barrier(arrays)


def orders_of(n):
    bits = list(range(n.bit_length() - 1))
    across = bits[-1]
    halved = bits[:-1]
    if len(halved) < 3:
        return [((halved, halved), across, (halved, halved))] * 2
    rest = halved[3:]
    ffn = (([0, 2, 1] + rest, [1, 0, 2] + rest), across, (rest + [1, 2, 0], rest + [2, 0, 1]))
    attention = (([1, 0, 2] + rest,) * 2, across, (rest + [1, 0, 2],) * 2)
    return [ffn, attention]


def position_tables(length):
    places = np.arange(length, dtype=np.float32)
    inverse = np.float32(10000.0) ** (np.arange(HALF, dtype=np.float32) * np.float32(-2.0 / HEAD_DIM))
    angles = inverse.astype(np.float32)[:, None] * places[None, :]
    return jnp.asarray(np.cos(angles)), jnp.asarray(np.sin(angles))


def per_device(
    sizes, tokens, segments, cotangent, attn_gain, w_query, w_key, w_value, w_out, ffn_gain,
    w_gate, w_up, w_down,
):
    _, half, width = tokens.shape
    kv_width = KV_HEADS * HEAD_DIM
    hidden = w_gate.shape[1]
    n = sizes[0]
    core = lax.axis_index("tensor")
    cut = half // 2
    tokens, cotangent = tokens[0].T, cotangent[0].T
    w_key, w_value, w_down = w_key.T, w_value.T, w_down.T

    tokens_got = swap(tokens)
    all_tables = position_tables(segments.shape[1])
    where = (segments, segments)
    projections = (w_query, w_key, w_value)

    act = shape((width, half), F32)
    low = shape((width, half), BF16)
    kv = shape((2 * kv_width, half), BF16)
    kv_f32 = shape((2 * kv_width, half), F32)
    wide = shape((2 * hidden, half), BF16)
    thin = shape((hidden, half), BF16)
    column = shape((width, 1), F32)
    square = shape((width, width), F32)
    heads_f32 = pltpu.VMEM((HEADS, BLOCK, BLOCK), F32)
    heads_low = pltpu.VMEM((HEADS, BLOCK, BLOCK), BF16)
    key_scratch = pltpu.VMEM((2 * KV_HEADS, half, HEAD_DIM), BF16)
    masks_shape = shape((2, 2, BLOCK, BLOCK), F32)
    rows_f32 = shape((16, half), F32)
    act_scratch = pltpu.VMEM((width, half), F32)
    low_scratch = pltpu.VMEM((width, half), BF16)

    def attend(query, kv_own, kv_other, masks=None):
        state, made = (), []
        for own, kv_part in ((True, kv_own), (False, kv_other)):

            def kernel(*refs, own=own):
                attend_kernel(own, *refs)

            state, new = run(
                kernel,
                where + (query, kv_part, tuple(state), () if masks is None else (masks[len(made)],)),
                ((rows_f32, rows_f32, act) if own else (low, rows_f32),
                 (masks_shape,) if masks is None else ()),
                [pltpu.VMEM((2, KV_HEADS, HEAD_DIM + 16, BLOCK), BF16),
                 pltpu.VMEM((4 * BLOCK, 8), jnp.int32), heads_f32],
                smem=1,
                name="attend_own" if own else "attend_other",
                us=4,
            )
            made.append(new[0] if masks is None else masks[len(made)])
        return (*state, made)

    def attend_back(query, kv_own, kv_other, masks, ctx, lse, grad, us=5):
        more = (ctx,)
        for own, kv_part, dkv in ((False, kv_other, kv), (True, kv_own, kv_f32)):

            def kernel(*refs, own=own):
                attend_back_kernel(own, *refs)

            (outs,) = run(
                kernel,
                (segments, query, kv_part, masks[0 if own else 1], lse, grad, more),
                ((act, dkv),) if own else ((act, rows_f32, dkv),),
                [key_scratch, heads_f32, heads_low, heads_low,
                 pltpu.VMEM((2, 2 * kv_width, BLOCK), F32)],
                smem=1,
                name="attend_back_own" if own else "attend_back_other",
                us=us,
            )
            if not own:
                more = outs[:2]
                got = swap(outs[2])
        return outs[0], outs[1], got

    table = shape((HALF, half), F32)
    tile_low, tile_kv = shape((width, cut), BF16), shape((2 * kv_width, cut), BF16)
    x_half = pltpu.VMEM((width, cut), F32)
    *halves, gain_col, ffn_gain_col, cos_table, sin_table, wq, wk, wv = run(
        first_kernel,
        in_hbm((tokens,) + projections + all_tables + (attn_gain, ffn_gain)),
        (tile_low, tile_low, tile_low, tile_kv, column, column, table, table)
        + tuple(shape(weight.shape, BF16) for weight in projections),
        [x_half, pltpu.VMEM((width,), F32), pltpu.VMEM((width,), F32),
         pltpu.SemaphoreType.DMA((10,))],
        hbm=8,
        name="first",
        us=2,
    )
    projections, tables = (wq, wk, wv), (cos_table, sin_table)
    (x1, normed1, query1, kv1), = run(
        second_kernel,
        (tokens_got, tuple(halves), gain_col) + tables + projections,
        ((low, low, low, kv),),
        [x_half],
        name="second",
        us=1,
    )
    kv1, cot_sent = tie(kv1, cotangent)
    kv1_other = swap(kv1)
    gate_pair = (w_gate, swap(w_gate))
    up_pair = (w_up, swap(w_up))
    down_pair = (w_down, swap(w_down))
    cot_got = swap(cot_sent)
    ctx1, lse1, masks = attend(query1, kv1, kv1_other)
    mid1, ffn1, gate1, up1, x2, normed2, query2, kv2 = run(
        middle_kernel,
        (x1, ctx1, w_out, ffn_gain_col, gate_pair, up_pair, down_pair, gain_col)
        + projections + tables,
        (act, low, wide, wide, act, low, low, kv),
        [pltpu.VMEM(wide.shape, BF16)],
        name="middle",
        us=6,
    )
    kv2_other = swap(kv2)
    ctx2, lse2, _ = attend(query2, kv2, kv2_other, masks)
    (
        mid2, cot, ffn2, kept2_own, kept2_other, grad_mid2, grad_mid_low2, grad_ctx2, dffn_gain2,
    ) = run(
        turn_kernel,
        (x2, ctx2, w_out, ffn_gain_col, gate_pair, up_pair, down_pair, cotangent, cot_got),
        (act, low, low, (thin,) * 3, (thin,) * 3, act, low, low, column),
        [act_scratch],
        name="turn",
        us=9,
    )
    dq2, dkv_own2, dkv_got2 = attend_back(query2, kv2, kv2_other, masks, ctx2, lse2, grad_ctx2)
    pad = 8 * max(n // 2, 1)
    stack_rows = -(-3 * width // pad) * pad
    stack_shape = shape((stack_rows, hidden), BF16)
    pre = shape((width + 2 * kv_width, half), BF16)
    dpre2, dgain2, low1, gstream, dffn, stack_other = run(
        other_kernel,
        (dq2, dkv_own2, dkv_got2, x2, grad_mid2, gain_col) + projections + tables
        + (ffn1, gate1, up1, gate_pair[1], up_pair[1], down_pair[1], ffn2, cot, kept2_other),
        (pre, column, low, act, act, stack_shape),
        [act_scratch, pltpu.VMEM((3,) + thin.shape, BF16)],
        name="other",
        us=8,
    )
    stack_got = swap(stack_other)
    stack_own, grad_mid1, grad_mid_low1, grad_ctx1, dffn_gain = run(
        own_kernel,
        (low1, gstream, dffn, ffn1, gate1, up1, gate_pair[0], up_pair[0], down_pair[0],
         ffn2, cot, kept2_own, mid1, w_out, ffn_gain_col, dffn_gain2),
        (stack_shape, act, low, low, column),
        [act_scratch, pltpu.VMEM((3,) + thin.shape, BF16)],
        name="own",
        us=7,
    )
    ffn_orders, pack_orders = orders_of(n)
    ffn = Stream("ffn", (stack_own, stack_got), sizes, ffn_orders)
    token = ffn.step(stack_own)
    grad_ctx1, token = tie(grad_ctx1, token)
    dq1, dkv_own1, dkv_got1 = attend_back(query1, kv1, kv1_other, masks, ctx1, lse1, grad_ctx1, 0)
    rows = -(-(2 * width + 2 * kv_width) // 2 // pad) * pad
    lanes = -(-width // 128) * 128
    lanes = lanes if lanes - width >= 2 else lanes + 128
    half_stack = shape((rows, lanes), BF16)
    tile_act = shape((width, cut), F32)
    dnormed1, pack_own, pack_other = run(
        last_kernel,
        (dq1, dkv_own1, dkv_got1, x1) + projections + tables
        + (dpre2, (normed1, normed2), (ctx1, ctx2), (grad_mid_low1, grad_mid_low2),
           dgain2, dffn_gain),
        (act, half_stack, half_stack),
        [pltpu.VMEM(pre.shape, BF16), act_scratch,
         pltpu.VMEM((width, 1), F32), pltpu.VMEM((2, rows, lanes), BF16)],
        name="last",
        us=0,
    )
    pack = Stream("pack", (pack_own, swap(pack_other)), sizes, pack_orders)
    token = pack_own
    for index, which in enumerate("fafafaafafafa"):
        token = (ffn if which == "f" else pack).step(token)
        if index == 1:
            ((output, output_sent),) = run(
                result_kernel,
                (mid2, (kept2_own[0], kept2_other[0]), down_pair),
                ((tile_low, tile_low),), after=token, name="result", us=0,
            )
            token = (token, output)
        if index == 3:
            ((grad_input, grad_input_sent),) = run(
                input_kernel,
                (x1, gain_col, dnormed1, grad_mid1), ((tile_act, tile_act),),
                [act_scratch, act_scratch, pltpu.VMEM((width, 1), F32)],
                after=token, name="input", us=0,
            )
            token = (token, grad_input)
        if index == 7:
            output = jnp.concatenate([output, swap(output_sent)], axis=1)
            grad_input = jnp.concatenate([grad_input, swap(grad_input_sent)], axis=1)
            token = (token, output, grad_input)
    while not (ffn.done and pack.done):
        token = pack.step(ffn.step(token))

    def finish(mine, part, after, update, us):
        def kernel(part_ref, *refs):
            finish_kernel(ffn, mine, part_ref, refs[:3], *refs[3:])

        count, rows, columns = part.shape
        *outs, token = run(
            kernel, (part,), (shape((width, hidden), F32),) * 3 + (shape((8, 128), F32),),
            [pltpu.VMEM(part.shape, F32), pltpu.SemaphoreType.DMA((count, rows // width + 2))],
            after=after, name="finish", us=us, hbm_outs=3, update=update,
        )
        return outs, token

    finished, token = finish(True, ffn.terms[0], token, (), 0)

    def kernel(own_ref, got_ref, out_ref, all_ref):
        pack_kernel(pack, own_ref, got_ref, out_ref, all_ref)

    (pack_sum,) = run(
        kernel, tuple(pack.terms), (half_stack,),
        [pltpu.VMEM((pack.chunks, rows // pack.chunks, lanes), BF16)],
        after=token, name="pack_all", us=0,
    )
    (dw_gate, dw_up, dw_down), token = finish(False, ffn.terms[1], pack_sum, finished, 3)
    half_rows = width + kv_width

    def kernel(*refs):
        unpack_kernel(half_rows, *refs)

    kv_square = shape((kv_width, width), F32)
    vector = shape((width,), F32)
    dgain, dffn_gain, dw_query, dw_key, dw_value, dw_out = run(
        kernel,
        (pack_sum, swap(pack_sum)),
        (vector, vector, square, kv_square, kv_square, square),
        [pltpu.VMEM((2, half_rows, width), F32)],
        after=token,
        name="unpack",
        us=2,
    )
    return (
        output.T[None],
        grad_input.T[None],
        dgain,
        dw_query,
        dw_key.T,
        dw_value.T,
        dw_out,
        dffn_gain,
        dw_gate,
        dw_up,
        dw_down.T,
    )


def solution(mesh):
    sizes = (mesh.shape["dp"], mesh.shape["tensor"])

    def local(*args):
        return per_device(sizes, *args)

    split = P("dp", "tensor", None)
    in_specs = (
        split, P("dp", None), split, P(), P(), P(), P(), P(), P(),
        P(None, "tensor"), P(None, "tensor"), P("tensor", None),
    )
    out_specs = (
        split, split, P(), P(), P(), P(), P(), P(),
        P(None, "tensor"), P(None, "tensor"), P("tensor", None),
    )
    return jax.shard_map(
        local, mesh=mesh, in_specs=in_specs, out_specs=out_specs, check_vma=False
    )
```

```python
import jax
import jax.numpy as jnp
import numpy as np
from jax import lax
from jax.experimental import pallas as pl
from jax.experimental.pallas import tpu as pltpu
from jax.sharding import PartitionSpec as P

HEADS = 9
KV_HEADS = 3
GROUP = HEADS // KV_HEADS
HEAD_DIM = 64
HALF = HEAD_DIM // 2
EPSILON = 1e-05
MASKED = -1e30
BLOCK = 256
SCALE = HEAD_DIM ** (-0.5)
F32 = jnp.float32
BF16 = jnp.bfloat16
VMEM_LIMIT = 16 * 2**20


def dot(left, right, left_dim, right_dim):
    return lax.dot_general(
        left, right, (((left_dim,), (right_dim,)), ((), ())), preferred_element_type=F32
    )


def pieces(size, step):
    return [slice(start, start + step) for start in range(0, size, step)]


def inverse_rms(x_ref):
    total = None
    for rows in pieces(x_ref.shape[0], 64):
        x = x_ref[rows, :]
        part = jnp.sum(x * x, axis=0, keepdims=True)
        total = part if total is None else total + part
    return lax.rsqrt(total / x_ref.shape[0] + EPSILON)


def norm_forward(x_ref, gain_ref, out_ref):
    scale = inverse_rms(x_ref)
    for rows in pieces(x_ref.shape[0], 64):
        out_ref[rows, :] = (x_ref[rows, :] * scale * gain_ref[rows, :]).astype(BF16)


def norm_backward(x_ref, gain_ref, grad_ref, add_ref, out_ref, gain_grad_ref):
    scale = inverse_rms(x_ref)
    inner = None
    for rows in pieces(x_ref.shape[0], 64):
        x, e = x_ref[rows, :], grad_ref[rows, :]
        xe = x * e
        gain_grad_ref[rows, :] = jnp.sum(xe * scale, axis=1, keepdims=True)
        part = jnp.sum(xe * gain_ref[rows, :], axis=0, keepdims=True)
        inner = part if inner is None else inner + part
    cubed = scale * scale * scale * (inner / x_ref.shape[0])
    for rows in pieces(x_ref.shape[0], 64):
        out_ref[rows, :] = (
            add_ref[rows, :].astype(F32)
            + scale * gain_ref[rows, :] * grad_ref[rows, :]
            - x_ref[rows, :] * cubed
        )


def gain_backward(x_ref, grad_ref, gain_grad_ref):
    scale = inverse_rms(x_ref)
    for rows in pieces(x_ref.shape[0], 64):
        gain_grad_ref[rows, :] = jnp.sum(
            x_ref[rows, :] * grad_ref[rows, :] * scale, axis=1, keepdims=True
        )


def rotated(x, cos_table, sin_table):
    front, back = x[:HALF], x[HALF:]
    return jnp.concatenate(
        [front * cos_table - back * sin_table, back * cos_table + front * sin_table], axis=0
    )


def project_qkv(normed_ref, wq_ref, wk_ref, wv_ref, cos_ref, sin_ref, q_ref, kv_ref):
    normed = normed_ref[...]
    cos_table, sin_table = cos_ref[...], sin_ref[...]
    key = dot(wk_ref[...], normed, 1, 0)
    for head in pieces(KV_HEADS * HEAD_DIM, HEAD_DIM):
        kv_ref[head, :] = rotated(key[head], cos_table, sin_table).astype(BF16)
    kv_ref[KV_HEADS * HEAD_DIM :, :] = dot(wv_ref[...], normed, 1, 0).astype(BF16)
    query = dot(wq_ref[...], normed, 0, 0)
    for head in pieces(HEADS * HEAD_DIM, HEAD_DIM):
        q_ref[head, :] = (rotated(query[head], cos_table, sin_table) * SCALE).astype(BF16)


def first_kernel(
    tokens_hbm, wq_hbm, wk_hbm, wv_hbm, cos_hbm, sin_hbm, gain_hbm, ffn_gain_hbm,
    low_ref, normed_ref, q_ref, kv_ref, gain_ref, ffn_gain_ref, cos_ref, sin_ref,
    wq_ref, wk_ref, wv_ref,
    x_ref, gain_in_ref, ffn_gain_in_ref, sems,
):
    cut = low_ref.shape[1]
    pairs = [
        (gain_hbm, gain_in_ref), (ffn_gain_hbm, ffn_gain_in_ref),
        (tokens_hbm.at[:, :cut], low_ref), (wk_hbm, wk_ref), (wv_hbm, wv_ref), (wq_hbm, wq_ref),
    ]
    for local, tile in enumerate(tile_places(lax.axis_index("tensor"))):
        cols = slice(local * cut, (local + 1) * cut)
        for source, target in ((cos_hbm, cos_ref), (sin_hbm, sin_ref)):
            pairs.append((source.at[:, tile_lanes(tile)], target.at[:, cols]))
    copies = [
        pltpu.make_async_copy(source, target, sems.at[index])
        for index, (source, target) in enumerate(pairs)
    ]
    for copy in copies:
        copy.start()
    copies[0].wait()
    copies[1].wait()
    for in_ref, column_ref in ((gain_in_ref, gain_ref), (ffn_gain_in_ref, ffn_gain_ref)):
        row = in_ref[...].reshape(1, -1)
        column_ref[...] = jnp.broadcast_to(row, (128, row.shape[1])).T[:, :1]
    copies[2].wait()
    x_ref[...] = low_ref[...].astype(F32)
    norm_forward(x_ref, gain_ref, normed_ref)
    for copy in copies[3:]:
        copy.wait()
    tables = (cos_ref.at[:, :cut], sin_ref.at[:, :cut])
    project_qkv(normed_ref, wq_ref, wk_ref, wv_ref, *tables, q_ref, kv_ref)


def second_kernel(
    got_ref, half_refs, gain_ref, cos_ref, sin_ref, wq_ref, wk_ref, wv_ref, full_refs, x_ref
):
    cut = x_ref.shape[1]
    for half_ref, full_ref in zip(half_refs, full_refs):
        full_ref[:, :cut] = half_ref[...]
    low_ref, normed_ref, q_ref, kv_ref = (ref.at[:, cut:] for ref in full_refs)
    low_ref[...] = got_ref[:, cut:]
    x_ref[...] = low_ref[...].astype(F32)
    norm_forward(x_ref, gain_ref, normed_ref)
    tables = (cos_ref.at[:, cut:], sin_ref.at[:, cut:])
    project_qkv(normed_ref, wq_ref, wk_ref, wv_ref, *tables, q_ref, kv_ref)


def tile_places(core):
    return 2 * core, 3 - 2 * core


def tile_lanes(tile):
    return pl.ds(pl.multiple_of(tile * BLOCK, BLOCK), BLOCK)


def set_labels(labels_ref, column_ref):
    column_ref[...] = jnp.broadcast_to(labels_ref[0:1, :], (8, labels_ref.shape[1])).T


def set_mask(bias_ref, labels_ref, column_ref, tile, kb):
    key_labels = column_ref[tile_lanes(kb), :1]
    key_place = kb * BLOCK + lax.broadcasted_iota(jnp.int32, (BLOCK, BLOCK), 0)
    place = tile * BLOCK + lax.broadcasted_iota(jnp.int32, (1, BLOCK), 1)
    allowed = (key_labels == labels_ref[0:1, tile_lanes(tile)]) & (key_place <= place)
    bias_ref[...] = jnp.where(allowed, 0.0, MASKED)


def first_block(segments_ref, tile):
    label = segments_ref[0, tile * BLOCK]
    count = jnp.int32(0)
    for kb in range(3):
        before = (kb < tile) & (segments_ref[0, kb * BLOCK + BLOCK - 1] < label)
        count = count + before.astype(jnp.int32)
    return count


def head_rows(head):
    return slice(head * HEAD_DIM, (head + 1) * HEAD_DIM)


def load_part(kv_ref, tok_ref):
    for head in range(2 * KV_HEADS):
        for cols in pieces(kv_ref.shape[1], BLOCK):
            tok_ref[head, cols, :] = kv_ref[head_rows(head), cols].T


def over_blocks(segments_ref, core, own, body):
    keys_of = tile_places(core if own else 1 - core)
    for local, tile in enumerate(tile_places(core)):
        cols = slice(local * BLOCK, (local + 1) * BLOCK)
        first = first_block(segments_ref, tile)

        def step(at, carry):
            kb = jnp.where(at == 0, keys_of[0], keys_of[1])

            @pl.when((kb >= first) & (kb <= tile))
            def _():
                body(local, tile, cols, kb, at)

            return carry

        lax.fori_loop(0, 2, step, 0)


def attend_kernel(
    own, segments_ref, labels_ref, q_ref, kv_ref, state_refs, mask_in_refs, out_refs, mask_out_refs,
    value_ref, column_ref, scores_ref,
):
    core = lax.axis_index("tensor")
    if mask_out_refs:
        set_labels(labels_ref, column_ref)
    (masks_ref,) = mask_in_refs or mask_out_refs
    for at, cols in enumerate(pieces(kv_ref.shape[1], BLOCK)):
        for group in range(KV_HEADS):
            value_ref[at, group, :HEAD_DIM, :] = kv_ref[head_rows(KV_HEADS + group), cols]
            value_ref[at, group, HEAD_DIM:, :] = jnp.ones((16, BLOCK), BF16)
    m_ref, l_ref, acc_ref = out_refs if own else state_refs
    if own:
        m_ref[...] = jnp.full(m_ref.shape, MASKED, F32)
        l_ref[...] = jnp.zeros(l_ref.shape, F32)
        acc_ref[...] = jnp.zeros(acc_ref.shape, F32)

    def body(local, tile, cols, kb, at):
        bias_ref = masks_ref.at[local, at]
        if mask_out_refs:
            set_mask(bias_ref, labels_ref, column_ref, tile, kb)
        keys = tile_lanes(at)

        def scores(group):
            key = kv_ref[head_rows(group), keys]
            for head in range(group * GROUP, (group + 1) * GROUP):
                scores_ref[head] = dot(key, q_ref[head_rows(head), cols], 0, 0) + bias_ref[...]

        def products(group):
            for head in range(group * GROUP, (group + 1) * GROUP):
                rows = head_rows(head)
                m_old = m_ref[head : head + 1, cols]
                m_new = jnp.maximum(m_old, jnp.max(scores_ref[head], axis=0, keepdims=True))
                m_ref[head : head + 1, cols] = m_new
                fade = jnp.exp(m_old - m_new)
                probs = jnp.exp(scores_ref[head] - m_new).astype(BF16)
                product = dot(value_ref[at, group], probs, 1, 0)
                l_ref[head : head + 1, cols] = (
                    l_ref[head : head + 1, cols] * fade + product[HEAD_DIM : HEAD_DIM + 1]
                )
                acc_ref[rows, cols] = acc_ref[rows, cols] * fade + product[:HEAD_DIM]

        scores(0)
        scores(1)
        products(0)
        scores(2)
        products(1)
        products(2)

    over_blocks(segments_ref, core, own, body)
    if not own:
        ctx_ref, lse_ref = out_refs
        for head in range(HEADS):
            total = l_ref[head : head + 1, :]
            ctx_ref[head_rows(head), :] = (acc_ref[head_rows(head), :] * (1.0 / total)).astype(BF16)
            lse_ref[head : head + 1, :] = m_ref[head : head + 1, :] + jnp.log(total)


def attend_back_kernel(
    own, segments_ref, q_ref, kv_ref, masks_ref, lse_ref, grad_ref, more_refs, out_refs,
    tok_ref, probs_ref, probs_low_ref, gs_ref, dkv_ref,
):
    core = lax.axis_index("tensor")
    load_part(kv_ref, tok_ref)
    if own:
        dq_in_ref, delta_ref = more_refs
        dq_ref, dkv_out_ref = out_refs
        dq_ref[...] = dq_in_ref[...]
    else:
        (ctx_ref,) = more_refs
        dq_ref, delta_ref, dkv_out_ref = out_refs
        dq_ref[...] = jnp.zeros(dq_ref.shape, F32)
        for head in range(HEADS):
            rows = head_rows(head)
            delta_ref[head : head + 1, :] = jnp.sum(
                grad_ref[rows, :].astype(F32) * ctx_ref[rows, :].astype(F32), axis=0, keepdims=True
            )
    dkv_ref[...] = jnp.zeros(dkv_ref.shape, F32)

    def body(local, tile, cols, kb, at):
        bias_ref = masks_ref.at[local, at]
        keys = tile_lanes(at)
        for head in range(HEADS):
            key = tok_ref[head // GROUP, keys, :]
            scores = dot(key, q_ref[head_rows(head), cols], 1, 0) + bias_ref[...]
            probs = jnp.exp(scores - lse_ref[head : head + 1, cols])
            probs_ref[head] = probs
            probs_low_ref[head] = probs.astype(BF16)
        for head in range(HEADS):
            value = tok_ref[KV_HEADS + head // GROUP, keys, :]
            grad_probs = dot(value, grad_ref[head_rows(head), cols], 1, 0)
            gs_ref[head] = (
                probs_ref[head] * (grad_probs - delta_ref[head : head + 1, cols])
            ).astype(BF16)
        for group in range(KV_HEADS):
            dv = dkv_ref[at, head_rows(KV_HEADS + group), :]
            for head in range(group * GROUP, (group + 1) * GROUP):
                dv = dv + dot(grad_ref[head_rows(head), cols], probs_low_ref[head], 1, 1)
            dkv_ref[at, head_rows(KV_HEADS + group), :] = dv
        for group in range(KV_HEADS):
            dk = dkv_ref[at, head_rows(group), :]
            for head in range(group * GROUP, (group + 1) * GROUP):
                dk = dk + dot(q_ref[head_rows(head), cols], gs_ref[head], 1, 1)
            dkv_ref[at, head_rows(group), :] = dk
        for head in range(HEADS):
            key_cols = kv_ref[head_rows(head // GROUP), keys]
            dq_ref[head_rows(head), cols] += dot(key_cols, gs_ref[head], 1, 0)

    over_blocks(segments_ref, core, own, body)
    for at, cols in enumerate(pieces(dkv_out_ref.shape[1], BLOCK)):
        dkv_out_ref[:, cols] = dkv_ref[at].astype(dkv_out_ref.dtype)


def middle_kernel(
    low_ref, ctx_ref, wo_ref, ffn_gain_ref, wg_refs, wu_refs, wd_refs,
    gain_ref, wq_ref, wk_ref, wv_ref, cos_ref, sin_ref,
    mid_ref, ffn_ref, gate_ref, up_ref, x2_ref, normed_ref, q_ref, kv_ref, product_ref,
):
    mid_ref[...] = low_ref[...].astype(F32) + dot(wo_ref[...], ctx_ref[...], 0, 0)
    norm_forward(mid_ref, ffn_gain_ref, ffn_ref)
    ffn_in = ffn_ref[...]
    half_hidden = wg_refs[0].shape[1]
    for part in range(2):
        for hidden in pieces(half_hidden, BLOCK):
            gate = dot(wg_refs[part][:, hidden], ffn_in, 0, 0)
            up = dot(wu_refs[part][:, hidden], ffn_in, 0, 0)
            rows = slice(part * half_hidden + hidden.start, part * half_hidden + hidden.stop)
            gate_ref[rows, :] = gate.astype(BF16)
            up_ref[rows, :] = up.astype(BF16)
            product_ref[rows, :] = (gate * jax.nn.sigmoid(gate) * up).astype(BF16)
    x2_ref[...] = (
        mid_ref[...]
        + dot(wd_refs[0][...], product_ref[:half_hidden, :], 1, 0)
        + dot(wd_refs[1][...], product_ref[half_hidden:, :], 1, 0)
    )
    norm_forward(x2_ref, gain_ref, normed_ref)
    project_qkv(normed_ref, wq_ref, wk_ref, wv_ref, cos_ref, sin_ref, q_ref, kv_ref)


def ffn_terms(gate, up, grad_product):
    sig = jax.nn.sigmoid(gate)
    silu = gate * sig
    grad_gate = (grad_product * up * (sig + silu * (1.0 - sig))).astype(BF16)
    grad_up = (grad_product * silu).astype(BF16)
    return (silu * up).astype(BF16), grad_gate, grad_up


def turn_kernel(
    x_ref, ctx_ref, wo_ref, ffn_gain_ref, wg_refs, wu_refs, wd_refs, cotangent_ref, cot_got_ref,
    mid_ref, cot_ref, ffn_ref, kept_own_refs, kept_other_refs,
    grad_mid_ref, grad_mid_low_ref, grad_ctx_ref, dgain_ref,
    acc_ref,
):
    mid_ref[...] = x_ref[...] + dot(wo_ref[...], ctx_ref[...], 0, 0)
    norm_forward(mid_ref, ffn_gain_ref, ffn_ref)
    ffn_in = ffn_ref[...]
    cut = cot_got_ref.shape[1] // 2
    cot_ref[:, :cut] = cotangent_ref[:, :cut]
    cot_ref[:, cut:] = cot_got_ref[:, cut:]
    grad_low = cot_ref[...]
    for part in range(2):
        for hidden in pieces(wg_refs[part].shape[1], BLOCK):
            gate = dot(wg_refs[part][:, hidden], ffn_in, 0, 0)
            up = dot(wu_refs[part][:, hidden], ffn_in, 0, 0)
            grad_product = dot(wd_refs[part][:, hidden], grad_low, 0, 0)
            kept = (kept_own_refs, kept_other_refs)[part]
            for ref, term in zip(kept, ffn_terms(gate, up, grad_product)):
                ref[hidden, :] = term
    acc_ref[...] = (
        dot(wg_refs[0][...], kept_own_refs[1][...], 1, 0)
        + dot(wu_refs[0][...], kept_own_refs[2][...], 1, 0)
        + dot(wg_refs[1][...], kept_other_refs[1][...], 1, 0)
        + dot(wu_refs[1][...], kept_other_refs[2][...], 1, 0)
    )
    norm_backward(mid_ref, ffn_gain_ref, acc_ref, cot_ref, grad_mid_ref, dgain_ref)
    grad_mid_low_ref[...] = grad_mid_ref[...].astype(BF16)
    grad_ctx_ref[...] = dot(wo_ref[...], grad_mid_low_ref[...], 1, 0).astype(BF16)


def result_kernel(mid_ref, product_refs, wd_refs, out_refs):
    result = (
        mid_ref[...]
        + dot(wd_refs[0][...], product_refs[0][...], 1, 0)
        + dot(wd_refs[1][...], product_refs[1][...], 1, 0)
    )
    cut = out_refs[0].shape[1]
    out_refs[0][...] = result[:, :cut].astype(BF16)
    out_refs[1][...] = result[:, cut:].astype(BF16)


def input_kernel(
    x_low_ref, gain_ref, dnormed_ref, grad_mid_ref, out_refs, x_ref, out_ref, dgain_ref
):
    x_ref[...] = x_low_ref[...].astype(F32)
    norm_backward(x_ref, gain_ref, dnormed_ref, grad_mid_ref, out_ref, dgain_ref)
    cut = out_refs[0].shape[1]
    out_refs[0][...] = out_ref[:, :cut]
    out_refs[1][...] = out_ref[:, cut:]


def qkv_back(
    dq_ref, dkv_own_ref, dkv_got_ref, wq_ref, wk_ref, wv_ref, cos_ref, sin_ref, dpre_ref, dnormed_ref
):
    cos_table, sin_table = cos_ref[...], sin_ref[...]
    width, kv_width = HEADS * HEAD_DIM, KV_HEADS * HEAD_DIM
    for head in pieces(width, HEAD_DIM):
        dpre_ref[head, :] = rotated(dq_ref[head, :] * SCALE, cos_table, -sin_table).astype(BF16)
    for head in pieces(kv_width, HEAD_DIM):
        total = dkv_own_ref[head, :] + dkv_got_ref[head, :].astype(F32)
        rows = slice(width + head.start, width + head.stop)
        dpre_ref[rows, :] = rotated(total, cos_table, -sin_table).astype(BF16)
    dpre_ref[width + kv_width :, :] = (
        dkv_own_ref[kv_width:, :] + dkv_got_ref[kv_width:, :].astype(F32)
    ).astype(BF16)
    dnormed_ref[...] = (
        dot(wq_ref[...], dpre_ref[:width, :], 1, 0)
        + dot(wk_ref[...], dpre_ref[width : width + kv_width, :], 0, 0)
        + dot(wv_ref[...], dpre_ref[width + kv_width :, :], 0, 0)
    )


def fill_stack(stack, width):
    if stack.shape[0] > 3 * width:
        stack[3 * width :, :] = jnp.zeros((stack.shape[0] - 3 * width, stack.shape[1]), BF16)


def ffn_back(
    part, stack, low, ffn1, ffn2, low2, gate_ref, up_ref, wg_ref, wu_ref, wd_ref, kept2_refs,
    acc_ref, terms_ref,
):
    width, half_hidden = wg_ref.shape
    for hidden in pieces(half_hidden, BLOCK):
        rows = slice(part * half_hidden + hidden.start, part * half_hidden + hidden.stop)
        grad_product = dot(wd_ref[:, hidden], low, 0, 0)
        terms = ffn_terms(gate_ref[rows, :].astype(F32), up_ref[rows, :].astype(F32), grad_product)
        for at, term in enumerate(terms):
            terms_ref[at, hidden, :] = term
    acc_ref[...] += dot(wg_ref[...], terms_ref[1], 1, 0) + dot(wu_ref[...], terms_ref[2], 1, 0)
    for at, (left1, left2, which) in enumerate(((ffn1, ffn2, 1), (ffn1, ffn2, 2), (low, low2, 0))):
        stack[at * width : (at + 1) * width, :] = (
            dot(left1, terms_ref[which], 1, 1) + dot(left2, kept2_refs[which][...], 1, 1)
        ).astype(BF16)
    fill_stack(stack, width)


def other_kernel(
    dq_ref, dkv_own_ref, dkv_got_ref, x_ref, grad_mid_ref,
    gain_ref, wq_ref, wk_ref, wv_ref, cos_ref, sin_ref,
    ffn1_ref, gate_ref, up_ref, wg_ref, wu_ref, wd_ref, ffn2_ref, low2_ref, kept2_refs,
    dpre_ref, dgain_ref, low_ref, gstream_ref, acc_ref, stack, dnormed_ref, terms_ref,
):
    qkv_back(
        dq_ref, dkv_own_ref, dkv_got_ref, wq_ref, wk_ref, wv_ref, cos_ref, sin_ref,
        dpre_ref, dnormed_ref,
    )
    norm_backward(x_ref, gain_ref, dnormed_ref, grad_mid_ref, gstream_ref, dgain_ref)
    low_ref[...] = gstream_ref[...].astype(BF16)
    acc_ref[...] = jnp.zeros(acc_ref.shape, F32)
    ffn_back(
        1, stack, low_ref[...], ffn1_ref[...], ffn2_ref[...], low2_ref[...],
        gate_ref, up_ref, wg_ref, wu_ref, wd_ref, kept2_refs, acc_ref, terms_ref,
    )


def own_kernel(
    low_ref, gstream_ref, acc_in_ref,
    ffn1_ref, gate_ref, up_ref, wg_ref, wu_ref, wd_ref, ffn2_ref, low2_ref, kept2_refs,
    mid_ref, wo_ref, ffn_gain_ref, dffn_gain2_ref,
    stack, grad_mid_ref, grad_mid_low_ref, grad_ctx_ref, dffn_gain_ref, acc_ref, terms_ref,
):
    acc_ref[...] = acc_in_ref[...]
    ffn_back(
        0, stack, low_ref[...], ffn1_ref[...], ffn2_ref[...], low2_ref[...],
        gate_ref, up_ref, wg_ref, wu_ref, wd_ref, kept2_refs, acc_ref, terms_ref,
    )
    norm_backward(mid_ref, ffn_gain_ref, acc_ref, gstream_ref, grad_mid_ref, dffn_gain_ref)
    dffn_gain_ref[...] += dffn_gain2_ref[...]
    grad_mid_low_ref[...] = grad_mid_ref[...].astype(BF16)
    grad_ctx_ref[...] = dot(wo_ref[...], grad_mid_low_ref[...], 1, 0).astype(BF16)


def last_kernel(
    dq_ref, dkv_own_ref, dkv_got_ref, x_low_ref, wq_ref, wk_ref, wv_ref, cos_ref, sin_ref,
    dpre2_ref, normed_refs, ctx_refs, grad_mid_low_refs, dgain2_ref, dffn_gain_ref,
    dnormed_ref, stack_own_ref, stack_other_ref,
    dpre_ref, x_ref, dgain_ref, stack_ref,
):
    x_ref[...] = x_low_ref[...].astype(F32)
    width, rows = x_ref.shape[0], stack_ref.shape[1]
    qkv_back(
        dq_ref, dkv_own_ref, dkv_got_ref, wq_ref, wk_ref, wv_ref, cos_ref, sin_ref,
        dpre_ref, dnormed_ref,
    )
    gain_backward(x_ref, dnormed_ref, dgain_ref)
    normed1, normed2 = (ref[...] for ref in normed_refs)
    dwq = dot(normed1, dpre_ref[:width, :], 1, 1) + dot(normed2, dpre2_ref[:width, :], 1, 1)
    dwkv = dot(dpre_ref[width:, :], normed1, 1, 1) + dot(dpre2_ref[width:, :], normed2, 1, 1)
    dwo = dot(ctx_refs[0][...], grad_mid_low_refs[0][...], 1, 1) + dot(
        ctx_refs[1][...], grad_mid_low_refs[1][...], 1, 1
    )
    half_rows = width + dwkv.shape[0] // 2
    rest = half_rows - width
    stack_ref[0, :width, :width] = dwq.astype(BF16)
    stack_ref[0, width:half_rows, :width] = dwo[:rest].astype(BF16)
    stack_ref[1, : width - rest, :width] = dwo[rest:].astype(BF16)
    stack_ref[1, width - rest : half_rows, :width] = dwkv.astype(BF16)
    lanes = stack_ref.shape[2] - width
    column = lax.broadcasted_iota(jnp.int32, (width, lanes), 1)
    gains = jnp.where(
        column == 0,
        dgain_ref[...] + dgain2_ref[...],
        jnp.where(column == 1, dffn_gain_ref[...], 0.0),
    ).astype(BF16)
    for part in range(2):
        stack_ref[part, :width, width:] = gains
        stack_ref[part, width:, width:] = jnp.zeros((rows - width, lanes), BF16)
        if rows > half_rows:
            stack_ref[part, half_rows:, :width] = jnp.zeros((rows - half_rows, width), BF16)
    core = lax.axis_index("tensor")
    stack_own_ref[...] = stack_ref[core]
    stack_other_ref[...] = stack_ref[1 - core]


def shape(dims, dtype):
    return jax.ShapeDtypeStruct(dims, dtype)


def run(
    kernel, args, outs, scratch=(), smem=0, hbm=0, after=(), name=None, us=5, limit=VMEM_LIMIT,
    hbm_outs=0, update=(),
):
    leaves, tree = jax.tree.flatten(args)
    out_leaves, out_tree = jax.tree.flatten(outs)
    late = jax.tree.leaves(after) + list(update)
    n_in, n_out = len(leaves), len(out_leaves)

    def body(*refs):
        ins = jax.tree.unflatten(tree, refs[:n_in])
        refs = refs[n_in + len(late) :]
        results = jax.tree.unflatten(out_tree, refs[:n_out])
        kernel(*ins, *results, *refs[n_out:])

    in_specs = [
        pl.BlockSpec(
            memory_space=pltpu.SMEM if index < smem else pltpu.HBM if index < hbm else pltpu.VMEM
        )
        for index in range(n_in)
    ] + [pl.BlockSpec(memory_space=pl.ANY)] * len(late)
    results = pl.pallas_call(
        body,
        out_shape=out_leaves,
        in_specs=in_specs,
        out_specs=[pl.BlockSpec(memory_space=pltpu.HBM if index < hbm_outs else pltpu.VMEM)
            for index in range(n_out)
        ],
        scratch_shapes=list(scratch),
        input_output_aliases={
            n_in + len(late) - len(update) + index: index for index in range(len(update))
        },
        compiler_params=pltpu.CompilerParams(vmem_limit_bytes=limit),
        cost_estimate=pl.CostEstimate(
            flops=int(us * 1e9) + 1, bytes_accessed=2**20 if us else 1, transcendentals=0
        ),
        name=name,
    )(*leaves, *late)
    return jax.tree.unflatten(out_tree, results)


def in_hbm(arrays):
    return tuple(pltpu.with_memory_space_constraint(array, pltpu.HBM) for array in arrays)


def swap(array):
    return lax.ppermute(array, "tensor", [(0, 1), (1, 0)])


def partners(sizes, bits):
    n, cores = sizes
    return [
        (place * cores + core, (place ^ (1 << bits[core])) * cores + core)
        for place in range(n)
        for core in range(cores)
    ]


def by_core(pair):
    return jnp.where(lax.axis_index("tensor") == 0, jnp.int32(pair[0]), jnp.int32(pair[1]))


def own_bit(bits):
    place = lax.axis_index("dp").astype(jnp.int32)
    return lax.shift_right_logical(place, by_core(bits)) & 1


def insert(index, rank, bit):
    low = index & (lax.shift_left(jnp.int32(1), rank) - 1)
    return lax.shift_left(index - low, jnp.int32(1)) + lax.shift_left(bit, rank) + low


def scatter_kernel(bits, ranks, sent, terms, out_ref):
    own, rank = own_bit(bits), by_core(ranks)
    half = 1 - own if sent else own

    def body(index, carry):
        at = insert(index, rank, half)
        total = terms[0][at].astype(F32)
        for term in terms[1:]:
            total = total + term[at].astype(F32)
        out_ref[index] = total.astype(BF16)
        return carry

    lax.fori_loop(0, out_ref.shape[0], body, 0)


def add_kernel(one_ref, two_ref, out_ref):
    out_ref[...] = (one_ref[...].astype(F32) + two_ref[...].astype(F32)).astype(BF16)


def join(bits, ranks, own_ref, got_ref, out_ref):
    own, rank = own_bit(bits), by_core(ranks)

    def body(index, carry):
        out_ref[insert(index, rank, own)] = own_ref[index]
        out_ref[insert(index, rank, 1 - own)] = got_ref[index]
        return carry

    lax.fori_loop(0, own_ref.shape[0], body, 0)


def ranks_of(dims, done):
    ranks = []
    for step in range(len(dims[0])):
        pair = []
        for order in dims:
            there = order[step + 1 :] if done == "after" else order[:step]
            pair.append(sum(other < order[step] for other in there))
        ranks.append(tuple(pair))
    return ranks


class Stream:
    def __init__(self, name, terms, sizes, orders):
        scatter, across, gather = orders
        self.name, self.sizes = name, sizes
        self.halvings = len(scatter[0])
        self.chunks = 1 << self.halvings
        self.bits = list(zip(*scatter)) + [(across, across)] + list(zip(*gather))
        self.ranks = ranks_of(scatter, "after") + [None] + ranks_of(gather, "before")
        self.terms = [term.reshape((self.chunks, -1) + term.shape[1:]) for term in terms]
        self.rounds = 2 * self.halvings + 1
        self.round = 0

    def call(self, kernel, args, counts, after):
        rows, columns = self.terms[0].shape[1:]
        outs = tuple(shape((count, rows, columns), BF16) for count in counts)
        return run(kernel, args, outs, after=after, name=f"{self.name}_{self.round}", us=0)

    def load(self, after):
        if self.round < self.halvings:
            half = self.terms[0].shape[0] // 2
            bits, ranks = self.bits[self.round], self.ranks[self.round]

            terms = tuple(self.terms)

            def part(which, after):
                def kernel(terms, out_ref):
                    scatter_kernel(bits, ranks, which, terms, out_ref)

                return self.call(kernel, (terms,), (half,), after)[0]

            sent = part(True, after)
            self.terms = [part(False, sent)]
            return sent
        if self.round <= self.halvings + 1:
            (sent,) = self.call(add_kernel, tuple(self.terms), (1,), after)
        else:
            bits, ranks = self.bits[self.round - 1], self.ranks[self.round - 1]

            def kernel(*refs):
                join(bits, ranks, *refs)

            (sent,) = self.call(
                kernel, tuple(self.terms), (2 * self.terms[0].shape[0],), after
            )
        self.terms = [sent]
        return sent

    def step(self, token):
        if self.done:
            return token
        sent = self.load(token)
        got = lax.ppermute(sent, ("dp", "tensor"), partners(self.sizes, self.bits[self.round]))
        self.terms = self.terms + [got]
        self.round += 1
        return sent

    @property
    def done(self):
        return self.round == self.rounds

    def join(self, out_ref, own_ref, got_ref):
        join(self.bits[-1], self.ranks[-1], own_ref, got_ref, out_ref)


def finish_kernel(stream, mine, part_ref, outs, token_ref, wide_ref, sems):
    count, rows = part_ref.shape[:2]
    token_ref[...] = jnp.zeros(token_ref.shape, F32)
    for index in range(count):
        wide_ref[index] = part_ref[index].astype(F32)
    width = outs[0].shape[0]
    own, core = own_bit(stream.bits[-1]), lax.axis_index("tensor")
    half = own if mine else 1 - own

    def copies(chunk, index):
        at, end, found = chunk * rows, (chunk + 1) * rows, []
        while at < end:
            which, inside = divmod(at, width)
            size = min(end - at, width - inside)
            if which == len(outs):
                break
            found.append(
                pltpu.make_async_copy(
                    wide_ref.at[index, at - chunk * rows : at - chunk * rows + size, :],
                    outs[which].at[inside : inside + size, :],
                    sems.at[index, len(found)],
                )
            )
            at += size
        return found

    for act in ("start", "wait"):
        for which, rank in enumerate(stream.ranks[-1]):
            for chunk in range(2 * count):
                bit, low = (chunk >> rank) & 1, chunk & ((1 << rank) - 1)
                index = ((chunk >> (rank + 1)) << rank) + low

                @pl.when((core == which) & (half == bit))
                def _():
                    for copy in copies(chunk, index):
                        getattr(copy, act)()


def pack_kernel(stream, own_ref, got_ref, out_ref, all_ref):
    stream.join(all_ref, own_ref, got_ref)
    rows = all_ref.shape[1]
    for chunk in range(all_ref.shape[0]):
        out_ref[chunk * rows : (chunk + 1) * rows, :] = all_ref[chunk]


def unpack_kernel(
    half_rows, pack_ref, pack_got_ref,
    gain_ref, ffn_gain_ref, dwq_ref, dwk_ref, dwv_ref, dwo_ref, all_ref,
):
    width, kv_width = dwq_ref.shape[0], dwk_ref.shape[0]
    core = lax.axis_index("tensor")
    for which, ref in ((core, pack_ref), (1 - core, pack_got_ref)):
        all_ref[which] = ref[:half_rows, :width].astype(F32)
    rest = half_rows - width
    dwq_ref[...] = all_ref[0, :width]
    dwo_ref[:rest, :] = all_ref[0, width:]
    dwo_ref[rest:, :] = all_ref[1, : width - rest]
    dwk_ref[...] = all_ref[1, width - rest : width - rest + kv_width]
    dwv_ref[...] = all_ref[1, width - rest + kv_width :]
    rows = pack_ref[:width, width:].astype(F32).T
    for at, ref in ((0, gain_ref), (1, ffn_gain_ref)):
        ref[...] = rows[at : at + 1, :].reshape(width)


def tie(*arrays):
    return lax.optimization_barrier(arrays)


def orders_of(n):
    bits = list(range(n.bit_length() - 1))
    across = bits[-1]
    halved = bits[:-1]
    if len(halved) < 3:
        return [((halved, halved), across, (halved, halved))] * 2
    rest = halved[3:]
    ffn = (([0, 2, 1] + rest, [1, 0, 2] + rest), across, (rest + [1, 2, 0], rest + [2, 0, 1]))
    attention = (([1, 0, 2] + rest,) * 2, across, (rest + [1, 0, 2],) * 2)
    return [ffn, attention]


def position_tables(length):
    places = np.arange(length, dtype=np.float32)
    inverse = np.float32(10000.0) ** (np.arange(HALF, dtype=np.float32) * np.float32(-2.0 / HEAD_DIM))
    angles = inverse.astype(np.float32)[:, None] * places[None, :]
    return jnp.asarray(np.cos(angles)), jnp.asarray(np.sin(angles))


def per_device(
    sizes, tokens, segments, cotangent, attn_gain, w_query, w_key, w_value, w_out, ffn_gain,
    w_gate, w_up, w_down,
):
    _, half, width = tokens.shape
    kv_width = KV_HEADS * HEAD_DIM
    hidden = w_gate.shape[1]
    n = sizes[0]
    core = lax.axis_index("tensor")
    cut = half // 2
    tokens, cotangent = tokens[0].T, cotangent[0].T
    w_key, w_value, w_down = w_key.T, w_value.T, w_down.T

    tokens_got = swap(tokens)
    all_tables = position_tables(segments.shape[1])
    where = (segments, segments)
    projections = (w_query, w_key, w_value)

    act = shape((width, half), F32)
    low = shape((width, half), BF16)
    kv = shape((2 * kv_width, half), BF16)
    kv_f32 = shape((2 * kv_width, half), F32)
    wide = shape((2 * hidden, half), BF16)
    thin = shape((hidden, half), BF16)
    column = shape((width, 1), F32)
    square = shape((width, width), F32)
    heads_f32 = pltpu.VMEM((HEADS, BLOCK, BLOCK), F32)
    heads_low = pltpu.VMEM((HEADS, BLOCK, BLOCK), BF16)
    key_scratch = pltpu.VMEM((2 * KV_HEADS, half, HEAD_DIM), BF16)
    masks_shape = shape((2, 2, BLOCK, BLOCK), F32)
    rows_f32 = shape((16, half), F32)
    act_scratch = pltpu.VMEM((width, half), F32)
    low_scratch = pltpu.VMEM((width, half), BF16)

    def attend(query, kv_own, kv_other, masks=None):
        state, made = (), []
        for own, kv_part in ((True, kv_own), (False, kv_other)):

            def kernel(*refs, own=own):
                attend_kernel(own, *refs)

            state, new = run(
                kernel,
                where + (query, kv_part, tuple(state), () if masks is None else (masks[len(made)],)),
                ((rows_f32, rows_f32, act) if own else (low, rows_f32),
                 (masks_shape,) if masks is None else ()),
                [pltpu.VMEM((2, KV_HEADS, HEAD_DIM + 16, BLOCK), BF16),
                 pltpu.VMEM((4 * BLOCK, 8), jnp.int32), heads_f32],
                smem=1,
                name="attend_own" if own else "attend_other",
                us=4,
            )
            made.append(new[0] if masks is None else masks[len(made)])
        return (*state, made)

    def attend_back(query, kv_own, kv_other, masks, ctx, lse, grad, us=5):
        more = (ctx,)
        for own, kv_part, dkv in ((False, kv_other, kv), (True, kv_own, kv_f32)):

            def kernel(*refs, own=own):
                attend_back_kernel(own, *refs)

            (outs,) = run(
                kernel,
                (segments, query, kv_part, masks[0 if own else 1], lse, grad, more),
                ((act, dkv),) if own else ((act, rows_f32, dkv),),
                [key_scratch, heads_f32, heads_low, heads_low,
                 pltpu.VMEM((2, 2 * kv_width, BLOCK), F32)],
                smem=1,
                name="attend_back_own" if own else "attend_back_other",
                us=us,
            )
            if not own:
                more = outs[:2]
                got = swap(outs[2])
        return outs[0], outs[1], got

    table = shape((HALF, half), F32)
    tile_low, tile_kv = shape((width, cut), BF16), shape((2 * kv_width, cut), BF16)
    x_half = pltpu.VMEM((width, cut), F32)
    *halves, gain_col, ffn_gain_col, cos_table, sin_table, wq, wk, wv = run(
        first_kernel,
        in_hbm((tokens,) + projections + all_tables + (attn_gain, ffn_gain)),
        (tile_low, tile_low, tile_low, tile_kv, column, column, table, table)
        + tuple(shape(weight.shape, BF16) for weight in projections),
        [x_half, pltpu.VMEM((width,), F32), pltpu.VMEM((width,), F32),
         pltpu.SemaphoreType.DMA((10,))],
        hbm=8,
        name="first",
        us=2,
    )
    projections, tables = (wq, wk, wv), (cos_table, sin_table)
    (x1, normed1, query1, kv1), = run(
        second_kernel,
        (tokens_got, tuple(halves), gain_col) + tables + projections,
        ((low, low, low, kv),),
        [x_half],
        name="second",
        us=1,
    )
    kv1, cot_sent = tie(kv1, cotangent)
    kv1_other = swap(kv1)
    gate_pair = (w_gate, swap(w_gate))
    up_pair = (w_up, swap(w_up))
    down_pair = (w_down, swap(w_down))
    cot_got = swap(cot_sent)
    ctx1, lse1, masks = attend(query1, kv1, kv1_other)
    mid1, ffn1, gate1, up1, x2, normed2, query2, kv2 = run(
        middle_kernel,
        (x1, ctx1, w_out, ffn_gain_col, gate_pair, up_pair, down_pair, gain_col)
        + projections + tables,
        (act, low, wide, wide, act, low, low, kv),
        [pltpu.VMEM(wide.shape, BF16)],
        name="middle",
        us=6,
    )
    kv2_other = swap(kv2)
    ctx2, lse2, _ = attend(query2, kv2, kv2_other, masks)
    (
        mid2, cot, ffn2, kept2_own, kept2_other, grad_mid2, grad_mid_low2, grad_ctx2, dffn_gain2,
    ) = run(
        turn_kernel,
        (x2, ctx2, w_out, ffn_gain_col, gate_pair, up_pair, down_pair, cotangent, cot_got),
        (act, low, low, (thin,) * 3, (thin,) * 3, act, low, low, column),
        [act_scratch],
        name="turn",
        us=9,
    )
    dq2, dkv_own2, dkv_got2 = attend_back(query2, kv2, kv2_other, masks, ctx2, lse2, grad_ctx2)
    pad = 8 * max(n // 2, 1)
    stack_rows = -(-3 * width // pad) * pad
    stack_shape = shape((stack_rows, hidden), BF16)
    pre = shape((width + 2 * kv_width, half), BF16)
    dpre2, dgain2, low1, gstream, dffn, stack_other = run(
        other_kernel,
        (dq2, dkv_own2, dkv_got2, x2, grad_mid2, gain_col) + projections + tables
        + (ffn1, gate1, up1, gate_pair[1], up_pair[1], down_pair[1], ffn2, cot, kept2_other),
        (pre, column, low, act, act, stack_shape),
        [act_scratch, pltpu.VMEM((3,) + thin.shape, BF16)],
        name="other",
        us=8,
    )
    stack_got = swap(stack_other)
    stack_own, grad_mid1, grad_mid_low1, grad_ctx1, dffn_gain = run(
        own_kernel,
        (low1, gstream, dffn, ffn1, gate1, up1, gate_pair[0], up_pair[0], down_pair[0],
         ffn2, cot, kept2_own, mid1, w_out, ffn_gain_col, dffn_gain2),
        (stack_shape, act, low, low, column),
        [act_scratch, pltpu.VMEM((3,) + thin.shape, BF16)],
        name="own",
        us=7,
    )
    ffn_orders, pack_orders = orders_of(n)
    ffn = Stream("ffn", (stack_own, stack_got), sizes, ffn_orders)
    token = ffn.step(stack_own)
    grad_ctx1, token = tie(grad_ctx1, token)
    dq1, dkv_own1, dkv_got1 = attend_back(query1, kv1, kv1_other, masks, ctx1, lse1, grad_ctx1, 0)
    rows = -(-(2 * width + 2 * kv_width) // 2 // pad) * pad
    lanes = -(-width // 128) * 128
    lanes = lanes if lanes - width >= 2 else lanes + 128
    half_stack = shape((rows, lanes), BF16)
    tile_act = shape((width, cut), F32)
    dnormed1, pack_own, pack_other = run(
        last_kernel,
        (dq1, dkv_own1, dkv_got1, x1) + projections + tables
        + (dpre2, (normed1, normed2), (ctx1, ctx2), (grad_mid_low1, grad_mid_low2),
           dgain2, dffn_gain),
        (act, half_stack, half_stack),
        [pltpu.VMEM(pre.shape, BF16), act_scratch,
         pltpu.VMEM((width, 1), F32), pltpu.VMEM((2, rows, lanes), BF16)],
        name="last",
        us=0,
    )
    pack = Stream("pack", (pack_own, swap(pack_other)), sizes, pack_orders)
    token = pack_own
    for index, which in enumerate("fafafaafafafa"):
        token = (ffn if which == "f" else pack).step(token)
        if index == 1:
            ((output, output_sent),) = run(
                result_kernel,
                (mid2, (kept2_own[0], kept2_other[0]), down_pair),
                ((tile_low, tile_low),), after=token, name="result", us=0,
            )
            token = (token, output)
        if index == 3:
            ((grad_input, grad_input_sent),) = run(
                input_kernel,
                (x1, gain_col, dnormed1, grad_mid1), ((tile_act, tile_act),),
                [act_scratch, act_scratch, pltpu.VMEM((width, 1), F32)],
                after=token, name="input", us=0,
            )
            token = (token, grad_input)
        if index == 11:
            output = jnp.concatenate([output, swap(output_sent)], axis=1)
            grad_input = jnp.concatenate([grad_input, swap(grad_input_sent)], axis=1)
            token = (token, output, grad_input)
    while not (ffn.done and pack.done):
        token = pack.step(ffn.step(token))

    def finish(mine, part, after, update, us):
        def kernel(part_ref, *refs):
            finish_kernel(ffn, mine, part_ref, refs[:3], *refs[3:])

        count, rows, columns = part.shape
        *outs, token = run(
            kernel, (part,), (shape((width, hidden), F32),) * 3 + (shape((8, 128), F32),),
            [pltpu.VMEM(part.shape, F32), pltpu.SemaphoreType.DMA((count, rows // width + 2))],
            after=after, name="finish", us=us, hbm_outs=3, update=update,
        )
        return outs, token

    finished, token = finish(True, ffn.terms[0], token, (), 0)

    def kernel(own_ref, got_ref, out_ref, all_ref):
        pack_kernel(pack, own_ref, got_ref, out_ref, all_ref)

    (pack_sum,) = run(
        kernel, tuple(pack.terms), (half_stack,),
        [pltpu.VMEM((pack.chunks, rows // pack.chunks, lanes), BF16)],
        after=token, name="pack_all", us=0,
    )
    (dw_gate, dw_up, dw_down), token = finish(False, ffn.terms[1], pack_sum, finished, 3)
    half_rows = width + kv_width

    def kernel(*refs):
        unpack_kernel(half_rows, *refs)

    kv_square = shape((kv_width, width), F32)
    vector = shape((width,), F32)
    dgain, dffn_gain, dw_query, dw_key, dw_value, dw_out = run(
        kernel,
        (pack_sum, swap(pack_sum)),
        (vector, vector, square, kv_square, kv_square, square),
        [pltpu.VMEM((2, half_rows, width), F32)],
        after=token,
        name="unpack",
        us=2,
    )
    return (
        output.T[None],
        grad_input.T[None],
        dgain,
        dw_query,
        dw_key.T,
        dw_value.T,
        dw_out,
        dffn_gain,
        dw_gate,
        dw_up,
        dw_down.T,
    )


def solution(mesh):
    sizes = (mesh.shape["dp"], mesh.shape["tensor"])

    def local(*args):
        return per_device(sizes, *args)

    split = P("dp", "tensor", None)
    in_specs = (
        split, P("dp", None), split, P(), P(), P(), P(), P(), P(),
        P(None, "tensor"), P(None, "tensor"), P("tensor", None),
    )
    out_specs = (
        split, split, P(), P(), P(), P(), P(), P(),
        P(None, "tensor"), P(None, "tensor"), P("tensor", None),
    )
    return jax.shard_map(
        local, mesh=mesh, in_specs=in_specs, out_specs=out_specs, check_vma=False
    )
```

```python
import jax
import jax.numpy as jnp
import numpy as np
from jax import lax
from jax.experimental import pallas as pl
from jax.experimental.pallas import tpu as pltpu
from jax.sharding import PartitionSpec as P

HEADS = 9
KV_HEADS = 3
GROUP = HEADS // KV_HEADS
HEAD_DIM = 64
HALF = HEAD_DIM // 2
EPSILON = 1e-05
MASKED = -1e30
BLOCK = 256
SCALE = HEAD_DIM ** (-0.5)
F32 = jnp.float32
BF16 = jnp.bfloat16
VMEM_LIMIT = 16 * 2**20


def dot(left, right, left_dim, right_dim):
    return lax.dot_general(
        left, right, (((left_dim,), (right_dim,)), ((), ())), preferred_element_type=F32
    )


def pieces(size, step):
    return [slice(start, start + step) for start in range(0, size, step)]


def inverse_rms(x_ref):
    total = None
    for rows in pieces(x_ref.shape[0], 64):
        x = x_ref[rows, :]
        part = jnp.sum(x * x, axis=0, keepdims=True)
        total = part if total is None else total + part
    return lax.rsqrt(total / x_ref.shape[0] + EPSILON)


def norm_forward(x_ref, gain_ref, out_ref):
    scale = inverse_rms(x_ref)
    for rows in pieces(x_ref.shape[0], 64):
        out_ref[rows, :] = (x_ref[rows, :] * scale * gain_ref[rows, :]).astype(BF16)


def norm_backward(x_ref, gain_ref, grad_ref, add_ref, out_ref, gain_grad_ref):
    scale = inverse_rms(x_ref)
    inner = None
    for rows in pieces(x_ref.shape[0], 64):
        x, e = x_ref[rows, :], grad_ref[rows, :]
        xe = x * e
        gain_grad_ref[rows, :] = jnp.sum(xe * scale, axis=1, keepdims=True)
        part = jnp.sum(xe * gain_ref[rows, :], axis=0, keepdims=True)
        inner = part if inner is None else inner + part
    cubed = scale * scale * scale * (inner / x_ref.shape[0])
    for rows in pieces(x_ref.shape[0], 64):
        out_ref[rows, :] = (
            add_ref[rows, :].astype(F32)
            + scale * gain_ref[rows, :] * grad_ref[rows, :]
            - x_ref[rows, :] * cubed
        )


def gain_backward(x_ref, grad_ref, gain_grad_ref):
    scale = inverse_rms(x_ref)
    for rows in pieces(x_ref.shape[0], 64):
        gain_grad_ref[rows, :] = jnp.sum(
            x_ref[rows, :] * grad_ref[rows, :] * scale, axis=1, keepdims=True
        )


def rotated(x, cos_table, sin_table):
    front, back = x[:HALF], x[HALF:]
    return jnp.concatenate(
        [front * cos_table - back * sin_table, back * cos_table + front * sin_table], axis=0
    )


def project_qkv(normed_ref, wq_ref, wk_ref, wv_ref, cos_ref, sin_ref, q_ref, kv_ref):
    normed = normed_ref[...]
    cos_table, sin_table = cos_ref[...], sin_ref[...]
    key = dot(wk_ref[...], normed, 1, 0)
    for head in pieces(KV_HEADS * HEAD_DIM, HEAD_DIM):
        kv_ref[head, :] = rotated(key[head], cos_table, sin_table).astype(BF16)
    kv_ref[KV_HEADS * HEAD_DIM :, :] = dot(wv_ref[...], normed, 1, 0).astype(BF16)
    query = dot(wq_ref[...], normed, 0, 0)
    for head in pieces(HEADS * HEAD_DIM, HEAD_DIM):
        q_ref[head, :] = (rotated(query[head], cos_table, sin_table) * SCALE).astype(BF16)


def first_kernel(
    tokens_hbm, wq_hbm, wk_hbm, wv_hbm, cos_hbm, sin_hbm, gain_hbm, ffn_gain_hbm,
    low_ref, normed_ref, q_ref, kv_ref, gain_ref, ffn_gain_ref, cos_ref, sin_ref,
    wq_ref, wk_ref, wv_ref,
    x_ref, gain_in_ref, ffn_gain_in_ref, sems,
):
    cut = low_ref.shape[1]
    pairs = [
        (gain_hbm, gain_in_ref), (ffn_gain_hbm, ffn_gain_in_ref),
        (tokens_hbm.at[:, :cut], low_ref), (wk_hbm, wk_ref), (wv_hbm, wv_ref), (wq_hbm, wq_ref),
    ]
    for local, tile in enumerate(tile_places(lax.axis_index("tensor"))):
        cols = slice(local * cut, (local + 1) * cut)
        for source, target in ((cos_hbm, cos_ref), (sin_hbm, sin_ref)):
            pairs.append((source.at[:, tile_lanes(tile)], target.at[:, cols]))
    copies = [
        pltpu.make_async_copy(source, target, sems.at[index])
        for index, (source, target) in enumerate(pairs)
    ]
    for copy in copies:
        copy.start()
    copies[0].wait()
    copies[1].wait()
    for in_ref, column_ref in ((gain_in_ref, gain_ref), (ffn_gain_in_ref, ffn_gain_ref)):
        row = in_ref[...].reshape(1, -1)
        column_ref[...] = jnp.broadcast_to(row, (128, row.shape[1])).T[:, :1]
    copies[2].wait()
    x_ref[...] = low_ref[...].astype(F32)
    norm_forward(x_ref, gain_ref, normed_ref)
    for copy in copies[3:]:
        copy.wait()
    tables = (cos_ref.at[:, :cut], sin_ref.at[:, :cut])
    project_qkv(normed_ref, wq_ref, wk_ref, wv_ref, *tables, q_ref, kv_ref)


def second_kernel(
    got_ref, half_refs, gain_ref, cos_ref, sin_ref, wq_ref, wk_ref, wv_ref, full_refs, x_ref
):
    cut = x_ref.shape[1]
    for half_ref, full_ref in zip(half_refs, full_refs):
        full_ref[:, :cut] = half_ref[...]
    low_ref, normed_ref, q_ref, kv_ref = (ref.at[:, cut:] for ref in full_refs)
    low_ref[...] = got_ref[:, cut:]
    x_ref[...] = low_ref[...].astype(F32)
    norm_forward(x_ref, gain_ref, normed_ref)
    tables = (cos_ref.at[:, cut:], sin_ref.at[:, cut:])
    project_qkv(normed_ref, wq_ref, wk_ref, wv_ref, *tables, q_ref, kv_ref)


def tile_places(core):
    return 2 * core, 3 - 2 * core


def tile_lanes(tile):
    return pl.ds(pl.multiple_of(tile * BLOCK, BLOCK), BLOCK)


def set_labels(labels_ref, column_ref):
    column_ref[...] = jnp.broadcast_to(labels_ref[0:1, :], (8, labels_ref.shape[1])).T


def set_mask(bias_ref, labels_ref, column_ref, tile, kb):
    key_labels = column_ref[tile_lanes(kb), :1]
    key_place = kb * BLOCK + lax.broadcasted_iota(jnp.int32, (BLOCK, BLOCK), 0)
    place = tile * BLOCK + lax.broadcasted_iota(jnp.int32, (1, BLOCK), 1)
    allowed = (key_labels == labels_ref[0:1, tile_lanes(tile)]) & (key_place <= place)
    bias_ref[...] = jnp.where(allowed, 0.0, MASKED)


def first_block(segments_ref, tile):
    label = segments_ref[0, tile * BLOCK]
    count = jnp.int32(0)
    for kb in range(3):
        before = (kb < tile) & (segments_ref[0, kb * BLOCK + BLOCK - 1] < label)
        count = count + before.astype(jnp.int32)
    return count


def head_rows(head):
    return slice(head * HEAD_DIM, (head + 1) * HEAD_DIM)


def load_part(kv_ref, tok_ref):
    for head in range(2 * KV_HEADS):
        for cols in pieces(kv_ref.shape[1], BLOCK):
            tok_ref[head, cols, :] = kv_ref[head_rows(head), cols].T


def over_blocks(segments_ref, core, own, body):
    keys_of = tile_places(core if own else 1 - core)
    for local, tile in enumerate(tile_places(core)):
        cols = slice(local * BLOCK, (local + 1) * BLOCK)
        first = first_block(segments_ref, tile)

        def step(at, carry):
            kb = jnp.where(at == 0, keys_of[0], keys_of[1])

            @pl.when((kb >= first) & (kb <= tile))
            def _():
                body(local, tile, cols, kb, at)

            return carry

        lax.fori_loop(0, 2, step, 0)


def attend_kernel(
    own, segments_ref, labels_ref, q_ref, kv_ref, state_refs, mask_in_refs, out_refs, mask_out_refs,
    value_ref, column_ref, scores_ref,
):
    core = lax.axis_index("tensor")
    if mask_out_refs:
        set_labels(labels_ref, column_ref)
    (masks_ref,) = mask_in_refs or mask_out_refs
    for at, cols in enumerate(pieces(kv_ref.shape[1], BLOCK)):
        for group in range(KV_HEADS):
            value_ref[at, group, :HEAD_DIM, :] = kv_ref[head_rows(KV_HEADS + group), cols]
            value_ref[at, group, HEAD_DIM:, :] = jnp.ones((16, BLOCK), BF16)
    m_ref, l_ref, acc_ref = out_refs if own else state_refs
    if own:
        m_ref[...] = jnp.full(m_ref.shape, MASKED, F32)
        l_ref[...] = jnp.zeros(l_ref.shape, F32)
        acc_ref[...] = jnp.zeros(acc_ref.shape, F32)

    def body(local, tile, cols, kb, at):
        bias_ref = masks_ref.at[local, at]
        if mask_out_refs:
            set_mask(bias_ref, labels_ref, column_ref, tile, kb)
        keys = tile_lanes(at)

        def scores(group):
            key = kv_ref[head_rows(group), keys]
            for head in range(group * GROUP, (group + 1) * GROUP):
                scores_ref[head] = dot(key, q_ref[head_rows(head), cols], 0, 0) + bias_ref[...]

        def products(group):
            for head in range(group * GROUP, (group + 1) * GROUP):
                rows = head_rows(head)
                m_old = m_ref[head : head + 1, cols]
                m_new = jnp.maximum(m_old, jnp.max(scores_ref[head], axis=0, keepdims=True))
                m_ref[head : head + 1, cols] = m_new
                fade = jnp.exp(m_old - m_new)
                probs = jnp.exp(scores_ref[head] - m_new).astype(BF16)
                product = dot(value_ref[at, group], probs, 1, 0)
                l_ref[head : head + 1, cols] = (
                    l_ref[head : head + 1, cols] * fade + product[HEAD_DIM : HEAD_DIM + 1]
                )
                acc_ref[rows, cols] = acc_ref[rows, cols] * fade + product[:HEAD_DIM]

        scores(0)
        scores(1)
        products(0)
        scores(2)
        products(1)
        products(2)

    over_blocks(segments_ref, core, own, body)
    if not own:
        ctx_ref, lse_ref = out_refs
        for head in range(HEADS):
            total = l_ref[head : head + 1, :]
            ctx_ref[head_rows(head), :] = (acc_ref[head_rows(head), :] * (1.0 / total)).astype(BF16)
            lse_ref[head : head + 1, :] = m_ref[head : head + 1, :] + jnp.log(total)


def attend_back_kernel(
    own, segments_ref, q_ref, kv_ref, masks_ref, lse_ref, grad_ref, more_refs, out_refs,
    tok_ref, probs_ref, probs_low_ref, gs_ref, dkv_ref,
):
    core = lax.axis_index("tensor")
    load_part(kv_ref, tok_ref)
    if own:
        (delta_ref,) = more_refs
        dq_ref, dkv_out_ref = out_refs
    else:
        (ctx_ref,) = more_refs
        dq_ref, delta_ref, dkv_out_ref = out_refs
        dq_ref[...] = jnp.zeros(dq_ref.shape, F32)
        for head in range(HEADS):
            rows = head_rows(head)
            delta_ref[head : head + 1, :] = jnp.sum(
                grad_ref[rows, :].astype(F32) * ctx_ref[rows, :].astype(F32), axis=0, keepdims=True
            )
    dkv_ref[...] = jnp.zeros(dkv_ref.shape, F32)

    def body(local, tile, cols, kb, at):
        bias_ref = masks_ref.at[local, at]
        keys = tile_lanes(at)
        for head in range(HEADS):
            key = tok_ref[head // GROUP, keys, :]
            scores = dot(key, q_ref[head_rows(head), cols], 1, 0) + bias_ref[...]
            probs = jnp.exp(scores - lse_ref[head : head + 1, cols])
            probs_ref[head] = probs
            probs_low_ref[head] = probs.astype(BF16)
        for head in range(HEADS):
            value = tok_ref[KV_HEADS + head // GROUP, keys, :]
            grad_probs = dot(value, grad_ref[head_rows(head), cols], 1, 0)
            gs_ref[head] = (
                probs_ref[head] * (grad_probs - delta_ref[head : head + 1, cols])
            ).astype(BF16)
        for group in range(KV_HEADS):
            dv = dkv_ref[at, head_rows(KV_HEADS + group), :]
            for head in range(group * GROUP, (group + 1) * GROUP):
                dv = dv + dot(grad_ref[head_rows(head), cols], probs_low_ref[head], 1, 1)
            dkv_ref[at, head_rows(KV_HEADS + group), :] = dv
        for group in range(KV_HEADS):
            dk = dkv_ref[at, head_rows(group), :]
            for head in range(group * GROUP, (group + 1) * GROUP):
                dk = dk + dot(q_ref[head_rows(head), cols], gs_ref[head], 1, 1)
            dkv_ref[at, head_rows(group), :] = dk
        for head in range(HEADS):
            key_cols = kv_ref[head_rows(head // GROUP), keys]
            dq_ref[head_rows(head), cols] += dot(key_cols, gs_ref[head], 1, 0)

    over_blocks(segments_ref, core, own, body)
    for at, cols in enumerate(pieces(dkv_out_ref.shape[1], BLOCK)):
        dkv_out_ref[:, cols] = dkv_ref[at].astype(dkv_out_ref.dtype)


def middle_kernel(
    low_ref, ctx_ref, wo_ref, ffn_gain_ref, wg_refs, wu_refs, wd_refs,
    gain_ref, wq_ref, wk_ref, wv_ref, cos_ref, sin_ref,
    mid_ref, ffn_ref, gate_ref, up_ref, x2_ref, normed_ref, q_ref, kv_ref, product_ref,
):
    mid_ref[...] = low_ref[...].astype(F32) + dot(wo_ref[...], ctx_ref[...], 0, 0)
    norm_forward(mid_ref, ffn_gain_ref, ffn_ref)
    ffn_in = ffn_ref[...]
    half_hidden = wg_refs[0].shape[1]
    for part in range(2):
        for hidden in pieces(half_hidden, BLOCK):
            gate = dot(wg_refs[part][:, hidden], ffn_in, 0, 0)
            up = dot(wu_refs[part][:, hidden], ffn_in, 0, 0)
            rows = slice(part * half_hidden + hidden.start, part * half_hidden + hidden.stop)
            gate_ref[rows, :] = gate.astype(BF16)
            up_ref[rows, :] = up.astype(BF16)
            product_ref[rows, :] = (gate * jax.nn.sigmoid(gate) * up).astype(BF16)
    x2_ref[...] = (
        mid_ref[...]
        + dot(wd_refs[0][...], product_ref[:half_hidden, :], 1, 0)
        + dot(wd_refs[1][...], product_ref[half_hidden:, :], 1, 0)
    )
    norm_forward(x2_ref, gain_ref, normed_ref)
    project_qkv(normed_ref, wq_ref, wk_ref, wv_ref, cos_ref, sin_ref, q_ref, kv_ref)


def ffn_terms(gate, up, grad_product):
    sig = jax.nn.sigmoid(gate)
    silu = gate * sig
    grad_gate = (grad_product * up * (sig + silu * (1.0 - sig))).astype(BF16)
    grad_up = (grad_product * silu).astype(BF16)
    return (silu * up).astype(BF16), grad_gate, grad_up


def turn_kernel(
    x_ref, ctx_ref, wo_ref, ffn_gain_ref, wg_refs, wu_refs, wd_refs, cotangent_ref, cot_got_ref,
    mid_ref, cot_ref, ffn_ref, kept_own_refs, kept_other_refs,
    grad_mid_ref, grad_mid_low_ref, grad_ctx_ref, dgain_ref,
    acc_ref,
):
    mid_ref[...] = x_ref[...] + dot(wo_ref[...], ctx_ref[...], 0, 0)
    norm_forward(mid_ref, ffn_gain_ref, ffn_ref)
    ffn_in = ffn_ref[...]
    cut = cot_got_ref.shape[1] // 2
    cot_ref[:, :cut] = cotangent_ref[:, :cut]
    cot_ref[:, cut:] = cot_got_ref[:, cut:]
    grad_low = cot_ref[...]
    for part in range(2):
        for hidden in pieces(wg_refs[part].shape[1], BLOCK):
            gate = dot(wg_refs[part][:, hidden], ffn_in, 0, 0)
            up = dot(wu_refs[part][:, hidden], ffn_in, 0, 0)
            grad_product = dot(wd_refs[part][:, hidden], grad_low, 0, 0)
            kept = (kept_own_refs, kept_other_refs)[part]
            for ref, term in zip(kept, ffn_terms(gate, up, grad_product)):
                ref[hidden, :] = term
    acc_ref[...] = (
        dot(wg_refs[0][...], kept_own_refs[1][...], 1, 0)
        + dot(wu_refs[0][...], kept_own_refs[2][...], 1, 0)
        + dot(wg_refs[1][...], kept_other_refs[1][...], 1, 0)
        + dot(wu_refs[1][...], kept_other_refs[2][...], 1, 0)
    )
    norm_backward(mid_ref, ffn_gain_ref, acc_ref, cot_ref, grad_mid_ref, dgain_ref)
    grad_mid_low_ref[...] = grad_mid_ref[...].astype(BF16)
    grad_ctx_ref[...] = dot(wo_ref[...], grad_mid_low_ref[...], 1, 0).astype(BF16)


def result_kernel(mid_ref, product_refs, wd_refs, out_refs):
    result = (
        mid_ref[...]
        + dot(wd_refs[0][...], product_refs[0][...], 1, 0)
        + dot(wd_refs[1][...], product_refs[1][...], 1, 0)
    )
    cut = out_refs[0].shape[1]
    out_refs[0][...] = result[:, :cut].astype(BF16)
    out_refs[1][...] = result[:, cut:].astype(BF16)


def input_kernel(
    x_low_ref, gain_ref, dnormed_ref, grad_mid_ref, out_refs, x_ref, out_ref, dgain_ref
):
    x_ref[...] = x_low_ref[...].astype(F32)
    norm_backward(x_ref, gain_ref, dnormed_ref, grad_mid_ref, out_ref, dgain_ref)
    cut = out_refs[0].shape[1]
    out_refs[0][...] = out_ref[:, :cut]
    out_refs[1][...] = out_ref[:, cut:]


def qkv_back(
    dq_ref, dkv_own_ref, dkv_got_ref, wq_ref, wk_ref, wv_ref, cos_ref, sin_ref, dpre_ref, dnormed_ref
):
    cos_table, sin_table = cos_ref[...], sin_ref[...]
    width, kv_width = HEADS * HEAD_DIM, KV_HEADS * HEAD_DIM
    for head in pieces(width, HEAD_DIM):
        dpre_ref[head, :] = rotated(dq_ref[head, :] * SCALE, cos_table, -sin_table).astype(BF16)
    for head in pieces(kv_width, HEAD_DIM):
        total = dkv_own_ref[head, :] + dkv_got_ref[head, :].astype(F32)
        rows = slice(width + head.start, width + head.stop)
        dpre_ref[rows, :] = rotated(total, cos_table, -sin_table).astype(BF16)
    dpre_ref[width + kv_width :, :] = (
        dkv_own_ref[kv_width:, :] + dkv_got_ref[kv_width:, :].astype(F32)
    ).astype(BF16)
    dnormed_ref[...] = (
        dot(wq_ref[...], dpre_ref[:width, :], 1, 0)
        + dot(wk_ref[...], dpre_ref[width : width + kv_width, :], 0, 0)
        + dot(wv_ref[...], dpre_ref[width + kv_width :, :], 0, 0)
    )


def fill_stack(stack, width):
    if stack.shape[0] > 3 * width:
        stack[3 * width :, :] = jnp.zeros((stack.shape[0] - 3 * width, stack.shape[1]), BF16)


def ffn_back(
    part, stack, low, ffn1, ffn2, low2, gate_ref, up_ref, wg_ref, wu_ref, wd_ref, kept2_refs,
    acc_ref, terms_ref,
):
    width, half_hidden = wg_ref.shape
    for hidden in pieces(half_hidden, BLOCK):
        rows = slice(part * half_hidden + hidden.start, part * half_hidden + hidden.stop)
        grad_product = dot(wd_ref[:, hidden], low, 0, 0)
        terms = ffn_terms(gate_ref[rows, :].astype(F32), up_ref[rows, :].astype(F32), grad_product)
        for at, term in enumerate(terms):
            terms_ref[at, hidden, :] = term
    acc_ref[...] += dot(wg_ref[...], terms_ref[1], 1, 0) + dot(wu_ref[...], terms_ref[2], 1, 0)
    for at, (left1, left2, which) in enumerate(((ffn1, ffn2, 1), (ffn1, ffn2, 2), (low, low2, 0))):
        stack[at * width : (at + 1) * width, :] = (
            dot(left1, terms_ref[which], 1, 1) + dot(left2, kept2_refs[which][...], 1, 1)
        ).astype(BF16)
    fill_stack(stack, width)


def other_kernel(
    dq_ref, dkv_own_ref, dkv_got_ref, x_ref, grad_mid_ref,
    gain_ref, wq_ref, wk_ref, wv_ref, cos_ref, sin_ref,
    ffn1_ref, gate_ref, up_ref, wg_ref, wu_ref, wd_ref, ffn2_ref, low2_ref, kept2_refs,
    dpre_ref, dgain_ref, low_ref, gstream_ref, acc_ref, stack, dnormed_ref, terms_ref,
):
    qkv_back(
        dq_ref, dkv_own_ref, dkv_got_ref, wq_ref, wk_ref, wv_ref, cos_ref, sin_ref,
        dpre_ref, dnormed_ref,
    )
    norm_backward(x_ref, gain_ref, dnormed_ref, grad_mid_ref, gstream_ref, dgain_ref)
    low_ref[...] = gstream_ref[...].astype(BF16)
    acc_ref[...] = jnp.zeros(acc_ref.shape, F32)
    ffn_back(
        1, stack, low_ref[...], ffn1_ref[...], ffn2_ref[...], low2_ref[...],
        gate_ref, up_ref, wg_ref, wu_ref, wd_ref, kept2_refs, acc_ref, terms_ref,
    )


def own_kernel(
    low_ref, gstream_ref, acc_in_ref,
    ffn1_ref, gate_ref, up_ref, wg_ref, wu_ref, wd_ref, ffn2_ref, low2_ref, kept2_refs,
    mid_ref, wo_ref, ffn_gain_ref, dffn_gain2_ref,
    stack, grad_mid_ref, grad_mid_low_ref, grad_ctx_ref, dffn_gain_ref, acc_ref, terms_ref,
):
    acc_ref[...] = acc_in_ref[...]
    ffn_back(
        0, stack, low_ref[...], ffn1_ref[...], ffn2_ref[...], low2_ref[...],
        gate_ref, up_ref, wg_ref, wu_ref, wd_ref, kept2_refs, acc_ref, terms_ref,
    )
    norm_backward(mid_ref, ffn_gain_ref, acc_ref, gstream_ref, grad_mid_ref, dffn_gain_ref)
    dffn_gain_ref[...] += dffn_gain2_ref[...]
    grad_mid_low_ref[...] = grad_mid_ref[...].astype(BF16)
    grad_ctx_ref[...] = dot(wo_ref[...], grad_mid_low_ref[...], 1, 0).astype(BF16)


def last_kernel(
    dq_ref, dkv_own_ref, dkv_got_ref, x_low_ref, wq_ref, wk_ref, wv_ref, cos_ref, sin_ref,
    dpre2_ref, normed_refs, ctx_refs, grad_mid_low_refs, dgain2_ref, dffn_gain_ref,
    dnormed_ref, stack_own_ref, stack_other_ref,
    dpre_ref, x_ref, dgain_ref, stack_ref,
):
    x_ref[...] = x_low_ref[...].astype(F32)
    width, rows = x_ref.shape[0], stack_ref.shape[1]
    qkv_back(
        dq_ref, dkv_own_ref, dkv_got_ref, wq_ref, wk_ref, wv_ref, cos_ref, sin_ref,
        dpre_ref, dnormed_ref,
    )
    gain_backward(x_ref, dnormed_ref, dgain_ref)
    normed1, normed2 = (ref[...] for ref in normed_refs)
    dwq = dot(normed1, dpre_ref[:width, :], 1, 1) + dot(normed2, dpre2_ref[:width, :], 1, 1)
    dwkv = dot(dpre_ref[width:, :], normed1, 1, 1) + dot(dpre2_ref[width:, :], normed2, 1, 1)
    dwo = dot(ctx_refs[0][...], grad_mid_low_refs[0][...], 1, 1) + dot(
        ctx_refs[1][...], grad_mid_low_refs[1][...], 1, 1
    )
    half_rows = width + dwkv.shape[0] // 2
    rest = half_rows - width
    stack_ref[0, :width, :width] = dwq.astype(BF16)
    stack_ref[0, width:half_rows, :width] = dwo[:rest].astype(BF16)
    stack_ref[1, : width - rest, :width] = dwo[rest:].astype(BF16)
    stack_ref[1, width - rest : half_rows, :width] = dwkv.astype(BF16)
    lanes = stack_ref.shape[2] - width
    column = lax.broadcasted_iota(jnp.int32, (width, lanes), 1)
    gains = jnp.where(
        column == 0,
        dgain_ref[...] + dgain2_ref[...],
        jnp.where(column == 1, dffn_gain_ref[...], 0.0),
    ).astype(BF16)
    for part in range(2):
        stack_ref[part, :width, width:] = gains
        stack_ref[part, width:, width:] = jnp.zeros((rows - width, lanes), BF16)
        if rows > half_rows:
            stack_ref[part, half_rows:, :width] = jnp.zeros((rows - half_rows, width), BF16)
    core = lax.axis_index("tensor")
    stack_own_ref[...] = stack_ref[core]
    stack_other_ref[...] = stack_ref[1 - core]


def shape(dims, dtype):
    return jax.ShapeDtypeStruct(dims, dtype)


def run(
    kernel, args, outs, scratch=(), smem=0, hbm=0, after=(), name=None, us=5, limit=VMEM_LIMIT,
    hbm_outs=0, update=(),
):
    leaves, tree = jax.tree.flatten(args)
    out_leaves, out_tree = jax.tree.flatten(outs)
    late = jax.tree.leaves(after) + list(update)
    n_in, n_out = len(leaves), len(out_leaves)

    def body(*refs):
        ins = jax.tree.unflatten(tree, refs[:n_in])
        refs = refs[n_in + len(late) :]
        results = jax.tree.unflatten(out_tree, refs[:n_out])
        kernel(*ins, *results, *refs[n_out:])

    in_specs = [
        pl.BlockSpec(
            memory_space=pltpu.SMEM if index < smem else pltpu.HBM if index < hbm else pltpu.VMEM
        )
        for index in range(n_in)
    ] + [pl.BlockSpec(memory_space=pl.ANY)] * (len(late) - len(update))
    in_specs += [
        pl.BlockSpec(memory_space=pltpu.HBM if index < hbm_outs else pltpu.VMEM)
        for index in range(len(update))
    ]
    results = pl.pallas_call(
        body,
        out_shape=out_leaves,
        in_specs=in_specs,
        out_specs=[pl.BlockSpec(memory_space=pltpu.HBM if index < hbm_outs else pltpu.VMEM)
            for index in range(n_out)
        ],
        scratch_shapes=list(scratch),
        input_output_aliases={
            n_in + len(late) - len(update) + index: index for index in range(len(update))
        },
        compiler_params=pltpu.CompilerParams(vmem_limit_bytes=limit),
        cost_estimate=pl.CostEstimate(
            flops=int(us * 1e9) + 1, bytes_accessed=2**20 if us else 1, transcendentals=0
        ),
        name=name,
    )(*leaves, *late)
    return jax.tree.unflatten(out_tree, results)


def in_hbm(arrays):
    return tuple(pltpu.with_memory_space_constraint(array, pltpu.HBM) for array in arrays)


def swap(array):
    return lax.ppermute(array, "tensor", [(0, 1), (1, 0)])


def partners(sizes, bits):
    n, cores = sizes
    return [
        (place * cores + core, (place ^ (1 << bits[core])) * cores + core)
        for place in range(n)
        for core in range(cores)
    ]


def by_core(pair):
    return jnp.where(lax.axis_index("tensor") == 0, jnp.int32(pair[0]), jnp.int32(pair[1]))


def own_bit(bits):
    place = lax.axis_index("dp").astype(jnp.int32)
    return lax.shift_right_logical(place, by_core(bits)) & 1


def insert(index, rank, bit):
    low = index & (lax.shift_left(jnp.int32(1), rank) - 1)
    return lax.shift_left(index - low, jnp.int32(1)) + lax.shift_left(bit, rank) + low


def scatter_kernel(bits, ranks, sent, terms, out_ref):
    own, rank = own_bit(bits), by_core(ranks)
    half = 1 - own if sent else own

    def body(index, carry):
        at = insert(index, rank, half)
        total = terms[0][at].astype(F32)
        for term in terms[1:]:
            total = total + term[at].astype(F32)
        out_ref[index] = total.astype(BF16)
        return carry

    lax.fori_loop(0, out_ref.shape[0], body, 0)


def add_kernel(one_ref, two_ref, out_ref):
    out_ref[...] = (one_ref[...].astype(F32) + two_ref[...].astype(F32)).astype(BF16)


def join(bits, ranks, own_ref, got_ref, out_ref):
    own, rank = own_bit(bits), by_core(ranks)

    def body(index, carry):
        out_ref[insert(index, rank, own)] = own_ref[index]
        out_ref[insert(index, rank, 1 - own)] = got_ref[index]
        return carry

    lax.fori_loop(0, own_ref.shape[0], body, 0)


def ranks_of(dims, done):
    ranks = []
    for step in range(len(dims[0])):
        pair = []
        for order in dims:
            there = order[step + 1 :] if done == "after" else order[:step]
            pair.append(sum(other < order[step] for other in there))
        ranks.append(tuple(pair))
    return ranks


class Stream:
    def __init__(self, name, terms, sizes, orders):
        scatter, across, gather = orders
        self.name, self.sizes = name, sizes
        self.halvings = len(scatter[0])
        self.chunks = 1 << self.halvings
        self.bits = list(zip(*scatter)) + [(across, across)] + list(zip(*gather))
        self.ranks = ranks_of(scatter, "after") + [None] + ranks_of(gather, "before")
        self.terms = [term.reshape((self.chunks, -1) + term.shape[1:]) for term in terms]
        self.rounds = 2 * self.halvings + 1
        self.round = 0

    def call(self, kernel, args, counts, after):
        rows, columns = self.terms[0].shape[1:]
        outs = tuple(shape((count, rows, columns), BF16) for count in counts)
        return run(kernel, args, outs, after=after, name=f"{self.name}_{self.round}", us=0)

    def load(self, after):
        if self.round < self.halvings:
            half = self.terms[0].shape[0] // 2
            bits, ranks = self.bits[self.round], self.ranks[self.round]

            terms = tuple(self.terms)

            def part(which, after):
                def kernel(terms, out_ref):
                    scatter_kernel(bits, ranks, which, terms, out_ref)

                return self.call(kernel, (terms,), (half,), after)[0]

            sent = part(True, after)
            self.terms = [part(False, sent)]
            return sent
        if self.round <= self.halvings + 1:
            (sent,) = self.call(add_kernel, tuple(self.terms), (1,), after)
        else:
            bits, ranks = self.bits[self.round - 1], self.ranks[self.round - 1]

            def kernel(*refs):
                join(bits, ranks, *refs)

            (sent,) = self.call(
                kernel, tuple(self.terms), (2 * self.terms[0].shape[0],), after
            )
        self.terms = [sent]
        return sent

    def step(self, token):
        if self.done:
            return token
        sent = self.load(token)
        got = lax.ppermute(sent, ("dp", "tensor"), partners(self.sizes, self.bits[self.round]))
        self.terms = self.terms + [got]
        self.round += 1
        return sent

    @property
    def done(self):
        return self.round == self.rounds

    def join(self, out_ref, own_ref, got_ref):
        join(self.bits[-1], self.ranks[-1], own_ref, got_ref, out_ref)


def finish_kernel(stream, mine, part_ref, outs, token_ref, wide_ref, sems):
    count, rows = part_ref.shape[:2]
    token_ref[...] = jnp.zeros(token_ref.shape, F32)
    for index in range(count):
        wide_ref[index] = part_ref[index].astype(F32)
    width = outs[0].shape[0]
    own, core = own_bit(stream.bits[-1]), lax.axis_index("tensor")
    half = own if mine else 1 - own

    def copies(chunk, index):
        at, end, found = chunk * rows, (chunk + 1) * rows, []
        while at < end:
            which, inside = divmod(at, width)
            size = min(end - at, width - inside)
            if which == len(outs):
                break
            found.append(
                pltpu.make_async_copy(
                    wide_ref.at[index, at - chunk * rows : at - chunk * rows + size, :],
                    outs[which].at[inside : inside + size, :],
                    sems.at[index, len(found)],
                )
            )
            at += size
        return found

    for act in ("start", "wait"):
        for which, rank in enumerate(stream.ranks[-1]):
            for chunk in range(2 * count):
                bit, low = (chunk >> rank) & 1, chunk & ((1 << rank) - 1)
                index = ((chunk >> (rank + 1)) << rank) + low

                @pl.when((core == which) & (half == bit))
                def _():
                    for copy in copies(chunk, index):
                        getattr(copy, act)()


def pack_kernel(stream, own_ref, got_ref, out_ref, all_ref):
    stream.join(all_ref, own_ref, got_ref)
    rows = all_ref.shape[1]
    for chunk in range(all_ref.shape[0]):
        out_ref[chunk * rows : (chunk + 1) * rows, :] = all_ref[chunk]


def unpack_kernel(
    half_rows, pack_ref, pack_got_ref,
    gain_ref, ffn_gain_ref, dwq_ref, dwk_ref, dwv_ref, dwo_ref, all_ref,
):
    width, kv_width = dwq_ref.shape[0], dwk_ref.shape[0]
    core = lax.axis_index("tensor")
    for which, ref in ((core, pack_ref), (1 - core, pack_got_ref)):
        all_ref[which] = ref[:half_rows, :width].astype(F32)
    rest = half_rows - width
    dwq_ref[...] = all_ref[0, :width]
    dwo_ref[:rest, :] = all_ref[0, width:]
    dwo_ref[rest:, :] = all_ref[1, : width - rest]
    dwk_ref[...] = all_ref[1, width - rest : width - rest + kv_width]
    dwv_ref[...] = all_ref[1, width - rest + kv_width :]
    rows = pack_ref[:width, width:].astype(F32).T
    for at, ref in ((0, gain_ref), (1, ffn_gain_ref)):
        ref[...] = rows[at : at + 1, :].reshape(width)


def tie(*arrays):
    return lax.optimization_barrier(arrays)


def orders_of(n):
    bits = list(range(n.bit_length() - 1))
    across = bits[-1]
    halved = bits[:-1]
    if len(halved) < 3:
        return [((halved, halved), across, (halved, halved))] * 2
    rest = halved[3:]
    ffn = (([0, 2, 1] + rest, [1, 0, 2] + rest), across, (rest + [1, 2, 0], rest + [2, 0, 1]))
    attention = (([1, 0, 2] + rest, [1, 0, 2] + rest), across, (rest + [0, 1, 2], rest + [1, 0, 2]))
    return [ffn, attention]


def position_tables(length):
    places = np.arange(length, dtype=np.float32)
    inverse = np.float32(10000.0) ** (np.arange(HALF, dtype=np.float32) * np.float32(-2.0 / HEAD_DIM))
    angles = inverse.astype(np.float32)[:, None] * places[None, :]
    return jnp.asarray(np.cos(angles)), jnp.asarray(np.sin(angles))


def per_device(
    sizes, tokens, segments, cotangent, attn_gain, w_query, w_key, w_value, w_out, ffn_gain,
    w_gate, w_up, w_down,
):
    _, half, width = tokens.shape
    kv_width = KV_HEADS * HEAD_DIM
    hidden = w_gate.shape[1]
    n = sizes[0]
    core = lax.axis_index("tensor")
    cut = half // 2
    tokens, cotangent = tokens[0].T, cotangent[0].T
    w_key, w_value, w_down = w_key.T, w_value.T, w_down.T

    tokens_got = swap(tokens)
    all_tables = position_tables(segments.shape[1])
    where = (segments, segments)
    projections = (w_query, w_key, w_value)

    act = shape((width, half), F32)
    low = shape((width, half), BF16)
    kv = shape((2 * kv_width, half), BF16)
    kv_f32 = shape((2 * kv_width, half), F32)
    wide = shape((2 * hidden, half), BF16)
    thin = shape((hidden, half), BF16)
    column = shape((width, 1), F32)
    square = shape((width, width), F32)
    heads_f32 = pltpu.VMEM((HEADS, BLOCK, BLOCK), F32)
    heads_low = pltpu.VMEM((HEADS, BLOCK, BLOCK), BF16)
    key_scratch = pltpu.VMEM((2 * KV_HEADS, half, HEAD_DIM), BF16)
    masks_shape = shape((2, 2, BLOCK, BLOCK), F32)
    rows_f32 = shape((16, half), F32)
    act_scratch = pltpu.VMEM((width, half), F32)
    low_scratch = pltpu.VMEM((width, half), BF16)

    def attend(query, kv_own, kv_other, masks=None):
        state, made = (), []
        for own, kv_part in ((True, kv_own), (False, kv_other)):

            def kernel(*refs, own=own):
                attend_kernel(own, *refs)

            state, new = run(
                kernel,
                where + (query, kv_part, tuple(state), () if masks is None else (masks[len(made)],)),
                ((rows_f32, rows_f32, act) if own else (low, rows_f32),
                 (masks_shape,) if masks is None else ()),
                [pltpu.VMEM((2, KV_HEADS, HEAD_DIM + 16, BLOCK), BF16),
                 pltpu.VMEM((4 * BLOCK, 8), jnp.int32), heads_f32],
                smem=1,
                name="attend_own" if own else "attend_other",
                us=4,
            )
            made.append(new[0] if masks is None else masks[len(made)])
        return (*state, made)

    def attend_back(query, kv_own, kv_other, masks, ctx, lse, grad, us=5):
        more, dq = (ctx,), ()
        for own, kv_part, dkv in ((False, kv_other, kv), (True, kv_own, kv_f32)):

            def kernel(*refs, own=own):
                attend_back_kernel(own, *refs)

            (outs,) = run(
                kernel,
                (segments, query, kv_part, masks[0 if own else 1], lse, grad, more),
                ((act, dkv),) if own else ((act, rows_f32, dkv),),
                [key_scratch, heads_f32, heads_low, heads_low,
                 pltpu.VMEM((2, 2 * kv_width, BLOCK), F32)],
                smem=1,
                name="attend_back_own" if own else "attend_back_other",
                us=us,
                update=dq,
            )
            if not own:
                dq, more = outs[:1], outs[1:2]
                got = swap(outs[2])
        return outs[0], outs[1], got

    table = shape((HALF, half), F32)
    tile_low, tile_kv = shape((width, cut), BF16), shape((2 * kv_width, cut), BF16)
    x_half = pltpu.VMEM((width, cut), F32)
    *halves, gain_col, ffn_gain_col, cos_table, sin_table, wq, wk, wv = run(
        first_kernel,
        in_hbm((tokens,) + projections + all_tables + (attn_gain, ffn_gain)),
        (tile_low, tile_low, tile_low, tile_kv, column, column, table, table)
        + tuple(shape(weight.shape, BF16) for weight in projections),
        [x_half, pltpu.VMEM((width,), F32), pltpu.VMEM((width,), F32),
         pltpu.SemaphoreType.DMA((10,))],
        hbm=8,
        name="first",
        us=2,
    )
    projections, tables = (wq, wk, wv), (cos_table, sin_table)
    (x1, normed1, query1, kv1), = run(
        second_kernel,
        (tokens_got, tuple(halves), gain_col) + tables + projections,
        ((low, low, low, kv),),
        [x_half],
        name="second",
        us=1,
    )
    kv1, cot_sent = tie(kv1, cotangent)
    kv1_other = swap(kv1)
    gate_pair = (w_gate, swap(w_gate))
    up_pair = (w_up, swap(w_up))
    down_pair = (w_down, swap(w_down))
    cot_got = swap(cot_sent)
    ctx1, lse1, masks = attend(query1, kv1, kv1_other)
    mid1, ffn1, gate1, up1, x2, normed2, query2, kv2 = run(
        middle_kernel,
        (x1, ctx1, w_out, ffn_gain_col, gate_pair, up_pair, down_pair, gain_col)
        + projections + tables,
        (act, low, wide, wide, act, low, low, kv),
        [pltpu.VMEM(wide.shape, BF16)],
        name="middle",
        us=6,
    )
    kv2_other = swap(kv2)
    ctx2, lse2, _ = attend(query2, kv2, kv2_other, masks)
    (
        mid2, cot, ffn2, kept2_own, kept2_other, grad_mid2, grad_mid_low2, grad_ctx2, dffn_gain2,
    ) = run(
        turn_kernel,
        (x2, ctx2, w_out, ffn_gain_col, gate_pair, up_pair, down_pair, cotangent, cot_got),
        (act, low, low, (thin,) * 3, (thin,) * 3, act, low, low, column),
        [act_scratch],
        name="turn",
        us=9,
    )
    dq2, dkv_own2, dkv_got2 = attend_back(query2, kv2, kv2_other, masks, ctx2, lse2, grad_ctx2)
    pad = 8 * max(n // 2, 1)
    stack_rows = -(-3 * width // pad) * pad
    stack_shape = shape((stack_rows, hidden), BF16)
    pre = shape((width + 2 * kv_width, half), BF16)
    dpre2, dgain2, low1, gstream, dffn, stack_other = run(
        other_kernel,
        (dq2, dkv_own2, dkv_got2, x2, grad_mid2, gain_col) + projections + tables
        + (ffn1, gate1, up1, gate_pair[1], up_pair[1], down_pair[1], ffn2, cot, kept2_other),
        (pre, column, low, act, act, stack_shape),
        [act_scratch, pltpu.VMEM((3,) + thin.shape, BF16)],
        name="other",
        us=8,
    )
    stack_got = swap(stack_other)
    stack_own, grad_mid1, grad_mid_low1, grad_ctx1, dffn_gain = run(
        own_kernel,
        (low1, gstream, dffn, ffn1, gate1, up1, gate_pair[0], up_pair[0], down_pair[0],
         ffn2, cot, kept2_own, mid1, w_out, ffn_gain_col, dffn_gain2),
        (stack_shape, act, low, low, column),
        [act_scratch, pltpu.VMEM((3,) + thin.shape, BF16)],
        name="own",
        us=7,
    )
    ffn_orders, pack_orders = orders_of(n)
    ffn = Stream("ffn", (stack_own, stack_got), sizes, ffn_orders)
    token = ffn.step(stack_own)
    grad_ctx1, token = tie(grad_ctx1, token)
    dq1, dkv_own1, dkv_got1 = attend_back(query1, kv1, kv1_other, masks, ctx1, lse1, grad_ctx1, 0)
    rows = -(-(2 * width + 2 * kv_width) // 2 // pad) * pad
    lanes = -(-width // 128) * 128
    lanes = lanes if lanes - width >= 2 else lanes + 128
    half_stack = shape((rows, lanes), BF16)
    tile_act = shape((width, cut), F32)
    dnormed1, pack_own, pack_other = run(
        last_kernel,
        (dq1, dkv_own1, dkv_got1, x1) + projections + tables
        + (dpre2, (normed1, normed2), (ctx1, ctx2), (grad_mid_low1, grad_mid_low2),
           dgain2, dffn_gain),
        (act, half_stack, half_stack),
        [pltpu.VMEM(pre.shape, BF16), act_scratch,
         pltpu.VMEM((width, 1), F32), pltpu.VMEM((2, rows, lanes), BF16)],
        name="last",
        us=0,
    )
    pack = Stream("pack", (pack_own, swap(pack_other)), sizes, pack_orders)
    token = pack_own
    for index, which in enumerate("fafafaafafafa"):
        token = (ffn if which == "f" else pack).step(token)
        if index == 1:
            ((output, output_sent),) = run(
                result_kernel,
                (mid2, (kept2_own[0], kept2_other[0]), down_pair),
                ((tile_low, tile_low),), after=token, name="result", us=0,
            )
            token = (token, output)
        if index == 3:
            ((grad_input, grad_input_sent),) = run(
                input_kernel,
                (x1, gain_col, dnormed1, grad_mid1), ((tile_act, tile_act),),
                [act_scratch, act_scratch, pltpu.VMEM((width, 1), F32)],
                after=token, name="input", us=0,
            )
            token = (token, grad_input)
        if index == 11:
            output = jnp.concatenate([output, swap(output_sent)], axis=1)
            grad_input = jnp.concatenate([grad_input, swap(grad_input_sent)], axis=1)
            token = (token, output, grad_input)
    while not (ffn.done and pack.done):
        token = pack.step(ffn.step(token))

    def finish(mine, part, after, update, us):
        def kernel(part_ref, *refs):
            finish_kernel(ffn, mine, part_ref, refs[:3], *refs[3:])

        count, rows, columns = part.shape
        *outs, token = run(
            kernel, (part,), (shape((width, hidden), F32),) * 3 + (shape((8, 128), F32),),
            [pltpu.VMEM(part.shape, F32), pltpu.SemaphoreType.DMA((count, rows // width + 2))],
            after=after, name="finish", us=us, hbm_outs=3, update=update,
        )
        return outs, token

    finished, token = finish(True, ffn.terms[0], token, (), 0)

    def kernel(own_ref, got_ref, out_ref, all_ref):
        pack_kernel(pack, own_ref, got_ref, out_ref, all_ref)

    (pack_sum,) = run(
        kernel, tuple(pack.terms), (half_stack,),
        [pltpu.VMEM((pack.chunks, rows // pack.chunks, lanes), BF16)],
        after=token, name="pack_all", us=0,
    )
    (dw_gate, dw_up, dw_down), token = finish(False, ffn.terms[1], pack_sum, finished, 3)
    half_rows = width + kv_width

    def kernel(*refs):
        unpack_kernel(half_rows, *refs)

    kv_square = shape((kv_width, width), F32)
    vector = shape((width,), F32)
    dgain, dffn_gain, dw_query, dw_key, dw_value, dw_out = run(
        kernel,
        (pack_sum, swap(pack_sum)),
        (vector, vector, square, kv_square, kv_square, square),
        [pltpu.VMEM((2, half_rows, width), F32)],
        after=token,
        name="unpack",
        us=2,
    )
    return (
        output.T[None],
        grad_input.T[None],
        dgain,
        dw_query,
        dw_key.T,
        dw_value.T,
        dw_out,
        dffn_gain,
        dw_gate,
        dw_up,
        dw_down.T,
    )


def solution(mesh):
    sizes = (mesh.shape["dp"], mesh.shape["tensor"])

    def local(*args):
        return per_device(sizes, *args)

    split = P("dp", "tensor", None)
    in_specs = (
        split, P("dp", None), split, P(), P(), P(), P(), P(), P(),
        P(None, "tensor"), P(None, "tensor"), P("tensor", None),
    )
    out_specs = (
        split, split, P(), P(), P(), P(), P(), P(),
        P(None, "tensor"), P(None, "tensor"), P("tensor", None),
    )
    return jax.shard_map(
        local, mesh=mesh, in_specs=in_specs, out_specs=out_specs, check_vma=False
    )
```

```python
import jax
import jax.numpy as jnp
import numpy as np
from jax import lax
from jax.experimental import pallas as pl
from jax.experimental.pallas import tpu as pltpu
from jax.sharding import PartitionSpec as P

HEADS = 9
KV_HEADS = 3
GROUP = HEADS // KV_HEADS
HEAD_DIM = 64
HALF = HEAD_DIM // 2
EPSILON = 1e-05
MASKED = -1e30
BLOCK = 256
SCALE = HEAD_DIM ** (-0.5)
F32 = jnp.float32
BF16 = jnp.bfloat16
VMEM_LIMIT = 16 * 2**20


def dot(left, right, left_dim, right_dim):
    return lax.dot_general(
        left, right, (((left_dim,), (right_dim,)), ((), ())), preferred_element_type=F32
    )


def pieces(size, step):
    return [slice(start, start + step) for start in range(0, size, step)]


def inverse_rms(x_ref):
    total = None
    for rows in pieces(x_ref.shape[0], 64):
        x = x_ref[rows, :]
        part = jnp.sum(x * x, axis=0, keepdims=True)
        total = part if total is None else total + part
    return lax.rsqrt(total / x_ref.shape[0] + EPSILON)


def norm_forward(x_ref, gain_ref, out_ref):
    scale = inverse_rms(x_ref)
    for rows in pieces(x_ref.shape[0], 64):
        out_ref[rows, :] = (x_ref[rows, :] * scale * gain_ref[rows, :]).astype(BF16)


def norm_backward(x_ref, gain_ref, grad_ref, add_ref, out_ref, gain_grad_ref):
    scale = inverse_rms(x_ref)
    inner = None
    for rows in pieces(x_ref.shape[0], 64):
        x, e = x_ref[rows, :], grad_ref[rows, :]
        xe = x * e
        gain_grad_ref[rows, :] = jnp.sum(xe * scale, axis=1, keepdims=True)
        part = jnp.sum(xe * gain_ref[rows, :], axis=0, keepdims=True)
        inner = part if inner is None else inner + part
    cubed = scale * scale * scale * (inner / x_ref.shape[0])
    for rows in pieces(x_ref.shape[0], 64):
        out_ref[rows, :] = (
            add_ref[rows, :].astype(F32)
            + scale * gain_ref[rows, :] * grad_ref[rows, :]
            - x_ref[rows, :] * cubed
        )


def gain_backward(x_ref, grad_ref, gain_grad_ref):
    scale = inverse_rms(x_ref)
    for rows in pieces(x_ref.shape[0], 64):
        gain_grad_ref[rows, :] = jnp.sum(
            x_ref[rows, :] * grad_ref[rows, :] * scale, axis=1, keepdims=True
        )


def rotated(x, cos_table, sin_table):
    front, back = x[:HALF], x[HALF:]
    return jnp.concatenate(
        [front * cos_table - back * sin_table, back * cos_table + front * sin_table], axis=0
    )


def project_qkv(normed_ref, wq_ref, wk_ref, wv_ref, cos_ref, sin_ref, q_ref, kv_ref):
    normed = normed_ref[...]
    cos_table, sin_table = cos_ref[...], sin_ref[...]
    key = dot(wk_ref[...], normed, 1, 0)
    for head in pieces(KV_HEADS * HEAD_DIM, HEAD_DIM):
        kv_ref[head, :] = rotated(key[head], cos_table, sin_table).astype(BF16)
    kv_ref[KV_HEADS * HEAD_DIM :, :] = dot(wv_ref[...], normed, 1, 0).astype(BF16)
    query = dot(wq_ref[...], normed, 0, 0)
    for head in pieces(HEADS * HEAD_DIM, HEAD_DIM):
        q_ref[head, :] = (rotated(query[head], cos_table, sin_table) * SCALE).astype(BF16)


def first_kernel(
    tokens_hbm, wq_hbm, wk_hbm, wv_hbm, cos_hbm, sin_hbm, gain_hbm, ffn_gain_hbm,
    low_ref, normed_ref, q_ref, kv_ref, gain_ref, ffn_gain_ref, cos_ref, sin_ref,
    wq_ref, wk_ref, wv_ref,
    x_ref, gain_in_ref, ffn_gain_in_ref, sems,
):
    cut = low_ref.shape[1]
    pairs = [
        (gain_hbm, gain_in_ref), (ffn_gain_hbm, ffn_gain_in_ref),
        (tokens_hbm.at[:, :cut], low_ref), (wk_hbm, wk_ref), (wv_hbm, wv_ref), (wq_hbm, wq_ref),
    ]
    for local, tile in enumerate(tile_places(lax.axis_index("tensor"))):
        cols = slice(local * cut, (local + 1) * cut)
        for source, target in ((cos_hbm, cos_ref), (sin_hbm, sin_ref)):
            pairs.append((source.at[:, tile_lanes(tile)], target.at[:, cols]))
    copies = [
        pltpu.make_async_copy(source, target, sems.at[index])
        for index, (source, target) in enumerate(pairs)
    ]
    for copy in copies:
        copy.start()
    copies[0].wait()
    copies[1].wait()
    for in_ref, column_ref in ((gain_in_ref, gain_ref), (ffn_gain_in_ref, ffn_gain_ref)):
        row = in_ref[...].reshape(1, -1)
        column_ref[...] = jnp.broadcast_to(row, (128, row.shape[1])).T[:, :1]
    copies[2].wait()
    x_ref[...] = low_ref[...].astype(F32)
    norm_forward(x_ref, gain_ref, normed_ref)
    for copy in copies[3:]:
        copy.wait()
    tables = (cos_ref.at[:, :cut], sin_ref.at[:, :cut])
    project_qkv(normed_ref, wq_ref, wk_ref, wv_ref, *tables, q_ref, kv_ref)


def second_kernel(
    got_ref, half_refs, gain_ref, cos_ref, sin_ref, wq_ref, wk_ref, wv_ref, full_refs, x_ref
):
    cut = x_ref.shape[1]
    for half_ref, full_ref in zip(half_refs, full_refs):
        full_ref[:, :cut] = half_ref[...]
    low_ref, normed_ref, q_ref, kv_ref = (ref.at[:, cut:] for ref in full_refs)
    low_ref[...] = got_ref[:, cut:]
    x_ref[...] = low_ref[...].astype(F32)
    norm_forward(x_ref, gain_ref, normed_ref)
    tables = (cos_ref.at[:, cut:], sin_ref.at[:, cut:])
    project_qkv(normed_ref, wq_ref, wk_ref, wv_ref, *tables, q_ref, kv_ref)


def tile_places(core):
    return 2 * core, 3 - 2 * core


def tile_lanes(tile):
    return pl.ds(pl.multiple_of(tile * BLOCK, BLOCK), BLOCK)


def set_labels(labels_ref, column_ref):
    column_ref[...] = jnp.broadcast_to(labels_ref[0:1, :], (8, labels_ref.shape[1])).T


def set_mask(bias_ref, labels_ref, column_ref, tile, kb):
    key_labels = column_ref[tile_lanes(kb), :1]
    key_place = kb * BLOCK + lax.broadcasted_iota(jnp.int32, (BLOCK, BLOCK), 0)
    place = tile * BLOCK + lax.broadcasted_iota(jnp.int32, (1, BLOCK), 1)
    allowed = (key_labels == labels_ref[0:1, tile_lanes(tile)]) & (key_place <= place)
    bias_ref[...] = jnp.where(allowed, 0.0, MASKED)


def first_block(segments_ref, tile):
    label = segments_ref[0, tile * BLOCK]
    count = jnp.int32(0)
    for kb in range(3):
        before = (kb < tile) & (segments_ref[0, kb * BLOCK + BLOCK - 1] < label)
        count = count + before.astype(jnp.int32)
    return count


def head_rows(head):
    return slice(head * HEAD_DIM, (head + 1) * HEAD_DIM)


def load_part(kv_ref, tok_ref):
    for head in range(2 * KV_HEADS):
        for cols in pieces(kv_ref.shape[1], BLOCK):
            tok_ref[head, cols, :] = kv_ref[head_rows(head), cols].T


def over_blocks(segments_ref, core, own, body):
    keys_of = tile_places(core if own else 1 - core)
    for local, tile in enumerate(tile_places(core)):
        cols = slice(local * BLOCK, (local + 1) * BLOCK)
        first = first_block(segments_ref, tile)

        def step(at, carry):
            kb = jnp.where(at == 0, keys_of[0], keys_of[1])

            @pl.when((kb >= first) & (kb <= tile))
            def _():
                body(local, tile, cols, kb, at)

            return carry

        lax.fori_loop(0, 2, step, 0)


def attend_kernel(
    own, segments_ref, labels_ref, q_ref, kv_ref, state_refs, mask_in_refs, out_refs, mask_out_refs,
    value_ref, column_ref, scores_ref,
):
    core = lax.axis_index("tensor")
    if mask_out_refs:
        set_labels(labels_ref, column_ref)
    (masks_ref,) = mask_in_refs or mask_out_refs
    for at, cols in enumerate(pieces(kv_ref.shape[1], BLOCK)):
        for group in range(KV_HEADS):
            value_ref[at, group, :HEAD_DIM, :] = kv_ref[head_rows(KV_HEADS + group), cols]
            value_ref[at, group, HEAD_DIM:, :] = jnp.ones((16, BLOCK), BF16)
    m_ref, l_ref, acc_ref = out_refs if own else state_refs
    if own:
        m_ref[...] = jnp.full(m_ref.shape, MASKED, F32)
        l_ref[...] = jnp.zeros(l_ref.shape, F32)
        acc_ref[...] = jnp.zeros(acc_ref.shape, F32)

    def body(local, tile, cols, kb, at):
        bias_ref = masks_ref.at[local, at]
        if mask_out_refs:
            set_mask(bias_ref, labels_ref, column_ref, tile, kb)
        keys = tile_lanes(at)

        def scores(group):
            key = kv_ref[head_rows(group), keys]
            for head in range(group * GROUP, (group + 1) * GROUP):
                scores_ref[head] = dot(key, q_ref[head_rows(head), cols], 0, 0) + bias_ref[...]

        def products(group):
            for head in range(group * GROUP, (group + 1) * GROUP):
                rows = head_rows(head)
                m_old = m_ref[head : head + 1, cols]
                m_new = jnp.maximum(m_old, jnp.max(scores_ref[head], axis=0, keepdims=True))
                m_ref[head : head + 1, cols] = m_new
                fade = jnp.exp(m_old - m_new)
                probs = jnp.exp(scores_ref[head] - m_new).astype(BF16)
                product = dot(value_ref[at, group], probs, 1, 0)
                l_ref[head : head + 1, cols] = (
                    l_ref[head : head + 1, cols] * fade + product[HEAD_DIM : HEAD_DIM + 1]
                )
                acc_ref[rows, cols] = acc_ref[rows, cols] * fade + product[:HEAD_DIM]

        scores(0)
        scores(1)
        products(0)
        scores(2)
        products(1)
        products(2)

    over_blocks(segments_ref, core, own, body)
    if not own:
        ctx_ref, lse_ref = out_refs
        for head in range(HEADS):
            total = l_ref[head : head + 1, :]
            ctx_ref[head_rows(head), :] = (acc_ref[head_rows(head), :] * (1.0 / total)).astype(BF16)
            lse_ref[head : head + 1, :] = m_ref[head : head + 1, :] + jnp.log(total)


def attend_back_kernel(
    own, segments_ref, q_ref, kv_ref, masks_ref, lse_ref, grad_ref, more_refs, out_refs,
    tok_ref, probs_ref, probs_low_ref, gs_ref, dkv_ref,
):
    core = lax.axis_index("tensor")
    load_part(kv_ref, tok_ref)
    if own:
        (delta_ref,) = more_refs
        dq_ref, dkv_out_ref = out_refs
    else:
        (ctx_ref,) = more_refs
        dq_ref, delta_ref, dkv_out_ref = out_refs
        dq_ref[...] = jnp.zeros(dq_ref.shape, F32)
        for head in range(HEADS):
            rows = head_rows(head)
            delta_ref[head : head + 1, :] = jnp.sum(
                grad_ref[rows, :].astype(F32) * ctx_ref[rows, :].astype(F32), axis=0, keepdims=True
            )
    dkv_ref[...] = jnp.zeros(dkv_ref.shape, F32)

    def body(local, tile, cols, kb, at):
        bias_ref = masks_ref.at[local, at]
        keys = tile_lanes(at)
        for head in range(HEADS):
            key = tok_ref[head // GROUP, keys, :]
            scores = dot(key, q_ref[head_rows(head), cols], 1, 0) + bias_ref[...]
            probs = jnp.exp(scores - lse_ref[head : head + 1, cols])
            probs_ref[head] = probs
            probs_low_ref[head] = probs.astype(BF16)
        for head in range(HEADS):
            value = tok_ref[KV_HEADS + head // GROUP, keys, :]
            grad_probs = dot(value, grad_ref[head_rows(head), cols], 1, 0)
            gs_ref[head] = (
                probs_ref[head] * (grad_probs - delta_ref[head : head + 1, cols])
            ).astype(BF16)
        for group in range(KV_HEADS):
            dv = dkv_ref[at, head_rows(KV_HEADS + group), :]
            for head in range(group * GROUP, (group + 1) * GROUP):
                dv = dv + dot(grad_ref[head_rows(head), cols], probs_low_ref[head], 1, 1)
            dkv_ref[at, head_rows(KV_HEADS + group), :] = dv
        for group in range(KV_HEADS):
            dk = dkv_ref[at, head_rows(group), :]
            for head in range(group * GROUP, (group + 1) * GROUP):
                dk = dk + dot(q_ref[head_rows(head), cols], gs_ref[head], 1, 1)
            dkv_ref[at, head_rows(group), :] = dk
        for head in range(HEADS):
            key_cols = kv_ref[head_rows(head // GROUP), keys]
            dq_ref[head_rows(head), cols] += dot(key_cols, gs_ref[head], 1, 0)

    over_blocks(segments_ref, core, own, body)
    for at, cols in enumerate(pieces(dkv_out_ref.shape[1], BLOCK)):
        dkv_out_ref[:, cols] = dkv_ref[at].astype(dkv_out_ref.dtype)


def middle_kernel(
    low_ref, ctx_ref, wo_ref, ffn_gain_ref, wg_refs, wu_refs, wd_refs,
    gain_ref, wq_ref, wk_ref, wv_ref, cos_ref, sin_ref,
    mid_ref, ffn_ref, gate_ref, up_ref, x2_ref, normed_ref, q_ref, kv_ref, product_ref,
):
    mid_ref[...] = low_ref[...].astype(F32) + dot(wo_ref[...], ctx_ref[...], 0, 0)
    norm_forward(mid_ref, ffn_gain_ref, ffn_ref)
    ffn_in = ffn_ref[...]
    half_hidden = wg_refs[0].shape[1]
    for part in range(2):
        for hidden in pieces(half_hidden, BLOCK):
            gate = dot(wg_refs[part][:, hidden], ffn_in, 0, 0)
            up = dot(wu_refs[part][:, hidden], ffn_in, 0, 0)
            rows = slice(part * half_hidden + hidden.start, part * half_hidden + hidden.stop)
            gate_ref[rows, :] = gate.astype(BF16)
            up_ref[rows, :] = up.astype(BF16)
            product_ref[rows, :] = (gate * jax.nn.sigmoid(gate) * up).astype(BF16)
    x2_ref[...] = (
        mid_ref[...]
        + dot(wd_refs[0][...], product_ref[:half_hidden, :], 1, 0)
        + dot(wd_refs[1][...], product_ref[half_hidden:, :], 1, 0)
    )
    norm_forward(x2_ref, gain_ref, normed_ref)
    project_qkv(normed_ref, wq_ref, wk_ref, wv_ref, cos_ref, sin_ref, q_ref, kv_ref)


def ffn_terms(gate, up, grad_product):
    sig = jax.nn.sigmoid(gate)
    silu = gate * sig
    grad_gate = (grad_product * up * (sig + silu * (1.0 - sig))).astype(BF16)
    grad_up = (grad_product * silu).astype(BF16)
    return (silu * up).astype(BF16), grad_gate, grad_up


def turn_kernel(
    x_ref, ctx_ref, wo_ref, ffn_gain_ref, wg_refs, wu_refs, wd_refs, cotangent_ref, cot_got_ref,
    mid_ref, cot_ref, ffn_ref, kept_own_refs, kept_other_refs,
    grad_mid_ref, grad_mid_low_ref, grad_ctx_ref, dgain_ref,
    acc_ref,
):
    mid_ref[...] = x_ref[...] + dot(wo_ref[...], ctx_ref[...], 0, 0)
    norm_forward(mid_ref, ffn_gain_ref, ffn_ref)
    ffn_in = ffn_ref[...]
    cut = cot_got_ref.shape[1] // 2
    cot_ref[:, :cut] = cotangent_ref[:, :cut]
    cot_ref[:, cut:] = cot_got_ref[:, cut:]
    grad_low = cot_ref[...]
    for part in range(2):
        for hidden in pieces(wg_refs[part].shape[1], BLOCK):
            gate = dot(wg_refs[part][:, hidden], ffn_in, 0, 0)
            up = dot(wu_refs[part][:, hidden], ffn_in, 0, 0)
            grad_product = dot(wd_refs[part][:, hidden], grad_low, 0, 0)
            kept = (kept_own_refs, kept_other_refs)[part]
            for ref, term in zip(kept, ffn_terms(gate, up, grad_product)):
                ref[hidden, :] = term
    acc_ref[...] = (
        dot(wg_refs[0][...], kept_own_refs[1][...], 1, 0)
        + dot(wu_refs[0][...], kept_own_refs[2][...], 1, 0)
        + dot(wg_refs[1][...], kept_other_refs[1][...], 1, 0)
        + dot(wu_refs[1][...], kept_other_refs[2][...], 1, 0)
    )
    norm_backward(mid_ref, ffn_gain_ref, acc_ref, cot_ref, grad_mid_ref, dgain_ref)
    grad_mid_low_ref[...] = grad_mid_ref[...].astype(BF16)
    grad_ctx_ref[...] = dot(wo_ref[...], grad_mid_low_ref[...], 1, 0).astype(BF16)


def result_kernel(mid_ref, product_refs, wd_refs, out_refs):
    result = (
        mid_ref[...]
        + dot(wd_refs[0][...], product_refs[0][...], 1, 0)
        + dot(wd_refs[1][...], product_refs[1][...], 1, 0)
    )
    cut = out_refs[0].shape[1]
    out_refs[0][...] = result[:, :cut].astype(BF16)
    out_refs[1][...] = result[:, cut:].astype(BF16)


def input_kernel(
    x_low_ref, gain_ref, dnormed_ref, grad_mid_ref, out_refs, x_ref, out_ref, dgain_ref
):
    x_ref[...] = x_low_ref[...].astype(F32)
    norm_backward(x_ref, gain_ref, dnormed_ref, grad_mid_ref, out_ref, dgain_ref)
    cut = out_refs[0].shape[1]
    out_refs[0][...] = out_ref[:, :cut]
    out_refs[1][...] = out_ref[:, cut:]


def qkv_back(
    dq_ref, dkv_own_ref, dkv_got_ref, wq_ref, wk_ref, wv_ref, cos_ref, sin_ref, dpre_ref, dnormed_ref
):
    cos_table, sin_table = cos_ref[...], sin_ref[...]
    width, kv_width = HEADS * HEAD_DIM, KV_HEADS * HEAD_DIM
    for head in pieces(width, HEAD_DIM):
        dpre_ref[head, :] = rotated(dq_ref[head, :] * SCALE, cos_table, -sin_table).astype(BF16)
    for head in pieces(kv_width, HEAD_DIM):
        total = dkv_own_ref[head, :] + dkv_got_ref[head, :].astype(F32)
        rows = slice(width + head.start, width + head.stop)
        dpre_ref[rows, :] = rotated(total, cos_table, -sin_table).astype(BF16)
    dpre_ref[width + kv_width :, :] = (
        dkv_own_ref[kv_width:, :] + dkv_got_ref[kv_width:, :].astype(F32)
    ).astype(BF16)
    dnormed_ref[...] = (
        dot(wq_ref[...], dpre_ref[:width, :], 1, 0)
        + dot(wk_ref[...], dpre_ref[width : width + kv_width, :], 0, 0)
        + dot(wv_ref[...], dpre_ref[width + kv_width :, :], 0, 0)
    )


def fill_stack(stack, width):
    if stack.shape[0] > 3 * width:
        stack[3 * width :, :] = jnp.zeros((stack.shape[0] - 3 * width, stack.shape[1]), BF16)


def ffn_back(
    part, stack, low, ffn1, ffn2, low2, gate_ref, up_ref, wg_ref, wu_ref, wd_ref, kept2_refs,
    acc_ref, terms_ref,
):
    width, half_hidden = wg_ref.shape
    for hidden in pieces(half_hidden, BLOCK):
        rows = slice(part * half_hidden + hidden.start, part * half_hidden + hidden.stop)
        grad_product = dot(wd_ref[:, hidden], low, 0, 0)
        terms = ffn_terms(gate_ref[rows, :].astype(F32), up_ref[rows, :].astype(F32), grad_product)
        for at, term in enumerate(terms):
            terms_ref[at, hidden, :] = term
    acc_ref[...] += dot(wg_ref[...], terms_ref[1], 1, 0) + dot(wu_ref[...], terms_ref[2], 1, 0)
    for at, (left1, left2, which) in enumerate(((ffn1, ffn2, 1), (ffn1, ffn2, 2), (low, low2, 0))):
        stack[at * width : (at + 1) * width, :] = (
            dot(left1, terms_ref[which], 1, 1) + dot(left2, kept2_refs[which][...], 1, 1)
        ).astype(BF16)
    fill_stack(stack, width)


def other_kernel(
    dq_ref, dkv_own_ref, dkv_got_ref, x_ref, grad_mid_ref,
    gain_ref, wq_ref, wk_ref, wv_ref, cos_ref, sin_ref,
    ffn1_ref, gate_ref, up_ref, wg_ref, wu_ref, wd_ref, ffn2_ref, low2_ref, kept2_refs,
    dpre_ref, dgain_ref, low_ref, gstream_ref, acc_ref, stack, dnormed_ref, terms_ref,
):
    qkv_back(
        dq_ref, dkv_own_ref, dkv_got_ref, wq_ref, wk_ref, wv_ref, cos_ref, sin_ref,
        dpre_ref, dnormed_ref,
    )
    norm_backward(x_ref, gain_ref, dnormed_ref, grad_mid_ref, gstream_ref, dgain_ref)
    low_ref[...] = gstream_ref[...].astype(BF16)
    acc_ref[...] = jnp.zeros(acc_ref.shape, F32)
    ffn_back(
        1, stack, low_ref[...], ffn1_ref[...], ffn2_ref[...], low2_ref[...],
        gate_ref, up_ref, wg_ref, wu_ref, wd_ref, kept2_refs, acc_ref, terms_ref,
    )


def own_kernel(
    low_ref, acc_in_ref,
    ffn1_ref, gate_ref, up_ref, wg_ref, wu_ref, wd_ref, ffn2_ref, low2_ref, kept2_refs,
    stack, acc_ref, terms_ref,
):
    acc_ref[...] = acc_in_ref[...]
    ffn_back(
        0, stack, low_ref[...], ffn1_ref[...], ffn2_ref[...], low2_ref[...],
        gate_ref, up_ref, wg_ref, wu_ref, wd_ref, kept2_refs, acc_ref, terms_ref,
    )


def context_kernel(
    gstream_ref, acc_ref, mid_ref, wo_ref, ffn_gain_ref, dffn_gain2_ref,
    grad_mid_ref, grad_mid_low_ref, grad_ctx_ref, dffn_gain_ref,
):
    norm_backward(mid_ref, ffn_gain_ref, acc_ref, gstream_ref, grad_mid_ref, dffn_gain_ref)
    dffn_gain_ref[...] += dffn_gain2_ref[...]
    grad_mid_low_ref[...] = grad_mid_ref[...].astype(BF16)
    grad_ctx_ref[...] = dot(wo_ref[...], grad_mid_low_ref[...], 1, 0).astype(BF16)


def last_kernel(
    dq_ref, dkv_own_ref, dkv_got_ref, x_low_ref, wq_ref, wk_ref, wv_ref, cos_ref, sin_ref,
    dpre2_ref, normed_refs, ctx_refs, grad_mid_low_refs, dgain2_ref, dffn_gain_ref,
    dnormed_ref, stack_own_ref, stack_other_ref,
    dpre_ref, x_ref, dgain_ref, stack_ref,
):
    x_ref[...] = x_low_ref[...].astype(F32)
    width, rows = x_ref.shape[0], stack_ref.shape[1]
    qkv_back(
        dq_ref, dkv_own_ref, dkv_got_ref, wq_ref, wk_ref, wv_ref, cos_ref, sin_ref,
        dpre_ref, dnormed_ref,
    )
    gain_backward(x_ref, dnormed_ref, dgain_ref)
    normed1, normed2 = (ref[...] for ref in normed_refs)
    dwq = dot(normed1, dpre_ref[:width, :], 1, 1) + dot(normed2, dpre2_ref[:width, :], 1, 1)
    dwkv = dot(dpre_ref[width:, :], normed1, 1, 1) + dot(dpre2_ref[width:, :], normed2, 1, 1)
    dwo = dot(ctx_refs[0][...], grad_mid_low_refs[0][...], 1, 1) + dot(
        ctx_refs[1][...], grad_mid_low_refs[1][...], 1, 1
    )
    half_rows = width + dwkv.shape[0] // 2
    rest = half_rows - width
    stack_ref[0, :width, :width] = dwq.astype(BF16)
    stack_ref[0, width:half_rows, :width] = dwo[:rest].astype(BF16)
    stack_ref[1, : width - rest, :width] = dwo[rest:].astype(BF16)
    stack_ref[1, width - rest : half_rows, :width] = dwkv.astype(BF16)
    lanes = stack_ref.shape[2] - width
    column = lax.broadcasted_iota(jnp.int32, (width, lanes), 1)
    gains = jnp.where(
        column == 0,
        dgain_ref[...] + dgain2_ref[...],
        jnp.where(column == 1, dffn_gain_ref[...], 0.0),
    ).astype(BF16)
    for part in range(2):
        stack_ref[part, :width, width:] = gains
        stack_ref[part, width:, width:] = jnp.zeros((rows - width, lanes), BF16)
        if rows > half_rows:
            stack_ref[part, half_rows:, :width] = jnp.zeros((rows - half_rows, width), BF16)
    core = lax.axis_index("tensor")
    stack_own_ref[...] = stack_ref[core]
    stack_other_ref[...] = stack_ref[1 - core]


def shape(dims, dtype):
    return jax.ShapeDtypeStruct(dims, dtype)


def run(
    kernel, args, outs, scratch=(), smem=0, hbm=0, after=(), name=None, us=5, limit=VMEM_LIMIT,
    hbm_outs=0, update=(),
):
    leaves, tree = jax.tree.flatten(args)
    out_leaves, out_tree = jax.tree.flatten(outs)
    late = jax.tree.leaves(after) + list(update)
    n_in, n_out = len(leaves), len(out_leaves)

    def body(*refs):
        ins = jax.tree.unflatten(tree, refs[:n_in])
        refs = refs[n_in + len(late) :]
        results = jax.tree.unflatten(out_tree, refs[:n_out])
        kernel(*ins, *results, *refs[n_out:])

    in_specs = [
        pl.BlockSpec(
            memory_space=pltpu.SMEM if index < smem else pltpu.HBM if index < hbm else pltpu.VMEM
        )
        for index in range(n_in)
    ] + [pl.BlockSpec(memory_space=pl.ANY)] * (len(late) - len(update))
    in_specs += [
        pl.BlockSpec(memory_space=pltpu.HBM if index < hbm_outs else pltpu.VMEM)
        for index in range(len(update))
    ]
    results = pl.pallas_call(
        body,
        out_shape=out_leaves,
        in_specs=in_specs,
        out_specs=[pl.BlockSpec(memory_space=pltpu.HBM if index < hbm_outs else pltpu.VMEM)
            for index in range(n_out)
        ],
        scratch_shapes=list(scratch),
        input_output_aliases={
            n_in + len(late) - len(update) + index: index for index in range(len(update))
        },
        compiler_params=pltpu.CompilerParams(vmem_limit_bytes=limit),
        cost_estimate=pl.CostEstimate(
            flops=int(us * 1e9) + 1, bytes_accessed=2**20 if us else 1, transcendentals=0
        ),
        name=name,
    )(*leaves, *late)
    return jax.tree.unflatten(out_tree, results)


def in_hbm(arrays):
    return tuple(pltpu.with_memory_space_constraint(array, pltpu.HBM) for array in arrays)


def swap(array):
    return lax.ppermute(array, "tensor", [(0, 1), (1, 0)])


def partners(sizes, bits):
    n, cores = sizes
    return [
        (place * cores + core, (place ^ (1 << bits[core])) * cores + core)
        for place in range(n)
        for core in range(cores)
    ]


def by_core(pair):
    return jnp.where(lax.axis_index("tensor") == 0, jnp.int32(pair[0]), jnp.int32(pair[1]))


def own_bit(bits):
    place = lax.axis_index("dp").astype(jnp.int32)
    return lax.shift_right_logical(place, by_core(bits)) & 1


def insert(index, rank, bit):
    low = index & (lax.shift_left(jnp.int32(1), rank) - 1)
    return lax.shift_left(index - low, jnp.int32(1)) + lax.shift_left(bit, rank) + low


def scatter_kernel(bits, ranks, sent, terms, out_ref):
    own, rank = own_bit(bits), by_core(ranks)
    half = 1 - own if sent else own

    def body(index, carry):
        at = insert(index, rank, half)
        total = terms[0][at].astype(F32)
        for term in terms[1:]:
            total = total + term[at].astype(F32)
        out_ref[index] = total.astype(BF16)
        return carry

    lax.fori_loop(0, out_ref.shape[0], body, 0)


def add_kernel(one_ref, two_ref, out_ref):
    out_ref[...] = (one_ref[...].astype(F32) + two_ref[...].astype(F32)).astype(BF16)


def join(bits, ranks, own_ref, got_ref, out_ref):
    own, rank = own_bit(bits), by_core(ranks)

    def body(index, carry):
        out_ref[insert(index, rank, own)] = own_ref[index]
        out_ref[insert(index, rank, 1 - own)] = got_ref[index]
        return carry

    lax.fori_loop(0, own_ref.shape[0], body, 0)


def ranks_of(dims, done):
    ranks = []
    for step in range(len(dims[0])):
        pair = []
        for order in dims:
            there = order[step + 1 :] if done == "after" else order[:step]
            pair.append(sum(other < order[step] for other in there))
        ranks.append(tuple(pair))
    return ranks


class Stream:
    def __init__(self, name, terms, sizes, orders):
        scatter, across, gather = orders
        self.name, self.sizes = name, sizes
        self.halvings = len(scatter[0])
        self.chunks = 1 << self.halvings
        self.bits = list(zip(*scatter)) + [(across, across)] + list(zip(*gather))
        self.ranks = ranks_of(scatter, "after") + [None] + ranks_of(gather, "before")
        self.terms = [term.reshape((self.chunks, -1) + term.shape[1:]) for term in terms]
        self.rounds = 2 * self.halvings + 1
        self.round = 0

    def call(self, kernel, args, counts, after):
        rows, columns = self.terms[0].shape[1:]
        outs = tuple(shape((count, rows, columns), BF16) for count in counts)
        return run(kernel, args, outs, after=after, name=f"{self.name}_{self.round}", us=0)

    def load(self, after):
        if self.round < self.halvings:
            half = self.terms[0].shape[0] // 2
            bits, ranks = self.bits[self.round], self.ranks[self.round]

            terms = tuple(self.terms)

            def part(which, after):
                def kernel(terms, out_ref):
                    scatter_kernel(bits, ranks, which, terms, out_ref)

                return self.call(kernel, (terms,), (half,), after)[0]

            sent = part(True, after)
            self.terms = [part(False, sent)]
            return sent
        if self.round <= self.halvings + 1:
            (sent,) = self.call(add_kernel, tuple(self.terms), (1,), after)
        else:
            bits, ranks = self.bits[self.round - 1], self.ranks[self.round - 1]

            def kernel(*refs):
                join(bits, ranks, *refs)

            (sent,) = self.call(
                kernel, tuple(self.terms), (2 * self.terms[0].shape[0],), after
            )
        self.terms = [sent]
        return sent

    def step(self, token):
        if self.done:
            return token
        sent = self.load(token)
        got = lax.ppermute(sent, ("dp", "tensor"), partners(self.sizes, self.bits[self.round]))
        self.terms = self.terms + [got]
        self.round += 1
        return sent

    @property
    def done(self):
        return self.round == self.rounds

    def join(self, out_ref, own_ref, got_ref):
        join(self.bits[-1], self.ranks[-1], own_ref, got_ref, out_ref)


def finish_kernel(stream, mine, part_ref, outs, token_ref, wide_ref, sems):
    count, rows = part_ref.shape[:2]
    token_ref[...] = jnp.zeros(token_ref.shape, F32)
    for index in range(count):
        wide_ref[index] = part_ref[index].astype(F32)
    width = outs[0].shape[0]
    own, core = own_bit(stream.bits[-1]), lax.axis_index("tensor")
    half = own if mine else 1 - own

    def copies(chunk, index):
        at, end, found = chunk * rows, (chunk + 1) * rows, []
        while at < end:
            which, inside = divmod(at, width)
            size = min(end - at, width - inside)
            if which == len(outs):
                break
            found.append(
                pltpu.make_async_copy(
                    wide_ref.at[index, at - chunk * rows : at - chunk * rows + size, :],
                    outs[which].at[inside : inside + size, :],
                    sems.at[index, len(found)],
                )
            )
            at += size
        return found

    for act in ("start", "wait"):
        for which, rank in enumerate(stream.ranks[-1]):
            for chunk in range(2 * count):
                bit, low = (chunk >> rank) & 1, chunk & ((1 << rank) - 1)
                index = ((chunk >> (rank + 1)) << rank) + low

                @pl.when((core == which) & (half == bit))
                def _():
                    for copy in copies(chunk, index):
                        getattr(copy, act)()


def pack_kernel(stream, own_ref, got_ref, out_ref, all_ref):
    stream.join(all_ref, own_ref, got_ref)
    rows = all_ref.shape[1]
    for chunk in range(all_ref.shape[0]):
        out_ref[chunk * rows : (chunk + 1) * rows, :] = all_ref[chunk]


def unpack_kernel(
    half_rows, pack_ref, pack_got_ref,
    gain_ref, ffn_gain_ref, dwq_ref, dwk_ref, dwv_ref, dwo_ref, all_ref,
):
    width, kv_width = dwq_ref.shape[0], dwk_ref.shape[0]
    core = lax.axis_index("tensor")
    for which, ref in ((core, pack_ref), (1 - core, pack_got_ref)):
        all_ref[which] = ref[:half_rows, :width].astype(F32)
    rest = half_rows - width
    dwq_ref[...] = all_ref[0, :width]
    dwo_ref[:rest, :] = all_ref[0, width:]
    dwo_ref[rest:, :] = all_ref[1, : width - rest]
    dwk_ref[...] = all_ref[1, width - rest : width - rest + kv_width]
    dwv_ref[...] = all_ref[1, width - rest + kv_width :]
    rows = pack_ref[:width, width:].astype(F32).T
    for at, ref in ((0, gain_ref), (1, ffn_gain_ref)):
        ref[...] = rows[at : at + 1, :].reshape(width)


def tie(*arrays):
    return lax.optimization_barrier(arrays)


def orders_of(n):
    bits = list(range(n.bit_length() - 1))
    across = bits[-1]
    halved = bits[:-1]
    if len(halved) < 3:
        return [((halved, halved), across, (halved, halved))] * 2
    rest = halved[3:]
    ffn = (([0, 2, 1] + rest, [1, 0, 2] + rest), across, (rest + [1, 2, 0], rest + [2, 0, 1]))
    attention = (([1, 0, 2] + rest, [1, 0, 2] + rest), across, (rest + [0, 1, 2], rest + [1, 0, 2]))
    return [ffn, attention]


def position_tables(length):
    places = np.arange(length, dtype=np.float32)
    inverse = np.float32(10000.0) ** (np.arange(HALF, dtype=np.float32) * np.float32(-2.0 / HEAD_DIM))
    angles = inverse.astype(np.float32)[:, None] * places[None, :]
    return jnp.asarray(np.cos(angles)), jnp.asarray(np.sin(angles))


def per_device(
    sizes, tokens, segments, cotangent, attn_gain, w_query, w_key, w_value, w_out, ffn_gain,
    w_gate, w_up, w_down,
):
    _, half, width = tokens.shape
    kv_width = KV_HEADS * HEAD_DIM
    hidden = w_gate.shape[1]
    n = sizes[0]
    core = lax.axis_index("tensor")
    cut = half // 2
    tokens, cotangent = tokens[0].T, cotangent[0].T
    w_key, w_value, w_down = w_key.T, w_value.T, w_down.T

    tokens_got = swap(tokens)
    all_tables = position_tables(segments.shape[1])
    where = (segments, segments)
    projections = (w_query, w_key, w_value)

    act = shape((width, half), F32)
    low = shape((width, half), BF16)
    kv = shape((2 * kv_width, half), BF16)
    kv_f32 = shape((2 * kv_width, half), F32)
    wide = shape((2 * hidden, half), BF16)
    thin = shape((hidden, half), BF16)
    column = shape((width, 1), F32)
    square = shape((width, width), F32)
    heads_f32 = pltpu.VMEM((HEADS, BLOCK, BLOCK), F32)
    heads_low = pltpu.VMEM((HEADS, BLOCK, BLOCK), BF16)
    key_scratch = pltpu.VMEM((2 * KV_HEADS, half, HEAD_DIM), BF16)
    masks_shape = shape((2, 2, BLOCK, BLOCK), F32)
    rows_f32 = shape((16, half), F32)
    act_scratch = pltpu.VMEM((width, half), F32)
    low_scratch = pltpu.VMEM((width, half), BF16)

    def attend(query, kv_own, kv_other, masks=None):
        state, made = (), []
        for own, kv_part in ((True, kv_own), (False, kv_other)):

            def kernel(*refs, own=own):
                attend_kernel(own, *refs)

            state, new = run(
                kernel,
                where + (query, kv_part, tuple(state), () if masks is None else (masks[len(made)],)),
                ((rows_f32, rows_f32, act) if own else (low, rows_f32),
                 (masks_shape,) if masks is None else ()),
                [pltpu.VMEM((2, KV_HEADS, HEAD_DIM + 16, BLOCK), BF16),
                 pltpu.VMEM((4 * BLOCK, 8), jnp.int32), heads_f32],
                smem=1,
                name="attend_own" if own else "attend_other",
                us=4,
            )
            made.append(new[0] if masks is None else masks[len(made)])
        return (*state, made)

    def attend_back(query, kv_own, kv_other, masks, ctx, lse, grad, us=5):
        more, dq = (ctx,), ()
        for own, kv_part, dkv in ((False, kv_other, kv), (True, kv_own, kv_f32)):

            def kernel(*refs, own=own):
                attend_back_kernel(own, *refs)

            (outs,) = run(
                kernel,
                (segments, query, kv_part, masks[0 if own else 1], lse, grad, more),
                ((act, dkv),) if own else ((act, rows_f32, dkv),),
                [key_scratch, heads_f32, heads_low, heads_low,
                 pltpu.VMEM((2, 2 * kv_width, BLOCK), F32)],
                smem=1,
                name="attend_back_own" if own else "attend_back_other",
                us=us,
                update=dq,
            )
            if not own:
                dq, more = outs[:1], outs[1:2]
                got = swap(outs[2])
        return outs[0], outs[1], got

    table = shape((HALF, half), F32)
    tile_low, tile_kv = shape((width, cut), BF16), shape((2 * kv_width, cut), BF16)
    x_half = pltpu.VMEM((width, cut), F32)
    *halves, gain_col, ffn_gain_col, cos_table, sin_table, wq, wk, wv = run(
        first_kernel,
        in_hbm((tokens,) + projections + all_tables + (attn_gain, ffn_gain)),
        (tile_low, tile_low, tile_low, tile_kv, column, column, table, table)
        + tuple(shape(weight.shape, BF16) for weight in projections),
        [x_half, pltpu.VMEM((width,), F32), pltpu.VMEM((width,), F32),
         pltpu.SemaphoreType.DMA((10,))],
        hbm=8,
        name="first",
        us=2,
    )
    projections, tables = (wq, wk, wv), (cos_table, sin_table)
    (x1, normed1, query1, kv1), = run(
        second_kernel,
        (tokens_got, tuple(halves), gain_col) + tables + projections,
        ((low, low, low, kv),),
        [x_half],
        name="second",
        us=1,
    )
    kv1, cot_sent = tie(kv1, cotangent)
    kv1_other = swap(kv1)
    gate_pair = (w_gate, swap(w_gate))
    up_pair = (w_up, swap(w_up))
    down_pair = (w_down, swap(w_down))
    cot_got = swap(cot_sent)
    ctx1, lse1, masks = attend(query1, kv1, kv1_other)
    mid1, ffn1, gate1, up1, x2, normed2, query2, kv2 = run(
        middle_kernel,
        (x1, ctx1, w_out, ffn_gain_col, gate_pair, up_pair, down_pair, gain_col)
        + projections + tables,
        (act, low, wide, wide, act, low, low, kv),
        [pltpu.VMEM(wide.shape, BF16)],
        name="middle",
        us=6,
    )
    kv2_other = swap(kv2)
    ctx2, lse2, _ = attend(query2, kv2, kv2_other, masks)
    (
        mid2, cot, ffn2, kept2_own, kept2_other, grad_mid2, grad_mid_low2, grad_ctx2, dffn_gain2,
    ) = run(
        turn_kernel,
        (x2, ctx2, w_out, ffn_gain_col, gate_pair, up_pair, down_pair, cotangent, cot_got),
        (act, low, low, (thin,) * 3, (thin,) * 3, act, low, low, column),
        [act_scratch],
        name="turn",
        us=9,
    )
    dq2, dkv_own2, dkv_got2 = attend_back(query2, kv2, kv2_other, masks, ctx2, lse2, grad_ctx2)
    pad = 8 * max(n // 2, 1)
    stack_rows = -(-3 * width // pad) * pad
    stack_shape = shape((stack_rows, hidden), BF16)
    pre = shape((width + 2 * kv_width, half), BF16)
    dpre2, dgain2, low1, gstream, dffn, stack_other = run(
        other_kernel,
        (dq2, dkv_own2, dkv_got2, x2, grad_mid2, gain_col) + projections + tables
        + (ffn1, gate1, up1, gate_pair[1], up_pair[1], down_pair[1], ffn2, cot, kept2_other),
        (pre, column, low, act, act, stack_shape),
        [act_scratch, pltpu.VMEM((3,) + thin.shape, BF16)],
        name="other",
        us=8,
    )
    stack_got = swap(stack_other)
    stack_own, dffn = run(
        own_kernel,
        (low1, dffn, ffn1, gate1, up1, gate_pair[0], up_pair[0], down_pair[0],
         ffn2, cot, kept2_own),
        (stack_shape, act),
        [pltpu.VMEM((3,) + thin.shape, BF16)],
        name="own",
        us=6,
    )
    ffn_orders, pack_orders = orders_of(n)
    ffn = Stream("ffn", (stack_own, stack_got), sizes, ffn_orders)
    token = ffn.step(stack_own)
    grad_mid1, grad_mid_low1, grad_ctx1, dffn_gain = run(
        context_kernel,
        (gstream, dffn, mid1, w_out, ffn_gain_col, dffn_gain2),
        (act, low, low, column),
        after=token,
        name="context",
        us=0,
    )
    dq1, dkv_own1, dkv_got1 = attend_back(query1, kv1, kv1_other, masks, ctx1, lse1, grad_ctx1, 0)
    rows = -(-(2 * width + 2 * kv_width) // 2 // pad) * pad
    lanes = -(-width // 128) * 128
    lanes = lanes if lanes - width >= 2 else lanes + 128
    half_stack = shape((rows, lanes), BF16)
    tile_act = shape((width, cut), F32)
    dnormed1, pack_own, pack_other = run(
        last_kernel,
        (dq1, dkv_own1, dkv_got1, x1) + projections + tables
        + (dpre2, (normed1, normed2), (ctx1, ctx2), (grad_mid_low1, grad_mid_low2),
           dgain2, dffn_gain),
        (act, half_stack, half_stack),
        [pltpu.VMEM(pre.shape, BF16), act_scratch,
         pltpu.VMEM((width, 1), F32), pltpu.VMEM((2, rows, lanes), BF16)],
        name="last",
        us=0,
    )
    pack = Stream("pack", (pack_own, swap(pack_other)), sizes, pack_orders)
    token = pack_own
    for index, which in enumerate("fafafaafafafa"):
        token = (ffn if which == "f" else pack).step(token)
        if index == 1:
            ((output, output_sent),) = run(
                result_kernel,
                (mid2, (kept2_own[0], kept2_other[0]), down_pair),
                ((tile_low, tile_low),), after=token, name="result", us=0,
            )
            token = (token, output)
        if index == 3:
            ((grad_input, grad_input_sent),) = run(
                input_kernel,
                (x1, gain_col, dnormed1, grad_mid1), ((tile_act, tile_act),),
                [act_scratch, act_scratch, pltpu.VMEM((width, 1), F32)],
                after=token, name="input", us=0,
            )
            token = (token, grad_input)
        if index == 11:
            output = jnp.concatenate([output, swap(output_sent)], axis=1)
            grad_input = jnp.concatenate([grad_input, swap(grad_input_sent)], axis=1)
            token = (token, output, grad_input)
    while not (ffn.done and pack.done):
        token = pack.step(ffn.step(token))

    def finish(mine, part, after, update, us):
        def kernel(part_ref, *refs):
            finish_kernel(ffn, mine, part_ref, refs[:3], *refs[3:])

        count, rows, columns = part.shape
        *outs, token = run(
            kernel, (part,), (shape((width, hidden), F32),) * 3 + (shape((8, 128), F32),),
            [pltpu.VMEM(part.shape, F32), pltpu.SemaphoreType.DMA((count, rows // width + 2))],
            after=after, name="finish", us=us, hbm_outs=3, update=update,
        )
        return outs, token

    finished, token = finish(True, ffn.terms[0], token, (), 0)

    def kernel(own_ref, got_ref, out_ref, all_ref):
        pack_kernel(pack, own_ref, got_ref, out_ref, all_ref)

    (pack_sum,) = run(
        kernel, tuple(pack.terms), (half_stack,),
        [pltpu.VMEM((pack.chunks, rows // pack.chunks, lanes), BF16)],
        after=token, name="pack_all", us=0,
    )
    (dw_gate, dw_up, dw_down), token = finish(False, ffn.terms[1], pack_sum, finished, 3)
    half_rows = width + kv_width

    def kernel(*refs):
        unpack_kernel(half_rows, *refs)

    kv_square = shape((kv_width, width), F32)
    vector = shape((width,), F32)
    dgain, dffn_gain, dw_query, dw_key, dw_value, dw_out = run(
        kernel,
        (pack_sum, swap(pack_sum)),
        (vector, vector, square, kv_square, kv_square, square),
        [pltpu.VMEM((2, half_rows, width), F32)],
        after=token,
        name="unpack",
        us=2,
    )
    return (
        output.T[None],
        grad_input.T[None],
        dgain,
        dw_query,
        dw_key.T,
        dw_value.T,
        dw_out,
        dffn_gain,
        dw_gate,
        dw_up,
        dw_down.T,
    )


def solution(mesh):
    sizes = (mesh.shape["dp"], mesh.shape["tensor"])

    def local(*args):
        return per_device(sizes, *args)

    split = P("dp", "tensor", None)
    in_specs = (
        split, P("dp", None), split, P(), P(), P(), P(), P(), P(),
        P(None, "tensor"), P(None, "tensor"), P("tensor", None),
    )
    out_specs = (
        split, split, P(), P(), P(), P(), P(), P(),
        P(None, "tensor"), P(None, "tensor"), P("tensor", None),
    )
    return jax.shard_map(
        local, mesh=mesh, in_specs=in_specs, out_specs=out_specs, check_vma=False
    )
```
